32 devices in a mesh: ctx: 8 (over z, core), pipe: 2 (over y), tp: 2 (over x).
Axes of the slice: x: 2, y: 2, z: 4, core: 2. Of those that a mesh axis runs over, the one named last changes fastest.
Arguments:
- section_inputs: bfloat16 [2, 4, 1, 1024, 1024], P('pipe', None, None, 'ctx', 'tp'), may hold values from -6 to 6
- doc_starts: int32 [4, 1, 4], replicated, may hold values from 0 to 1023, as said below
- ln_gains: float32 [2, 2, 1024], P('pipe')
- ln_shifts: float32 [2, 2, 1024], P('pipe'), may hold values from -3 to 3
- qkv_weight: bfloat16 [2, 1024, 3072], P('pipe', None, 'tp'), may hold values from -0.1875 to 0.1875
- qkv_bias: float32 [2, 3072], P('pipe', 'tp'), may hold values from -3 to 3
- feature_weight: float32 [2, 16, 64], P('pipe', 'tp'), may hold values from 0.25 to 4
- dense_weight: bfloat16 [2, 1024, 1024], P('pipe', 'tp'), may hold values from -1.5 to 1.5
- out_bias: float32 [2, 1024], P('pipe', 'tp'), may hold values from -3 to 3
- up_weight: bfloat16 [2, 1024, 4096], P('pipe', None, 'tp')
- up_bias: float32 [2, 4096], P('pipe', 'tp'), may hold values from -3 to 3
- down_weight: bfloat16 [2, 4096, 1024], P('pipe', 'tp'), may hold values from -0.09375 to 0.09375
Outputs:
- section_ends: float32 [2, 4, 1, 1024, 1024], P('pipe', None, None, 'ctx', 'tp')
- ln_gain_grad: float32 [2, 2, 1024], P('pipe', None, 'tp')
- ln_shift_grad: float32 [2, 2, 1024], P('pipe', None, 'tp')
- qkv_weight_grad: float32 [2, 1024, 3072], P('pipe', None, 'tp')
- qkv_bias_grad: float32 [2, 3072], P('pipe', 'tp')
- feature_weight_grad: float32 [2, 16, 64], P('pipe', 'tp')
- dense_weight_grad: float32 [2, 1024, 1024], P('pipe', 'tp')
- out_bias_grad: float32 [2, 1024], P('pipe', 'tp')
- up_weight_grad: float32 [2, 1024, 4096], P('pipe', None, 'tp')
- up_bias_grad: float32 [2, 4096], P('pipe', 'tp')
- down_weight_grad: float32 [2, 4096, 1024], P('pipe', 'tp')
The draws below stay inside these ranges and needn't reach their ends.
Inputs may be any that keep to these rules, and one draw needn't show every extreme that they name: `doc_starts`: in each row the 4 offsets rise strictly from 0 and stay below 1024; each is the first token of a document that runs to the next offset or to the row's end.
All inputs are finite; a program needn't handle non-finite values.
Results may differ from the reference program's by a relative error of at most 0.012.
The reference program's roundings to bfloat16 on the way count: a program that leaves them out, or rounds other values in their place, can miss the bound.
Values may be sent and summed in bfloat16 or wider, within the bound.
A program may use at most 320 MiB of HBM per device.

```python
import math
import jax
import jax.numpy as jnp
from jax import lax

D = 1024
HEADS = 16
HD = 64
ROT = 16
FF = 4096
FEAT = 64
BLOCK = 64
NDOC = 4
MB = 4
ROWS = 1
TOK_DEV = 128
SEQ_LEN = 1024


def draw_doc_starts(key, part):
    key = jax.random.fold_in(key, 7)
    key_rows = jax.random.fold_in(key, 0)
    key_head = jax.random.fold_in(key, 1)
    key_pick = jax.random.fold_in(key, 3)
    row_count = MB * ROWS
    row_keys = jax.random.split(key_rows, row_count)

    def pick_general(row_key):
        chosen = jax.random.permutation(row_key, SEQ_LEN - 1)[:NDOC - 1] + 1
        return jnp.sort(chosen).astype(jnp.int32)
    general = jax.vmap(pick_general)(row_keys)
    head_part = jnp.sort(jax.random.permutation(key_head, TOK_DEV - 1)[:NDOC - 2] + 1).astype(jnp.int32)
    tail_part = jnp.full((1,), SEQ_LEN - 1, jnp.int32)
    special = jnp.concatenate([head_part, tail_part])
    spanning = jax.random.randint(key_pick, (), 0, row_count)
    chosen_rows = jnp.where((jnp.arange(row_count) == spanning)[:, None], special[None, :], general)
    zero_column = jnp.zeros((row_count, 1), jnp.int32)
    return jnp.concatenate([zero_column, chosen_rows.astype(jnp.int32)], axis=1).reshape(MB, ROWS, NDOC)


def draw_ln_gains(key, part):
    key = jax.random.fold_in(key, 11)
    feature_pos = jnp.arange(D, dtype=jnp.float32) / D - 0.5
    rising = jnp.exp(math.log(3.0) * feature_pos)
    rough = jax.random.uniform(key, (2, 2, D), jnp.float32, 0.75, 1.25)
    return (rising[None, None, :] * rough).astype(jnp.float32)


def draw_up_weight(key, part):
    key = jax.random.fold_in(key, 13)
    key_own, key_common = jax.random.split(key)
    own = jax.random.normal(key_own, (2, D, FF), jnp.float32)
    common = jax.random.normal(key_common, (2, 1, FF), jnp.float32)
    return ((own + common) / math.sqrt(D)).astype(jnp.bfloat16)


def levels(rng, shape, cuts, low, largest):
    level = 1.0
    for dim, shards_of in cuts:
        heights = jax.random.uniform(jax.random.fold_in(jax.random.fold_in(rng, 6), dim), (shards_of,), jnp.float32, low / len(cuts), largest / len(cuts))
        level = level * jnp.repeat(jnp.exp(heights), shape[dim] // shards_of).reshape((-1,) + (1,) * (len(shape) - 1 - dim))
    return level


def scatter_about(stream_key, extent, scale, bound, cuts=(), held_as=jnp.bfloat16):
    factor_of = levels(stream_key, extent, cuts, -0.22, 0.18) if cuts else 1.0
    drawn = jax.random.normal(stream_key, extent, jnp.float32) * scale * factor_of
    return jnp.minimum(jnp.maximum(drawn, -bound), bound).astype(held_as)


def setup_inputs(seed: int = 0) -> dict:
    key_list = jax.random.split(jax.random.key(seed), 13)
    section_inputs = scatter_about(key_list[0], (2, MB, ROWS, SEQ_LEN, D), 1.0, 6.0, ((0, 2), (3, 8), (4, 2)))
    doc_starts = draw_doc_starts(jax.random.fold_in(key_list[12], 71), 0)
    ln_gains = draw_ln_gains(jax.random.fold_in(key_list[12], 71), 0)
    ln_shifts = scatter_about(key_list[3], (2, 2, D), 0.5, 3.0, ((0, 2),), jnp.float32)
    qkv_weight = scatter_about(key_list[4], (2, D, HEADS * 3 * HD), D ** -0.5, 0.1875, ((0, 2), (2, 2)))
    qkv_bias = scatter_about(key_list[5], (2, HEADS * 3 * HD), 0.5, 3.0, ((0, 2), (1, 2)), jnp.float32)
    feature_weight = jnp.clip(jnp.exp(math.log(4.0) - 2.7725887 * jax.random.uniform(key_list[6], (2, HEADS, FEAT), jnp.float32) ** levels(key_list[6], (2, HEADS, FEAT), ((0, 2), (1, 2)), -0.2, 0.2)), 0.25, 4.0)
    dense_weight = scatter_about(key_list[7], (2, HEADS * HD, D), (HD // 4) ** -0.5, 1.5, ((0, 2), (1, 2)))
    out_bias = scatter_about(key_list[8], (2, D), 0.5, 3.0, ((0, 2), (1, 2)), jnp.float32)
    up_weight = draw_up_weight(jax.random.fold_in(key_list[12], 71), 0)
    up_bias = scatter_about(key_list[10], (2, FF), 0.5, 3.0, ((0, 2), (1, 2)), jnp.float32)
    down_weight = scatter_about(key_list[11], (2, FF, D), FF ** -0.5, 0.09375, ((0, 2), (1, 2)))
    return {"section_inputs": section_inputs, "doc_starts": doc_starts, "ln_gains": ln_gains, "ln_shifts": ln_shifts, "qkv_weight": qkv_weight, "qkv_bias": qkv_bias, "feature_weight": feature_weight, "dense_weight": dense_weight, "out_bias": out_bias, "up_weight": up_weight, "up_bias": up_bias, "down_weight": down_weight}


HIGH = lax.Precision.HIGHEST
norm_eps = 1e-05

@jax.custom_vjp
def low(v):
    return lax.optimization_barrier(v.astype(jnp.bfloat16)).astype(jnp.float32)

@jax.custom_vjp
def low_back(v):
    return v

def low_keep(v):
    return (low(v), None)

def low_pass(kept, grad):
    return (grad,)

def back_keep(v):
    return (v, None)

def back_low(kept, grad):
    return (low(grad),)
low.defvjp(low_keep, low_pass)
low_back.defvjp(back_keep, back_low)

def feature_table():
    index_rows = jnp.arange(HD, dtype=jnp.int32)[:, None]
    index_cols = jnp.arange(HD, dtype=jnp.int32)[None, :]
    cosine = jnp.cos(math.pi * (index_rows.astype(jnp.float32) + 0.5) * index_cols.astype(jnp.float32) / HD)
    scaling = jnp.where(index_cols == 0, math.sqrt(1.0 / HD), math.sqrt(2.0 / HD))
    lattice_index = (jnp.arange(HD, dtype=jnp.int32)[:, None] + 1) * (17 * jnp.arange(FEAT, dtype=jnp.int32)[None, :] + 5) % 257
    lattice = math.sqrt(2.0) * jnp.cos(2.0 * math.pi * lattice_index.astype(jnp.float32) / 257.0)
    return jnp.dot(cosine * scaling, lattice, precision=HIGH) / math.sqrt(HD)

def layer_norm(values, gain_row, shift_row):
    centered = values - lax.optimization_barrier(jnp.mean(values, axis=-1, keepdims=True))
    spread = lax.optimization_barrier(jnp.mean(centered * centered, axis=-1, keepdims=True))
    return centered * lax.rsqrt(spread + norm_eps) * gain_row + shift_row

def rotate(values, rot_cos, rot_sin):
    half_rot = ROT // 2
    first_half = values[..., :half_rot]
    second_half = values[..., half_rot:ROT]
    return jnp.concatenate([first_half * rot_cos - second_half * rot_sin, second_half * rot_cos + first_half * rot_sin, values[..., ROT:]], axis=-1)

def block_step(carried, pieces):
    state_sum, key_total = carried
    query_feat, key_feat, value_low, seg_ids, resets = pieces
    causal = jnp.arange(BLOCK)[:, None] >= jnp.arange(BLOCK)[None, :]
    keep_mask = (causal & (seg_ids[:, None] == seg_ids[None, :])).astype(jnp.float32)
    enters = ((seg_ids == seg_ids[0]) & (resets[0] == 0)).astype(jnp.float32)
    leaves = (seg_ids == seg_ids[-1]).astype(jnp.float32)
    passing = enters[-1]
    scores = jnp.einsum('ihf,jhf->hij', query_feat, key_feat, precision=HIGH) * keep_mask[None]
    numerator = jnp.einsum('hij,jhd->ihd', low(scores), value_low, precision=HIGH)
    numerator = numerator + enters[:, None, None] * jnp.einsum('ihf,hfd->ihd', query_feat, low(state_sum), precision=HIGH)
    denominator = lax.optimization_barrier(jnp.sum(scores, axis=-1)).T + enters[:, None] * jnp.einsum('ihf,hf->ih', query_feat, key_total, precision=HIGH)
    output = numerator / denominator[:, :, None]
    weighted = key_feat * leaves[:, None, None]
    new_state = passing * state_sum + jnp.einsum('jhf,jhd->hfd', weighted, value_low, precision=HIGH)
    new_total = passing * key_total + lax.optimization_barrier(jnp.sum(weighted, axis=0))
    return ((new_state, new_total), output)

def linear_attention(query_feat, key_feat, value_low, seg_ids, resets):
    blocks = SEQ_LEN // BLOCK
    pieces = (query_feat.reshape(blocks, BLOCK, HEADS, FEAT), key_feat.reshape(blocks, BLOCK, HEADS, FEAT), value_low.reshape(blocks, BLOCK, HEADS, HD), seg_ids.reshape(blocks, BLOCK), resets.reshape(blocks, BLOCK))
    initial = (jnp.zeros((HEADS, FEAT, HD), jnp.float32), jnp.zeros((HEADS, FEAT), jnp.float32))
    final_carry, outputs = lax.scan(jax.checkpoint(block_step), initial, pieces)
    return outputs.reshape(SEQ_LEN, HEADS, HD)

def run_layer(inputs, weights, seg_ids, resets, rot_cos, rot_sin, exp_table):
    gain_rows, shift_rows, qkv_weight, qkv_bias, feat_weight, dense_weight, out_bias, up_weight, up_bias, down_weight = weights
    first_norm = low(layer_norm(inputs, gain_rows[0], shift_rows[0]))
    second_norm = low(layer_norm(inputs, gain_rows[1], shift_rows[1]))
    projected = low_back(jnp.dot(first_norm, qkv_weight, precision=HIGH) + qkv_bias)
    projected = projected.reshape(SEQ_LEN, HEADS, 3, HD)
    queries = rotate(projected[:, :, 0], rot_cos, rot_sin)
    keys_rot = rotate(projected[:, :, 1], rot_cos, rot_sin)
    query_feat = low(feat_weight * jnp.exp(jnp.einsum('thd,df->thf', queries, exp_table, precision=HIGH)))
    key_feat = low(feat_weight * jnp.exp(jnp.einsum('thd,df->thf', keys_rot, exp_table, precision=HIGH)))
    value_low = low(projected[:, :, 2])
    attended = linear_attention(query_feat, key_feat, value_low, seg_ids, resets)
    attended = low(low_back(attended)).reshape(SEQ_LEN, HEADS * HD)
    pre_act = low_back(jnp.dot(second_norm, up_weight, precision=HIGH) + up_bias)
    hidden = low(jax.nn.gelu(pre_act, approximate=False))
    return inputs + jnp.dot(attended, dense_weight, precision=HIGH) + jnp.dot(hidden, down_weight, precision=HIGH) + out_bias

def whole_row(param_set, row_input, starts):
    positions = jnp.arange(SEQ_LEN, dtype=jnp.int32)
    seg_ids = lax.optimization_barrier(jnp.sum((starts[None, :] <= positions[:, None]).astype(jnp.int32), axis=1)) - 1
    resets = jnp.any(starts[None, :] == positions[:, None], axis=1).astype(jnp.int32)
    inv_freq = 10000.0 ** (-(2.0 * jnp.arange(ROT // 2).astype(jnp.float32)) / ROT)
    angles = positions.astype(jnp.float32)[:, None] * inv_freq[None, :]
    rot_cos = jnp.cos(angles)[:, None, :]
    rot_sin = jnp.sin(angles)[:, None, :]
    exp_table = feature_table()
    layer_zero = tuple((member[0] for member in param_set))
    layer_one = tuple((member[1] for member in param_set))
    first_out = run_layer(row_input, layer_zero, seg_ids, resets, rot_cos, rot_sin, exp_table)
    passed = low(low_back(first_out))
    return run_layer(passed, layer_one, seg_ids, resets, rot_cos, rot_sin, exp_table)

def reference(section_inputs, doc_starts, ln_gains, ln_shifts, qkv_weight, qkv_bias, feature_weight, dense_weight, out_bias, up_weight, up_bias, down_weight):
    params = tuple((member.astype(jnp.float32) for member in (ln_gains, ln_shifts, qkv_weight, qkv_bias, feature_weight, dense_weight, out_bias, up_weight, up_bias, down_weight)))
    inputs_all = section_inputs[0].astype(jnp.float32).reshape(MB * ROWS, SEQ_LEN, D)
    cotangent = section_inputs[1].astype(jnp.float32).reshape(MB * ROWS, SEQ_LEN, D)
    starts_all = doc_starts.reshape(MB * ROWS, NDOC)

    def forward(param_set, row_inputs):

        def one_row(row_pair):
            return whole_row(param_set, row_pair[0], row_pair[1])
        return lax.map(jax.checkpoint(one_row), (row_inputs, starts_all))
    outputs, pullback = jax.vjp(forward, params, inputs_all)
    param_grads, input_grad = pullback(cotangent)
    section_ends = jnp.stack([input_grad, outputs]).reshape(2, MB, ROWS, SEQ_LEN, D)
    return (section_ends, param_grads[0], param_grads[1], param_grads[2], param_grads[3], param_grads[4], param_grads[5], param_grads[6], param_grads[7], param_grads[8], param_grads[9])
```

```python
from functools import partial
import math

import jax
import jax.numpy as jnp
from jax import lax
from jax.experimental import pallas as pl
from jax.experimental.pallas import tpu as pltpu
from jax.sharding import PartitionSpec as P

D = 1024
HD = 64
ROT = 16
FEAT = 64
MB = 4
ROWS = 1
NDOC = 4
PAIR = 2 * HD

BF = jnp.bfloat16
F32 = jnp.float32
HIGHEST = lax.Precision.HIGHEST
norm_eps = 1e-05
VMEM_LIMIT = 56 * 1024 * 1024


def feature_table():
    index_rows = jnp.arange(HD, dtype=jnp.int32)[:, None]
    index_cols = jnp.arange(HD, dtype=jnp.int32)[None, :]
    cosine = jnp.cos(
        math.pi * (index_rows.astype(F32) + 0.5) * index_cols.astype(F32) / HD
    )
    scaling = jnp.where(index_cols == 0, math.sqrt(1.0 / HD), math.sqrt(2.0 / HD))
    lattice_index = (
        (jnp.arange(HD, dtype=jnp.int32)[:, None] + 1)
        * (17 * jnp.arange(FEAT, dtype=jnp.int32)[None, :] + 5)
        % 257
    )
    lattice = math.sqrt(2.0) * jnp.cos(2.0 * math.pi * lattice_index.astype(F32) / 257.0)
    return jnp.dot(cosine * scaling, lattice, precision=HIGHEST) / math.sqrt(HD)


def table_pair():
    table = feature_table()
    zero = jnp.zeros_like(table)
    both = jnp.concatenate(
        [jnp.concatenate([table, zero], 1), jnp.concatenate([zero, table], 1)], 0
    )
    high = lax.reduce_precision(both, 8, 7).astype(BF)
    return high, (both - high.astype(F32)).astype(BF)


def rotary_tables(place, tokens):
    half = ROT // 2
    positions = place * tokens + jnp.arange(tokens, dtype=jnp.int32)
    inv_freq = 10000.0 ** (-(2.0 * jnp.arange(half).astype(F32)) / ROT)
    angles = positions.astype(F32)[:, None] * inv_freq[None, :]
    cos, sin = jnp.cos(angles), jnp.sin(angles)
    rest = jnp.ones((tokens, HD - ROT), F32)
    none = jnp.zeros((tokens, half), F32)
    same = jnp.concatenate([cos, cos, rest], 1)
    down = jnp.concatenate([-sin, none, 0.0 * rest], 1)
    up = jnp.concatenate([none, sin, 0.0 * rest], 1)
    return tuple(jnp.concatenate([t, t], 1) for t in (same, down, up))


def dot(a, b, ca=1, cb=0):
    return lax.dot_general(a, b, (((ca,), (cb,)), ((), ())), preferred_element_type=F32)


def split_dot(a, b, cb=0):
    high = a.astype(BF)
    low = (a - high.astype(F32)).astype(BF)
    return dot(high, b, 1, cb) + dot(low, b, 1, cb)


def lane_masks(rows):
    low = lax.broadcasted_iota(jnp.int32, (rows, PAIR), 1) < HD
    first = low.astype(F32)
    return low, first.astype(BF), (1.0 - first).astype(BF)


def count_starts(starts_ref, row, position):
    total = jnp.int32(0)
    for n in range(NDOC):
        total = total + (starts_ref[row, n] <= position).astype(jnp.int32)
    return total


def seg_grid(starts_ref, row, base, shape, dim):
    position = base + lax.broadcasted_iota(jnp.int32, shape, dim)
    total = jnp.zeros(shape, jnp.int32)
    for n in range(NDOC):
        total = total + (starts_ref[row, n] <= position).astype(jnp.int32)
    return total


def causal_mask(starts_ref, row, base, tokens):
    shape = (tokens, tokens)
    same = seg_grid(starts_ref, row, base, shape, 0) == seg_grid(starts_ref, row, base, shape, 1)
    earlier = lax.broadcasted_iota(jnp.int32, shape, 1) <= lax.broadcasted_iota(
        jnp.int32, shape, 0
    )
    rows = lax.broadcasted_iota(jnp.int32, shape, 0) < tokens // 2
    cols = lax.broadcasted_iota(jnp.int32, shape, 1) < tokens // 2
    mask = same & earlier
    return mask.astype(F32), (mask & (rows == cols)).astype(F32)


def middle_state(starts_ref, row, base, tokens, k, v, state_in, total_in, low):
    half = tokens // 2
    end = count_starts(starts_ref, row, base + half - 1)
    passing = (end == count_starts(starts_ref, row, base - 1)).astype(F32)
    seg = seg_grid(starts_ref, row, base, (half, PAIR), 0)
    key = k[:half] * (seg == end).astype(F32).astype(BF)
    state = passing * state_in.astype(F32) + compact(dot(key, v[:half], 0, 0), low)
    total = passing * total_in + jnp.sum(key.astype(F32), 0, keepdims=True)
    later = seg_grid(starts_ref, row, base + half, (half, PAIR), 0)
    return state.astype(BF), total, (later == end).astype(F32)


def entering_mask(starts_ref, row, base, tokens):
    seg = seg_grid(starts_ref, row, base, (tokens, PAIR), 0)
    return (seg == count_starts(starts_ref, row, base - 1)).astype(F32)


def leaving_mask(starts_ref, row, base, tokens):
    seg = seg_grid(starts_ref, row, base, (tokens, PAIR), 0)
    return (seg == count_starts(starts_ref, row, base + tokens - 1)).astype(F32)


def rotate(x, same, down, up):
    half = ROT // 2
    return x * same + pltpu.roll(x, PAIR - half, 1) * down + pltpu.roll(x, half, 1) * up


def rotate_back(x, same, down, up):
    half = ROT // 2
    return x * same + pltpu.roll(x * down, half, 1) + pltpu.roll(x * up, PAIR - half, 1)


def compact(state, low):
    return jnp.where(low[:HD], state[:HD], state[HD:])


def spread(state, first, second):
    return jnp.concatenate([state * first[:HD], state * second[:HD]], 0)


def features_kernel(
    starts_ref, place_ref, norm_ref, weight_ref, bias_ref, feat_ref,
    same_ref, down_ref, up_ref, high_ref, low_ref,
    q_ref, k_ref, v_ref, state_ref, total_ref,
):
    tokens = same_ref.shape[0]
    base = place_ref[0, 0] * tokens
    low, first, second = lane_masks(tokens)
    feat = feat_ref[0]
    for row in range(MB * ROWS):
        here = slice(row * tokens, (row + 1) * tokens)
        proj = dot(norm_ref[here, :], weight_ref[...]) + bias_ref[0]
        c0, c1, c2 = proj[:, :PAIR], proj[:, PAIR : 2 * PAIR], proj[:, 2 * PAIR :]
        query = jnp.where(low, c0, c1)
        key = pltpu.roll(jnp.where(low, c2, c0), HD, 1)
        value = jnp.where(low, c1, c2).astype(BF)
        out = []
        for x in (query, key):
            x = rotate(x, same_ref[...], down_ref[...], up_ref[...])
            arg = split_dot(x, high_ref[...]) + dot(x.astype(BF), low_ref[...])
            out.append((feat * jnp.exp(arg)).astype(BF))
        q_ref[here, :] = out[0]
        k_ref[here, :] = out[1]
        v_ref[here, :] = value
        leaving = leaving_mask(starts_ref, row, base, tokens)
        key_out = out[1] * leaving.astype(BF)
        state_ref[0, row] = compact(dot(key_out, value, 0, 0), low).astype(BF)
        total_ref[0, row : row + 1, :] = jnp.sum(key_out.astype(F32), 0, keepdims=True)


def attend_kernel(
    starts_ref, place_ref, q_ref, k_ref, v_ref, state_ref, total_ref, low_ref, out_ref, den_ref
):
    tokens = q_ref.shape[0] // (MB * ROWS)
    base = place_ref[0, 0] * tokens
    low, first, second = lane_masks(tokens)
    ones = head_ones()
    for row in range(MB * ROWS):
        here = slice(row * tokens, (row + 1) * tokens)
        q, k, v = q_ref[here, :], k_ref[here, :], v_ref[here, :]
        mask, mask_in = causal_mask(starts_ref, row, base, tokens)
        enter = entering_mask(starts_ref, row, base, tokens)
        state, total = state_ref[0, row], total_ref[0, row : row + 1, :]
        middle, _, reach = middle_state(starts_ref, row, base, tokens, k, v, state, total, low)
        half = tokens // 2
        num = jnp.concatenate(
            [
                dot(q[:half] * enter[:half].astype(BF), spread(state, first, second)),
                dot(q[half:] * reach.astype(BF), spread(middle, first, second)),
            ],
            0,
        )
        for head in (first, second):
            scores = dot(q * head, k, 1, 1) * mask_in
            num = num + dot(scores.astype(BF), v * head)
        totals = dot(mask.astype(BF), k) + enter * total
        den = split_dot(q.astype(F32) * totals, ones)
        att = num / den
        low_ref[here, :] = att.astype(BF)
        out_ref[here, :] = att
        den_ref[here, :] = den


def head_ones():
    rows = lax.broadcasted_iota(jnp.int32, (PAIR, PAIR), 0) < HD
    cols = lax.broadcasted_iota(jnp.int32, (PAIR, PAIR), 1) < HD
    return (rows == cols).astype(F32).astype(BF)


def head_spread():
    rows = lax.broadcasted_iota(jnp.int32, (PAIR, 2 * PAIR), 0) < HD
    cols = lax.broadcasted_iota(jnp.int32, (PAIR, 2 * PAIR), 1) < PAIR
    return (rows == cols).astype(F32).astype(BF)


def back_state_kernel(
    starts_ref, place_ref, q_ref, ga_ref, att_ref, den_ref, state_ref, total_ref
):
    tokens = q_ref.shape[0] // (MB * ROWS)
    base = place_ref[0, 0] * tokens
    low, first, second = lane_masks(tokens)
    ones = head_ones()
    for row in range(MB * ROWS):
        here = slice(row * tokens, (row + 1) * tokens)
        grad_num = (ga_ref[here, :].astype(F32) / den_ref[here, :]).astype(BF)
        grad_den = -split_dot(grad_num.astype(F32) * att_ref[here, :], ones)
        enter = entering_mask(starts_ref, row, base, tokens)
        query = q_ref[here, :] * enter.astype(BF)
        state_ref[0, row] = compact(dot(query, grad_num, 0, 0), low)
        total_ref[0, row : row + 1, :] = jnp.sum(grad_den * query.astype(F32), 0, keepdims=True)


def back_kernel(
    starts_ref, place_ref, q_ref, k_ref, v_ref, ga_ref, att_ref, den_ref,
    state_ref, total_ref, later_ref, later_total_ref, feat_ref,
    same_ref, down_ref, up_ref, high_ref, low_ref,
    grad_ref, sums_ref,
):
    tokens = q_ref.shape[0] // (MB * ROWS)
    base = place_ref[0, 0] * tokens
    low, first, second = lane_masks(tokens)
    spreading = head_spread()
    feat_sum = jnp.zeros((1, PAIR), F32)
    bias_sum = [jnp.zeros((1, PAIR), F32) for _ in range(3)]
    for row in range(MB * ROWS):
        here = slice(row * tokens, (row + 1) * tokens)
        q, k, v = q_ref[here, :], k_ref[here, :], v_ref[here, :]
        grad_num = (ga_ref[here, :].astype(F32) / den_ref[here, :]).astype(BF)
        both = -split_dot(grad_num.astype(F32) * att_ref[here, :], spreading)
        dens = (both[:, :PAIR], both[:, PAIR:])
        grad_den = jnp.where(low, dens[0], dens[1])
        mask, mask_in = causal_mask(starts_ref, row, base, tokens)
        enter = entering_mask(starts_ref, row, base, tokens)
        leave = leaving_mask(starts_ref, row, base, tokens)
        state, total = state_ref[0, row], total_ref[0, row : row + 1, :]
        middle, middle_total, reach = middle_state(
            starts_ref, row, base, tokens, k, v, state, total, low
        )
        half = tokens // 2
        gq = jnp.concatenate(
            [
                enter[:half]
                * (dot(grad_num[:half], spread(state, first, second), 1, 1) + grad_den[:half] * total),
                reach
                * (
                    dot(grad_num[half:], spread(middle, first, second), 1, 1)
                    + grad_den[half:] * middle_total
                ),
            ],
            0,
        )
        later = later_ref[0, row]
        later_high = later.astype(BF)
        later_low = spread((later - later_high.astype(F32)).astype(BF), first, second)
        later_high = spread(later_high, first, second)
        gk = leave * (
            dot(v, later_high, 1, 1) + dot(v, later_low, 1, 1) + later_total_ref[0, row : row + 1, :]
        )
        gv = leave * (dot(k, later_high) + dot(k, later_low))
        for head, den in zip((first, second), dens):
            q_head, grad_head = q * head, grad_num * head
            scores = (dot(q_head, k, 1, 1) * mask).astype(BF)
            grad_scores = dot(grad_head, v, 1, 1) + den
            gq = gq + dot((grad_scores * mask_in).astype(BF), k * head)
            gk = gk + dot((grad_scores * mask).astype(BF), q_head, 0, 0)
            gv = gv + dot(scores, grad_head, 0, 0)
        arg_grads = (gq * q.astype(F32), gk * k.astype(F32))
        feat_sum = feat_sum + jnp.sum(arg_grads[0] + arg_grads[1], 0, keepdims=True)
        turned = []
        for x in arg_grads:
            x = split_dot(x, high_ref[...], 1) + dot(x.astype(BF), low_ref[...], 1, 1)
            turned.append(rotate_back(x, same_ref[...], down_ref[...], up_ref[...]))
        dq, dk = turned[0], pltpu.roll(turned[1], HD, 1)
        parts = (jnp.where(low, dq, dk), jnp.where(low, gv, dq), jnp.where(low, dk, gv))
        for n, part in enumerate(parts):
            part = part.astype(BF)
            grad_ref[here, n * PAIR : (n + 1) * PAIR] = part
            bias_sum[n] = bias_sum[n] + jnp.sum(part.astype(F32), 0, keepdims=True)
    sums_ref[0, 0:1, :] = feat_sum / feat_ref[0]
    for n in range(3):
        sums_ref[0, n + 1 : n + 2, :] = bias_sum[n]


SMEM = pl.BlockSpec(memory_space=pltpu.SMEM)


def whole(shape):
    return pl.BlockSpec(shape, lambda p: (0,) * len(shape))


def column(rows, width):
    return pl.BlockSpec((rows, width), lambda p: (0, p))


def stacked(*shape):
    return pl.BlockSpec((1,) + shape, lambda p: (p,) + (0,) * len(shape))


def call(kernel, pairs, in_specs, out_specs, out_shape, flops):
    return pl.pallas_call(
        kernel,
        grid=(pairs,),
        in_specs=in_specs,
        out_specs=out_specs,
        out_shape=out_shape,
        compiler_params=pltpu.CompilerParams(vmem_limit_bytes=VMEM_LIMIT),
        cost_estimate=pl.CostEstimate(flops=flops, bytes_accessed=8 << 20, transcendentals=0),
    )


def shaped(shape, dtype):
    return jax.ShapeDtypeStruct(shape, dtype)


def gather_tp(value):
    if lax.axis_size("tp") != 2:
        return lax.all_gather(value, "tp", axis=1, tiled=True)
    other = lax.ppermute(value, "tp", [(0, 1), (1, 0)])
    return jnp.where(
        lax.axis_index("tp") == 0,
        jnp.concatenate([value, other], 1),
        jnp.concatenate([other, value], 1),
    )


def scatter_tp(value):
    peers = lax.axis_size("tp")
    if peers != 2:
        return lax.psum_scatter(value, "tp", scatter_dimension=1, tiled=True)
    me = lax.axis_index("tp")
    width = value.shape[1] // 2
    left, right = value[:, :width], value[:, width:]
    other = lax.ppermute(jnp.where(me == 0, right, left).astype(BF), "tp", [(0, 1), (1, 0)])
    return jnp.where(me == 0, left, right) + other.astype(F32)


def local(
    section_inputs,
    doc_starts,
    ln_gains,
    ln_shifts,
    qkv_weight,
    qkv_bias,
    feature_weight,
    dense_weight,
    out_bias,
    up_weight,
    up_bias,
    down_weight,
):
    section = lax.axis_index("pipe")
    place = lax.axis_index("ctx")
    peers = lax.axis_size("ctx")
    width = section_inputs.shape[-1]
    tokens = section_inputs.shape[3]
    rows = MB * ROWS
    total = rows * tokens
    heads = feature_weight.shape[1]
    pairs = heads // 2
    gain, shift = ln_gains[0], ln_shifts[0]
    w_qkv, w_dense, w_up, w_down = qkv_weight[0], dense_weight[0], up_weight[0], down_weight[0]
    b_qkv = qkv_bias[0].reshape(pairs, 1, 3 * PAIR)
    b_up, b_out = up_bias[0], out_bias[0]
    feat = feature_weight[0].reshape(pairs, 1, PAIR)
    starts = doc_starts.reshape(rows, NDOC)
    place_in = place.astype(jnp.int32).reshape(1, 1)
    high, low = table_pair()
    same, down, up = rotary_tables(place, tokens)
    tables = (same, down, up, high, low)
    table_specs = [whole((tokens, PAIR))] * 3 + [whole((PAIR, PAIR))] * 2
    state_shape = shaped((pairs, rows, HD, PAIR), BF)
    total_shape = shaped((pairs, 8, PAIR), F32)
    state_spec, total_spec = stacked(rows, HD, PAIR), stacked(8, PAIR)
    low_shape, full_shape = shaped((total, pairs * PAIR), BF), shaped((total, pairs * PAIR), F32)
    unit = 2 * rows * tokens * PAIR * PAIR * pairs

    ends = jnp.arange(peers, dtype=jnp.int32)[:, None, None] * tokens
    seg_last = jnp.sum((starts[None] <= ends + tokens - 1).astype(jnp.int32), 2)
    seg_prev = jnp.sum((starts[None] <= ends - 1).astype(jnp.int32), 2)
    order = jnp.arange(peers)[:, None]
    from_earlier = ((order < place) & (seg_last == seg_prev[place][None])).astype(F32)
    from_later = ((order > place) & (seg_prev == seg_last[place][None])).astype(F32)

    def carried(state, totals, weights):
        states, sums = lax.all_gather((state, totals), "ctx")
        state_in = jnp.sum(states.astype(F32) * weights[:, None, :, None, None], 0)
        padded = jnp.concatenate([weights, jnp.zeros((peers, 8 - rows), F32)], 1)
        total_in = jnp.sum(jnp.where(padded[:, None, :, None] > 0, sums, 0.0), 0)
        return state_in.astype(state.dtype), total_in

    def forward(u_low, own):
        u = u_low.astype(F32)
        centered = u - jnp.mean(u, -1, keepdims=True)
        inv = lax.rsqrt(jnp.mean(centered * centered, -1, keepdims=True) + norm_eps)
        xhat = centered * inv
        first = (xhat * gain[0] + shift[0]).astype(BF)
        second = (xhat * gain[1] + shift[1]).astype(BF)
        q, k, v, state, totals = call(
            features_kernel,
            pairs,
            [SMEM, SMEM, whole((total, D)), column(D, 3 * PAIR), stacked(1, 3 * PAIR),
             stacked(1, PAIR)] + table_specs,
            [column(total, PAIR)] * 3 + [state_spec, total_spec],
            [low_shape] * 3 + [state_shape, total_shape],
            30 * unit,
        )(starts, place_in, first, w_qkv, b_qkv, feat, *tables)
        state_in, total_in = carried(state, totals, from_earlier)
        pre = jnp.dot(second, w_up, preferred_element_type=F32) + b_up
        hidden = jax.nn.gelu(pre, approximate=False).astype(BF)
        mlp = jnp.dot(hidden, w_down, preferred_element_type=F32)
        att_low, att, den = call(
            attend_kernel,
            pairs,
            [SMEM, SMEM] + [column(total, PAIR)] * 3 + [state_spec, total_spec],
            [column(total, PAIR)] * 3,
            [low_shape, full_shape, full_shape],
            8 * unit,
        )(starts, place_in, q, k, v, state_in, total_in)
        part = jnp.dot(att_low, w_dense, preferred_element_type=F32) + mlp
        out = scatter_tp(part) + own.astype(F32) + b_out
        kept = (xhat, inv, first, second, q, k, v, pre, hidden, att_low, att, den, state_in, total_in)
        return out, kept

    def backward(dy, own, kept, want):
        xhat, inv, first, second, q, k, v, pre, hidden, att_low, att, den, state_in, total_in = kept
        ga = lax.dot_general(
            dy, w_dense, (((1,), (1,)), ((), ())), preferred_element_type=F32
        ).astype(BF)
        state, totals = call(
            back_state_kernel,
            pairs,
            [SMEM, SMEM] + [column(total, PAIR)] * 4,
            [state_spec, total_spec],
            [shaped(state_shape.shape, F32), total_shape],
            3 * unit,
        )(starts, place_in, q, ga, att, den)
        later, later_total = carried(state, totals, from_later)
        grad_hidden = lax.dot_general(
            dy, w_down, (((1,), (1,)), ((), ())), preferred_element_type=F32
        )
        cdf = 0.5 * (1.0 + lax.erf(pre * math.sqrt(0.5)))
        slope = cdf + pre * jnp.exp(-0.5 * pre * pre) * (1.0 / math.sqrt(2.0 * math.pi))
        grad_pre = (grad_hidden * slope).astype(BF)
        grad_second = lax.dot_general(
            grad_pre, w_up, (((1,), (1,)), ((), ())), preferred_element_type=F32
        )
        grad_proj, sums = call(
            back_kernel,
            pairs,
            [SMEM, SMEM] + [column(total, PAIR)] * 6
            + [state_spec, total_spec, state_spec, total_spec, stacked(1, PAIR)] + table_specs,
            [column(total, 3 * PAIR), stacked(8, PAIR)],
            [shaped((total, pairs * 3 * PAIR), BF), shaped((pairs, 8, PAIR), F32)],
            20 * unit,
        )(starts, place_in, q, k, v, ga, att, den, state_in, total_in, later, later_total, feat, *tables)
        grad_first = lax.dot_general(
            grad_proj, w_qkv, (((1,), (1,)), ((), ())), preferred_element_type=F32
        )
        both = grad_first * gain[0] + grad_second * gain[1]
        part = inv * (
            both
            - jnp.mean(both, -1, keepdims=True)
            - xhat * jnp.mean(both * xhat, -1, keepdims=True)
        )
        grad_input = scatter_tp(part) + own.astype(F32)
        if not want:
            return grad_input, None

        def weight_grad(a, b):
            return lax.dot_general(
                a, b, (((0,), (0,)), ((), ())), preferred_element_type=F32
            ).astype(BF)

        large = (
            weight_grad(hidden, dy),
            weight_grad(second, grad_pre),
            weight_grad(att_low, dy),
            weight_grad(first, grad_proj),
        )
        norm_sums = jnp.stack(
            [
                jnp.sum(grad_first * xhat, 0),
                jnp.sum(grad_second * xhat, 0),
                jnp.sum(grad_first, 0),
                jnp.sum(grad_second, 0),
            ]
        )
        small = (
            sums[:, 1:4, :].reshape(pairs * 3 * PAIR),
            sums[:, 0, :].reshape(heads, FEAT),
            jnp.sum(own.astype(F32), 0),
            jnp.sum(grad_pre.astype(F32), 0),
        )
        return grad_input, (large, norm_sums, small)

    mine = section_inputs[0].reshape(total, width)
    mine_full = gather_tp(mine)
    y0, _ = forward(mine_full, mine)
    sent = lax.ppermute(y0.astype(BF), "pipe", [(0, 1)])
    own_in = jnp.where(section == 0, mine, sent)
    full_in = jnp.where(section == 0, mine_full, gather_tp(sent))
    y1, kept = forward(full_in, own_in)
    du1, _ = backward(mine_full, mine, kept, False)
    sent = lax.ppermute(du1.astype(BF), "pipe", [(1, 0)])
    own_grad = jnp.where(section == 1, mine, sent)
    full_grad = jnp.where(section == 1, mine_full, gather_tp(sent))
    du0, (large, norm_sums, small) = backward(full_grad, own_grad, kept, True)
    g_down, g_up, g_dense, g_qkv = (
        g.astype(F32) for g in lax.psum(large, "ctx")
    )
    norm_sums = lax.psum(norm_sums, ("ctx", "tp"))
    norm_sums = lax.dynamic_slice_in_dim(norm_sums, lax.axis_index("tp") * width, width, 1)
    g_qkv_bias, g_feat, g_out_bias, g_up_bias = lax.psum(small, "ctx")
    section_ends = jnp.where(section == 0, du0, y1).reshape(1, MB, ROWS, tokens, width)
    grads = (
        norm_sums[:2], norm_sums[2:], g_qkv, g_qkv_bias, g_feat, g_dense, g_out_bias,
        g_up, g_up_bias, g_down,
    )
    return (section_ends,) + tuple(g[None] for g in grads)


def solution(mesh):
    in_specs = (
        P("pipe", None, None, "ctx", "tp"),
        P(),
        P("pipe", None, None),
        P("pipe", None, None),
        P("pipe", None, "tp"),
        P("pipe", "tp"),
        P("pipe", "tp", None),
        P("pipe", "tp", None),
        P("pipe", "tp"),
        P("pipe", None, "tp"),
        P("pipe", "tp"),
        P("pipe", "tp", None),
    )
    out_specs = (
        P("pipe", None, None, "ctx", "tp"),
        P("pipe", None, "tp"),
        P("pipe", None, "tp"),
        P("pipe", None, "tp"),
        P("pipe", "tp"),
        P("pipe", "tp", None),
        P("pipe", "tp", None),
        P("pipe", "tp"),
        P("pipe", None, "tp"),
        P("pipe", "tp"),
        P("pipe", "tp", None),
    )
    return jax.shard_map(local, mesh=mesh, in_specs=in_specs, out_specs=out_specs, check_vma=False)
```

```python
from functools import partial
import math

import jax
import jax.numpy as jnp
from jax import lax
from jax.experimental import pallas as pl
from jax.experimental.pallas import tpu as pltpu
from jax.sharding import PartitionSpec as P

D = 1024
HD = 64
ROT = 16
FEAT = 64
MB = 4
ROWS = 1
NDOC = 4
PAIR = 2 * HD

BF = jnp.bfloat16
F32 = jnp.float32
HIGHEST = lax.Precision.HIGHEST
norm_eps = 1e-05
VMEM_LIMIT = 56 * 1024 * 1024
REDUCE_LIMIT = 60 * 1024 * 1024


def feature_table():
    index_rows = jnp.arange(HD, dtype=jnp.int32)[:, None]
    index_cols = jnp.arange(HD, dtype=jnp.int32)[None, :]
    cosine = jnp.cos(
        math.pi * (index_rows.astype(F32) + 0.5) * index_cols.astype(F32) / HD
    )
    scaling = jnp.where(index_cols == 0, math.sqrt(1.0 / HD), math.sqrt(2.0 / HD))
    lattice_index = (
        (jnp.arange(HD, dtype=jnp.int32)[:, None] + 1)
        * (17 * jnp.arange(FEAT, dtype=jnp.int32)[None, :] + 5)
        % 257
    )
    lattice = math.sqrt(2.0) * jnp.cos(2.0 * math.pi * lattice_index.astype(F32) / 257.0)
    return jnp.dot(cosine * scaling, lattice, precision=HIGHEST) / math.sqrt(HD)


def table_pair():
    table = feature_table()
    zero = jnp.zeros_like(table)
    both = jnp.concatenate(
        [jnp.concatenate([table, zero], 1), jnp.concatenate([zero, table], 1)], 0
    )
    high = lax.reduce_precision(both, 8, 7).astype(BF)
    return high, (both - high.astype(F32)).astype(BF)


def rotary_tables(place, tokens):
    half = ROT // 2
    positions = place * tokens + jnp.arange(tokens, dtype=jnp.int32)
    inv_freq = 10000.0 ** (-(2.0 * jnp.arange(half).astype(F32)) / ROT)
    angles = positions.astype(F32)[:, None] * inv_freq[None, :]
    cos, sin = jnp.cos(angles), jnp.sin(angles)
    rest = jnp.ones((tokens, HD - ROT), F32)
    none = jnp.zeros((tokens, half), F32)
    same = jnp.concatenate([cos, cos, rest], 1)
    down = jnp.concatenate([-sin, none, 0.0 * rest], 1)
    up = jnp.concatenate([none, sin, 0.0 * rest], 1)
    return tuple(jnp.concatenate([t, t], 1) for t in (same, down, up))


def dot(a, b, ca=1, cb=0):
    return lax.dot_general(a, b, (((ca,), (cb,)), ((), ())), preferred_element_type=F32)


def split_dot(a, b, cb=0):
    high = a.astype(BF)
    low = (a - high.astype(F32)).astype(BF)
    return dot(high, b, 1, cb) + dot(low, b, 1, cb)


def lane_masks(rows):
    low = lax.broadcasted_iota(jnp.int32, (rows, PAIR), 1) < HD
    first = low.astype(F32)
    return low, first.astype(BF), (1.0 - first).astype(BF)


def count_starts(starts_ref, row, position):
    total = jnp.int32(0)
    for n in range(NDOC):
        total = total + (starts_ref[row, n] <= position).astype(jnp.int32)
    return total


def seg_grid(starts_ref, row, base, shape, dim):
    position = base + lax.broadcasted_iota(jnp.int32, shape, dim)
    total = jnp.zeros(shape, jnp.int32)
    for n in range(NDOC):
        total = total + (starts_ref[row, n] <= position).astype(jnp.int32)
    return total


def causal_mask(starts_ref, row, base, tokens):
    shape = (tokens, tokens)
    same = seg_grid(starts_ref, row, base, shape, 0) == seg_grid(starts_ref, row, base, shape, 1)
    earlier = lax.broadcasted_iota(jnp.int32, shape, 1) <= lax.broadcasted_iota(
        jnp.int32, shape, 0
    )
    rows = lax.broadcasted_iota(jnp.int32, shape, 0) < tokens // 2
    cols = lax.broadcasted_iota(jnp.int32, shape, 1) < tokens // 2
    mask = same & earlier
    return mask.astype(F32), (mask & (rows == cols)).astype(F32)


def middle_state(starts_ref, row, base, tokens, k, v, state_in, total_in, low):
    half = tokens // 2
    end = count_starts(starts_ref, row, base + half - 1)
    passing = (end == count_starts(starts_ref, row, base - 1)).astype(F32)
    seg = seg_grid(starts_ref, row, base, (half, PAIR), 0)
    key = k[:half] * (seg == end).astype(F32).astype(BF)
    state = passing * state_in.astype(F32) + compact(dot(key, v[:half], 0, 0), low)
    total = passing * total_in + jnp.sum(key.astype(F32), 0, keepdims=True)
    later = seg_grid(starts_ref, row, base + half, (half, PAIR), 0)
    return state.astype(BF), total, (later == end).astype(F32)


def entering_mask(starts_ref, row, base, tokens):
    seg = seg_grid(starts_ref, row, base, (tokens, PAIR), 0)
    return (seg == count_starts(starts_ref, row, base - 1)).astype(F32)


def leaving_mask(starts_ref, row, base, tokens):
    seg = seg_grid(starts_ref, row, base, (tokens, PAIR), 0)
    return (seg == count_starts(starts_ref, row, base + tokens - 1)).astype(F32)


def rotate(x, same, down, up):
    half = ROT // 2
    return x * same + pltpu.roll(x, PAIR - half, 1) * down + pltpu.roll(x, half, 1) * up


def rotate_back(x, same, down, up):
    half = ROT // 2
    return x * same + pltpu.roll(x * down, half, 1) + pltpu.roll(x * up, PAIR - half, 1)


def compact(state, low):
    return jnp.where(low[:HD], state[:HD], state[HD:])


def spread(state, first, second):
    return jnp.concatenate([state * first[:HD], state * second[:HD]], 0)


def features_kernel(
    starts_ref, place_ref, norm_ref, weight_ref, bias_ref, feat_ref,
    same_ref, down_ref, up_ref, high_ref, low_ref,
    q_ref, k_ref, v_ref, state_ref, total_ref,
):
    tokens = same_ref.shape[0]
    base = place_ref[0, 0] * tokens
    low, first, second = lane_masks(tokens)
    feat = feat_ref[0]
    for row in range(MB * ROWS):
        here = slice(row * tokens, (row + 1) * tokens)
        proj = dot(norm_ref[here, :], weight_ref[...]) + bias_ref[0]
        c0, c1, c2 = proj[:, :PAIR], proj[:, PAIR : 2 * PAIR], proj[:, 2 * PAIR :]
        query = jnp.where(low, c0, c1)
        key = pltpu.roll(jnp.where(low, c2, c0), HD, 1)
        value = jnp.where(low, c1, c2).astype(BF)
        out = []
        for x in (query, key):
            x = rotate(x, same_ref[...], down_ref[...], up_ref[...])
            arg = split_dot(x, high_ref[...]) + dot(x.astype(BF), low_ref[...])
            out.append((feat * jnp.exp(arg)).astype(BF))
        q_ref[here, :] = out[0]
        k_ref[here, :] = out[1]
        v_ref[here, :] = value
        leaving = leaving_mask(starts_ref, row, base, tokens)
        key_out = out[1] * leaving.astype(BF)
        state_ref[0, row] = compact(dot(key_out, value, 0, 0), low).astype(BF)
        total_ref[0, row : row + 1, :] = jnp.sum(key_out.astype(F32), 0, keepdims=True)


def attend_kernel(
    starts_ref, place_ref, q_ref, k_ref, v_ref, state_ref, total_ref, low_ref, out_ref, den_ref
):
    tokens = q_ref.shape[0] // (MB * ROWS)
    base = place_ref[0, 0] * tokens
    low, first, second = lane_masks(tokens)
    ones = head_ones()
    for row in range(MB * ROWS):
        here = slice(row * tokens, (row + 1) * tokens)
        q, k, v = q_ref[here, :], k_ref[here, :], v_ref[here, :]
        mask, mask_in = causal_mask(starts_ref, row, base, tokens)
        enter = entering_mask(starts_ref, row, base, tokens)
        state, total = state_ref[0, row], total_ref[0, row : row + 1, :]
        middle, _, reach = middle_state(starts_ref, row, base, tokens, k, v, state, total, low)
        half = tokens // 2
        num = jnp.concatenate(
            [
                dot(q[:half] * enter[:half].astype(BF), spread(state, first, second)),
                dot(q[half:] * reach.astype(BF), spread(middle, first, second)),
            ],
            0,
        )
        for head in (first, second):
            scores = dot(q * head, k, 1, 1) * mask_in
            num = num + dot(scores.astype(BF), v * head)
        totals = dot(mask.astype(BF), k) + enter * total
        den = split_dot(q.astype(F32) * totals, ones)
        att = num / den
        low_ref[here, :] = att.astype(BF)
        out_ref[here, :] = att
        den_ref[here, :] = den


def head_ones():
    rows = lax.broadcasted_iota(jnp.int32, (PAIR, PAIR), 0) < HD
    cols = lax.broadcasted_iota(jnp.int32, (PAIR, PAIR), 1) < HD
    return (rows == cols).astype(F32).astype(BF)


def head_spread():
    rows = lax.broadcasted_iota(jnp.int32, (PAIR, 2 * PAIR), 0) < HD
    cols = lax.broadcasted_iota(jnp.int32, (PAIR, 2 * PAIR), 1) < PAIR
    return (rows == cols).astype(F32).astype(BF)


def back_state_kernel(
    starts_ref, place_ref, q_ref, ga_ref, att_ref, den_ref, state_ref, total_ref
):
    tokens = q_ref.shape[0] // (MB * ROWS)
    base = place_ref[0, 0] * tokens
    low, first, second = lane_masks(tokens)
    ones = head_ones()
    for row in range(MB * ROWS):
        here = slice(row * tokens, (row + 1) * tokens)
        grad_num = (ga_ref[here, :].astype(F32) / den_ref[here, :]).astype(BF)
        grad_den = -split_dot(grad_num.astype(F32) * att_ref[here, :], ones)
        enter = entering_mask(starts_ref, row, base, tokens)
        query = q_ref[here, :] * enter.astype(BF)
        state_ref[0, row] = compact(dot(query, grad_num, 0, 0), low)
        total_ref[0, row : row + 1, :] = jnp.sum(grad_den * query.astype(F32), 0, keepdims=True)


def back_kernel(
    starts_ref, place_ref, q_ref, k_ref, v_ref, ga_ref, att_ref, den_ref,
    state_ref, total_ref, later_ref, later_total_ref, feat_ref,
    same_ref, down_ref, up_ref, high_ref, low_ref,
    grad_ref, sums_ref,
):
    tokens = q_ref.shape[0] // (MB * ROWS)
    base = place_ref[0, 0] * tokens
    low, first, second = lane_masks(tokens)
    spreading = head_spread()
    feat_sum = jnp.zeros((1, PAIR), F32)
    bias_sum = [jnp.zeros((1, PAIR), F32) for _ in range(3)]
    for row in range(MB * ROWS):
        here = slice(row * tokens, (row + 1) * tokens)
        q, k, v = q_ref[here, :], k_ref[here, :], v_ref[here, :]
        grad_num = (ga_ref[here, :].astype(F32) / den_ref[here, :]).astype(BF)
        both = -split_dot(grad_num.astype(F32) * att_ref[here, :], spreading)
        dens = (both[:, :PAIR], both[:, PAIR:])
        grad_den = jnp.where(low, dens[0], dens[1])
        mask, mask_in = causal_mask(starts_ref, row, base, tokens)
        enter = entering_mask(starts_ref, row, base, tokens)
        leave = leaving_mask(starts_ref, row, base, tokens)
        state, total = state_ref[0, row], total_ref[0, row : row + 1, :]
        middle, middle_total, reach = middle_state(
            starts_ref, row, base, tokens, k, v, state, total, low
        )
        half = tokens // 2
        gq = jnp.concatenate(
            [
                enter[:half]
                * (dot(grad_num[:half], spread(state, first, second), 1, 1) + grad_den[:half] * total),
                reach
                * (
                    dot(grad_num[half:], spread(middle, first, second), 1, 1)
                    + grad_den[half:] * middle_total
                ),
            ],
            0,
        )
        later = later_ref[0, row]
        later_high = later.astype(BF)
        later_low = spread((later - later_high.astype(F32)).astype(BF), first, second)
        later_high = spread(later_high, first, second)
        gk = leave * (
            dot(v, later_high, 1, 1) + dot(v, later_low, 1, 1) + later_total_ref[0, row : row + 1, :]
        )
        gv = leave * (dot(k, later_high) + dot(k, later_low))
        for head, den in zip((first, second), dens):
            q_head, grad_head = q * head, grad_num * head
            scores = (dot(q_head, k, 1, 1) * mask).astype(BF)
            grad_scores = dot(grad_head, v, 1, 1) + den
            gq = gq + dot((grad_scores * mask_in).astype(BF), k * head)
            gk = gk + dot((grad_scores * mask).astype(BF), q_head, 0, 0)
            gv = gv + dot(scores, grad_head, 0, 0)
        arg_grads = (gq * q.astype(F32), gk * k.astype(F32))
        feat_sum = feat_sum + jnp.sum(arg_grads[0] + arg_grads[1], 0, keepdims=True)
        turned = []
        for x in arg_grads:
            x = split_dot(x, high_ref[...], 1) + dot(x.astype(BF), low_ref[...], 1, 1)
            turned.append(rotate_back(x, same_ref[...], down_ref[...], up_ref[...]))
        dq, dk = turned[0], pltpu.roll(turned[1], HD, 1)
        parts = (jnp.where(low, dq, dk), jnp.where(low, gv, dq), jnp.where(low, dk, gv))
        for n, part in enumerate(parts):
            part = part.astype(BF)
            grad_ref[here, n * PAIR : (n + 1) * PAIR] = part
            bias_sum[n] = bias_sum[n] + jnp.sum(part.astype(F32), 0, keepdims=True)
    sums_ref[0, 0:1, :] = feat_sum / feat_ref[0]
    for n in range(3):
        sums_ref[0, n + 1 : n + 2, :] = bias_sum[n]


SMEM = pl.BlockSpec(memory_space=pltpu.SMEM)


def whole(shape):
    return pl.BlockSpec(shape, lambda p: (0,) * len(shape))


def column(rows, width):
    return pl.BlockSpec((rows, width), lambda p: (0, p))


def stacked(*shape):
    return pl.BlockSpec((1,) + shape, lambda p: (p,) + (0,) * len(shape))


def call(kernel, pairs, in_specs, out_specs, out_shape, flops):
    return pl.pallas_call(
        kernel,
        grid=(pairs,),
        in_specs=in_specs,
        out_specs=out_specs,
        out_shape=out_shape,
        compiler_params=pltpu.CompilerParams(vmem_limit_bytes=VMEM_LIMIT),
        cost_estimate=pl.CostEstimate(flops=flops, bytes_accessed=8 << 20, transcendentals=0),
    )


def shaped(shape, dtype):
    return jax.ShapeDtypeStruct(shape, dtype)


CHUNK = 256
PANEL = 512
RING = 4
LAG = 6


def reduce_kernel(plan, *refs):
    count, terms = plan
    factors, small_ref = refs[: 2 * len(terms)], refs[2 * len(terms)]
    outs = refs[2 * len(terms) + 1 : 3 * len(terms) + 2]
    (
        work, give, take, part, outside, inside,
        give_send, give_recv, part_send, outer_recv, inner_recv, total_send,
        final_send, final_recv, own_sem,
    ) = refs[3 * len(terms) + 2 :]
    half = CHUNK // 2
    place, peers = lax.axis_index("ctx"), lax.axis_size("ctx")
    core, z, chips = place % 2, place // 2, peers // 2
    below = z < chips // 2
    middle = (z == chips // 2 - 1) | (z == chips // 2)
    has_outer = (z != 0) & (z != chips - 1)
    step = jnp.where(below, 2, -2)
    inner, outer, twin = place + step, place - step, place + 1 - 2 * core
    mine = pl.ds(pl.multiple_of(core * half, half), half)
    theirs = pl.ds(pl.multiple_of((1 - core) * half, half), half)

    def remote(src, dst, send, recv, to):
        return pltpu.make_async_remote_copy(
            src_ref=src, dst_ref=dst, send_sem=send, recv_sem=recv,
            device_id={"ctx": to}, device_id_type=pl.DeviceIdType.MESH,
        )

    def give_copy(t):
        return remote(give.at[t], take.at[t], give_send.at[t], give_recv.at[t], twin)

    def to_outside(t):
        return remote(part.at[t], outside.at[t], part_send.at[t], outer_recv.at[t], inner)

    def across(t):
        return remote(part.at[t], inside.at[t], part_send.at[t], inner_recv.at[t], inner)

    def outward(t):
        return remote(take.at[t], inside.at[t], total_send.at[t], inner_recv.at[t], outer)

    def final_copy(t, target):
        return remote(take.at[t], target, final_send.at[t], final_recv.at[t], twin)

    def own_copy(t, target):
        return pltpu.make_async_copy(take.at[t], target, own_sem.at[t])

    def block_of(j, panels):
        rows = (j // panels) * CHUNK
        return rows, pl.ds(pl.multiple_of((j % panels) * PANEL, PANEL), PANEL)

    def deliver(t, target):
        final_copy(t, target).start()
        own_copy(t, target).start()

    some_target = outs[-1].at[mine]

    barrier = pltpu.get_barrier_semaphore()
    for peer in (inner, twin):
        pl.semaphore_signal(
            barrier, inc=1, device_id={"ctx": peer}, device_id_type=pl.DeviceIdType.MESH
        )

    @pl.when(has_outer)
    def _():
        pl.semaphore_signal(
            barrier, inc=1, device_id={"ctx": outer}, device_id_type=pl.DeviceIdType.MESH
        )

    pl.semaphore_wait(barrier, 2 + has_outer.astype(jnp.int32))
    lag = jnp.where(middle, 2, LAG)

    def one(t, carry):
        slot = t % RING
        begin = 0
        for n, (blocks, panels) in enumerate(terms):
            left, right = factors[2 * n], factors[2 * n + 1]

            @pl.when((t >= begin) & (t < begin + blocks * panels))
            def _(left=left, right=right, panels=panels, begin=begin):
                start, cols = block_of(t - begin, panels)
                rows = pl.ds(pl.multiple_of(start, CHUNK), CHUNK)
                work[slot] = dot(left[:, rows], right[:, cols], 0, 0)

            begin += blocks * panels

        @pl.when(t == begin)
        def _():
            work[slot] = small_ref[...]

        @pl.when(t < count)
        def _():
            give[t] = work[slot, theirs, :].astype(BF)
            give_copy(t).start()

        tb = t - 1

        @pl.when((tb >= 0) & (tb < count))
        def _():
            give_copy(tb).wait_recv()
            total = work[(t + RING - 1) % RING, mine, :] + take[tb].astype(F32)

            @pl.when(has_outer)
            def _():
                to_outside(tb).wait_recv()
                part[tb] = (total + outside[tb].astype(F32)).astype(BF)

            @pl.when(jnp.logical_not(has_outer))
            def _():
                part[tb] = total.astype(BF)

            @pl.when(middle)
            def _():
                across(tb).start()

            @pl.when(jnp.logical_not(middle))
            def _():
                to_outside(tb).start()

        tc = t - lag

        @pl.when((tc >= 0) & (tc < count))
        def _():
            across(tc).wait_recv()

            @pl.when(middle)
            def _():
                take[tc] = (part[tc].astype(F32) + inside[tc].astype(F32)).astype(BF)

            @pl.when(jnp.logical_not(middle))
            def _():
                take[tc] = inside[tc]

            @pl.when(has_outer)
            def _():
                outward(tc).start()

            begin = 0
            for n, (blocks, panels) in enumerate(terms):

                @pl.when((tc >= begin) & (tc < begin + blocks * panels))
                def _(n=n, panels=panels, begin=begin):
                    start, cols = block_of(tc - begin, panels)
                    rows = pl.ds(pl.multiple_of(start + core * half, half), half)
                    deliver(tc, outs[n].at[rows, cols])

                begin += blocks * panels

            @pl.when(tc == begin)
            def _():
                deliver(tc, some_target)

        return carry

    lax.fori_loop(0, count + LAG, one, 0)

    def drain(t, carry):
        give_copy(t).wait_send()
        across(t).wait_send()
        final_copy(t, some_target).wait_send()
        final_copy(t, some_target).wait_recv()
        own_copy(t, some_target).wait()

        @pl.when(has_outer)
        def _():
            outward(t).wait_send()

        return carry

    lax.fori_loop(0, count, drain, 0)


def reduce_over_ctx(factors, small):
    terms = tuple((a.shape[1] // CHUNK, b.shape[1] // PANEL) for a, b in factors)
    count = sum(x * y for x, y in terms) + 1
    half = CHUNK // 2
    flat = [x for pair in factors for x in pair] + [small]
    slots = pltpu.VMEM((count, half, PANEL), BF)
    sums = pl.pallas_call(
        partial(reduce_kernel, (count, terms)),
        in_specs=[pl.BlockSpec(memory_space=pltpu.VMEM)] * len(flat),
        out_specs=[pl.BlockSpec(memory_space=pl.ANY)] * (len(terms) + 1),
        out_shape=[shaped((a.shape[1], b.shape[1]), BF) for a, b in factors]
        + [shaped((CHUNK, PANEL), BF)],
        scratch_shapes=[pltpu.VMEM((RING, CHUNK, PANEL), F32)]
        + [slots] * 5
        + [pltpu.SemaphoreType.DMA((count,))] * 9,
        compiler_params=pltpu.CompilerParams(
            collective_id=0, has_side_effects=True, vmem_limit_bytes=REDUCE_LIMIT
        ),
        cost_estimate=pl.CostEstimate(
            flops=count * 2 * CHUNK * PANEL * 512, bytes_accessed=40 << 20, transcendentals=0
        ),
    )(*flat)
    return [g.astype(F32) for g in sums[:-1]], sums[-1].astype(F32)


def fits_reduce(factors):
    even = lax.axis_size("ctx") % 4 == 0
    return even and all(
        a.shape[1] % CHUNK == 0 and b.shape[1] % PANEL == 0 for a, b in factors
    )


def gather_tp(value):
    if lax.axis_size("tp") != 2:
        return lax.all_gather(value, "tp", axis=1, tiled=True)
    other = lax.ppermute(value, "tp", [(0, 1), (1, 0)])
    return jnp.where(
        lax.axis_index("tp") == 0,
        jnp.concatenate([value, other], 1),
        jnp.concatenate([other, value], 1),
    )


def scatter_tp(value):
    peers = lax.axis_size("tp")
    if peers != 2:
        return lax.psum_scatter(value, "tp", scatter_dimension=1, tiled=True)
    me = lax.axis_index("tp")
    width = value.shape[1] // 2
    left, right = value[:, :width], value[:, width:]
    other = lax.ppermute(jnp.where(me == 0, right, left).astype(BF), "tp", [(0, 1), (1, 0)])
    return jnp.where(me == 0, left, right) + other.astype(F32)


def local(
    section_inputs,
    doc_starts,
    ln_gains,
    ln_shifts,
    qkv_weight,
    qkv_bias,
    feature_weight,
    dense_weight,
    out_bias,
    up_weight,
    up_bias,
    down_weight,
):
    section = lax.axis_index("pipe")
    place = lax.axis_index("ctx")
    peers = lax.axis_size("ctx")
    width = section_inputs.shape[-1]
    tokens = section_inputs.shape[3]
    rows = MB * ROWS
    total = rows * tokens
    heads = feature_weight.shape[1]
    pairs = heads // 2
    gain, shift = ln_gains[0], ln_shifts[0]
    w_qkv, w_dense, w_up, w_down = qkv_weight[0], dense_weight[0], up_weight[0], down_weight[0]
    b_qkv = qkv_bias[0].reshape(pairs, 1, 3 * PAIR)
    b_up, b_out = up_bias[0], out_bias[0]
    feat = feature_weight[0].reshape(pairs, 1, PAIR)
    starts = doc_starts.reshape(rows, NDOC)
    place_in = place.astype(jnp.int32).reshape(1, 1)
    high, low = table_pair()
    same, down, up = rotary_tables(place, tokens)
    tables = (same, down, up, high, low)
    table_specs = [whole((tokens, PAIR))] * 3 + [whole((PAIR, PAIR))] * 2
    state_shape = shaped((pairs, rows, HD, PAIR), BF)
    total_shape = shaped((pairs, 8, PAIR), F32)
    state_spec, total_spec = stacked(rows, HD, PAIR), stacked(8, PAIR)
    low_shape, full_shape = shaped((total, pairs * PAIR), BF), shaped((total, pairs * PAIR), F32)
    unit = 2 * rows * tokens * PAIR * PAIR * pairs

    ends = jnp.arange(peers, dtype=jnp.int32)[:, None, None] * tokens
    seg_last = jnp.sum((starts[None] <= ends + tokens - 1).astype(jnp.int32), 2)
    seg_prev = jnp.sum((starts[None] <= ends - 1).astype(jnp.int32), 2)
    order = jnp.arange(peers)[:, None]
    from_earlier = ((order < place) & (seg_last == seg_prev[place][None])).astype(F32)
    from_later = ((order > place) & (seg_prev == seg_last[place][None])).astype(F32)

    def carried(state, totals, weights):
        states, sums = lax.all_gather((state, totals), "ctx")
        state_in = jnp.sum(states.astype(F32) * weights[:, None, :, None, None], 0)
        padded = jnp.concatenate([weights, jnp.zeros((peers, 8 - rows), F32)], 1)
        total_in = jnp.sum(jnp.where(padded[:, None, :, None] > 0, sums, 0.0), 0)
        return state_in.astype(state.dtype), total_in

    def forward(u_low, own):
        u = u_low.astype(F32)
        centered = u - jnp.mean(u, -1, keepdims=True)
        inv = lax.rsqrt(jnp.mean(centered * centered, -1, keepdims=True) + norm_eps)
        xhat = centered * inv
        first = (xhat * gain[0] + shift[0]).astype(BF)
        second = (xhat * gain[1] + shift[1]).astype(BF)
        q, k, v, state, totals = call(
            features_kernel,
            pairs,
            [SMEM, SMEM, whole((total, D)), column(D, 3 * PAIR), stacked(1, 3 * PAIR),
             stacked(1, PAIR)] + table_specs,
            [column(total, PAIR)] * 3 + [state_spec, total_spec],
            [low_shape] * 3 + [state_shape, total_shape],
            30 * unit,
        )(starts, place_in, first, w_qkv, b_qkv, feat, *tables)
        state_in, total_in = carried(state, totals, from_earlier)
        pre = jnp.dot(second, w_up, preferred_element_type=F32) + b_up
        hidden = jax.nn.gelu(pre, approximate=False).astype(BF)
        mlp = jnp.dot(hidden, w_down, preferred_element_type=F32)
        att_low, att, den = call(
            attend_kernel,
            pairs,
            [SMEM, SMEM] + [column(total, PAIR)] * 3 + [state_spec, total_spec],
            [column(total, PAIR)] * 3,
            [low_shape, full_shape, full_shape],
            8 * unit,
        )(starts, place_in, q, k, v, state_in, total_in)
        part = jnp.dot(att_low, w_dense, preferred_element_type=F32) + mlp
        out = scatter_tp(part) + own.astype(F32) + b_out
        kept = (xhat, inv, first, second, q, k, v, pre, hidden, att_low, att, den, state_in, total_in)
        return out, kept

    def backward(dy, own, kept, want):
        xhat, inv, first, second, q, k, v, pre, hidden, att_low, att, den, state_in, total_in = kept
        ga = lax.dot_general(
            dy, w_dense, (((1,), (1,)), ((), ())), preferred_element_type=F32
        ).astype(BF)
        state, totals = call(
            back_state_kernel,
            pairs,
            [SMEM, SMEM] + [column(total, PAIR)] * 4,
            [state_spec, total_spec],
            [shaped(state_shape.shape, F32), total_shape],
            3 * unit,
        )(starts, place_in, q, ga, att, den)
        later, later_total = carried(state, totals, from_later)
        grad_hidden = lax.dot_general(
            dy, w_down, (((1,), (1,)), ((), ())), preferred_element_type=F32
        )
        cdf = 0.5 * (1.0 + lax.erf(pre * math.sqrt(0.5)))
        slope = cdf + pre * jnp.exp(-0.5 * pre * pre) * (1.0 / math.sqrt(2.0 * math.pi))
        grad_pre = (grad_hidden * slope).astype(BF)
        grad_second = lax.dot_general(
            grad_pre, w_up, (((1,), (1,)), ((), ())), preferred_element_type=F32
        )
        grad_proj, sums = call(
            back_kernel,
            pairs,
            [SMEM, SMEM] + [column(total, PAIR)] * 6
            + [state_spec, total_spec, state_spec, total_spec, stacked(1, PAIR)] + table_specs,
            [column(total, 3 * PAIR), stacked(8, PAIR)],
            [shaped((total, pairs * 3 * PAIR), BF), shaped((pairs, 8, PAIR), F32)],
            20 * unit,
        )(starts, place_in, q, k, v, ga, att, den, state_in, total_in, later, later_total, feat, *tables)
        grad_first = lax.dot_general(
            grad_proj, w_qkv, (((1,), (1,)), ((), ())), preferred_element_type=F32
        )
        both = grad_first * gain[0] + grad_second * gain[1]
        part = inv * (
            both
            - jnp.mean(both, -1, keepdims=True)
            - xhat * jnp.mean(both * xhat, -1, keepdims=True)
        )
        grad_input = scatter_tp(part) + own.astype(F32)
        if not want:
            return grad_input, None

        large = ((hidden, dy), (second, grad_pre), (att_low, dy), (first, grad_proj))
        norm_sums = jnp.stack(
            [
                jnp.sum(grad_first * xhat, 0),
                jnp.sum(grad_second * xhat, 0),
                jnp.sum(grad_first, 0),
                jnp.sum(grad_second, 0),
            ]
        )
        small = (
            sums[:, 1:4, :].reshape(pairs * 3 * PAIR),
            sums[:, 0, :].reshape(heads, FEAT),
            jnp.sum(own.astype(F32), 0),
            jnp.sum(grad_pre.astype(F32), 0),
        )
        return grad_input, (large, norm_sums, small)

    mine = section_inputs[0].reshape(total, width)
    mine_full = gather_tp(mine)
    y0, _ = forward(mine_full, mine)
    sent = lax.ppermute(y0.astype(BF), "pipe", [(0, 1)])
    own_in = jnp.where(section == 0, mine, sent)
    full_in = jnp.where(section == 0, mine_full, gather_tp(sent))
    y1, kept = forward(full_in, own_in)
    du1, _ = backward(mine_full, mine, kept, False)
    sent = lax.ppermute(du1.astype(BF), "pipe", [(1, 0)])
    own_grad = jnp.where(section == 1, mine, sent)
    full_grad = jnp.where(section == 1, mine_full, gather_tp(sent))
    du0, (large, norm_sums, small) = backward(full_grad, own_grad, kept, True)
    if lax.axis_size("tp") == 2:
        me = lax.axis_index("tp")
        away = lax.dynamic_slice_in_dim(norm_sums, (1 - me) * width, width, 1)
        norm_sums = lax.dynamic_slice_in_dim(norm_sums, me * width, width, 1)
        norm_sums = norm_sums + lax.ppermute(away, "tp", [(0, 1), (1, 0)])
    else:
        norm_sums = lax.psum_scatter(norm_sums, "tp", scatter_dimension=1, tiled=True)
    small = small + (norm_sums,)
    if fits_reduce(large):
        flat = jnp.concatenate([x.reshape(-1) for x in small])
        flat = jnp.pad(flat, (0, CHUNK * PANEL - flat.size)).reshape(CHUNK, PANEL)
        (g_down, g_up, g_dense, g_qkv), flat = reduce_over_ctx(large, flat)
        flat, summed, begin = flat.reshape(-1), [], 0
        for x in small:
            summed.append(flat[begin : begin + x.size].reshape(x.shape))
            begin += x.size
    else:
        products = tuple(dot(a, b, 0, 0).astype(BF) for a, b in large)
        g_down, g_up, g_dense, g_qkv = (g.astype(F32) for g in lax.psum(products, "ctx"))
        summed = lax.psum(small, "ctx")
    g_qkv_bias, g_feat, g_out_bias, g_up_bias, norm_sums = summed
    section_ends = jnp.where(section == 0, du0, y1).reshape(1, MB, ROWS, tokens, width)
    grads = (
        norm_sums[:2], norm_sums[2:], g_qkv, g_qkv_bias, g_feat, g_dense, g_out_bias,
        g_up, g_up_bias, g_down,
    )
    return (section_ends,) + tuple(g[None] for g in grads)


def solution(mesh):
    in_specs = (
        P("pipe", None, None, "ctx", "tp"),
        P(),
        P("pipe", None, None),
        P("pipe", None, None),
        P("pipe", None, "tp"),
        P("pipe", "tp"),
        P("pipe", "tp", None),
        P("pipe", "tp", None),
        P("pipe", "tp"),
        P("pipe", None, "tp"),
        P("pipe", "tp"),
        P("pipe", "tp", None),
    )
    out_specs = (
        P("pipe", None, None, "ctx", "tp"),
        P("pipe", None, "tp"),
        P("pipe", None, "tp"),
        P("pipe", None, "tp"),
        P("pipe", "tp"),
        P("pipe", "tp", None),
        P("pipe", "tp", None),
        P("pipe", "tp"),
        P("pipe", None, "tp"),
        P("pipe", "tp"),
        P("pipe", "tp", None),
    )
    return jax.shard_map(local, mesh=mesh, in_specs=in_specs, out_specs=out_specs, check_vma=False)
```

```python
from functools import partial
import math

import jax
import jax.numpy as jnp
from jax import lax
from jax.experimental import pallas as pl
from jax.experimental.pallas import tpu as pltpu
from jax.sharding import PartitionSpec as P

D = 1024
HD = 64
ROT = 16
FEAT = 64
MB = 4
ROWS = 1
NDOC = 4
PAIR = 2 * HD
HELD = HD + 8
TILE = 256
HOP = 2

BF = jnp.bfloat16
F32 = jnp.float32
HIGHEST = lax.Precision.HIGHEST
norm_eps = 1e-05
VMEM_LIMIT = 56 * 1024 * 1024
REDUCE_LIMIT = 60 * 1024 * 1024


def feature_table():
    index_rows = jnp.arange(HD, dtype=jnp.int32)[:, None]
    index_cols = jnp.arange(HD, dtype=jnp.int32)[None, :]
    cosine = jnp.cos(
        math.pi * (index_rows.astype(F32) + 0.5) * index_cols.astype(F32) / HD
    )
    scaling = jnp.where(index_cols == 0, math.sqrt(1.0 / HD), math.sqrt(2.0 / HD))
    lattice_index = (
        (jnp.arange(HD, dtype=jnp.int32)[:, None] + 1)
        * (17 * jnp.arange(FEAT, dtype=jnp.int32)[None, :] + 5)
        % 257
    )
    lattice = math.sqrt(2.0) * jnp.cos(2.0 * math.pi * lattice_index.astype(F32) / 257.0)
    return jnp.dot(cosine * scaling, lattice, precision=HIGHEST) / math.sqrt(HD)


def table_pair():
    table = feature_table()
    zero = jnp.zeros_like(table)
    both = jnp.concatenate(
        [jnp.concatenate([table, zero], 1), jnp.concatenate([zero, table], 1)], 0
    )
    high = lax.reduce_precision(both, 8, 7).astype(BF)
    return high, (both - high.astype(F32)).astype(BF)


def rotary_tables(place, tokens):
    half = ROT // 2
    positions = place * tokens + jnp.arange(tokens, dtype=jnp.int32)
    inv_freq = 10000.0 ** (-(2.0 * jnp.arange(half).astype(F32)) / ROT)
    angles = positions.astype(F32)[:, None] * inv_freq[None, :]
    cos, sin = jnp.cos(angles), jnp.sin(angles)
    rest = jnp.ones((tokens, HD - ROT), F32)
    none = jnp.zeros((tokens, half), F32)
    same = jnp.concatenate([cos, cos, rest], 1)
    down = jnp.concatenate([-sin, none, 0.0 * rest], 1)
    up = jnp.concatenate([none, sin, 0.0 * rest], 1)
    return tuple(jnp.concatenate([t, t], 1) for t in (same, down, up))


def dot(a, b, ca=1, cb=0):
    return lax.dot_general(a, b, (((ca,), (cb,)), ((), ())), preferred_element_type=F32)


def split_dot(a, b, cb=0):
    high = a.astype(BF)
    low = (a - high.astype(F32)).astype(BF)
    return dot(high, b, 1, cb) + dot(low, b, 1, cb)


def lane_masks(rows):
    low = lax.broadcasted_iota(jnp.int32, (rows, PAIR), 1) < HD
    first = low.astype(F32)
    return low, first.astype(BF), (1.0 - first).astype(BF)


def count_starts(starts_ref, row, position):
    total = jnp.int32(0)
    for n in range(NDOC):
        total = total + (starts_ref[row, n] <= position).astype(jnp.int32)
    return total


def seg_grid(starts_ref, row, base, shape, dim):
    position = base + lax.broadcasted_iota(jnp.int32, shape, dim)
    total = jnp.zeros(shape, jnp.int32)
    for n in range(NDOC):
        total = total + (starts_ref[row, n] <= position).astype(jnp.int32)
    return total


def causal_mask(starts_ref, row, base, tokens):
    shape = (tokens, tokens)
    same = seg_grid(starts_ref, row, base, shape, 0) == seg_grid(starts_ref, row, base, shape, 1)
    earlier = lax.broadcasted_iota(jnp.int32, shape, 1) <= lax.broadcasted_iota(
        jnp.int32, shape, 0
    )
    rows = lax.broadcasted_iota(jnp.int32, shape, 0) < tokens // 2
    cols = lax.broadcasted_iota(jnp.int32, shape, 1) < tokens // 2
    mask = same & earlier
    return mask.astype(F32), (mask & (rows == cols)).astype(F32)


def middle_state(starts_ref, row, base, tokens, k, v, state_in, total_in, low):
    half = tokens // 2
    end = count_starts(starts_ref, row, base + half - 1)
    passing = (end == count_starts(starts_ref, row, base - 1)).astype(F32)
    seg = seg_grid(starts_ref, row, base, (half, PAIR), 0)
    key = k[:half] * (seg == end).astype(F32).astype(BF)
    state = passing * state_in + compact(dot(key, v[:half], 0, 0), low)
    total = passing * total_in + jnp.sum(key.astype(F32), 0, keepdims=True)
    later = seg_grid(starts_ref, row, base + half, (half, PAIR), 0)
    return state.astype(BF), total, (later == end).astype(F32)


def entering_mask(starts_ref, row, base, tokens):
    seg = seg_grid(starts_ref, row, base, (tokens, PAIR), 0)
    return (seg == count_starts(starts_ref, row, base - 1)).astype(F32)


def leaving_mask(starts_ref, row, base, tokens):
    seg = seg_grid(starts_ref, row, base, (tokens, PAIR), 0)
    return (seg == count_starts(starts_ref, row, base + tokens - 1)).astype(F32)


def rotate(x, same, down, up):
    half = ROT // 2
    return x * same + pltpu.roll(x, PAIR - half, 1) * down + pltpu.roll(x, half, 1) * up


def rotate_back(x, same, down, up):
    half = ROT // 2
    return x * same + pltpu.roll(x * down, half, 1) + pltpu.roll(x * up, PAIR - half, 1)


def compact(state, low):
    return jnp.where(low[:HD], state[:HD], state[HD:])


def spread(state, first, second):
    return jnp.concatenate([state * first[:HD], state * second[:HD]], 0)


def keep_state(state_ref, row, product, summands, low):
    state_ref[row, 0, :HD] = compact(product, low)
    total = jnp.sum(summands, 0, keepdims=True)
    state_ref[row, 0, HD:] = jnp.broadcast_to(total, (HELD - HD, PAIR))


def features_kernel(
    starts_ref, place_ref, norm_ref, weight_ref, bias_ref, feat_ref,
    same_ref, down_ref, up_ref, high_ref, low_ref,
    q_ref, k_ref, v_ref, state_ref,
):
    tokens = same_ref.shape[0]
    base = place_ref[0, 0] * tokens
    low, first, second = lane_masks(tokens)
    feat = feat_ref[0]
    for row in range(MB * ROWS):
        here = slice(row * tokens, (row + 1) * tokens)
        proj = dot(norm_ref[here, :], weight_ref[...]) + bias_ref[0]
        c0, c1, c2 = proj[:, :PAIR], proj[:, PAIR : 2 * PAIR], proj[:, 2 * PAIR :]
        query = jnp.where(low, c0, c1)
        key = pltpu.roll(jnp.where(low, c2, c0), HD, 1)
        value = jnp.where(low, c1, c2).astype(BF)
        out = []
        for x in (query, key):
            x = rotate(x, same_ref[...], down_ref[...], up_ref[...])
            arg = split_dot(x, high_ref[...]) + dot(x.astype(BF), low_ref[...])
            out.append((feat * jnp.exp(arg)).astype(BF))
        q_ref[here, :] = out[0]
        k_ref[here, :] = out[1]
        v_ref[here, :] = value
        leaving = leaving_mask(starts_ref, row, base, tokens)
        key_out = out[1] * leaving.astype(BF)
        keep_state(state_ref, row, dot(key_out, value, 0, 0), key_out.astype(F32), low)


def attend_kernel(
    starts_ref, place_ref, q_ref, k_ref, v_ref, state_ref, low_ref, out_ref, den_ref
):
    tokens = q_ref.shape[0] // (MB * ROWS)
    base = place_ref[0, 0] * tokens
    low, first, second = lane_masks(tokens)
    ones = head_ones()
    for row in range(MB * ROWS):
        here = slice(row * tokens, (row + 1) * tokens)
        q, k, v = q_ref[here, :], k_ref[here, :], v_ref[here, :]
        mask, mask_in = causal_mask(starts_ref, row, base, tokens)
        enter = entering_mask(starts_ref, row, base, tokens)
        carry, total = state_ref[row, 0, :HD], state_ref[row, 0, HD : HD + 1]
        state = carry.astype(BF)
        middle, _, reach = middle_state(starts_ref, row, base, tokens, k, v, carry, total, low)
        half = tokens // 2
        num = jnp.concatenate(
            [
                dot(q[:half] * enter[:half].astype(BF), spread(state, first, second)),
                dot(q[half:] * reach.astype(BF), spread(middle, first, second)),
            ],
            0,
        )
        for head in (first, second):
            scores = dot(q * head, k, 1, 1) * mask_in
            num = num + dot(scores.astype(BF), v * head)
        totals = dot(mask.astype(BF), k) + enter * total
        den = split_dot(q.astype(F32) * totals, ones)
        att = num / den
        low_ref[here, :] = att.astype(BF)
        out_ref[here, :] = att
        den_ref[here, :] = den


def head_ones():
    rows = lax.broadcasted_iota(jnp.int32, (PAIR, PAIR), 0) < HD
    cols = lax.broadcasted_iota(jnp.int32, (PAIR, PAIR), 1) < HD
    return (rows == cols).astype(F32).astype(BF)


def head_spread():
    rows = lax.broadcasted_iota(jnp.int32, (PAIR, 2 * PAIR), 0) < HD
    cols = lax.broadcasted_iota(jnp.int32, (PAIR, 2 * PAIR), 1) < PAIR
    return (rows == cols).astype(F32).astype(BF)


def back_state_kernel(
    starts_ref, place_ref, q_ref, ga_ref, att_ref, den_ref, state_ref
):
    tokens = q_ref.shape[0] // (MB * ROWS)
    base = place_ref[0, 0] * tokens
    low, first, second = lane_masks(tokens)
    ones = head_ones()
    for row in range(MB * ROWS):
        here = slice(row * tokens, (row + 1) * tokens)
        grad_num = (ga_ref[here, :].astype(F32) / den_ref[here, :]).astype(BF)
        grad_den = -split_dot(grad_num.astype(F32) * att_ref[here, :], ones)
        enter = entering_mask(starts_ref, row, base, tokens)
        query = q_ref[here, :] * enter.astype(BF)
        keep_state(state_ref, row, dot(query, grad_num, 0, 0), grad_den * query.astype(F32), low)


def back_kernel(
    starts_ref, place_ref, q_ref, k_ref, v_ref, ga_ref, att_ref, den_ref,
    state_ref, later_ref, feat_ref,
    same_ref, down_ref, up_ref, high_ref, low_ref,
    grad_ref, sums_ref,
):
    tokens = q_ref.shape[0] // (MB * ROWS)
    base = place_ref[0, 0] * tokens
    low, first, second = lane_masks(tokens)
    spreading = head_spread()
    feat_sum = jnp.zeros((1, PAIR), F32)
    bias_sum = [jnp.zeros((1, PAIR), F32) for _ in range(3)]
    for row in range(MB * ROWS):
        here = slice(row * tokens, (row + 1) * tokens)
        q, k, v = q_ref[here, :], k_ref[here, :], v_ref[here, :]
        grad_num = (ga_ref[here, :].astype(F32) / den_ref[here, :]).astype(BF)
        both = -split_dot(grad_num.astype(F32) * att_ref[here, :], spreading)
        dens = (both[:, :PAIR], both[:, PAIR:])
        grad_den = jnp.where(low, dens[0], dens[1])
        mask, mask_in = causal_mask(starts_ref, row, base, tokens)
        enter = entering_mask(starts_ref, row, base, tokens)
        leave = leaving_mask(starts_ref, row, base, tokens)
        carry, total = state_ref[row, 0, :HD], state_ref[row, 0, HD : HD + 1]
        state = carry.astype(BF)
        middle, middle_total, reach = middle_state(
            starts_ref, row, base, tokens, k, v, carry, total, low
        )
        half = tokens // 2
        gq = jnp.concatenate(
            [
                enter[:half]
                * (dot(grad_num[:half], spread(state, first, second), 1, 1) + grad_den[:half] * total),
                reach
                * (
                    dot(grad_num[half:], spread(middle, first, second), 1, 1)
                    + grad_den[half:] * middle_total
                ),
            ],
            0,
        )
        later = later_ref[row, 0, :HD]
        later_high = later.astype(BF)
        later_low = spread((later - later_high.astype(F32)).astype(BF), first, second)
        later_high = spread(later_high, first, second)
        gk = leave * (
            dot(v, later_high, 1, 1) + dot(v, later_low, 1, 1) + later_ref[row, 0, HD : HD + 1]
        )
        gv = leave * (dot(k, later_high) + dot(k, later_low))
        for head, den in zip((first, second), dens):
            q_head, grad_head = q * head, grad_num * head
            scores = (dot(q_head, k, 1, 1) * mask).astype(BF)
            grad_scores = dot(grad_head, v, 1, 1) + den
            gq = gq + dot((grad_scores * mask_in).astype(BF), k * head)
            gk = gk + dot((grad_scores * mask).astype(BF), q_head, 0, 0)
            gv = gv + dot(scores, grad_head, 0, 0)
        arg_grads = (gq * q.astype(F32), gk * k.astype(F32))
        feat_sum = feat_sum + jnp.sum(arg_grads[0] + arg_grads[1], 0, keepdims=True)
        turned = []
        for x in arg_grads:
            x = split_dot(x, high_ref[...], 1) + dot(x.astype(BF), low_ref[...], 1, 1)
            turned.append(rotate_back(x, same_ref[...], down_ref[...], up_ref[...]))
        dq, dk = turned[0], pltpu.roll(turned[1], HD, 1)
        parts = (jnp.where(low, dq, dk), jnp.where(low, gv, dq), jnp.where(low, dk, gv))
        for n, part in enumerate(parts):
            part = part.astype(BF)
            grad_ref[here, n * PAIR : (n + 1) * PAIR] = part
            bias_sum[n] = bias_sum[n] + jnp.sum(part.astype(F32), 0, keepdims=True)
    sums_ref[0, 0:1, :] = feat_sum / feat_ref[0]
    for n in range(3):
        sums_ref[0, n + 1 : n + 2, :] = bias_sum[n]


SMEM = pl.BlockSpec(memory_space=pltpu.SMEM)


def whole(shape):
    return pl.BlockSpec(shape, lambda p: (0,) * len(shape))


def column(rows, width):
    return pl.BlockSpec((rows, width), lambda p: (0, p))


def stacked(*shape):
    return pl.BlockSpec((1,) + shape, lambda p: (p,) + (0,) * len(shape))


def call(kernel, pairs, in_specs, out_specs, out_shape, flops):
    return pl.pallas_call(
        kernel,
        grid=(pairs,),
        in_specs=in_specs,
        out_specs=out_specs,
        out_shape=out_shape,
        compiler_params=pltpu.CompilerParams(vmem_limit_bytes=VMEM_LIMIT),
        cost_estimate=pl.CostEstimate(flops=flops, bytes_accessed=8 << 20, transcendentals=0),
    )


def shaped(shape, dtype):
    return jax.ShapeDtypeStruct(shape, dtype)


CHUNK = 256
PANEL = 512
RING = 4
LAG = 6


def reduce_kernel(plan, *refs):
    count, terms = plan
    factors, small_ref = refs[: 2 * len(terms)], refs[2 * len(terms)]
    outs = refs[2 * len(terms) + 1 : 3 * len(terms) + 2]
    (
        work, give, take, part, outside, inside,
        give_send, give_recv, part_send, outer_recv, inner_recv, total_send,
        final_send, final_recv, own_sem,
    ) = refs[3 * len(terms) + 2 :]
    half = CHUNK // 2
    place, peers = lax.axis_index("ctx"), lax.axis_size("ctx")
    core, z, chips = place % 2, place // 2, peers // 2
    below = z < chips // 2
    middle = (z == chips // 2 - 1) | (z == chips // 2)
    has_outer = (z != 0) & (z != chips - 1)
    step = jnp.where(below, 2, -2)
    inner, outer, twin = place + step, place - step, place + 1 - 2 * core
    mine = pl.ds(pl.multiple_of(core * half, half), half)
    theirs = pl.ds(pl.multiple_of((1 - core) * half, half), half)

    def remote(src, dst, send, recv, to):
        return pltpu.make_async_remote_copy(
            src_ref=src, dst_ref=dst, send_sem=send, recv_sem=recv,
            device_id={"ctx": to}, device_id_type=pl.DeviceIdType.MESH,
        )

    def give_copy(t):
        return remote(give.at[t], take.at[t], give_send.at[t], give_recv.at[t], twin)

    def to_outside(t):
        return remote(part.at[t], outside.at[t], part_send.at[t], outer_recv.at[t], inner)

    def across(t):
        return remote(part.at[t], inside.at[t], part_send.at[t], inner_recv.at[t], inner)

    def outward(t):
        return remote(take.at[t], inside.at[t], total_send.at[t], inner_recv.at[t], outer)

    def final_copy(t, target):
        return remote(take.at[t], target, final_send.at[t], final_recv.at[t], twin)

    def own_copy(t, target):
        return pltpu.make_async_copy(take.at[t], target, own_sem.at[t])

    def block_of(j, panels):
        rows = (j // panels) * CHUNK
        return rows, pl.ds(pl.multiple_of((j % panels) * PANEL, PANEL), PANEL)

    def deliver(t, target):
        final_copy(t, target).start()
        own_copy(t, target).start()

    some_target = outs[-1].at[mine]

    barrier = pltpu.get_barrier_semaphore()
    for peer in (inner, twin):
        pl.semaphore_signal(
            barrier, inc=1, device_id={"ctx": peer}, device_id_type=pl.DeviceIdType.MESH
        )

    @pl.when(has_outer)
    def _():
        pl.semaphore_signal(
            barrier, inc=1, device_id={"ctx": outer}, device_id_type=pl.DeviceIdType.MESH
        )

    pl.semaphore_wait(barrier, 2 + has_outer.astype(jnp.int32))
    lag = jnp.where(middle, 2, LAG)

    def one(t, carry):
        slot = t % RING
        begin = 0
        for n, (blocks, panels) in enumerate(terms):
            left, right = factors[2 * n], factors[2 * n + 1]

            @pl.when((t >= begin) & (t < begin + blocks * panels))
            def _(left=left, right=right, panels=panels, begin=begin):
                start, cols = block_of(t - begin, panels)
                rows = pl.ds(pl.multiple_of(start, CHUNK), CHUNK)
                work[slot] = dot(left[:, rows], right[:, cols], 0, 0)

            begin += blocks * panels

        @pl.when(t == begin)
        def _():
            work[slot] = small_ref[...]

        @pl.when(t < count)
        def _():
            give[t] = work[slot, theirs, :].astype(BF)
            give_copy(t).start()

        tb = t - 1

        @pl.when((tb >= 0) & (tb < count))
        def _():
            give_copy(tb).wait_recv()
            total = work[(t + RING - 1) % RING, mine, :] + take[tb].astype(F32)

            @pl.when(has_outer)
            def _():
                to_outside(tb).wait_recv()
                part[tb] = (total + outside[tb].astype(F32)).astype(BF)

            @pl.when(jnp.logical_not(has_outer))
            def _():
                part[tb] = total.astype(BF)

            @pl.when(middle)
            def _():
                across(tb).start()

            @pl.when(jnp.logical_not(middle))
            def _():
                to_outside(tb).start()

        tc = t - lag

        @pl.when((tc >= 0) & (tc < count))
        def _():
            across(tc).wait_recv()

            @pl.when(middle)
            def _():
                take[tc] = (part[tc].astype(F32) + inside[tc].astype(F32)).astype(BF)

            @pl.when(jnp.logical_not(middle))
            def _():
                take[tc] = inside[tc]

            @pl.when(has_outer)
            def _():
                outward(tc).start()

            begin = 0
            for n, (blocks, panels) in enumerate(terms):

                @pl.when((tc >= begin) & (tc < begin + blocks * panels))
                def _(n=n, panels=panels, begin=begin):
                    start, cols = block_of(tc - begin, panels)
                    rows = pl.ds(pl.multiple_of(start + core * half, half), half)
                    deliver(tc, outs[n].at[rows, cols])

                begin += blocks * panels

            @pl.when(tc == begin)
            def _():
                deliver(tc, some_target)

        return carry

    lax.fori_loop(0, count + LAG, one, 0)

    def drain(t, carry):
        give_copy(t).wait_send()
        across(t).wait_send()
        final_copy(t, some_target).wait_send()
        final_copy(t, some_target).wait_recv()
        own_copy(t, some_target).wait()

        @pl.when(has_outer)
        def _():
            outward(t).wait_send()

        return carry

    lax.fori_loop(0, count, drain, 0)


def reduce_over_ctx(factors, small):
    terms = tuple((a.shape[1] // CHUNK, b.shape[1] // PANEL) for a, b in factors)
    count = sum(x * y for x, y in terms) + 1
    half = CHUNK // 2
    flat = [x for pair in factors for x in pair] + [small]
    slots = pltpu.VMEM((count, half, PANEL), BF)
    sums = pl.pallas_call(
        partial(reduce_kernel, (count, terms)),
        in_specs=[pl.BlockSpec(memory_space=pltpu.VMEM)] * len(flat),
        out_specs=[pl.BlockSpec(memory_space=pl.ANY)] * (len(terms) + 1),
        out_shape=[shaped((a.shape[1], b.shape[1]), BF) for a, b in factors]
        + [shaped((CHUNK, PANEL), BF)],
        scratch_shapes=[pltpu.VMEM((RING, CHUNK, PANEL), F32)]
        + [slots] * 5
        + [pltpu.SemaphoreType.DMA((count,))] * 9,
        compiler_params=pltpu.CompilerParams(
            collective_id=0, has_side_effects=True, vmem_limit_bytes=REDUCE_LIMIT
        ),
        cost_estimate=pl.CostEstimate(
            flops=count * 2 * CHUNK * PANEL * 512, bytes_accessed=40 << 20, transcendentals=0
        ),
    )(*flat)
    return [g.astype(F32) for g in sums[:-1]], sums[-1].astype(F32)


def fits_reduce(factors):
    even = lax.axis_size("ctx") % 4 == 0
    return even and all(
        a.shape[1] % CHUNK == 0 and b.shape[1] % PANEL == 0 for a, b in factors
    )


def exchange(forward, starts_ref, own_ref, got_ref, bufs, tokens):
    (twin_buf, in_buf, out_buf, back_buf, twin_sem, send_sem, recv_sem, back_send, back_recv) = bufs
    rows, pairs = own_ref.shape[:2]
    part = rows // 2
    chunks, width = in_buf.shape[:2]
    split = pairs // width
    place, chips = lax.axis_index("ctx"), lax.axis_size("ctx") // 2
    core, z = place % 2, place // 2
    away = z if forward else chips - 1 - z
    first, last = away == 0, away == chips - 1
    step = 2 if forward else -2
    twin = place + 1 - 2 * core
    leads = core == (0 if forward else 1)
    lead = 2 * z + (0 if forward else 1)
    other = 2 * z + (1 if forward else 0)

    def remote(src, dst, send, recv, to):
        return pltpu.make_async_remote_copy(
            src_ref=src, dst_ref=dst, send_sem=send, recv_sem=recv,
            device_id={"ctx": to}, device_id_type=pl.DeviceIdType.MESH,
        )

    def twin_copy():
        theirs = own_ref.at[pl.ds((1 - core) * part, part)]
        return remote(theirs, twin_buf, twin_sem.at[0], twin_sem.at[1], twin)

    def onward(j):
        return remote(out_buf.at[j], in_buf.at[j], send_sem.at[j], recv_sem.at[j], place + step)

    def where_of(j):
        return core * part + j // split, pl.ds((j % split) * width, width)

    def back(j):
        row, cols = where_of(j)
        return remote(back_buf.at[j], got_ref.at[row, cols], back_send.at[j], back_recv.at[j], twin)

    def passing(row, at):
        end = count_starts(starts_ref, row, at * tokens + tokens - 1)
        return (end == count_starts(starts_ref, row, at * tokens - 1)).astype(F32)

    def begin():
        barrier = pltpu.get_barrier_semaphore()

        def greet(peer):
            pl.semaphore_signal(
                barrier, inc=1, device_id={"ctx": peer}, device_id_type=pl.DeviceIdType.MESH
            )

        greet(twin)

        @pl.when(jnp.logical_not(first))
        def _():
            greet(place - step)

        pl.semaphore_wait(barrier, 2 - last.astype(jnp.int32))
        twin_copy().start()

    def advance(i):
        @pl.when(i == 0)
        def _():
            twin_copy().wait_recv()

        j = i - HOP * away

        @pl.when((j >= 0) & (j < chunks))
        def _():
            row, cols = where_of(j)

            @pl.when(first)
            def _():
                in_buf[j] = jnp.zeros(in_buf.shape[1:], F32)

            @pl.when(jnp.logical_not(first))
            def _():
                onward(j).wait_recv()

            mine, theirs = own_ref[row, cols], twin_buf[j // split, cols]
            entering_lead = in_buf[j]
            entering_other = jnp.where(leads, mine, theirs) + passing(row, lead) * entering_lead

            @pl.when(jnp.logical_not(last))
            def _():
                out_buf[j] = (
                    jnp.where(leads, theirs, mine) + passing(row, other) * entering_other
                )
                onward(j).start()

            got_ref[row, cols] = jnp.where(leads, entering_lead, entering_other)
            back_buf[j] = jnp.where(leads, entering_other, entering_lead)
            back(j).start()

    def finish():
        twin_copy().wait_send()

        def one(j, carry):
            back(j).wait_send()
            back(j).wait_recv()

            @pl.when(jnp.logical_not(last))
            def _():
                onward(j).wait_send()

            return carry

        lax.fori_loop(0, chunks, one, 0)

    return begin, advance, finish, (chips - 1) * HOP + chunks


def exchange_scratch(rows, pairs):
    width = pairs // 2 if pairs % 2 == 0 else pairs
    chunks = rows // 2 * (pairs // width)
    one = pltpu.VMEM((chunks, width, HELD, PAIR), F32)
    return [
        pltpu.VMEM((rows // 2, pairs, HELD, PAIR), F32), one, one, one,
        pltpu.SemaphoreType.DMA((2,)),
    ] + [pltpu.SemaphoreType.DMA((chunks,))] * 4


def tile(n):
    return pl.ds(pl.multiple_of(n * TILE, TILE), TILE)


def run_tiles(first_count, first_body, second_count, second_body, link):
    begin, advance, finish, steps = link
    begin()
    both = first_count + second_count

    def one(i, carry):
        @pl.when(i < first_count)
        def _():
            first_body(i)

        @pl.when((i >= first_count) & (i < both))
        def _():
            second_body(i - first_count)

        advance(i)
        return carry

    lax.fori_loop(0, max(both, steps), one, 0)
    finish()


def start_all(count, copy):
    def one(n, carry):
        copy(n).start()
        return carry

    lax.fori_loop(0, count, one, 0)


def feed_forward_kernel(
    tokens, starts_ref, own_ref, norm_ref, up_ref, bias_ref, down_ref,
    pre_ref, hidden_ref, mlp_ref, got_ref,
    up_buf, down_buf, up_sem, down_sem, *bufs,
):
    ups, downs = up_ref.shape[1] // TILE, down_ref.shape[1] // TILE

    def up_copy(n):
        return pltpu.make_async_copy(up_ref.at[:, tile(n)], up_buf.at[:, tile(n)], up_sem.at[n])

    def down_copy(n):
        return pltpu.make_async_copy(
            down_ref.at[:, tile(n)], down_buf.at[:, tile(n)], down_sem.at[n]
        )

    start_all(ups, up_copy)
    start_all(downs, down_copy)

    def up(n):
        up_copy(n).wait()
        pre = dot(norm_ref[...], up_buf[:, tile(n)]) + bias_ref[:, tile(n)]
        pre_ref[:, tile(n)] = pre
        hidden = 0.5 * pre * (1.0 + lax.erf(pre * math.sqrt(0.5)))
        hidden_ref[:, tile(n)] = hidden.astype(BF)

    def down(n):
        down_copy(n).wait()
        mlp_ref[:, tile(n)] = dot(hidden_ref[...], down_buf[:, tile(n)])

    run_tiles(ups, up, downs, down, exchange(True, starts_ref, own_ref, got_ref, bufs, tokens))


def feed_backward_kernel(
    tokens, starts_ref, own_ref, grad_ref, pre_ref, down_ref, up_ref,
    grad_pre_ref, grad_norm_ref, got_ref,
    pre_buf, down_buf, up_buf, pre_sem, down_sem, up_sem, *bufs,
):
    downs, ups = down_ref.shape[0] // TILE, up_ref.shape[0] // TILE

    def pre_copy(n):
        return pltpu.make_async_copy(pre_ref.at[:, tile(n)], pre_buf.at[:, tile(n)], pre_sem.at[n])

    def down_copy(n):
        return pltpu.make_async_copy(down_ref.at[tile(n)], down_buf.at[tile(n)], down_sem.at[n])

    def up_copy(n):
        return pltpu.make_async_copy(up_ref.at[tile(n)], up_buf.at[tile(n)], up_sem.at[n])

    start_all(downs, down_copy)
    start_all(downs, pre_copy)
    start_all(ups, up_copy)

    def down(n):
        down_copy(n).wait()
        pre_copy(n).wait()
        grad = dot(grad_ref[...], down_buf[tile(n), :], 1, 1)
        pre = pre_buf[:, tile(n)]
        cdf = 0.5 * (1.0 + lax.erf(pre * math.sqrt(0.5)))
        slope = cdf + pre * jnp.exp(-0.5 * pre * pre) * (1.0 / math.sqrt(2.0 * math.pi))
        grad_pre_ref[:, tile(n)] = (grad * slope).astype(BF)

    def up(n):
        up_copy(n).wait()
        grad_norm_ref[:, tile(n)] = dot(grad_pre_ref[...], up_buf[tile(n), :], 1, 1)

    run_tiles(downs, down, ups, up, exchange(False, starts_ref, own_ref, got_ref, bufs, tokens))


IN_VMEM = pl.BlockSpec(memory_space=pltpu.VMEM)
ANYWHERE = pl.BlockSpec(memory_space=pl.ANY)


def link_call(kernel, number, in_specs, out_shape, scratch, flops):
    return pl.pallas_call(
        kernel,
        in_specs=in_specs,
        out_specs=[IN_VMEM] * len(out_shape),
        out_shape=out_shape,
        scratch_shapes=scratch,
        compiler_params=pltpu.CompilerParams(
            collective_id=number, has_side_effects=True, vmem_limit_bytes=VMEM_LIMIT
        ),
        cost_estimate=pl.CostEstimate(flops=flops, bytes_accessed=16 << 20, transcendentals=0),
    )


def feed_forward(starts, state, norm, w_up, b_up, w_down):
    total, units = norm.shape[0], w_up.shape[1]
    rows, pairs = state.shape[:2]
    return link_call(
        partial(feed_forward_kernel, total // rows),
        1,
        [SMEM, IN_VMEM, IN_VMEM, ANYWHERE, IN_VMEM, ANYWHERE],
        [
            shaped((total, units), F32), shaped((total, units), BF), shaped((total, D), F32),
            shaped(state.shape, F32),
        ],
        [
            pltpu.VMEM(w_up.shape, BF), pltpu.VMEM(w_down.shape, BF),
            pltpu.SemaphoreType.DMA((units // TILE,)), pltpu.SemaphoreType.DMA((D // TILE,)),
        ]
        + exchange_scratch(rows, pairs),
        4 * total * units * D,
    )(starts, state, norm, w_up, b_up.reshape(1, units), w_down)


def feed_backward(starts, state, grad, pre, w_down, w_up):
    total, units = pre.shape
    rows, pairs = state.shape[:2]
    return link_call(
        partial(feed_backward_kernel, total // rows),
        2,
        [SMEM, IN_VMEM, IN_VMEM, ANYWHERE, ANYWHERE, ANYWHERE],
        [shaped((total, units), BF), shaped((total, D), F32), shaped(state.shape, F32)],
        [
            pltpu.VMEM(pre.shape, F32), pltpu.VMEM(w_down.shape, BF), pltpu.VMEM(w_up.shape, BF),
            pltpu.SemaphoreType.DMA((units // TILE,)), pltpu.SemaphoreType.DMA((units // TILE,)),
            pltpu.SemaphoreType.DMA((D // TILE,)),
        ]
        + exchange_scratch(rows, pairs),
        4 * total * units * D,
    )(starts, state, grad, pre, w_down, w_up)


def gather_tp(value):
    if lax.axis_size("tp") != 2:
        return lax.all_gather(value, "tp", axis=1, tiled=True)
    other = lax.ppermute(value, "tp", [(0, 1), (1, 0)])
    return jnp.where(
        lax.axis_index("tp") == 0,
        jnp.concatenate([value, other], 1),
        jnp.concatenate([other, value], 1),
    )


def scatter_tp(value):
    peers = lax.axis_size("tp")
    if peers != 2:
        return lax.psum_scatter(value, "tp", scatter_dimension=1, tiled=True)
    me = lax.axis_index("tp")
    width = value.shape[1] // 2
    left, right = value[:, :width], value[:, width:]
    other = lax.ppermute(jnp.where(me == 0, right, left).astype(BF), "tp", [(0, 1), (1, 0)])
    return jnp.where(me == 0, left, right) + other.astype(F32)


def local(
    section_inputs,
    doc_starts,
    ln_gains,
    ln_shifts,
    qkv_weight,
    qkv_bias,
    feature_weight,
    dense_weight,
    out_bias,
    up_weight,
    up_bias,
    down_weight,
):
    section = lax.axis_index("pipe")
    place = lax.axis_index("ctx")
    width = section_inputs.shape[-1]
    tokens = section_inputs.shape[3]
    rows = MB * ROWS
    total = rows * tokens
    heads = feature_weight.shape[1]
    pairs = heads // 2
    gain, shift = ln_gains[0], ln_shifts[0]
    w_qkv, w_dense, w_up, w_down = qkv_weight[0], dense_weight[0], up_weight[0], down_weight[0]
    b_qkv = qkv_bias[0].reshape(pairs, 1, 3 * PAIR)
    b_up, b_out = up_bias[0], out_bias[0]
    feat = feature_weight[0].reshape(pairs, 1, PAIR)
    starts = doc_starts.reshape(rows, NDOC)
    place_in = place.astype(jnp.int32).reshape(1, 1)
    high, low = table_pair()
    same, down, up = rotary_tables(place, tokens)
    tables = (same, down, up, high, low)
    table_specs = [whole((tokens, PAIR))] * 3 + [whole((PAIR, PAIR))] * 2
    state_shape = shaped((rows, pairs, HELD, PAIR), F32)
    state_spec = pl.BlockSpec((rows, 1, HELD, PAIR), lambda p: (0, p, 0, 0))
    low_shape, full_shape = shaped((total, pairs * PAIR), BF), shaped((total, pairs * PAIR), F32)
    unit = 2 * rows * tokens * PAIR * PAIR * pairs

    def forward(u_low, own):
        u = u_low.astype(F32)
        centered = u - jnp.mean(u, -1, keepdims=True)
        inv = lax.rsqrt(jnp.mean(centered * centered, -1, keepdims=True) + norm_eps)
        xhat = centered * inv
        first = (xhat * gain[0] + shift[0]).astype(BF)
        second = (xhat * gain[1] + shift[1]).astype(BF)
        q, k, v, state = call(
            features_kernel,
            pairs,
            [SMEM, SMEM, whole((total, D)), column(D, 3 * PAIR), stacked(1, 3 * PAIR),
             stacked(1, PAIR)] + table_specs,
            [column(total, PAIR)] * 3 + [state_spec],
            [low_shape] * 3 + [state_shape],
            30 * unit,
        )(starts, place_in, first, w_qkv, b_qkv, feat, *tables)
        pre, hidden, mlp, state_in = feed_forward(starts, state, second, w_up, b_up, w_down)
        att_low, att, den = call(
            attend_kernel,
            pairs,
            [SMEM, SMEM] + [column(total, PAIR)] * 3 + [state_spec],
            [column(total, PAIR)] * 3,
            [low_shape, full_shape, full_shape],
            8 * unit,
        )(starts, place_in, q, k, v, state_in)
        part = jnp.dot(att_low, w_dense, preferred_element_type=F32) + mlp
        out = scatter_tp(part) + own.astype(F32) + b_out
        kept = (xhat, inv, first, second, q, k, v, pre, hidden, att_low, att, den, state_in)
        return out, kept

    def backward(dy, own, kept, want):
        xhat, inv, first, second, q, k, v, pre, hidden, att_low, att, den, state_in = kept
        ga = lax.dot_general(
            dy, w_dense, (((1,), (1,)), ((), ())), preferred_element_type=F32
        ).astype(BF)
        (state,) = call(
            back_state_kernel,
            pairs,
            [SMEM, SMEM] + [column(total, PAIR)] * 4,
            [state_spec],
            [state_shape],
            3 * unit,
        )(starts, place_in, q, ga, att, den)
        grad_pre, grad_second, later = feed_backward(starts, state, dy, pre, w_down, w_up)
        grad_proj, sums = call(
            back_kernel,
            pairs,
            [SMEM, SMEM] + [column(total, PAIR)] * 6
            + [state_spec, state_spec, stacked(1, PAIR)] + table_specs,
            [column(total, 3 * PAIR), stacked(8, PAIR)],
            [shaped((total, pairs * 3 * PAIR), BF), shaped((pairs, 8, PAIR), F32)],
            20 * unit,
        )(starts, place_in, q, k, v, ga, att, den, state_in, later, feat, *tables)
        grad_first = lax.dot_general(
            grad_proj, w_qkv, (((1,), (1,)), ((), ())), preferred_element_type=F32
        )
        both = grad_first * gain[0] + grad_second * gain[1]
        part = inv * (
            both
            - jnp.mean(both, -1, keepdims=True)
            - xhat * jnp.mean(both * xhat, -1, keepdims=True)
        )
        grad_input = scatter_tp(part) + own.astype(F32)
        if not want:
            return grad_input, None

        large = ((hidden, dy), (second, grad_pre), (att_low, dy), (first, grad_proj))
        norm_sums = jnp.stack(
            [
                jnp.sum(grad_first * xhat, 0),
                jnp.sum(grad_second * xhat, 0),
                jnp.sum(grad_first, 0),
                jnp.sum(grad_second, 0),
            ]
        )
        small = (
            sums[:, 1:4, :].reshape(pairs * 3 * PAIR),
            sums[:, 0, :].reshape(heads, FEAT),
            jnp.sum(own.astype(F32), 0),
            jnp.sum(grad_pre.astype(F32), 0),
        )
        return grad_input, (large, norm_sums, small)

    mine = section_inputs[0].reshape(total, width)
    mine_full = gather_tp(mine)
    y0, _ = forward(mine_full, mine)
    sent = lax.ppermute(y0.astype(BF), "pipe", [(0, 1)])
    own_in = jnp.where(section == 0, mine, sent)
    full_in = jnp.where(section == 0, mine_full, gather_tp(sent))
    y1, kept = forward(full_in, own_in)
    du1, _ = backward(mine_full, mine, kept, False)
    sent = lax.ppermute(du1.astype(BF), "pipe", [(1, 0)])
    own_grad = jnp.where(section == 1, mine, sent)
    full_grad = jnp.where(section == 1, mine_full, gather_tp(sent))
    du0, (large, norm_sums, small) = backward(full_grad, own_grad, kept, True)
    if lax.axis_size("tp") == 2:
        me = lax.axis_index("tp")
        away = lax.dynamic_slice_in_dim(norm_sums, (1 - me) * width, width, 1)
        norm_sums = lax.dynamic_slice_in_dim(norm_sums, me * width, width, 1)
        norm_sums = norm_sums + lax.ppermute(away, "tp", [(0, 1), (1, 0)])
    else:
        norm_sums = lax.psum_scatter(norm_sums, "tp", scatter_dimension=1, tiled=True)
    small = small + (norm_sums,)
    if fits_reduce(large):
        flat = jnp.concatenate([x.reshape(-1) for x in small])
        flat = jnp.pad(flat, (0, CHUNK * PANEL - flat.size)).reshape(CHUNK, PANEL)
        (g_down, g_up, g_dense, g_qkv), flat = reduce_over_ctx(large, flat)
        flat, summed, begin = flat.reshape(-1), [], 0
        for x in small:
            summed.append(flat[begin : begin + x.size].reshape(x.shape))
            begin += x.size
    else:
        products = tuple(dot(a, b, 0, 0).astype(BF) for a, b in large)
        g_down, g_up, g_dense, g_qkv = (g.astype(F32) for g in lax.psum(products, "ctx"))
        summed = lax.psum(small, "ctx")
    g_qkv_bias, g_feat, g_out_bias, g_up_bias, norm_sums = summed
    section_ends = jnp.where(section == 0, du0, y1).reshape(1, MB, ROWS, tokens, width)
    grads = (
        norm_sums[:2], norm_sums[2:], g_qkv, g_qkv_bias, g_feat, g_dense, g_out_bias,
        g_up, g_up_bias, g_down,
    )
    return (section_ends,) + tuple(g[None] for g in grads)


def solution(mesh):
    in_specs = (
        P("pipe", None, None, "ctx", "tp"),
        P(),
        P("pipe", None, None),
        P("pipe", None, None),
        P("pipe", None, "tp"),
        P("pipe", "tp"),
        P("pipe", "tp", None),
        P("pipe", "tp", None),
        P("pipe", "tp"),
        P("pipe", None, "tp"),
        P("pipe", "tp"),
        P("pipe", "tp", None),
    )
    out_specs = (
        P("pipe", None, None, "ctx", "tp"),
        P("pipe", None, "tp"),
        P("pipe", None, "tp"),
        P("pipe", None, "tp"),
        P("pipe", "tp"),
        P("pipe", "tp", None),
        P("pipe", "tp", None),
        P("pipe", "tp"),
        P("pipe", None, "tp"),
        P("pipe", "tp"),
        P("pipe", "tp", None),
    )
    return jax.shard_map(local, mesh=mesh, in_specs=in_specs, out_specs=out_specs, check_vma=False)
```

```python
from functools import partial
import math

import jax
import jax.numpy as jnp
from jax import lax
from jax.experimental import pallas as pl
from jax.experimental.pallas import tpu as pltpu
from jax.sharding import PartitionSpec as P

D = 1024
HD = 64
ROT = 16
FEAT = 64
MB = 4
ROWS = 1
NDOC = 4
PAIR = 2 * HD
HELD = HD + 8
TILE = 256
HOP = 2

BF = jnp.bfloat16
F32 = jnp.float32
HIGHEST = lax.Precision.HIGHEST
norm_eps = 1e-05
VMEM_LIMIT = 56 * 1024 * 1024
REDUCE_LIMIT = 60 * 1024 * 1024


def feature_table():
    index_rows = jnp.arange(HD, dtype=jnp.int32)[:, None]
    index_cols = jnp.arange(HD, dtype=jnp.int32)[None, :]
    cosine = jnp.cos(
        math.pi * (index_rows.astype(F32) + 0.5) * index_cols.astype(F32) / HD
    )
    scaling = jnp.where(index_cols == 0, math.sqrt(1.0 / HD), math.sqrt(2.0 / HD))
    lattice_index = (
        (jnp.arange(HD, dtype=jnp.int32)[:, None] + 1)
        * (17 * jnp.arange(FEAT, dtype=jnp.int32)[None, :] + 5)
        % 257
    )
    lattice = math.sqrt(2.0) * jnp.cos(2.0 * math.pi * lattice_index.astype(F32) / 257.0)
    return jnp.dot(cosine * scaling, lattice, precision=HIGHEST) / math.sqrt(HD)


def table_pair():
    table = feature_table()
    zero = jnp.zeros_like(table)
    both = jnp.concatenate(
        [jnp.concatenate([table, zero], 1), jnp.concatenate([zero, table], 1)], 0
    )
    high = lax.reduce_precision(both, 8, 7).astype(BF)
    return high, (both - high.astype(F32)).astype(BF)


def rotary_tables(place, tokens):
    half = ROT // 2
    positions = place * tokens + jnp.arange(tokens, dtype=jnp.int32)
    inv_freq = 10000.0 ** (-(2.0 * jnp.arange(half).astype(F32)) / ROT)
    angles = positions.astype(F32)[:, None] * inv_freq[None, :]
    cos, sin = jnp.cos(angles), jnp.sin(angles)
    rest = jnp.ones((tokens, HD - ROT), F32)
    none = jnp.zeros((tokens, half), F32)
    same = jnp.concatenate([cos, cos, rest], 1)
    down = jnp.concatenate([-sin, none, 0.0 * rest], 1)
    up = jnp.concatenate([none, sin, 0.0 * rest], 1)
    return tuple(jnp.concatenate([t, t], 1) for t in (same, down, up))


def dot(a, b, ca=1, cb=0):
    return lax.dot_general(a, b, (((ca,), (cb,)), ((), ())), preferred_element_type=F32)


def split_dot(a, b, cb=0):
    high = a.astype(BF)
    low = (a - high.astype(F32)).astype(BF)
    return dot(high, b, 1, cb) + dot(low, b, 1, cb)


def lane_masks(rows):
    low = lax.broadcasted_iota(jnp.int32, (rows, PAIR), 1) < HD
    first = low.astype(F32)
    return low, first.astype(BF), (1.0 - first).astype(BF)


def count_starts(starts_ref, row, position):
    total = jnp.int32(0)
    for n in range(NDOC):
        total = total + (starts_ref[row, n] <= position).astype(jnp.int32)
    return total


def seg_grid(starts_ref, row, base, shape, dim):
    position = base + lax.broadcasted_iota(jnp.int32, shape, dim)
    total = jnp.zeros(shape, jnp.int32)
    for n in range(NDOC):
        total = total + (starts_ref[row, n] <= position).astype(jnp.int32)
    return total


def causal_mask(starts_ref, row, base, tokens):
    shape = (tokens, tokens)
    same = seg_grid(starts_ref, row, base, shape, 0) == seg_grid(starts_ref, row, base, shape, 1)
    earlier = lax.broadcasted_iota(jnp.int32, shape, 1) <= lax.broadcasted_iota(
        jnp.int32, shape, 0
    )
    rows = lax.broadcasted_iota(jnp.int32, shape, 0) < tokens // 2
    cols = lax.broadcasted_iota(jnp.int32, shape, 1) < tokens // 2
    mask = same & earlier
    return mask.astype(F32), (mask & (rows == cols)).astype(F32)


def middle_state(starts_ref, row, base, tokens, k, v, state_in, total_in, low):
    half = tokens // 2
    end = count_starts(starts_ref, row, base + half - 1)
    passing = (end == count_starts(starts_ref, row, base - 1)).astype(F32)
    seg = seg_grid(starts_ref, row, base, (half, PAIR), 0)
    key = k[:half] * (seg == end).astype(F32).astype(BF)
    state = passing * state_in + compact(dot(key, v[:half], 0, 0), low)
    total = passing * total_in + jnp.sum(key.astype(F32), 0, keepdims=True)
    later = seg_grid(starts_ref, row, base + half, (half, PAIR), 0)
    return state.astype(BF), total, (later == end).astype(F32)


def entering_mask(starts_ref, row, base, tokens):
    seg = seg_grid(starts_ref, row, base, (tokens, PAIR), 0)
    return (seg == count_starts(starts_ref, row, base - 1)).astype(F32)


def leaving_mask(starts_ref, row, base, tokens):
    seg = seg_grid(starts_ref, row, base, (tokens, PAIR), 0)
    return (seg == count_starts(starts_ref, row, base + tokens - 1)).astype(F32)


def rotate(x, same, down, up):
    half = ROT // 2
    return x * same + pltpu.roll(x, PAIR - half, 1) * down + pltpu.roll(x, half, 1) * up


def rotate_back(x, same, down, up):
    half = ROT // 2
    return x * same + pltpu.roll(x * down, half, 1) + pltpu.roll(x * up, PAIR - half, 1)


def compact(state, low):
    return jnp.where(low[:HD], state[:HD], state[HD:])


def spread(state, first, second):
    return jnp.concatenate([state * first[:HD], state * second[:HD]], 0)


def keep_state(state_ref, row, product, summands, low):
    state_ref[row, 0, :HD] = compact(product, low)
    total = jnp.sum(summands, 0, keepdims=True)
    state_ref[row, 0, HD:] = jnp.broadcast_to(total, (HELD - HD, PAIR))


def features_kernel(
    starts_ref, place_ref, norm_ref, weight_ref, bias_ref, feat_ref,
    same_ref, down_ref, up_ref, high_ref, low_ref,
    q_ref, k_ref, v_ref, state_ref,
):
    tokens = same_ref.shape[0]
    base = place_ref[0, 0] * tokens
    low, first, second = lane_masks(tokens)
    feat = feat_ref[0]
    for row in range(MB * ROWS):
        here = slice(row * tokens, (row + 1) * tokens)
        proj = dot(norm_ref[here, :], weight_ref[...]) + bias_ref[0]
        c0, c1, c2 = proj[:, :PAIR], proj[:, PAIR : 2 * PAIR], proj[:, 2 * PAIR :]
        query = jnp.where(low, c0, c1)
        key = pltpu.roll(jnp.where(low, c2, c0), HD, 1)
        value = jnp.where(low, c1, c2).astype(BF)
        out = []
        for x in (query, key):
            x = rotate(x, same_ref[...], down_ref[...], up_ref[...])
            arg = split_dot(x, high_ref[...]) + dot(x.astype(BF), low_ref[...])
            out.append((feat * jnp.exp(arg)).astype(BF))
        q_ref[here, :] = out[0]
        k_ref[here, :] = out[1]
        v_ref[here, :] = value
        leaving = leaving_mask(starts_ref, row, base, tokens)
        key_out = out[1] * leaving.astype(BF)
        keep_state(state_ref, row, dot(key_out, value, 0, 0), key_out.astype(F32), low)


def attend_kernel(
    starts_ref, place_ref, q_ref, k_ref, v_ref, state_ref, low_ref, out_ref, den_ref
):
    tokens = q_ref.shape[0] // (MB * ROWS)
    base = place_ref[0, 0] * tokens
    low, first, second = lane_masks(tokens)
    ones = head_ones()
    for row in range(MB * ROWS):
        here = slice(row * tokens, (row + 1) * tokens)
        q, k, v = q_ref[here, :], k_ref[here, :], v_ref[here, :]
        mask, mask_in = causal_mask(starts_ref, row, base, tokens)
        enter = entering_mask(starts_ref, row, base, tokens)
        carry, total = state_ref[row, 0, :HD], state_ref[row, 0, HD : HD + 1]
        state = carry.astype(BF)
        middle, _, reach = middle_state(starts_ref, row, base, tokens, k, v, carry, total, low)
        half = tokens // 2
        num = jnp.concatenate(
            [
                dot(q[:half] * enter[:half].astype(BF), spread(state, first, second)),
                dot(q[half:] * reach.astype(BF), spread(middle, first, second)),
            ],
            0,
        )
        for head in (first, second):
            scores = dot(q * head, k, 1, 1) * mask_in
            num = num + dot(scores.astype(BF), v * head)
        totals = dot(mask.astype(BF), k) + enter * total
        den = split_dot(q.astype(F32) * totals, ones)
        att = num / den
        low_ref[here, :] = att.astype(BF)
        out_ref[here, :] = att
        den_ref[here, :] = den


def head_ones():
    rows = lax.broadcasted_iota(jnp.int32, (PAIR, PAIR), 0) < HD
    cols = lax.broadcasted_iota(jnp.int32, (PAIR, PAIR), 1) < HD
    return (rows == cols).astype(F32).astype(BF)


def head_spread():
    rows = lax.broadcasted_iota(jnp.int32, (PAIR, 2 * PAIR), 0) < HD
    cols = lax.broadcasted_iota(jnp.int32, (PAIR, 2 * PAIR), 1) < PAIR
    return (rows == cols).astype(F32).astype(BF)


def back_state_kernel(
    starts_ref, place_ref, q_ref, ga_ref, att_ref, den_ref, state_ref
):
    tokens = q_ref.shape[0] // (MB * ROWS)
    base = place_ref[0, 0] * tokens
    low, first, second = lane_masks(tokens)
    ones = head_ones()
    for row in range(MB * ROWS):
        here = slice(row * tokens, (row + 1) * tokens)
        grad_num = (ga_ref[here, :].astype(F32) / den_ref[here, :]).astype(BF)
        grad_den = -split_dot(grad_num.astype(F32) * att_ref[here, :], ones)
        enter = entering_mask(starts_ref, row, base, tokens)
        query = q_ref[here, :] * enter.astype(BF)
        keep_state(state_ref, row, dot(query, grad_num, 0, 0), grad_den * query.astype(F32), low)


def back_kernel(
    starts_ref, place_ref, q_ref, k_ref, v_ref, ga_ref, att_ref, den_ref,
    state_ref, later_ref, feat_ref,
    same_ref, down_ref, up_ref, high_ref, low_ref,
    grad_ref, sums_ref,
):
    tokens = q_ref.shape[0] // (MB * ROWS)
    base = place_ref[0, 0] * tokens
    low, first, second = lane_masks(tokens)
    spreading = head_spread()
    feat_sum = jnp.zeros((1, PAIR), F32)
    bias_sum = [jnp.zeros((1, PAIR), F32) for _ in range(3)]
    for row in range(MB * ROWS):
        here = slice(row * tokens, (row + 1) * tokens)
        q, k, v = q_ref[here, :], k_ref[here, :], v_ref[here, :]
        grad_num = (ga_ref[here, :].astype(F32) / den_ref[here, :]).astype(BF)
        both = -split_dot(grad_num.astype(F32) * att_ref[here, :], spreading)
        dens = (both[:, :PAIR], both[:, PAIR:])
        grad_den = jnp.where(low, dens[0], dens[1])
        mask, mask_in = causal_mask(starts_ref, row, base, tokens)
        enter = entering_mask(starts_ref, row, base, tokens)
        leave = leaving_mask(starts_ref, row, base, tokens)
        carry, total = state_ref[row, 0, :HD], state_ref[row, 0, HD : HD + 1]
        state = carry.astype(BF)
        middle, middle_total, reach = middle_state(
            starts_ref, row, base, tokens, k, v, carry, total, low
        )
        half = tokens // 2
        gq = jnp.concatenate(
            [
                enter[:half]
                * (dot(grad_num[:half], spread(state, first, second), 1, 1) + grad_den[:half] * total),
                reach
                * (
                    dot(grad_num[half:], spread(middle, first, second), 1, 1)
                    + grad_den[half:] * middle_total
                ),
            ],
            0,
        )
        later = later_ref[row, 0, :HD]
        later_high = later.astype(BF)
        later_low = spread((later - later_high.astype(F32)).astype(BF), first, second)
        later_high = spread(later_high, first, second)
        gk = leave * (
            dot(v, later_high, 1, 1) + dot(v, later_low, 1, 1) + later_ref[row, 0, HD : HD + 1]
        )
        gv = leave * (dot(k, later_high) + dot(k, later_low))
        for head, den in zip((first, second), dens):
            q_head, grad_head = q * head, grad_num * head
            scores = (dot(q_head, k, 1, 1) * mask).astype(BF)
            grad_scores = dot(grad_head, v, 1, 1) + den
            gq = gq + dot((grad_scores * mask_in).astype(BF), k * head)
            gk = gk + dot((grad_scores * mask).astype(BF), q_head, 0, 0)
            gv = gv + dot(scores, grad_head, 0, 0)
        arg_grads = (gq * q.astype(F32), gk * k.astype(F32))
        feat_sum = feat_sum + jnp.sum(arg_grads[0] + arg_grads[1], 0, keepdims=True)
        turned = []
        for x in arg_grads:
            x = split_dot(x, high_ref[...], 1) + dot(x.astype(BF), low_ref[...], 1, 1)
            turned.append(rotate_back(x, same_ref[...], down_ref[...], up_ref[...]))
        dq, dk = turned[0], pltpu.roll(turned[1], HD, 1)
        parts = (jnp.where(low, dq, dk), jnp.where(low, gv, dq), jnp.where(low, dk, gv))
        for n, part in enumerate(parts):
            part = part.astype(BF)
            grad_ref[here, n * PAIR : (n + 1) * PAIR] = part
            bias_sum[n] = bias_sum[n] + jnp.sum(part.astype(F32), 0, keepdims=True)
    sums_ref[0, 0:1, :] = feat_sum / feat_ref[0]
    for n in range(3):
        sums_ref[0, n + 1 : n + 2, :] = bias_sum[n]


SMEM = pl.BlockSpec(memory_space=pltpu.SMEM)


def whole(shape):
    return pl.BlockSpec(shape, lambda p: (0,) * len(shape))


def column(rows, width):
    return pl.BlockSpec((rows, width), lambda p: (0, p))


def stacked(*shape):
    return pl.BlockSpec((1,) + shape, lambda p: (p,) + (0,) * len(shape))


def call(kernel, pairs, in_specs, out_specs, out_shape, flops):
    return pl.pallas_call(
        kernel,
        grid=(pairs,),
        in_specs=in_specs,
        out_specs=out_specs,
        out_shape=out_shape,
        compiler_params=pltpu.CompilerParams(vmem_limit_bytes=VMEM_LIMIT),
        cost_estimate=pl.CostEstimate(flops=flops, bytes_accessed=8 << 20, transcendentals=0),
    )


def shaped(shape, dtype):
    return jax.ShapeDtypeStruct(shape, dtype)


CHUNK = 256
PANEL = 512
RING = 4
LAG = 6


def reduce_kernel(plan, *refs):
    count, terms = plan
    factors, small_ref = refs[: 2 * len(terms)], refs[2 * len(terms)]
    outs = refs[2 * len(terms) + 1 : 3 * len(terms) + 2]
    (
        work, give, take, part, outside, inside,
        give_send, give_recv, part_send, outer_recv, inner_recv, total_send,
        final_send, final_recv, own_sem,
    ) = refs[3 * len(terms) + 2 :]
    half = CHUNK // 2
    place, peers = lax.axis_index("ctx"), lax.axis_size("ctx")
    core, z, chips = place % 2, place // 2, peers // 2
    below = z < chips // 2
    middle = (z == chips // 2 - 1) | (z == chips // 2)
    has_outer = (z != 0) & (z != chips - 1)
    step = jnp.where(below, 2, -2)
    inner, outer, twin = place + step, place - step, place + 1 - 2 * core
    mine = pl.ds(pl.multiple_of(core * half, half), half)
    theirs = pl.ds(pl.multiple_of((1 - core) * half, half), half)

    def remote(src, dst, send, recv, to):
        return pltpu.make_async_remote_copy(
            src_ref=src, dst_ref=dst, send_sem=send, recv_sem=recv,
            device_id={"ctx": to}, device_id_type=pl.DeviceIdType.MESH,
        )

    def give_copy(t):
        return remote(give.at[t], take.at[t], give_send.at[t], give_recv.at[t], twin)

    def to_outside(t):
        return remote(part.at[t], outside.at[t], part_send.at[t], outer_recv.at[t], inner)

    def across(t):
        return remote(part.at[t], inside.at[t], part_send.at[t], inner_recv.at[t], inner)

    def outward(t):
        return remote(take.at[t], inside.at[t], total_send.at[t], inner_recv.at[t], outer)

    def final_copy(t, target):
        return remote(take.at[t], target, final_send.at[t], final_recv.at[t], twin)

    def own_copy(t, target):
        return pltpu.make_async_copy(take.at[t], target, own_sem.at[t])

    def block_of(j, panels):
        rows = (j // panels) * CHUNK
        return rows, pl.ds(pl.multiple_of((j % panels) * PANEL, PANEL), PANEL)

    def deliver(t, target):
        final_copy(t, target).start()
        own_copy(t, target).start()

    some_target = outs[-1].at[mine]

    barrier = pltpu.get_barrier_semaphore()
    for peer in (inner, twin):
        pl.semaphore_signal(
            barrier, inc=1, device_id={"ctx": peer}, device_id_type=pl.DeviceIdType.MESH
        )

    @pl.when(has_outer)
    def _():
        pl.semaphore_signal(
            barrier, inc=1, device_id={"ctx": outer}, device_id_type=pl.DeviceIdType.MESH
        )

    pl.semaphore_wait(barrier, 2 + has_outer.astype(jnp.int32))
    lag = jnp.where(middle, 2, LAG)

    def one(t, carry):
        slot = t % RING
        begin = 0
        for n, (blocks, panels) in enumerate(terms):
            left, right = factors[2 * n], factors[2 * n + 1]

            @pl.when((t >= begin) & (t < begin + blocks * panels))
            def _(left=left, right=right, panels=panels, begin=begin):
                start, cols = block_of(t - begin, panels)
                rows = pl.ds(pl.multiple_of(start, CHUNK), CHUNK)
                work[slot] = dot(left[:, rows], right[:, cols], 0, 0)

            begin += blocks * panels

        @pl.when(t == begin)
        def _():
            work[slot] = small_ref[...]

        @pl.when(t < count)
        def _():
            give[t] = work[slot, theirs, :].astype(BF)
            give_copy(t).start()

        tb = t - 1

        @pl.when((tb >= 0) & (tb < count))
        def _():
            give_copy(tb).wait_recv()
            total = work[(t + RING - 1) % RING, mine, :] + take[tb].astype(F32)

            @pl.when(has_outer)
            def _():
                to_outside(tb).wait_recv()
                part[tb] = (total + outside[tb].astype(F32)).astype(BF)

            @pl.when(jnp.logical_not(has_outer))
            def _():
                part[tb] = total.astype(BF)

            @pl.when(middle)
            def _():
                across(tb).start()

            @pl.when(jnp.logical_not(middle))
            def _():
                to_outside(tb).start()

        tc = t - lag

        @pl.when((tc >= 0) & (tc < count))
        def _():
            across(tc).wait_recv()

            @pl.when(middle)
            def _():
                take[tc] = (part[tc].astype(F32) + inside[tc].astype(F32)).astype(BF)

            @pl.when(jnp.logical_not(middle))
            def _():
                take[tc] = inside[tc]

            @pl.when(has_outer)
            def _():
                outward(tc).start()

            begin = 0
            for n, (blocks, panels) in enumerate(terms):

                @pl.when((tc >= begin) & (tc < begin + blocks * panels))
                def _(n=n, panels=panels, begin=begin):
                    start, cols = block_of(tc - begin, panels)
                    rows = pl.ds(pl.multiple_of(start + core * half, half), half)
                    deliver(tc, outs[n].at[rows, cols])

                begin += blocks * panels

            @pl.when(tc == begin)
            def _():
                deliver(tc, some_target)

        return carry

    lax.fori_loop(0, count + LAG, one, 0)

    def drain(t, carry):
        give_copy(t).wait_send()
        across(t).wait_send()
        final_copy(t, some_target).wait_send()
        final_copy(t, some_target).wait_recv()
        own_copy(t, some_target).wait()

        @pl.when(has_outer)
        def _():
            outward(t).wait_send()

        return carry

    lax.fori_loop(0, count, drain, 0)


def reduce_over_ctx(factors, small):
    terms = tuple((a.shape[1] // CHUNK, b.shape[1] // PANEL) for a, b in factors)
    count = sum(x * y for x, y in terms) + 1
    half = CHUNK // 2
    flat = [x for pair in factors for x in pair] + [small]
    slots = pltpu.VMEM((count, half, PANEL), BF)
    sums = pl.pallas_call(
        partial(reduce_kernel, (count, terms)),
        in_specs=[pl.BlockSpec(memory_space=pltpu.VMEM)] * len(flat),
        out_specs=[pl.BlockSpec(memory_space=pl.ANY)] * (len(terms) + 1),
        out_shape=[shaped((a.shape[1], b.shape[1]), BF) for a, b in factors]
        + [shaped((CHUNK, PANEL), BF)],
        scratch_shapes=[pltpu.VMEM((RING, CHUNK, PANEL), F32)]
        + [slots] * 5
        + [pltpu.SemaphoreType.DMA((count,))] * 9,
        compiler_params=pltpu.CompilerParams(
            collective_id=0, has_side_effects=True, vmem_limit_bytes=REDUCE_LIMIT
        ),
        cost_estimate=pl.CostEstimate(
            flops=count * 2 * CHUNK * PANEL * 512, bytes_accessed=40 << 20, transcendentals=0
        ),
    )(*flat)
    return [g.astype(F32) for g in sums[:-1]], sums[-1].astype(F32)


def fits_reduce(factors):
    even = lax.axis_size("ctx") % 4 == 0
    return even and all(
        a.shape[1] % CHUNK == 0 and b.shape[1] % PANEL == 0 for a, b in factors
    )


def exchange(forward, starts_ref, own_ref, got_ref, bufs, tokens):
    (twin_buf, in_buf, out_buf, back_buf, twin_sem, send_sem, recv_sem, back_send, back_recv) = bufs
    rows, pairs = own_ref.shape[:2]
    part = rows // 2
    chunks, width = in_buf.shape[:2]
    split = pairs // width
    place, chips = lax.axis_index("ctx"), lax.axis_size("ctx") // 2
    core, z = place % 2, place // 2
    away = z if forward else chips - 1 - z
    first, last = away == 0, away == chips - 1
    step = 2 if forward else -2
    twin = place + 1 - 2 * core
    leads = core == (0 if forward else 1)
    lead = 2 * z + (0 if forward else 1)
    other = 2 * z + (1 if forward else 0)

    def remote(src, dst, send, recv, to):
        return pltpu.make_async_remote_copy(
            src_ref=src, dst_ref=dst, send_sem=send, recv_sem=recv,
            device_id={"ctx": to}, device_id_type=pl.DeviceIdType.MESH,
        )

    def twin_copy():
        theirs = own_ref.at[pl.ds((1 - core) * part, part)]
        return remote(theirs, twin_buf, twin_sem.at[0], twin_sem.at[1], twin)

    def onward(j):
        return remote(out_buf.at[j], in_buf.at[j], send_sem.at[j], recv_sem.at[j], place + step)

    def where_of(j):
        return core * part + j // split, pl.ds((j % split) * width, width)

    def back(j):
        row, cols = where_of(j)
        return remote(back_buf.at[j], got_ref.at[row, cols], back_send.at[j], back_recv.at[j], twin)

    def passing(row, at):
        end = count_starts(starts_ref, row, at * tokens + tokens - 1)
        return (end == count_starts(starts_ref, row, at * tokens - 1)).astype(F32)

    def begin():
        barrier = pltpu.get_barrier_semaphore()

        def greet(peer):
            pl.semaphore_signal(
                barrier, inc=1, device_id={"ctx": peer}, device_id_type=pl.DeviceIdType.MESH
            )

        greet(twin)

        @pl.when(jnp.logical_not(first))
        def _():
            greet(place - step)

        pl.semaphore_wait(barrier, 2 - last.astype(jnp.int32))
        twin_copy().start()

    def advance(i):
        @pl.when(i == 0)
        def _():
            twin_copy().wait_recv()

        j = i - HOP * away

        @pl.when((j >= 0) & (j < chunks))
        def _():
            row, cols = where_of(j)

            @pl.when(first)
            def _():
                in_buf[j] = jnp.zeros(in_buf.shape[1:], F32)

            @pl.when(jnp.logical_not(first))
            def _():
                onward(j).wait_recv()

            mine, theirs = own_ref[row, cols], twin_buf[j // split, cols]
            entering_lead = in_buf[j]
            entering_other = jnp.where(leads, mine, theirs) + passing(row, lead) * entering_lead

            @pl.when(jnp.logical_not(last))
            def _():
                out_buf[j] = (
                    jnp.where(leads, theirs, mine) + passing(row, other) * entering_other
                )
                onward(j).start()

            got_ref[row, cols] = jnp.where(leads, entering_lead, entering_other)
            back_buf[j] = jnp.where(leads, entering_other, entering_lead)
            back(j).start()

    def finish():
        twin_copy().wait_send()

        def one(j, carry):
            back(j).wait_send()
            back(j).wait_recv()

            @pl.when(jnp.logical_not(last))
            def _():
                onward(j).wait_send()

            return carry

        lax.fori_loop(0, chunks, one, 0)

    return begin, advance, finish, (chips - 1) * HOP + chunks


def exchange_scratch(rows, pairs):
    width = pairs // 2 if pairs % 2 == 0 else pairs
    chunks = rows // 2 * (pairs // width)
    one = pltpu.VMEM((chunks, width, HELD, PAIR), F32)
    return [
        pltpu.VMEM((rows // 2, pairs, HELD, PAIR), F32), one, one, one,
        pltpu.SemaphoreType.DMA((2,)),
    ] + [pltpu.SemaphoreType.DMA((chunks,))] * 4


def tile(n):
    return pl.ds(pl.multiple_of(n * TILE, TILE), TILE)


def run_tiles(first_count, first_body, second_count, second_body, link):
    begin, advance, finish, steps = link
    begin()
    both = first_count + second_count

    def one(i, carry):
        @pl.when(i < first_count)
        def _():
            first_body(i)

        @pl.when((i >= first_count) & (i < both))
        def _():
            second_body(i - first_count)

        advance(i)
        return carry

    lax.fori_loop(0, max(both, steps), one, 0)
    finish()


def start_all(count, copy):
    def one(n, carry):
        copy(n).start()
        return carry

    lax.fori_loop(0, count, one, 0)


def feed_forward_kernel(
    tokens, starts_ref, own_ref, norm_ref, up_ref, bias_ref, down_ref,
    pre_ref, hidden_ref, mlp_ref, got_ref,
    up_buf, down_buf, up_sem, down_sem, *bufs,
):
    ups, downs = up_ref.shape[1] // TILE, down_ref.shape[1] // TILE

    def up_copy(n):
        return pltpu.make_async_copy(up_ref.at[:, tile(n)], up_buf.at[:, tile(n)], up_sem.at[n])

    def down_copy(n):
        return pltpu.make_async_copy(
            down_ref.at[:, tile(n)], down_buf.at[:, tile(n)], down_sem.at[n]
        )

    start_all(ups, up_copy)
    start_all(downs, down_copy)

    def up(n):
        up_copy(n).wait()
        pre = dot(norm_ref[...], up_buf[:, tile(n)]) + bias_ref[:, tile(n)]
        pre_ref[:, tile(n)] = pre
        hidden = 0.5 * pre * (1.0 + lax.erf(pre * math.sqrt(0.5)))
        hidden_ref[:, tile(n)] = hidden.astype(BF)

    def down(n):
        down_copy(n).wait()
        mlp_ref[:, tile(n)] = dot(hidden_ref[...], down_buf[:, tile(n)])

    run_tiles(ups, up, downs, down, exchange(True, starts_ref, own_ref, got_ref, bufs, tokens))


def feed_backward_kernel(
    tokens, starts_ref, own_ref, grad_ref, pre_ref, down_ref, up_ref,
    grad_pre_ref, grad_norm_ref, got_ref,
    pre_buf, down_buf, up_buf, pre_sem, down_sem, up_sem, *bufs,
):
    downs, ups = down_ref.shape[0] // TILE, up_ref.shape[0] // TILE

    def pre_copy(n):
        return pltpu.make_async_copy(pre_ref.at[:, tile(n)], pre_buf.at[:, tile(n)], pre_sem.at[n])

    def down_copy(n):
        return pltpu.make_async_copy(down_ref.at[tile(n)], down_buf.at[tile(n)], down_sem.at[n])

    def up_copy(n):
        return pltpu.make_async_copy(up_ref.at[tile(n)], up_buf.at[tile(n)], up_sem.at[n])

    start_all(downs, down_copy)
    start_all(downs, pre_copy)
    start_all(ups, up_copy)

    def down(n):
        down_copy(n).wait()
        pre_copy(n).wait()
        grad = dot(grad_ref[...], down_buf[tile(n), :], 1, 1)
        pre = pre_buf[:, tile(n)]
        cdf = 0.5 * (1.0 + lax.erf(pre * math.sqrt(0.5)))
        slope = cdf + pre * jnp.exp(-0.5 * pre * pre) * (1.0 / math.sqrt(2.0 * math.pi))
        grad_pre_ref[:, tile(n)] = (grad * slope).astype(BF)

    def up(n):
        up_copy(n).wait()
        grad_norm_ref[:, tile(n)] = dot(grad_pre_ref[...], up_buf[tile(n), :], 1, 1)

    run_tiles(downs, down, ups, up, exchange(False, starts_ref, own_ref, got_ref, bufs, tokens))


IN_VMEM = pl.BlockSpec(memory_space=pltpu.VMEM)
ANYWHERE = pl.BlockSpec(memory_space=pl.ANY)


def link_call(kernel, number, in_specs, out_shape, scratch, flops):
    return pl.pallas_call(
        kernel,
        in_specs=in_specs,
        out_specs=[IN_VMEM] * len(out_shape),
        out_shape=out_shape,
        scratch_shapes=scratch,
        compiler_params=pltpu.CompilerParams(
            collective_id=number, has_side_effects=True, vmem_limit_bytes=VMEM_LIMIT
        ),
        cost_estimate=pl.CostEstimate(flops=flops, bytes_accessed=16 << 20, transcendentals=0),
    )


def feed_forward(starts, state, norm, w_up, b_up, w_down):
    total, units = norm.shape[0], w_up.shape[1]
    rows, pairs = state.shape[:2]
    return link_call(
        partial(feed_forward_kernel, total // rows),
        1,
        [SMEM, IN_VMEM, IN_VMEM, ANYWHERE, IN_VMEM, ANYWHERE],
        [
            shaped((total, units), F32), shaped((total, units), BF), shaped((total, D), F32),
            shaped(state.shape, F32),
        ],
        [
            pltpu.VMEM(w_up.shape, BF), pltpu.VMEM(w_down.shape, BF),
            pltpu.SemaphoreType.DMA((units // TILE,)), pltpu.SemaphoreType.DMA((D // TILE,)),
        ]
        + exchange_scratch(rows, pairs),
        4 * total * units * D,
    )(starts, state, norm, w_up, b_up.reshape(1, units), w_down)


def feed_backward(starts, state, grad, pre, w_down, w_up):
    total, units = pre.shape
    rows, pairs = state.shape[:2]
    return link_call(
        partial(feed_backward_kernel, total // rows),
        2,
        [SMEM, IN_VMEM, IN_VMEM, ANYWHERE, ANYWHERE, ANYWHERE],
        [shaped((total, units), BF), shaped((total, D), F32), shaped(state.shape, F32)],
        [
            pltpu.VMEM(pre.shape, F32), pltpu.VMEM(w_down.shape, BF), pltpu.VMEM(w_up.shape, BF),
            pltpu.SemaphoreType.DMA((units // TILE,)), pltpu.SemaphoreType.DMA((units // TILE,)),
            pltpu.SemaphoreType.DMA((D // TILE,)),
        ]
        + exchange_scratch(rows, pairs),
        4 * total * units * D,
    )(starts, state, grad, pre, w_down, w_up)


STEPS = 8


def hand_over_kernel(sender, part_ref, base_ref, full_ref, out_ref, *bufs):
    (
        away_buf, sum_buf, pass_buf,
        sum_send, sum_recv, pass_send, pass_recv, spread_send, spread_recv,
    ) = bufs
    width = base_ref.shape[1]
    height = base_ref.shape[0] // STEPS
    pipe, tp = lax.axis_index("pipe"), lax.axis_index("tp")
    sends = pipe == sender
    own = pl.ds(pl.multiple_of(tp * width, width), width)
    away = pl.ds(pl.multiple_of((1 - tp) * width, width), width)

    def rows(c):
        return slice(c * height, (c + 1) * height)

    def remote(src, dst, send, recv, to):
        return pltpu.make_async_remote_copy(
            src_ref=src, dst_ref=dst, send_sem=send, recv_sem=recv,
            device_id=to, device_id_type=pl.DeviceIdType.MESH,
        )

    def sum_copy(c):
        return remote(away_buf.at[c], sum_buf.at[c], sum_send.at[c], sum_recv.at[c], {"tp": 1 - tp})

    def pass_copy(c):
        target = out_ref.at[rows(c), own]
        return remote(pass_buf.at[c], target, pass_send.at[c], pass_recv.at[c], {"pipe": 1 - pipe})

    def spread_copy(c):
        piece = out_ref.at[rows(c), own]
        return remote(piece, piece, spread_send.at[c], spread_recv.at[c], {"tp": 1 - tp})

    barrier = pltpu.get_barrier_semaphore()

    def greet(to):
        pl.semaphore_signal(barrier, inc=1, device_id=to, device_id_type=pl.DeviceIdType.MESH)

    greet({"tp": 1 - tp})

    @pl.when(jnp.logical_not(sends))
    def _():
        greet({"pipe": 1 - pipe})

    pl.semaphore_wait(barrier, 1 + sends.astype(jnp.int32))

    @pl.when(sends)
    def _():
        for c in range(STEPS):
            away_buf[c] = part_ref[rows(c), away].astype(BF)
            sum_copy(c).start()
        for c in range(STEPS):
            out_ref[rows(c), :] = full_ref[rows(c), :]
            sum_copy(c).wait_recv()
            total = part_ref[rows(c), own] + sum_buf[c].astype(F32) + base_ref[rows(c), :]
            pass_buf[c] = total.astype(BF)
            pass_copy(c).start()
        for c in range(STEPS):
            sum_copy(c).wait_send()
            pass_copy(c).wait_send()

    @pl.when(jnp.logical_not(sends))
    def _():
        for c in range(STEPS):
            pass_copy(c).wait_recv()
            spread_copy(c).start()
        for c in range(STEPS):
            spread_copy(c).wait_send()
            spread_copy(c).wait_recv()


def hand_over(sender, part, base, full):
    total, width = base.shape
    piece = pltpu.VMEM((STEPS, total // STEPS, width), BF)
    return pl.pallas_call(
        partial(hand_over_kernel, sender),
        in_specs=[IN_VMEM] * 3,
        out_specs=IN_VMEM,
        out_shape=shaped(full.shape, BF),
        scratch_shapes=[piece] * 3 + [pltpu.SemaphoreType.DMA((STEPS,))] * 6,
        compiler_params=pltpu.CompilerParams(
            collective_id=3 + sender, has_side_effects=True, vmem_limit_bytes=VMEM_LIMIT
        ),
        cost_estimate=pl.CostEstimate(flops=1 << 20, bytes_accessed=8 << 20, transcendentals=0),
    )(part, base, full)


def gather_tp(value):
    if lax.axis_size("tp") != 2:
        return lax.all_gather(value, "tp", axis=1, tiled=True)
    other = lax.ppermute(value, "tp", [(0, 1), (1, 0)])
    return jnp.where(
        lax.axis_index("tp") == 0,
        jnp.concatenate([value, other], 1),
        jnp.concatenate([other, value], 1),
    )


def scatter_tp(value):
    peers = lax.axis_size("tp")
    if peers != 2:
        return lax.psum_scatter(value, "tp", scatter_dimension=1, tiled=True)
    me = lax.axis_index("tp")
    width = value.shape[1] // 2
    left, right = value[:, :width], value[:, width:]
    other = lax.ppermute(jnp.where(me == 0, right, left).astype(BF), "tp", [(0, 1), (1, 0)])
    return jnp.where(me == 0, left, right) + other.astype(F32)


def local(
    section_inputs,
    doc_starts,
    ln_gains,
    ln_shifts,
    qkv_weight,
    qkv_bias,
    feature_weight,
    dense_weight,
    out_bias,
    up_weight,
    up_bias,
    down_weight,
):
    section = lax.axis_index("pipe")
    place = lax.axis_index("ctx")
    width = section_inputs.shape[-1]
    tokens = section_inputs.shape[3]
    rows = MB * ROWS
    total = rows * tokens
    heads = feature_weight.shape[1]
    pairs = heads // 2
    gain, shift = ln_gains[0], ln_shifts[0]
    w_qkv, w_dense, w_up, w_down = qkv_weight[0], dense_weight[0], up_weight[0], down_weight[0]
    b_qkv = qkv_bias[0].reshape(pairs, 1, 3 * PAIR)
    b_up, b_out = up_bias[0], out_bias[0]
    feat = feature_weight[0].reshape(pairs, 1, PAIR)
    starts = doc_starts.reshape(rows, NDOC)
    place_in = place.astype(jnp.int32).reshape(1, 1)
    high, low = table_pair()
    same, down, up = rotary_tables(place, tokens)
    tables = (same, down, up, high, low)
    table_specs = [whole((tokens, PAIR))] * 3 + [whole((PAIR, PAIR))] * 2
    state_shape = shaped((rows, pairs, HELD, PAIR), F32)
    state_spec = pl.BlockSpec((rows, 1, HELD, PAIR), lambda p: (0, p, 0, 0))
    low_shape, full_shape = shaped((total, pairs * PAIR), BF), shaped((total, pairs * PAIR), F32)
    unit = 2 * rows * tokens * PAIR * PAIR * pairs

    def forward(u_low):
        u = u_low.astype(F32)
        centered = u - jnp.mean(u, -1, keepdims=True)
        inv = lax.rsqrt(jnp.mean(centered * centered, -1, keepdims=True) + norm_eps)
        xhat = centered * inv
        first = (xhat * gain[0] + shift[0]).astype(BF)
        second = (xhat * gain[1] + shift[1]).astype(BF)
        q, k, v, state = call(
            features_kernel,
            pairs,
            [SMEM, SMEM, whole((total, D)), column(D, 3 * PAIR), stacked(1, 3 * PAIR),
             stacked(1, PAIR)] + table_specs,
            [column(total, PAIR)] * 3 + [state_spec],
            [low_shape] * 3 + [state_shape],
            30 * unit,
        )(starts, place_in, first, w_qkv, b_qkv, feat, *tables)
        pre, hidden, mlp, state_in = feed_forward(starts, state, second, w_up, b_up, w_down)
        att_low, att, den = call(
            attend_kernel,
            pairs,
            [SMEM, SMEM] + [column(total, PAIR)] * 3 + [state_spec],
            [column(total, PAIR)] * 3,
            [low_shape, full_shape, full_shape],
            8 * unit,
        )(starts, place_in, q, k, v, state_in)
        part = jnp.dot(att_low, w_dense, preferred_element_type=F32) + mlp
        kept = (xhat, inv, first, second, q, k, v, pre, hidden, att_low, att, den, state_in)
        return part, kept

    def backward(dy, own, kept, want):
        xhat, inv, first, second, q, k, v, pre, hidden, att_low, att, den, state_in = kept
        ga = lax.dot_general(
            dy, w_dense, (((1,), (1,)), ((), ())), preferred_element_type=F32
        ).astype(BF)
        (state,) = call(
            back_state_kernel,
            pairs,
            [SMEM, SMEM] + [column(total, PAIR)] * 4,
            [state_spec],
            [state_shape],
            3 * unit,
        )(starts, place_in, q, ga, att, den)
        grad_pre, grad_second, later = feed_backward(starts, state, dy, pre, w_down, w_up)
        grad_proj, sums = call(
            back_kernel,
            pairs,
            [SMEM, SMEM] + [column(total, PAIR)] * 6
            + [state_spec, state_spec, stacked(1, PAIR)] + table_specs,
            [column(total, 3 * PAIR), stacked(8, PAIR)],
            [shaped((total, pairs * 3 * PAIR), BF), shaped((pairs, 8, PAIR), F32)],
            20 * unit,
        )(starts, place_in, q, k, v, ga, att, den, state_in, later, feat, *tables)
        grad_first = lax.dot_general(
            grad_proj, w_qkv, (((1,), (1,)), ((), ())), preferred_element_type=F32
        )
        both = grad_first * gain[0] + grad_second * gain[1]
        part = inv * (
            both
            - jnp.mean(both, -1, keepdims=True)
            - xhat * jnp.mean(both * xhat, -1, keepdims=True)
        )
        if not want:
            return part, None

        large = ((hidden, dy), (second, grad_pre), (att_low, dy), (first, grad_proj))
        norm_sums = jnp.stack(
            [
                jnp.sum(grad_first * xhat, 0),
                jnp.sum(grad_second * xhat, 0),
                jnp.sum(grad_first, 0),
                jnp.sum(grad_second, 0),
            ]
        )
        small = (
            sums[:, 1:4, :].reshape(pairs * 3 * PAIR),
            sums[:, 0, :].reshape(heads, FEAT),
            jnp.sum(own.astype(F32), 0),
            jnp.sum(grad_pre.astype(F32), 0),
        )
        return part, (large, norm_sums, small)

    mine = section_inputs[0].reshape(total, width)
    mine_full = gather_tp(mine)
    tp_place = lax.axis_index("tp")

    def own_part(full):
        return lax.dynamic_slice_in_dim(full, tp_place * width, width, 1)

    def next_section(sender, part, base):
        if lax.axis_size("tp") == 2 and total % (16 * STEPS) == 0:
            return hand_over(sender, part, base, mine_full)
        sent = (scatter_tp(part) + base).astype(BF)
        sent = lax.ppermute(sent, "pipe", [(sender, 1 - sender)])
        return jnp.where(section == sender, mine_full, gather_tp(sent))

    wide = mine.astype(F32)
    part, _ = forward(mine_full)
    full_in = next_section(0, part, wide + b_out)
    part, kept = forward(full_in)
    y1 = scatter_tp(part) + own_part(full_in).astype(F32) + b_out
    part, _ = backward(mine_full, mine, kept, False)
    full_grad = next_section(1, part, wide)
    y1, full_grad = lax.optimization_barrier((y1, full_grad))
    own_grad = own_part(full_grad)
    part, (large, norm_sums, small) = backward(full_grad, own_grad, kept, True)
    du0 = scatter_tp(part) + own_grad.astype(F32)
    if lax.axis_size("tp") == 2:
        me = lax.axis_index("tp")
        away = lax.dynamic_slice_in_dim(norm_sums, (1 - me) * width, width, 1)
        norm_sums = lax.dynamic_slice_in_dim(norm_sums, me * width, width, 1)
        norm_sums = norm_sums + lax.ppermute(away, "tp", [(0, 1), (1, 0)])
    else:
        norm_sums = lax.psum_scatter(norm_sums, "tp", scatter_dimension=1, tiled=True)
    small = small + (norm_sums,)
    if fits_reduce(large):
        flat = jnp.concatenate([x.reshape(-1) for x in small])
        flat = jnp.pad(flat, (0, CHUNK * PANEL - flat.size)).reshape(CHUNK, PANEL)
        (g_down, g_up, g_dense, g_qkv), flat = reduce_over_ctx(large, flat)
        flat, summed, begin = flat.reshape(-1), [], 0
        for x in small:
            summed.append(flat[begin : begin + x.size].reshape(x.shape))
            begin += x.size
    else:
        products = tuple(dot(a, b, 0, 0).astype(BF) for a, b in large)
        g_down, g_up, g_dense, g_qkv = (g.astype(F32) for g in lax.psum(products, "ctx"))
        summed = lax.psum(small, "ctx")
    g_qkv_bias, g_feat, g_out_bias, g_up_bias, norm_sums = summed
    section_ends = jnp.where(section == 0, du0, y1).reshape(1, MB, ROWS, tokens, width)
    grads = (
        norm_sums[:2], norm_sums[2:], g_qkv, g_qkv_bias, g_feat, g_dense, g_out_bias,
        g_up, g_up_bias, g_down,
    )
    return (section_ends,) + tuple(g[None] for g in grads)


def solution(mesh):
    in_specs = (
        P("pipe", None, None, "ctx", "tp"),
        P(),
        P("pipe", None, None),
        P("pipe", None, None),
        P("pipe", None, "tp"),
        P("pipe", "tp"),
        P("pipe", "tp", None),
        P("pipe", "tp", None),
        P("pipe", "tp"),
        P("pipe", None, "tp"),
        P("pipe", "tp"),
        P("pipe", "tp", None),
    )
    out_specs = (
        P("pipe", None, None, "ctx", "tp"),
        P("pipe", None, "tp"),
        P("pipe", None, "tp"),
        P("pipe", None, "tp"),
        P("pipe", "tp"),
        P("pipe", "tp", None),
        P("pipe", "tp", None),
        P("pipe", "tp"),
        P("pipe", None, "tp"),
        P("pipe", "tp"),
        P("pipe", "tp", None),
    )
    return jax.shard_map(local, mesh=mesh, in_specs=in_specs, out_specs=out_specs, check_vma=False)
```

```python
from functools import partial
import math

import jax
import jax.numpy as jnp
from jax import lax
from jax.experimental import pallas as pl
from jax.experimental.pallas import tpu as pltpu
from jax.sharding import PartitionSpec as P

D = 1024
HD = 64
ROT = 16
FEAT = 64
MB = 4
ROWS = 1
NDOC = 4
PAIR = 2 * HD
HELD = HD + 8
TILE = 256
HOP = 2

BF = jnp.bfloat16
F32 = jnp.float32
HIGHEST = lax.Precision.HIGHEST
norm_eps = 1e-05
VMEM_LIMIT = 56 * 1024 * 1024
REDUCE_LIMIT = 60 * 1024 * 1024


def feature_table():
    index_rows = jnp.arange(HD, dtype=jnp.int32)[:, None]
    index_cols = jnp.arange(HD, dtype=jnp.int32)[None, :]
    cosine = jnp.cos(
        math.pi * (index_rows.astype(F32) + 0.5) * index_cols.astype(F32) / HD
    )
    scaling = jnp.where(index_cols == 0, math.sqrt(1.0 / HD), math.sqrt(2.0 / HD))
    lattice_index = (
        (jnp.arange(HD, dtype=jnp.int32)[:, None] + 1)
        * (17 * jnp.arange(FEAT, dtype=jnp.int32)[None, :] + 5)
        % 257
    )
    lattice = math.sqrt(2.0) * jnp.cos(2.0 * math.pi * lattice_index.astype(F32) / 257.0)
    return jnp.dot(cosine * scaling, lattice, precision=HIGHEST) / math.sqrt(HD)


def table_pair():
    table = feature_table()
    zero = jnp.zeros_like(table)
    both = jnp.concatenate(
        [jnp.concatenate([table, zero], 1), jnp.concatenate([zero, table], 1)], 0
    )
    high = lax.reduce_precision(both, 8, 7).astype(BF)
    return high, (both - high.astype(F32)).astype(BF)


def rotary_tables(place, tokens):
    half = ROT // 2
    positions = place * tokens + jnp.arange(tokens, dtype=jnp.int32)
    inv_freq = 10000.0 ** (-(2.0 * jnp.arange(half).astype(F32)) / ROT)
    angles = positions.astype(F32)[:, None] * inv_freq[None, :]
    cos, sin = jnp.cos(angles), jnp.sin(angles)
    rest = jnp.ones((tokens, HD - ROT), F32)
    none = jnp.zeros((tokens, half), F32)
    same = jnp.concatenate([cos, cos, rest], 1)
    down = jnp.concatenate([-sin, none, 0.0 * rest], 1)
    up = jnp.concatenate([none, sin, 0.0 * rest], 1)
    return tuple(jnp.concatenate([t, t], 1) for t in (same, down, up))


def dot(a, b, ca=1, cb=0):
    return lax.dot_general(a, b, (((ca,), (cb,)), ((), ())), preferred_element_type=F32)


def split_dot(a, b, cb=0):
    high = a.astype(BF)
    low = (a - high.astype(F32)).astype(BF)
    return dot(high, b, 1, cb) + dot(low, b, 1, cb)


def lane_masks(rows):
    low = lax.broadcasted_iota(jnp.int32, (rows, PAIR), 1) < HD
    first = low.astype(F32)
    return low, first.astype(BF), (1.0 - first).astype(BF)


def count_starts(starts_ref, row, position):
    total = jnp.int32(0)
    for n in range(NDOC):
        total = total + (starts_ref[row, n] <= position).astype(jnp.int32)
    return total


def seg_grid(starts_ref, row, base, shape, dim):
    position = base + lax.broadcasted_iota(jnp.int32, shape, dim)
    total = jnp.zeros(shape, jnp.int32)
    for n in range(NDOC):
        total = total + (starts_ref[row, n] <= position).astype(jnp.int32)
    return total


def causal_mask(starts_ref, row, base, tokens):
    shape = (tokens, tokens)
    same = seg_grid(starts_ref, row, base, shape, 0) == seg_grid(starts_ref, row, base, shape, 1)
    earlier = lax.broadcasted_iota(jnp.int32, shape, 1) <= lax.broadcasted_iota(
        jnp.int32, shape, 0
    )
    rows = lax.broadcasted_iota(jnp.int32, shape, 0) < tokens // 2
    cols = lax.broadcasted_iota(jnp.int32, shape, 1) < tokens // 2
    mask = same & earlier
    return mask.astype(F32), (mask & (rows == cols)).astype(F32)


def middle_state(starts_ref, row, base, tokens, k, v, state_in, total_in, low):
    half = tokens // 2
    end = count_starts(starts_ref, row, base + half - 1)
    passing = (end == count_starts(starts_ref, row, base - 1)).astype(F32)
    seg = seg_grid(starts_ref, row, base, (half, PAIR), 0)
    key = k[:half] * (seg == end).astype(F32).astype(BF)
    state = passing * state_in + compact(dot(key, v[:half], 0, 0), low)
    total = passing * total_in + jnp.sum(key.astype(F32), 0, keepdims=True)
    later = seg_grid(starts_ref, row, base + half, (half, PAIR), 0)
    return state.astype(BF), total, (later == end).astype(F32)


def entering_mask(starts_ref, row, base, tokens):
    seg = seg_grid(starts_ref, row, base, (tokens, PAIR), 0)
    return (seg == count_starts(starts_ref, row, base - 1)).astype(F32)


def leaving_mask(starts_ref, row, base, tokens):
    seg = seg_grid(starts_ref, row, base, (tokens, PAIR), 0)
    return (seg == count_starts(starts_ref, row, base + tokens - 1)).astype(F32)


def rotate(x, same, down, up):
    half = ROT // 2
    return x * same + pltpu.roll(x, PAIR - half, 1) * down + pltpu.roll(x, half, 1) * up


def rotate_back(x, same, down, up):
    half = ROT // 2
    return x * same + pltpu.roll(x * down, half, 1) + pltpu.roll(x * up, PAIR - half, 1)


def compact(state, low):
    return jnp.where(low[:HD], state[:HD], state[HD:])


def spread(state, first, second):
    return jnp.concatenate([state * first[:HD], state * second[:HD]], 0)


def keep_state(state_ref, row, product, summands, low):
    state_ref[row, 0, :HD] = compact(product, low)
    total = jnp.sum(summands, 0, keepdims=True)
    state_ref[row, 0, HD:] = jnp.broadcast_to(total, (HELD - HD, PAIR))


def features_kernel(
    starts_ref, place_ref, norm_ref, weight_ref, bias_ref, feat_ref,
    same_ref, down_ref, up_ref, high_ref, low_ref,
    q_ref, k_ref, v_ref, state_ref,
):
    tokens = same_ref.shape[0]
    base = place_ref[0, 0] * tokens
    low, first, second = lane_masks(tokens)
    feat = feat_ref[0]
    for row in range(MB * ROWS):
        here = slice(row * tokens, (row + 1) * tokens)
        proj = dot(norm_ref[here, :], weight_ref[...]) + bias_ref[0]
        c0, c1, c2 = proj[:, :PAIR], proj[:, PAIR : 2 * PAIR], proj[:, 2 * PAIR :]
        query = jnp.where(low, c0, c1)
        key = pltpu.roll(jnp.where(low, c2, c0), HD, 1)
        value = jnp.where(low, c1, c2).astype(BF)
        out = []
        for x in (query, key):
            x = rotate(x, same_ref[...], down_ref[...], up_ref[...])
            arg = split_dot(x, high_ref[...]) + dot(x.astype(BF), low_ref[...])
            out.append((feat * jnp.exp(arg)).astype(BF))
        q_ref[here, :] = out[0]
        k_ref[here, :] = out[1]
        v_ref[here, :] = value
        leaving = leaving_mask(starts_ref, row, base, tokens)
        key_out = out[1] * leaving.astype(BF)
        keep_state(state_ref, row, dot(key_out, value, 0, 0), key_out.astype(F32), low)


def attend_kernel(
    starts_ref, place_ref, q_ref, k_ref, v_ref, state_ref, low_ref, out_ref, den_ref
):
    tokens = q_ref.shape[0] // (MB * ROWS)
    base = place_ref[0, 0] * tokens
    low, first, second = lane_masks(tokens)
    ones = head_ones()
    for row in range(MB * ROWS):
        here = slice(row * tokens, (row + 1) * tokens)
        q, k, v = q_ref[here, :], k_ref[here, :], v_ref[here, :]
        mask, mask_in = causal_mask(starts_ref, row, base, tokens)
        enter = entering_mask(starts_ref, row, base, tokens)
        carry, total = state_ref[row, 0, :HD], state_ref[row, 0, HD : HD + 1]
        state = carry.astype(BF)
        middle, _, reach = middle_state(starts_ref, row, base, tokens, k, v, carry, total, low)
        half = tokens // 2
        num = jnp.concatenate(
            [
                dot(q[:half] * enter[:half].astype(BF), spread(state, first, second)),
                dot(q[half:] * reach.astype(BF), spread(middle, first, second)),
            ],
            0,
        )
        for head in (first, second):
            scores = dot(q * head, k, 1, 1) * mask_in
            num = num + dot(scores.astype(BF), v * head)
        totals = dot(mask.astype(BF), k) + enter * total
        den = split_dot(q.astype(F32) * totals, ones)
        att = num / den
        low_ref[here, :] = att.astype(BF)
        out_ref[here, :] = att
        den_ref[here, :] = den


def head_ones():
    rows = lax.broadcasted_iota(jnp.int32, (PAIR, PAIR), 0) < HD
    cols = lax.broadcasted_iota(jnp.int32, (PAIR, PAIR), 1) < HD
    return (rows == cols).astype(F32).astype(BF)


def head_spread():
    rows = lax.broadcasted_iota(jnp.int32, (PAIR, 2 * PAIR), 0) < HD
    cols = lax.broadcasted_iota(jnp.int32, (PAIR, 2 * PAIR), 1) < PAIR
    return (rows == cols).astype(F32).astype(BF)


def back_state_kernel(
    starts_ref, place_ref, q_ref, ga_ref, att_ref, den_ref, state_ref
):
    tokens = q_ref.shape[0] // (MB * ROWS)
    base = place_ref[0, 0] * tokens
    low, first, second = lane_masks(tokens)
    ones = head_ones()
    for row in range(MB * ROWS):
        here = slice(row * tokens, (row + 1) * tokens)
        grad_num = (ga_ref[here, :].astype(F32) / den_ref[here, :]).astype(BF)
        grad_den = -split_dot(grad_num.astype(F32) * att_ref[here, :], ones)
        enter = entering_mask(starts_ref, row, base, tokens)
        query = q_ref[here, :] * enter.astype(BF)
        keep_state(state_ref, row, dot(query, grad_num, 0, 0), grad_den * query.astype(F32), low)


def back_unit(starts_ref, row, base, q, k, v, ga, att, den, held, later_held, tables):
    same, down, up, high, low_table = tables
    tokens = q.shape[0]
    half = tokens // 2
    low, first, second = lane_masks(tokens)
    grad_num = (ga.astype(F32) / den).astype(BF)
    both = -split_dot(grad_num.astype(F32) * att, head_spread())
    dens = (both[:, :PAIR], both[:, PAIR:])
    grad_den = jnp.where(low, dens[0], dens[1])
    mask, mask_in = causal_mask(starts_ref, row, base, tokens)
    enter = entering_mask(starts_ref, row, base, tokens)
    leave = leaving_mask(starts_ref, row, base, tokens)
    carry, total = held[:HD], held[HD : HD + 1]
    middle, middle_total, reach = middle_state(
        starts_ref, row, base, tokens, k, v, carry, total, low
    )
    state, middle = spread(carry.astype(BF), first, second), spread(middle, first, second)
    gq = jnp.concatenate(
        [
            enter[:half] * (dot(grad_num[:half], state, 1, 1) + grad_den[:half] * total),
            reach * (dot(grad_num[half:], middle, 1, 1) + grad_den[half:] * middle_total),
        ],
        0,
    )
    later = later_held[:HD]
    later_high = later.astype(BF)
    later_low = spread((later - later_high.astype(F32)).astype(BF), first, second)
    later_high = spread(later_high, first, second)
    gk = leave * (
        dot(v, later_high, 1, 1) + dot(v, later_low, 1, 1) + later_held[HD : HD + 1]
    )
    gv = leave * (dot(k, later_high) + dot(k, later_low))
    for head, grad_head_den in zip((first, second), dens):
        q_head, grad_head = q * head, grad_num * head
        scores = (dot(q_head, k, 1, 1) * mask).astype(BF)
        grad_scores = dot(grad_head, v, 1, 1) + grad_head_den
        gq = gq + dot((grad_scores * mask_in).astype(BF), k * head)
        gk = gk + dot((grad_scores * mask).astype(BF), q_head, 0, 0)
        gv = gv + dot(scores, grad_head, 0, 0)
    arg_grads = (gq * q.astype(F32), gk * k.astype(F32))
    feat_sum = jnp.sum(arg_grads[0] + arg_grads[1], 0, keepdims=True)
    turned = []
    for x in arg_grads:
        x = split_dot(x, high, 1) + dot(x.astype(BF), low_table, 1, 1)
        turned.append(rotate_back(x, same, down, up))
    dq, dk = turned[0], pltpu.roll(turned[1], HD, 1)
    parts = (jnp.where(low, dq, dk), jnp.where(low, gv, dq), jnp.where(low, dk, gv))
    return tuple(part.astype(BF) for part in parts), feat_sum


def back_kernel(
    starts_ref, place_ref, q_ref, k_ref, v_ref, ga_ref, att_ref, den_ref,
    state_ref, later_ref, feat_ref,
    same_ref, down_ref, up_ref, high_ref, low_ref,
    grad_ref, sums_ref,
):
    tokens = q_ref.shape[0] // (MB * ROWS)
    base = place_ref[0, 0] * tokens
    tables = tuple(t[...] for t in (same_ref, down_ref, up_ref, high_ref, low_ref))
    sums_ref[...] = jnp.zeros_like(sums_ref)
    for row in range(MB * ROWS):
        here = slice(row * tokens, (row + 1) * tokens)
        values = [r[here, :] for r in (q_ref, k_ref, v_ref, ga_ref, att_ref, den_ref)]
        parts, feat_sum = back_unit(
            starts_ref, row, base, *values, state_ref[row, 0], later_ref[row, 0], tables
        )
        sums_ref[0, 0:1, :] += feat_sum / feat_ref[0]
        for n, part in enumerate(parts):
            grad_ref[here, n * PAIR : (n + 1) * PAIR] = part
            sums_ref[0, n + 1 : n + 2, :] += jnp.sum(part.astype(F32), 0, keepdims=True)


SMEM = pl.BlockSpec(memory_space=pltpu.SMEM)


def whole(shape):
    return pl.BlockSpec(shape, lambda p: (0,) * len(shape))


def column(rows, width):
    return pl.BlockSpec((rows, width), lambda p: (0, p))


def stacked(*shape):
    return pl.BlockSpec((1,) + shape, lambda p: (p,) + (0,) * len(shape))


def call(kernel, pairs, in_specs, out_specs, out_shape, flops):
    return pl.pallas_call(
        kernel,
        grid=(pairs,),
        in_specs=in_specs,
        out_specs=out_specs,
        out_shape=out_shape,
        compiler_params=pltpu.CompilerParams(vmem_limit_bytes=VMEM_LIMIT),
        cost_estimate=pl.CostEstimate(flops=flops, bytes_accessed=8 << 20, transcendentals=0),
    )


def shaped(shape, dtype):
    return jax.ShapeDtypeStruct(shape, dtype)


CHUNK = 256
PANEL = 512
RING = 4
LAG = 6


def last_kernel(plan, *refs):
    count, terms = plan
    (
        starts_ref, hidden_ref, dy_ref, second_ref, grad_pre_ref, low_ref, first_ref,
        q_ref, k_ref, v_ref, ga_ref, att_ref, den_ref, state_ref, later_ref, feat_ref,
        same_ref, down_ref, up_ref, high_table_ref, low_table_ref,
        qkv_ref, grad_second_ref, xhat_ref, inv_ref, gain_ref, small_in_ref,
    ) = refs[:27]
    outs, du_ref = refs[27:32], refs[32]
    (
        proj, small_ref, away_buf, come_buf, norm_sum, norm_away, norm_come,
        sum_send, sum_recv, norm_sem,
        work, give, take, outside, inside,
        give_send, give_recv, part_send, outer_recv, inner_recv, total_send,
        final_send, final_recv, own_sem,
    ) = refs[33:]
    part = give
    factors = (
        hidden_ref, dy_ref, second_ref, grad_pre_ref, low_ref, dy_ref, first_ref, proj
    )
    rows, pairs = state_ref.shape[:2]
    tokens, width = q_ref.shape[0] // rows, du_ref.shape[1]
    units = rows * pairs
    tp = lax.axis_index("tp")
    my_cols = pl.ds(pl.multiple_of(tp * width, width), width)
    half = CHUNK // 2
    place, peers = lax.axis_index("ctx"), lax.axis_size("ctx")
    core, z, chips = place % 2, place // 2, peers // 2
    below = z < chips // 2
    middle = (z == chips // 2 - 1) | (z == chips // 2)
    has_outer = (z != 0) & (z != chips - 1)
    step = jnp.where(below, 2, -2)
    inner, outer, twin = place + step, place - step, place + 1 - 2 * core
    mine = pl.ds(pl.multiple_of(core * half, half), half)
    theirs = pl.ds(pl.multiple_of((1 - core) * half, half), half)

    def remote(src, dst, send, recv, to):
        return pltpu.make_async_remote_copy(
            src_ref=src, dst_ref=dst, send_sem=send, recv_sem=recv,
            device_id={"ctx": to}, device_id_type=pl.DeviceIdType.MESH,
        )

    def to_tp(src, dst, send, recv):
        return pltpu.make_async_remote_copy(
            src_ref=src, dst_ref=dst, send_sem=send, recv_sem=recv,
            device_id={"tp": 1 - tp}, device_id_type=pl.DeviceIdType.MESH,
        )

    def sum_copy(m):
        return to_tp(away_buf.at[m], come_buf.at[m], sum_send.at[m], sum_recv.at[m])

    def norm_copy():
        return to_tp(norm_away, norm_come, norm_sem.at[0], norm_sem.at[1])

    def split_cols(x):
        left, right = x[:, :width], x[:, width:]
        return jnp.where(tp == 0, left, right), jnp.where(tp == 0, right, left)

    def row_block(m):
        return pl.ds(pl.multiple_of(m * tokens, tokens), tokens)

    def attention_step(i):
        p, row = i // rows, i % rows
        here, cols = row_block(row), pl.ds(pl.multiple_of(p * PAIR, PAIR), PAIR)
        tables = tuple(
            t[...] for t in (same_ref, down_ref, up_ref, high_table_ref, low_table_ref)
        )
        values = [r[here, cols] for r in (q_ref, k_ref, v_ref, ga_ref, att_ref, den_ref)]
        parts, feat_sum = back_unit(
            starts_ref, row, place * tokens, *values, state_ref[row, p], later_ref[row, p], tables
        )
        line = (lax.broadcasted_iota(jnp.int32, (8, PAIR), 0) == p).astype(F32)
        small_ref[:8, 3 * PAIR : 4 * PAIR] += line * (feat_sum / feat_ref[p])
        for n, piece in enumerate(parts):
            proj[here, pl.ds(pl.multiple_of((3 * p + n) * PAIR, PAIR), PAIR)] = piece
            small_ref[:8, n * PAIR : (n + 1) * PAIR] += line * jnp.sum(
                piece.astype(F32), 0, keepdims=True
            )

    def norm_step(m):
        here = row_block(m)
        one, two, xhat = dot(proj[here, :], qkv_ref[...], 1, 1), grad_second_ref[here, :], xhat_ref[here, :]
        for n, x in enumerate((one * xhat, two * xhat, one, two)):
            norm_sum[n : n + 1, :] += jnp.sum(x, 0, keepdims=True)
        both = one * gain_ref[0:1, :] + two * gain_ref[1:2, :]
        leaving = inv_ref[here, :] * (
            both
            - jnp.mean(both, -1, keepdims=True)
            - xhat * jnp.mean(both * xhat, -1, keepdims=True)
        )
        kept, sent = split_cols(leaving)
        away_buf[m] = sent.astype(BF)
        sum_copy(m).start()
        du_ref[here, :] = kept + dy_ref[here, my_cols].astype(F32)

    def other_work(i):
        @pl.when(i < units)
        def _():
            attention_step(i)

        @pl.when((i >= units) & (i < units + rows))
        def _():
            norm_step(i - units)

        @pl.when(i == units + rows)
        def _():
            kept, sent = split_cols(norm_sum[...])
            norm_away[...] = sent
            norm_copy().start()
            small_ref[16:24, :] = kept

        late = i - (units + rows + 3)

        @pl.when((late >= 0) & (late < rows))
        def _():
            sum_copy(late).wait()
            du_ref[row_block(late), :] += come_buf[late].astype(F32)

        @pl.when(late == rows)
        def _():
            norm_copy().wait()
            small_ref[16:24, :] += norm_come[...]

    def give_copy(t):
        return remote(give.at[t], take.at[t], give_send.at[t], give_recv.at[t], twin)

    def to_outside(t):
        return remote(part.at[t], outside.at[t], part_send.at[t], outer_recv.at[t], inner)

    def across(t):
        return remote(part.at[t], inside.at[t], part_send.at[t], inner_recv.at[t], inner)

    def outward(t):
        return remote(take.at[t], inside.at[t], total_send.at[t], inner_recv.at[t], outer)

    def final_copy(t, target):
        return remote(take.at[t], target, final_send.at[t], final_recv.at[t], twin)

    def own_copy(t, target):
        return pltpu.make_async_copy(take.at[t], target, own_sem.at[t])

    def block_of(j, panels):
        rows = (j // panels) * CHUNK
        return rows, pl.ds(pl.multiple_of((j % panels) * PANEL, PANEL), PANEL)

    def deliver(t, target):
        final_copy(t, target).start()
        own_copy(t, target).start()

    some_target = outs[-1].at[mine]

    barrier = pltpu.get_barrier_semaphore()
    for peer in ({"ctx": inner}, {"ctx": twin}, {"tp": 1 - tp}):
        pl.semaphore_signal(barrier, inc=1, device_id=peer, device_id_type=pl.DeviceIdType.MESH)

    @pl.when(has_outer)
    def _():
        pl.semaphore_signal(
            barrier, inc=1, device_id={"ctx": outer}, device_id_type=pl.DeviceIdType.MESH
        )

    pl.semaphore_wait(barrier, 3 + has_outer.astype(jnp.int32))
    small_ref[...] = jnp.zeros_like(small_ref)
    small_ref[8:16, :] = small_in_ref[...]
    norm_sum[...] = jnp.zeros_like(norm_sum)
    lag = jnp.where(middle, 2, LAG)

    def one(t, carry):
        slot = t % RING
        begin = 0
        for n, (blocks, panels) in enumerate(terms):
            left, right = factors[2 * n], factors[2 * n + 1]

            @pl.when((t >= begin) & (t < begin + blocks * panels))
            def _(left=left, right=right, panels=panels, begin=begin):
                start, cols = block_of(t - begin, panels)
                rows = pl.ds(pl.multiple_of(start, CHUNK), CHUNK)
                work[slot] = dot(left[:, rows], right[:, cols], 0, 0)

            begin += blocks * panels

        @pl.when(t == begin)
        def _():
            work[slot] = small_ref[...]

        @pl.when(t < count)
        def _():
            give[t] = work[slot, theirs, :].astype(BF)
            give_copy(t).start()

        tb = t - 1

        @pl.when((tb >= 0) & (tb < count))
        def _():
            give_copy(tb).wait()
            total = work[(t + RING - 1) % RING, mine, :] + take[tb].astype(F32)

            @pl.when(has_outer)
            def _():
                to_outside(tb).wait_recv()
                part[tb] = (total + outside[tb].astype(F32)).astype(BF)

            @pl.when(jnp.logical_not(has_outer))
            def _():
                part[tb] = total.astype(BF)

            @pl.when(middle)
            def _():
                across(tb).start()

            @pl.when(jnp.logical_not(middle))
            def _():
                to_outside(tb).start()

        tc = t - lag

        @pl.when((tc >= 0) & (tc < count))
        def _():
            across(tc).wait_recv()

            @pl.when(middle)
            def _():
                take[tc] = (part[tc].astype(F32) + inside[tc].astype(F32)).astype(BF)

            @pl.when(jnp.logical_not(middle))
            def _():
                take[tc] = inside[tc]

            @pl.when(has_outer)
            def _():
                outward(tc).start()

            begin = 0
            for n, (blocks, panels) in enumerate(terms):

                @pl.when((tc >= begin) & (tc < begin + blocks * panels))
                def _(n=n, panels=panels, begin=begin):
                    start, cols = block_of(tc - begin, panels)
                    rows = pl.ds(pl.multiple_of(start + core * half, half), half)
                    deliver(tc, outs[n].at[rows, cols])

                begin += blocks * panels

            @pl.when(tc == begin)
            def _():
                deliver(tc, some_target)

        other_work(t)
        return carry

    lax.fori_loop(0, count + LAG, one, 0)

    def drain(t, carry):
        across(t).wait_send()
        final_copy(t, some_target).wait_send()
        final_copy(t, some_target).wait_recv()
        own_copy(t, some_target).wait()

        @pl.when(has_outer)
        def _():
            outward(t).wait_send()

        return carry

    lax.fori_loop(0, count, drain, 0)


def last_call(starts, factors, attention, norms, small):
    shapes = [(a.shape[1], b.shape[1]) for a, b in factors[:3]]
    first, qkv = factors[3][0], norms[0]
    shapes.append((first.shape[1], qkv.shape[1]))
    terms = tuple((x // CHUNK, y // PANEL) for x, y in shapes)
    count = sum(x * y for x, y in terms) + 1
    total, width = first.shape[0], D // 2
    rows, tokens = MB * ROWS, total // (MB * ROWS)
    slots = pltpu.VMEM((count, CHUNK // 2, PANEL), BF)
    flat = [factors[0][0], factors[0][1], factors[1][0], factors[1][1], factors[2][0], first]
    flat = flat + list(attention) + list(norms) + [small]
    dma = pltpu.SemaphoreType.DMA
    *sums, du = pl.pallas_call(
        partial(last_kernel, (count, terms)),
        in_specs=[SMEM] + [IN_VMEM] * len(flat),
        out_specs=[ANYWHERE] * 5 + [IN_VMEM],
        out_shape=[shaped(x, BF) for x in shapes]
        + [shaped((CHUNK, PANEL), BF), shaped((total, width), F32)],
        scratch_shapes=[
            pltpu.VMEM((total, qkv.shape[1]), BF),
            pltpu.VMEM((CHUNK, PANEL), F32),
            pltpu.VMEM((rows, tokens, width), BF),
            pltpu.VMEM((rows, tokens, width), BF),
            pltpu.VMEM((8, D), F32),
            pltpu.VMEM((8, width), F32),
            pltpu.VMEM((8, width), F32),
            dma((rows,)), dma((rows,)), dma((2,)),
            pltpu.VMEM((RING, CHUNK, PANEL), F32),
        ]
        + [slots] * 4
        + [dma((count,))] * 9,
        compiler_params=pltpu.CompilerParams(
            collective_id=0, has_side_effects=True, vmem_limit_bytes=REDUCE_LIMIT
        ),
        cost_estimate=pl.CostEstimate(
            flops=count * 2 * CHUNK * PANEL * 512, bytes_accessed=40 << 20, transcendentals=0
        ),
    )(starts, *flat)
    return [g.astype(F32) for g in sums[:-1]], sums[-1].astype(F32), du


def fits_last(factors, qkv, pairs):
    sizes = [(a.shape[1], b.shape[1]) for a, b in factors] + [qkv.shape]
    even = all(x % CHUNK == 0 and y % PANEL == 0 for x, y in sizes)
    ahead = sum(x // CHUNK * (y // PANEL) for x, y in sizes[:-1])
    units = MB * ROWS * (pairs + 2) + 8
    line = lax.axis_size("ctx") % 4 == 0 and lax.axis_size("tp") == 2
    return even and line and units <= ahead and pairs <= 8


def exchange(forward, starts_ref, own_ref, got_ref, bufs, tokens):
    (twin_buf, in_buf, out_buf, back_buf, twin_sem, send_sem, recv_sem, back_send, back_recv) = bufs
    rows, pairs = own_ref.shape[:2]
    part = rows // 2
    chunks, width = in_buf.shape[:2]
    split = pairs // width
    place, chips = lax.axis_index("ctx"), lax.axis_size("ctx") // 2
    core, z = place % 2, place // 2
    away = z if forward else chips - 1 - z
    first, last = away == 0, away == chips - 1
    step = 2 if forward else -2
    twin = place + 1 - 2 * core
    leads = core == (0 if forward else 1)
    lead = 2 * z + (0 if forward else 1)
    other = 2 * z + (1 if forward else 0)

    def remote(src, dst, send, recv, to):
        return pltpu.make_async_remote_copy(
            src_ref=src, dst_ref=dst, send_sem=send, recv_sem=recv,
            device_id={"ctx": to}, device_id_type=pl.DeviceIdType.MESH,
        )

    def twin_copy():
        theirs = own_ref.at[pl.ds((1 - core) * part, part)]
        return remote(theirs, twin_buf, twin_sem.at[0], twin_sem.at[1], twin)

    def onward(j):
        return remote(out_buf.at[j], in_buf.at[j], send_sem.at[j], recv_sem.at[j], place + step)

    def where_of(j):
        return core * part + j // split, pl.ds((j % split) * width, width)

    def back(j):
        row, cols = where_of(j)
        return remote(back_buf.at[j], got_ref.at[row, cols], back_send.at[j], back_recv.at[j], twin)

    def passing(row, at):
        end = count_starts(starts_ref, row, at * tokens + tokens - 1)
        return (end == count_starts(starts_ref, row, at * tokens - 1)).astype(F32)

    def begin():
        barrier = pltpu.get_barrier_semaphore()

        def greet(peer):
            pl.semaphore_signal(
                barrier, inc=1, device_id={"ctx": peer}, device_id_type=pl.DeviceIdType.MESH
            )

        greet(twin)

        @pl.when(jnp.logical_not(first))
        def _():
            greet(place - step)

        pl.semaphore_wait(barrier, 2 - last.astype(jnp.int32))
        twin_copy().start()

    def advance(i):
        @pl.when(i == 0)
        def _():
            twin_copy().wait_recv()

        j = i - HOP * away

        @pl.when((j >= 0) & (j < chunks))
        def _():
            row, cols = where_of(j)

            @pl.when(first)
            def _():
                in_buf[j] = jnp.zeros(in_buf.shape[1:], F32)

            @pl.when(jnp.logical_not(first))
            def _():
                onward(j).wait_recv()

            mine, theirs = own_ref[row, cols], twin_buf[j // split, cols]
            entering_lead = in_buf[j]
            entering_other = jnp.where(leads, mine, theirs) + passing(row, lead) * entering_lead

            @pl.when(jnp.logical_not(last))
            def _():
                out_buf[j] = (
                    jnp.where(leads, theirs, mine) + passing(row, other) * entering_other
                )
                onward(j).start()

            got_ref[row, cols] = jnp.where(leads, entering_lead, entering_other)
            back_buf[j] = jnp.where(leads, entering_other, entering_lead)
            back(j).start()

    def finish():
        twin_copy().wait_send()

        def one(j, carry):
            back(j).wait_send()
            back(j).wait_recv()

            @pl.when(jnp.logical_not(last))
            def _():
                onward(j).wait_send()

            return carry

        lax.fori_loop(0, chunks, one, 0)

    return begin, advance, finish, (chips - 1) * HOP + chunks


def exchange_scratch(rows, pairs):
    width = pairs // 2 if pairs % 2 == 0 else pairs
    chunks = rows // 2 * (pairs // width)
    one = pltpu.VMEM((chunks, width, HELD, PAIR), F32)
    return [
        pltpu.VMEM((rows // 2, pairs, HELD, PAIR), F32), one, one, one,
        pltpu.SemaphoreType.DMA((2,)),
    ] + [pltpu.SemaphoreType.DMA((chunks,))] * 4


def tile(n):
    return pl.ds(pl.multiple_of(n * TILE, TILE), TILE)


def run_tiles(first_count, first_body, second_count, second_body, link):
    begin, advance, finish, steps = link
    begin()
    both = first_count + second_count

    def one(i, carry):
        @pl.when(i < first_count)
        def _():
            first_body(i)

        @pl.when((i >= first_count) & (i < both))
        def _():
            second_body(i - first_count)

        advance(i)
        return carry

    lax.fori_loop(0, max(both, steps), one, 0)
    finish()


def start_all(count, copy):
    def one(n, carry):
        copy(n).start()
        return carry

    lax.fori_loop(0, count, one, 0)


def feed_forward_kernel(
    tokens, starts_ref, own_ref, norm_ref, up_ref, bias_ref, down_ref,
    pre_ref, hidden_ref, mlp_ref, got_ref,
    up_buf, down_buf, up_sem, down_sem, *bufs,
):
    ups, downs = up_ref.shape[1] // TILE, down_ref.shape[1] // TILE

    def up_copy(n):
        return pltpu.make_async_copy(up_ref.at[:, tile(n)], up_buf.at[:, tile(n)], up_sem.at[n])

    def down_copy(n):
        return pltpu.make_async_copy(
            down_ref.at[:, tile(n)], down_buf.at[:, tile(n)], down_sem.at[n]
        )

    start_all(ups, up_copy)
    start_all(downs, down_copy)

    def up(n):
        up_copy(n).wait()
        pre = dot(norm_ref[...], up_buf[:, tile(n)]) + bias_ref[:, tile(n)]
        pre_ref[:, tile(n)] = pre
        hidden = 0.5 * pre * (1.0 + lax.erf(pre * math.sqrt(0.5)))
        hidden_ref[:, tile(n)] = hidden.astype(BF)

    def down(n):
        down_copy(n).wait()
        mlp_ref[:, tile(n)] = dot(hidden_ref[...], down_buf[:, tile(n)])

    run_tiles(ups, up, downs, down, exchange(True, starts_ref, own_ref, got_ref, bufs, tokens))


def feed_backward_kernel(
    tokens, starts_ref, own_ref, grad_ref, pre_ref, down_ref, up_ref,
    grad_pre_ref, grad_norm_ref, got_ref,
    pre_buf, down_buf, up_buf, pre_sem, down_sem, up_sem, *bufs,
):
    downs, ups = down_ref.shape[0] // TILE, up_ref.shape[0] // TILE

    def pre_copy(n):
        return pltpu.make_async_copy(pre_ref.at[:, tile(n)], pre_buf.at[:, tile(n)], pre_sem.at[n])

    def down_copy(n):
        return pltpu.make_async_copy(down_ref.at[tile(n)], down_buf.at[tile(n)], down_sem.at[n])

    def up_copy(n):
        return pltpu.make_async_copy(up_ref.at[tile(n)], up_buf.at[tile(n)], up_sem.at[n])

    start_all(downs, down_copy)
    start_all(downs, pre_copy)
    start_all(ups, up_copy)

    def down(n):
        down_copy(n).wait()
        pre_copy(n).wait()
        grad = dot(grad_ref[...], down_buf[tile(n), :], 1, 1)
        pre = pre_buf[:, tile(n)]
        cdf = 0.5 * (1.0 + lax.erf(pre * math.sqrt(0.5)))
        slope = cdf + pre * jnp.exp(-0.5 * pre * pre) * (1.0 / math.sqrt(2.0 * math.pi))
        grad_pre_ref[:, tile(n)] = (grad * slope).astype(BF)

    def up(n):
        up_copy(n).wait()
        grad_norm_ref[:, tile(n)] = dot(grad_pre_ref[...], up_buf[tile(n), :], 1, 1)

    run_tiles(downs, down, ups, up, exchange(False, starts_ref, own_ref, got_ref, bufs, tokens))


IN_VMEM = pl.BlockSpec(memory_space=pltpu.VMEM)
ANYWHERE = pl.BlockSpec(memory_space=pl.ANY)


def link_call(kernel, number, in_specs, out_shape, scratch, flops):
    return pl.pallas_call(
        kernel,
        in_specs=in_specs,
        out_specs=[IN_VMEM] * len(out_shape),
        out_shape=out_shape,
        scratch_shapes=scratch,
        compiler_params=pltpu.CompilerParams(
            collective_id=number, has_side_effects=True, vmem_limit_bytes=VMEM_LIMIT
        ),
        cost_estimate=pl.CostEstimate(flops=flops, bytes_accessed=16 << 20, transcendentals=0),
    )


def feed_forward(starts, state, norm, w_up, b_up, w_down):
    total, units = norm.shape[0], w_up.shape[1]
    rows, pairs = state.shape[:2]
    return link_call(
        partial(feed_forward_kernel, total // rows),
        1,
        [SMEM, IN_VMEM, IN_VMEM, ANYWHERE, IN_VMEM, ANYWHERE],
        [
            shaped((total, units), F32), shaped((total, units), BF), shaped((total, D), F32),
            shaped(state.shape, F32),
        ],
        [
            pltpu.VMEM(w_up.shape, BF), pltpu.VMEM(w_down.shape, BF),
            pltpu.SemaphoreType.DMA((units // TILE,)), pltpu.SemaphoreType.DMA((D // TILE,)),
        ]
        + exchange_scratch(rows, pairs),
        4 * total * units * D,
    )(starts, state, norm, w_up, b_up.reshape(1, units), w_down)


def feed_backward(starts, state, grad, pre, w_down, w_up):
    total, units = pre.shape
    rows, pairs = state.shape[:2]
    return link_call(
        partial(feed_backward_kernel, total // rows),
        2,
        [SMEM, IN_VMEM, IN_VMEM, ANYWHERE, ANYWHERE, ANYWHERE],
        [shaped((total, units), BF), shaped((total, D), F32), shaped(state.shape, F32)],
        [
            pltpu.VMEM(pre.shape, F32), pltpu.VMEM(w_down.shape, BF), pltpu.VMEM(w_up.shape, BF),
            pltpu.SemaphoreType.DMA((units // TILE,)), pltpu.SemaphoreType.DMA((units // TILE,)),
            pltpu.SemaphoreType.DMA((D // TILE,)),
        ]
        + exchange_scratch(rows, pairs),
        4 * total * units * D,
    )(starts, state, grad, pre, w_down, w_up)


STEPS = 8


def hand_over_kernel(sender, part_ref, base_ref, full_ref, out_ref, *bufs):
    (
        away_buf, sum_buf, pass_buf,
        sum_send, sum_recv, pass_send, pass_recv, spread_send, spread_recv,
    ) = bufs
    width = base_ref.shape[1]
    height = base_ref.shape[0] // STEPS
    pipe, tp = lax.axis_index("pipe"), lax.axis_index("tp")
    sends = pipe == sender
    own = pl.ds(pl.multiple_of(tp * width, width), width)
    away = pl.ds(pl.multiple_of((1 - tp) * width, width), width)

    def rows(c):
        return slice(c * height, (c + 1) * height)

    def remote(src, dst, send, recv, to):
        return pltpu.make_async_remote_copy(
            src_ref=src, dst_ref=dst, send_sem=send, recv_sem=recv,
            device_id=to, device_id_type=pl.DeviceIdType.MESH,
        )

    def sum_copy(c):
        return remote(away_buf.at[c], sum_buf.at[c], sum_send.at[c], sum_recv.at[c], {"tp": 1 - tp})

    def pass_copy(c):
        target = out_ref.at[rows(c), own]
        return remote(pass_buf.at[c], target, pass_send.at[c], pass_recv.at[c], {"pipe": 1 - pipe})

    def spread_copy(c):
        piece = out_ref.at[rows(c), own]
        return remote(piece, piece, spread_send.at[c], spread_recv.at[c], {"tp": 1 - tp})

    barrier = pltpu.get_barrier_semaphore()

    def greet(to):
        pl.semaphore_signal(barrier, inc=1, device_id=to, device_id_type=pl.DeviceIdType.MESH)

    greet({"tp": 1 - tp})

    @pl.when(jnp.logical_not(sends))
    def _():
        greet({"pipe": 1 - pipe})

    pl.semaphore_wait(barrier, 1 + sends.astype(jnp.int32))

    @pl.when(sends)
    def _():
        for c in range(STEPS):
            away_buf[c] = part_ref[rows(c), away].astype(BF)
            sum_copy(c).start()
        for c in range(STEPS):
            out_ref[rows(c), :] = full_ref[rows(c), :]
            sum_copy(c).wait_recv()
            total = part_ref[rows(c), own] + sum_buf[c].astype(F32) + base_ref[rows(c), :]
            pass_buf[c] = total.astype(BF)
            pass_copy(c).start()
        for c in range(STEPS):
            sum_copy(c).wait_send()
            pass_copy(c).wait_send()

    @pl.when(jnp.logical_not(sends))
    def _():
        for c in range(STEPS):
            pass_copy(c).wait_recv()
            spread_copy(c).start()
        for c in range(STEPS):
            spread_copy(c).wait_send()
            spread_copy(c).wait_recv()


def hand_over(sender, part, base, full):
    total, width = base.shape
    piece = pltpu.VMEM((STEPS, total // STEPS, width), BF)
    return pl.pallas_call(
        partial(hand_over_kernel, sender),
        in_specs=[IN_VMEM] * 3,
        out_specs=IN_VMEM,
        out_shape=shaped(full.shape, BF),
        scratch_shapes=[piece] * 3 + [pltpu.SemaphoreType.DMA((STEPS,))] * 6,
        compiler_params=pltpu.CompilerParams(
            collective_id=3 + sender, has_side_effects=True, vmem_limit_bytes=VMEM_LIMIT
        ),
        cost_estimate=pl.CostEstimate(flops=1 << 20, bytes_accessed=8 << 20, transcendentals=0),
    )(part, base, full)


def gather_tp(value):
    if lax.axis_size("tp") != 2:
        return lax.all_gather(value, "tp", axis=1, tiled=True)
    other = lax.ppermute(value, "tp", [(0, 1), (1, 0)])
    return jnp.where(
        lax.axis_index("tp") == 0,
        jnp.concatenate([value, other], 1),
        jnp.concatenate([other, value], 1),
    )


def scatter_tp(value):
    peers = lax.axis_size("tp")
    if peers != 2:
        return lax.psum_scatter(value, "tp", scatter_dimension=1, tiled=True)
    me = lax.axis_index("tp")
    width = value.shape[1] // 2
    left, right = value[:, :width], value[:, width:]
    other = lax.ppermute(jnp.where(me == 0, right, left).astype(BF), "tp", [(0, 1), (1, 0)])
    return jnp.where(me == 0, left, right) + other.astype(F32)


def local(
    section_inputs,
    doc_starts,
    ln_gains,
    ln_shifts,
    qkv_weight,
    qkv_bias,
    feature_weight,
    dense_weight,
    out_bias,
    up_weight,
    up_bias,
    down_weight,
):
    section = lax.axis_index("pipe")
    place = lax.axis_index("ctx")
    width = section_inputs.shape[-1]
    tokens = section_inputs.shape[3]
    rows = MB * ROWS
    total = rows * tokens
    heads = feature_weight.shape[1]
    pairs = heads // 2
    gain, shift = ln_gains[0], ln_shifts[0]
    w_qkv, w_dense, w_up, w_down = qkv_weight[0], dense_weight[0], up_weight[0], down_weight[0]
    b_qkv = qkv_bias[0].reshape(pairs, 1, 3 * PAIR)
    b_up, b_out = up_bias[0], out_bias[0]
    feat = feature_weight[0].reshape(pairs, 1, PAIR)
    starts = doc_starts.reshape(rows, NDOC)
    place_in = place.astype(jnp.int32).reshape(1, 1)
    high, low = table_pair()
    same, down, up = rotary_tables(place, tokens)
    tables = (same, down, up, high, low)
    table_specs = [whole((tokens, PAIR))] * 3 + [whole((PAIR, PAIR))] * 2
    state_shape = shaped((rows, pairs, HELD, PAIR), F32)
    state_spec = pl.BlockSpec((rows, 1, HELD, PAIR), lambda p: (0, p, 0, 0))
    low_shape, full_shape = shaped((total, pairs * PAIR), BF), shaped((total, pairs * PAIR), F32)
    unit = 2 * rows * tokens * PAIR * PAIR * pairs

    def forward(u_low):
        u = u_low.astype(F32)
        centered = u - jnp.mean(u, -1, keepdims=True)
        inv = lax.rsqrt(jnp.mean(centered * centered, -1, keepdims=True) + norm_eps)
        xhat = centered * inv
        first = (xhat * gain[0] + shift[0]).astype(BF)
        second = (xhat * gain[1] + shift[1]).astype(BF)
        q, k, v, state = call(
            features_kernel,
            pairs,
            [SMEM, SMEM, whole((total, D)), column(D, 3 * PAIR), stacked(1, 3 * PAIR),
             stacked(1, PAIR)] + table_specs,
            [column(total, PAIR)] * 3 + [state_spec],
            [low_shape] * 3 + [state_shape],
            30 * unit,
        )(starts, place_in, first, w_qkv, b_qkv, feat, *tables)
        pre, hidden, mlp, state_in = feed_forward(starts, state, second, w_up, b_up, w_down)
        att_low, att, den = call(
            attend_kernel,
            pairs,
            [SMEM, SMEM] + [column(total, PAIR)] * 3 + [state_spec],
            [column(total, PAIR)] * 3,
            [low_shape, full_shape, full_shape],
            8 * unit,
        )(starts, place_in, q, k, v, state_in)
        part = jnp.dot(att_low, w_dense, preferred_element_type=F32) + mlp
        kept = (xhat, inv, first, second, q, k, v, pre, hidden, att_low, att, den, state_in)
        return part, kept

    def backward(dy, own, kept, want):
        xhat, inv, first, second, q, k, v, pre, hidden, att_low, att, den, state_in = kept
        ga = lax.dot_general(
            dy, w_dense, (((1,), (1,)), ((), ())), preferred_element_type=F32
        ).astype(BF)
        (state,) = call(
            back_state_kernel,
            pairs,
            [SMEM, SMEM] + [column(total, PAIR)] * 4,
            [state_spec],
            [state_shape],
            3 * unit,
        )(starts, place_in, q, ga, att, den)
        grad_pre, grad_second, later = feed_backward(starts, state, dy, pre, w_down, w_up)
        large = ((hidden, dy), (second, grad_pre), (att_low, dy))
        up_sum = jnp.sum(grad_pre.astype(F32), 0) if want else None
        out_sum = jnp.sum(own.astype(F32), 0)
        if want and fits_last(large, w_qkv, pairs):
            extra = jnp.concatenate([up_sum, out_sum])
            extra = jnp.pad(extra, (0, 8 * PANEL - extra.size)).reshape(8, PANEL)
            weights, flat, du = last_call(
                starts,
                large + ((first, None),),
                (q, k, v, ga, att, den, state_in, later, feat) + tables,
                (w_qkv, grad_second, xhat, inv, gain),
                extra,
            )
            ends = up_sum.size // PANEL
            little = (
                flat[:pairs, : 3 * PAIR].reshape(-1),
                flat[:pairs, 3 * PAIR :].reshape(heads, FEAT),
                flat[8 + ends : 8 + ends + out_sum.size // PANEL].reshape(-1),
                flat[8 : 8 + ends].reshape(-1),
                flat[16:20],
            )
            return du, (weights, little)
        grad_proj, sums = call(
            back_kernel,
            pairs,
            [SMEM, SMEM] + [column(total, PAIR)] * 6
            + [state_spec, state_spec, stacked(1, PAIR)] + table_specs,
            [column(total, 3 * PAIR), stacked(8, PAIR)],
            [shaped((total, pairs * 3 * PAIR), BF), shaped((pairs, 8, PAIR), F32)],
            20 * unit,
        )(starts, place_in, q, k, v, ga, att, den, state_in, later, feat, *tables)
        grad_first = lax.dot_general(
            grad_proj, w_qkv, (((1,), (1,)), ((), ())), preferred_element_type=F32
        )
        both = grad_first * gain[0] + grad_second * gain[1]
        part = inv * (
            both
            - jnp.mean(both, -1, keepdims=True)
            - xhat * jnp.mean(both * xhat, -1, keepdims=True)
        )
        if not want:
            return part, None
        norm_sums = jnp.stack(
            [
                jnp.sum(grad_first * xhat, 0),
                jnp.sum(grad_second * xhat, 0),
                jnp.sum(grad_first, 0),
                jnp.sum(grad_second, 0),
            ]
        )
        norm_sums = lax.psum_scatter(norm_sums, "tp", scatter_dimension=1, tiled=True)
        little = (
            sums[:, 1:4, :].reshape(pairs * 3 * PAIR),
            sums[:, 0, :].reshape(heads, FEAT),
            out_sum,
            up_sum,
            norm_sums,
        )
        products = tuple(dot(a, b, 0, 0).astype(BF) for a, b in large + ((first, grad_proj),))
        weights = [g.astype(F32) for g in lax.psum(products, "ctx")]
        return scatter_tp(part) + own.astype(F32), (weights, lax.psum(little, "ctx"))

    mine = section_inputs[0].reshape(total, width)
    mine_full = gather_tp(mine)
    tp_place = lax.axis_index("tp")

    def own_part(full):
        return lax.dynamic_slice_in_dim(full, tp_place * width, width, 1)

    def next_section(sender, part, base):
        if lax.axis_size("tp") == 2 and total % (16 * STEPS) == 0:
            return hand_over(sender, part, base, mine_full)
        sent = (scatter_tp(part) + base).astype(BF)
        sent = lax.ppermute(sent, "pipe", [(sender, 1 - sender)])
        return jnp.where(section == sender, mine_full, gather_tp(sent))

    wide = mine.astype(F32)
    part, _ = forward(mine_full)
    full_in = next_section(0, part, wide + b_out)
    part, kept = forward(full_in)
    y1 = scatter_tp(part) + own_part(full_in).astype(F32) + b_out
    part, _ = backward(mine_full, mine, kept, False)
    full_grad = next_section(1, part, wide)
    y1, full_grad = lax.optimization_barrier((y1, full_grad))
    own_grad = own_part(full_grad)
    du0, (weights, little) = backward(full_grad, own_grad, kept, True)
    g_down, g_up, g_dense, g_qkv = weights
    g_qkv_bias, g_feat, g_out_bias, g_up_bias, norm_sums = little
    section_ends = jnp.where(section == 0, du0, y1).reshape(1, MB, ROWS, tokens, width)
    grads = (
        norm_sums[:2], norm_sums[2:], g_qkv, g_qkv_bias, g_feat, g_dense, g_out_bias,
        g_up, g_up_bias, g_down,
    )
    return (section_ends,) + tuple(g[None] for g in grads)


def solution(mesh):
    in_specs = (
        P("pipe", None, None, "ctx", "tp"),
        P(),
        P("pipe", None, None),
        P("pipe", None, None),
        P("pipe", None, "tp"),
        P("pipe", "tp"),
        P("pipe", "tp", None),
        P("pipe", "tp", None),
        P("pipe", "tp"),
        P("pipe", None, "tp"),
        P("pipe", "tp"),
        P("pipe", "tp", None),
    )
    out_specs = (
        P("pipe", None, None, "ctx", "tp"),
        P("pipe", None, "tp"),
        P("pipe", None, "tp"),
        P("pipe", None, "tp"),
        P("pipe", "tp"),
        P("pipe", "tp", None),
        P("pipe", "tp", None),
        P("pipe", "tp"),
        P("pipe", None, "tp"),
        P("pipe", "tp"),
        P("pipe", "tp", None),
    )
    return jax.shard_map(local, mesh=mesh, in_specs=in_specs, out_specs=out_specs, check_vma=False)
```

```python
from functools import partial
import math

import jax
import jax.numpy as jnp
from jax import lax
from jax.experimental import pallas as pl
from jax.experimental.pallas import tpu as pltpu
from jax.sharding import PartitionSpec as P

D = 1024
HD = 64
ROT = 16
FEAT = 64
MB = 4
ROWS = 1
NDOC = 4
PAIR = 2 * HD
HELD = HD + 8
TILE = 256
HOP = 3

BF = jnp.bfloat16
F32 = jnp.float32
HIGHEST = lax.Precision.HIGHEST
norm_eps = 1e-05
VMEM_LIMIT = 56 * 1024 * 1024
REDUCE_LIMIT = 60 * 1024 * 1024


def feature_table():
    index_rows = jnp.arange(HD, dtype=jnp.int32)[:, None]
    index_cols = jnp.arange(HD, dtype=jnp.int32)[None, :]
    cosine = jnp.cos(
        math.pi * (index_rows.astype(F32) + 0.5) * index_cols.astype(F32) / HD
    )
    scaling = jnp.where(index_cols == 0, math.sqrt(1.0 / HD), math.sqrt(2.0 / HD))
    lattice_index = (
        (jnp.arange(HD, dtype=jnp.int32)[:, None] + 1)
        * (17 * jnp.arange(FEAT, dtype=jnp.int32)[None, :] + 5)
        % 257
    )
    lattice = math.sqrt(2.0) * jnp.cos(2.0 * math.pi * lattice_index.astype(F32) / 257.0)
    return jnp.dot(cosine * scaling, lattice, precision=HIGHEST) / math.sqrt(HD)


def table_pair():
    table = feature_table()
    zero = jnp.zeros_like(table)
    both = jnp.concatenate(
        [jnp.concatenate([table, zero], 1), jnp.concatenate([zero, table], 1)], 0
    )
    high = lax.reduce_precision(both, 8, 7).astype(BF)
    return high, (both - high.astype(F32)).astype(BF)


def rotary_tables(place, tokens):
    half = ROT // 2
    positions = place * tokens + jnp.arange(tokens, dtype=jnp.int32)
    inv_freq = 10000.0 ** (-(2.0 * jnp.arange(half).astype(F32)) / ROT)
    angles = positions.astype(F32)[:, None] * inv_freq[None, :]
    cos, sin = jnp.cos(angles), jnp.sin(angles)
    rest = jnp.ones((tokens, HD - ROT), F32)
    none = jnp.zeros((tokens, half), F32)
    same = jnp.concatenate([cos, cos, rest], 1)
    down = jnp.concatenate([-sin, none, 0.0 * rest], 1)
    up = jnp.concatenate([none, sin, 0.0 * rest], 1)
    return tuple(jnp.concatenate([t, t], 1) for t in (same, down, up))


def dot(a, b, ca=1, cb=0):
    return lax.dot_general(a, b, (((ca,), (cb,)), ((), ())), preferred_element_type=F32)


def split_dot(a, b, cb=0):
    high = a.astype(BF)
    low = (a - high.astype(F32)).astype(BF)
    return dot(high, b, 1, cb) + dot(low, b, 1, cb)


def lane_masks(rows):
    low = lax.broadcasted_iota(jnp.int32, (rows, PAIR), 1) < HD
    first = low.astype(F32)
    return low, first.astype(BF), (1.0 - first).astype(BF)


def count_starts(starts_ref, row, position):
    total = jnp.int32(0)
    for n in range(NDOC):
        total = total + (starts_ref[row, n] <= position).astype(jnp.int32)
    return total


def seg_grid(starts_ref, row, base, shape, dim):
    position = base + lax.broadcasted_iota(jnp.int32, shape, dim)
    total = jnp.zeros(shape, jnp.int32)
    for n in range(NDOC):
        total = total + (starts_ref[row, n] <= position).astype(jnp.int32)
    return total


def causal_mask(starts_ref, row, base, tokens):
    shape = (tokens, tokens)
    same = seg_grid(starts_ref, row, base, shape, 0) == seg_grid(starts_ref, row, base, shape, 1)
    earlier = lax.broadcasted_iota(jnp.int32, shape, 1) <= lax.broadcasted_iota(
        jnp.int32, shape, 0
    )
    rows = lax.broadcasted_iota(jnp.int32, shape, 0) < tokens // 2
    cols = lax.broadcasted_iota(jnp.int32, shape, 1) < tokens // 2
    mask = same & earlier
    return mask.astype(F32), (mask & (rows == cols)).astype(F32)


def middle_state(starts_ref, row, base, tokens, k, v, state_in, total_in, low):
    half = tokens // 2
    end = count_starts(starts_ref, row, base + half - 1)
    passing = (end == count_starts(starts_ref, row, base - 1)).astype(F32)
    seg = seg_grid(starts_ref, row, base, (half, PAIR), 0)
    key = k[:half] * (seg == end).astype(F32).astype(BF)
    state = passing * state_in + compact(dot(key, v[:half], 0, 0), low)
    total = passing * total_in + jnp.sum(key.astype(F32), 0, keepdims=True)
    later = seg_grid(starts_ref, row, base + half, (half, PAIR), 0)
    return state.astype(BF), total, (later == end).astype(F32)


def entering_mask(starts_ref, row, base, tokens):
    seg = seg_grid(starts_ref, row, base, (tokens, PAIR), 0)
    return (seg == count_starts(starts_ref, row, base - 1)).astype(F32)


def leaving_mask(starts_ref, row, base, tokens):
    seg = seg_grid(starts_ref, row, base, (tokens, PAIR), 0)
    return (seg == count_starts(starts_ref, row, base + tokens - 1)).astype(F32)


def rotate(x, same, down, up):
    half = ROT // 2
    return x * same + pltpu.roll(x, PAIR - half, 1) * down + pltpu.roll(x, half, 1) * up


def rotate_back(x, same, down, up):
    half = ROT // 2
    return x * same + pltpu.roll(x * down, half, 1) + pltpu.roll(x * up, PAIR - half, 1)


def compact(state, low):
    return jnp.where(low[:HD], state[:HD], state[HD:])


def spread(state, first, second):
    return jnp.concatenate([state * first[:HD], state * second[:HD]], 0)


def keep_state(state_ref, row, product, summands, low):
    state_ref[row, 0, :HD] = compact(product, low)
    total = jnp.sum(summands, 0, keepdims=True)
    state_ref[row, 0, HD:] = jnp.broadcast_to(total, (HELD - HD, PAIR))


def features_kernel(
    starts_ref, place_ref, norm_ref, weight_ref, bias_ref, feat_ref,
    same_ref, down_ref, up_ref, high_ref, low_ref,
    q_ref, k_ref, v_ref, state_ref,
):
    tokens = same_ref.shape[0]
    base = place_ref[0, 0] * tokens
    low, first, second = lane_masks(tokens)
    feat = feat_ref[0]
    proj = dot(norm_ref[...], weight_ref[...]) + bias_ref[0]
    c0, c1, c2 = proj[:, :PAIR], proj[:, PAIR : 2 * PAIR], proj[:, 2 * PAIR :]
    left = lane_masks(proj.shape[0])[0]
    v_ref[...] = jnp.where(left, c1, c2).astype(BF)
    same, down, up = (
        jnp.concatenate([t[...]] * (MB * ROWS), 0) for t in (same_ref, down_ref, up_ref)
    )
    query, key = jnp.where(left, c0, c1), pltpu.roll(jnp.where(left, c2, c0), HD, 1)
    for x, out_ref in ((query, q_ref), (key, k_ref)):
        x = rotate(x, same, down, up)
        arg = split_dot(x, high_ref[...]) + dot(x.astype(BF), low_ref[...])
        out_ref[...] = (feat * jnp.exp(arg)).astype(BF)
    for row in range(MB * ROWS):
        here = slice(row * tokens, (row + 1) * tokens)
        leaving = leaving_mask(starts_ref, row, base, tokens)
        key_out = k_ref[here, :] * leaving.astype(BF)
        keep_state(state_ref, row, dot(key_out, v_ref[here, :], 0, 0), key_out.astype(F32), low)


def attend_kernel(
    starts_ref, place_ref, q_ref, k_ref, v_ref, state_ref, low_ref, out_ref, den_ref
):
    tokens = q_ref.shape[0] // (MB * ROWS)
    base = place_ref[0, 0] * tokens
    low, first, second = lane_masks(tokens)
    ones = head_ones()
    for row in range(MB * ROWS):
        here = slice(row * tokens, (row + 1) * tokens)
        q, k, v = q_ref[here, :], k_ref[here, :], v_ref[here, :]
        mask, mask_in = causal_mask(starts_ref, row, base, tokens)
        enter = entering_mask(starts_ref, row, base, tokens)
        carry, total = state_ref[row, 0, :HD], state_ref[row, 0, HD : HD + 1]
        state = carry.astype(BF)
        middle, _, reach = middle_state(starts_ref, row, base, tokens, k, v, carry, total, low)
        half = tokens // 2
        num = jnp.concatenate(
            [
                dot(q[:half] * enter[:half].astype(BF), spread(state, first, second)),
                dot(q[half:] * reach.astype(BF), spread(middle, first, second)),
            ],
            0,
        )
        for head in (first, second):
            scores = dot(q * head, k, 1, 1) * mask_in
            num = num + dot(scores.astype(BF), v * head)
        totals = dot(mask.astype(BF), k) + enter * total
        den = split_dot(q.astype(F32) * totals, ones)
        att = num / den
        low_ref[here, :] = att.astype(BF)
        out_ref[here, :] = att
        den_ref[here, :] = den


def head_ones():
    rows = lax.broadcasted_iota(jnp.int32, (PAIR, PAIR), 0) < HD
    cols = lax.broadcasted_iota(jnp.int32, (PAIR, PAIR), 1) < HD
    return (rows == cols).astype(F32).astype(BF)


def head_spread():
    rows = lax.broadcasted_iota(jnp.int32, (PAIR, 2 * PAIR), 0) < HD
    cols = lax.broadcasted_iota(jnp.int32, (PAIR, 2 * PAIR), 1) < PAIR
    return (rows == cols).astype(F32).astype(BF)


def back_state_kernel(
    starts_ref, place_ref, q_ref, ga_ref, att_ref, den_ref, state_ref
):
    tokens = q_ref.shape[0] // (MB * ROWS)
    base = place_ref[0, 0] * tokens
    low, first, second = lane_masks(tokens)
    ones = head_ones()
    for row in range(MB * ROWS):
        here = slice(row * tokens, (row + 1) * tokens)
        grad_num = (ga_ref[here, :].astype(F32) / den_ref[here, :]).astype(BF)
        grad_den = -split_dot(grad_num.astype(F32) * att_ref[here, :], ones)
        enter = entering_mask(starts_ref, row, base, tokens)
        query = q_ref[here, :] * enter.astype(BF)
        keep_state(state_ref, row, dot(query, grad_num, 0, 0), grad_den * query.astype(F32), low)


def back_unit(starts_ref, row, base, q, k, v, ga, att, den, held, later_held, tables):
    same, down, up, high, low_table = tables
    tokens = q.shape[0]
    half = tokens // 2
    low, first, second = lane_masks(tokens)
    grad_num = (ga.astype(F32) / den).astype(BF)
    both = -split_dot(grad_num.astype(F32) * att, head_spread())
    dens = (both[:, :PAIR], both[:, PAIR:])
    grad_den = jnp.where(low, dens[0], dens[1])
    mask, mask_in = causal_mask(starts_ref, row, base, tokens)
    enter = entering_mask(starts_ref, row, base, tokens)
    leave = leaving_mask(starts_ref, row, base, tokens)
    carry, total = held[:HD], held[HD : HD + 1]
    middle, middle_total, reach = middle_state(
        starts_ref, row, base, tokens, k, v, carry, total, low
    )
    state, middle = spread(carry.astype(BF), first, second), spread(middle, first, second)
    gq = jnp.concatenate(
        [
            enter[:half] * (dot(grad_num[:half], state, 1, 1) + grad_den[:half] * total),
            reach * (dot(grad_num[half:], middle, 1, 1) + grad_den[half:] * middle_total),
        ],
        0,
    )
    later = later_held[:HD]
    later_high = later.astype(BF)
    later_low = spread((later - later_high.astype(F32)).astype(BF), first, second)
    later_high = spread(later_high, first, second)
    gk = leave * (
        dot(v, later_high, 1, 1) + dot(v, later_low, 1, 1) + later_held[HD : HD + 1]
    )
    gv = leave * (dot(k, later_high) + dot(k, later_low))
    for head, grad_head_den in zip((first, second), dens):
        q_head, grad_head = q * head, grad_num * head
        scores = (dot(q_head, k, 1, 1) * mask).astype(BF)
        grad_scores = dot(grad_head, v, 1, 1) + grad_head_den
        gq = gq + dot((grad_scores * mask_in).astype(BF), k * head)
        gk = gk + dot((grad_scores * mask).astype(BF), q_head, 0, 0)
        gv = gv + dot(scores, grad_head, 0, 0)
    arg_grads = (gq * q.astype(F32), gk * k.astype(F32))
    feat_sum = jnp.sum(arg_grads[0] + arg_grads[1], 0, keepdims=True)
    turned = []
    for x in arg_grads:
        x = split_dot(x, high, 1) + dot(x.astype(BF), low_table, 1, 1)
        turned.append(rotate_back(x, same, down, up))
    dq, dk = turned[0], pltpu.roll(turned[1], HD, 1)
    parts = (jnp.where(low, dq, dk), jnp.where(low, gv, dq), jnp.where(low, dk, gv))
    return tuple(part.astype(BF) for part in parts), feat_sum


def back_kernel(
    starts_ref, place_ref, q_ref, k_ref, v_ref, ga_ref, att_ref, den_ref,
    state_ref, later_ref, feat_ref,
    same_ref, down_ref, up_ref, high_ref, low_ref,
    grad_ref, sums_ref,
):
    tokens = q_ref.shape[0] // (MB * ROWS)
    base = place_ref[0, 0] * tokens
    tables = tuple(t[...] for t in (same_ref, down_ref, up_ref, high_ref, low_ref))
    sums_ref[...] = jnp.zeros_like(sums_ref)
    for row in range(MB * ROWS):
        here = slice(row * tokens, (row + 1) * tokens)
        values = [r[here, :] for r in (q_ref, k_ref, v_ref, ga_ref, att_ref, den_ref)]
        parts, feat_sum = back_unit(
            starts_ref, row, base, *values, state_ref[row, 0], later_ref[row, 0], tables
        )
        sums_ref[0, 0:1, :] += feat_sum / feat_ref[0]
        for n, part in enumerate(parts):
            grad_ref[here, n * PAIR : (n + 1) * PAIR] = part
            sums_ref[0, n + 1 : n + 2, :] += jnp.sum(part.astype(F32), 0, keepdims=True)


SMEM = pl.BlockSpec(memory_space=pltpu.SMEM)


def whole(shape):
    return pl.BlockSpec(shape, lambda p: (0,) * len(shape))


def column(rows, width):
    return pl.BlockSpec((rows, width), lambda p: (0, p))


def stacked(*shape):
    return pl.BlockSpec((1,) + shape, lambda p: (p,) + (0,) * len(shape))


def call(kernel, pairs, in_specs, out_specs, out_shape, flops):
    return pl.pallas_call(
        kernel,
        grid=(pairs,),
        in_specs=in_specs,
        out_specs=out_specs,
        out_shape=out_shape,
        compiler_params=pltpu.CompilerParams(vmem_limit_bytes=VMEM_LIMIT),
        cost_estimate=pl.CostEstimate(flops=flops, bytes_accessed=8 << 20, transcendentals=0),
    )


def shaped(shape, dtype):
    return jax.ShapeDtypeStruct(shape, dtype)


CHUNK = 256
PANEL = 512
RING = 4
LATER = (2, 3, 5, 20, 21, 22)
LAG = 7


def last_kernel(plan, *refs):
    count, terms = plan
    (
        starts_ref, hidden_ref, dy_ref, second_any, grad_pre_any, low_ref, first_any,
        q_ref, k_ref, v_ref, ga_ref, att_ref, den_ref, state_ref, later_ref, feat_ref,
        same_ref, down_ref, up_ref, high_table_ref, low_table_ref,
        qkv_any, grad_second_any, xhat_any, inv_ref, gain_ref, small_in_ref,
    ) = refs[:27]
    outs, du_ref = refs[27:32], refs[32]
    (
        proj, small_ref, away_buf, come_buf, norm_sum, norm_away, norm_come,
        sum_send, sum_recv, norm_sem,
        work, give, take, outside, inside,
        give_send, give_recv, part_send, outer_recv, inner_recv, total_send,
        final_send, final_recv, own_sem,
        second_ref, grad_pre_ref, first_ref, qkv_ref, grad_second_ref, xhat_ref, load_sem,
    ) = refs[33:]
    part = give
    later_loads = [
        pltpu.make_async_copy(source, buffer, load_sem.at[n])
        for n, (source, buffer) in enumerate(
            (
                (second_any, second_ref), (grad_pre_any, grad_pre_ref), (qkv_any, qkv_ref),
                (grad_second_any, grad_second_ref), (xhat_any, xhat_ref), (first_any, first_ref),
            )
        )
    ]
    factors = (
        hidden_ref, dy_ref, second_ref, grad_pre_ref, low_ref, dy_ref, first_ref, proj
    )
    rows, pairs = state_ref.shape[:2]
    tokens, width = q_ref.shape[0] // rows, du_ref.shape[1]
    units = rows * pairs
    tp = lax.axis_index("tp")
    my_cols = pl.ds(pl.multiple_of(tp * width, width), width)
    half = CHUNK // 2
    place, peers = lax.axis_index("ctx"), lax.axis_size("ctx")
    core, z, chips = place % 2, place // 2, peers // 2
    below = z < chips // 2
    middle = (z == chips // 2 - 1) | (z == chips // 2)
    has_outer = (z != 0) & (z != chips - 1)
    step = jnp.where(below, 2, -2)
    inner, outer, twin = place + step, place - step, place + 1 - 2 * core
    mine = pl.ds(pl.multiple_of(core * half, half), half)
    theirs = pl.ds(pl.multiple_of((1 - core) * half, half), half)

    def remote(src, dst, send, recv, to):
        return pltpu.make_async_remote_copy(
            src_ref=src, dst_ref=dst, send_sem=send, recv_sem=recv,
            device_id={"ctx": to}, device_id_type=pl.DeviceIdType.MESH,
        )

    def to_tp(src, dst, send, recv):
        return pltpu.make_async_remote_copy(
            src_ref=src, dst_ref=dst, send_sem=send, recv_sem=recv,
            device_id={"tp": 1 - tp}, device_id_type=pl.DeviceIdType.MESH,
        )

    def sum_copy(m):
        return to_tp(away_buf.at[m], come_buf.at[m], sum_send.at[m], sum_recv.at[m])

    def norm_copy():
        return to_tp(norm_away, norm_come, norm_sem.at[0], norm_sem.at[1])

    def split_cols(x):
        left, right = x[:, :width], x[:, width:]
        return jnp.where(tp == 0, left, right), jnp.where(tp == 0, right, left)

    def row_block(m):
        return pl.ds(pl.multiple_of(m * tokens, tokens), tokens)

    def attention_step(i):
        p, row = i // rows, i % rows
        here, cols = row_block(row), pl.ds(pl.multiple_of(p * PAIR, PAIR), PAIR)
        tables = tuple(
            t[...] for t in (same_ref, down_ref, up_ref, high_table_ref, low_table_ref)
        )
        values = [r[here, cols] for r in (q_ref, k_ref, v_ref, ga_ref, att_ref, den_ref)]
        parts, feat_sum = back_unit(
            starts_ref, row, place * tokens, *values, state_ref[row, p], later_ref[row, p], tables
        )
        line = (lax.broadcasted_iota(jnp.int32, (8, PAIR), 0) == p).astype(F32)
        small_ref[:8, 3 * PAIR : 4 * PAIR] += line * (feat_sum / feat_ref[p])
        for n, piece in enumerate(parts):
            proj[here, pl.ds(pl.multiple_of((3 * p + n) * PAIR, PAIR), PAIR)] = piece
            small_ref[:8, n * PAIR : (n + 1) * PAIR] += line * jnp.sum(
                piece.astype(F32), 0, keepdims=True
            )

    def norm_step(m):
        here = row_block(m)
        one, two, xhat = dot(proj[here, :], qkv_ref[...], 1, 1), grad_second_ref[here, :], xhat_ref[here, :]
        for n, x in enumerate((one * xhat, two * xhat, one, two)):
            norm_sum[n : n + 1, :] += jnp.sum(x, 0, keepdims=True)
        both = one * gain_ref[0:1, :] + two * gain_ref[1:2, :]
        leaving = inv_ref[here, :] * (
            both
            - jnp.mean(both, -1, keepdims=True)
            - xhat * jnp.mean(both * xhat, -1, keepdims=True)
        )
        kept, sent = split_cols(leaving)
        away_buf[m] = sent.astype(BF)
        sum_copy(m).start()
        du_ref[here, :] = kept + dy_ref[here, my_cols].astype(F32)

    def other_work(i):
        @pl.when(i < units)
        def _():
            attention_step(i)

        @pl.when((i >= units) & (i < units + rows))
        def _():
            norm_step(i - units)

        @pl.when(i == units + rows)
        def _():
            kept, sent = split_cols(norm_sum[...])
            norm_away[...] = sent
            norm_copy().start()
            small_ref[16:24, :] = kept

        late = i - (units + rows + 3)

        @pl.when((late >= 0) & (late < rows))
        def _():
            sum_copy(late).wait()
            du_ref[row_block(late), :] += come_buf[late].astype(F32)

        @pl.when(late == rows)
        def _():
            norm_copy().wait()
            small_ref[16:24, :] += norm_come[...]

    def give_copy(t):
        return remote(give.at[t], take.at[t], give_send.at[t], give_recv.at[t], twin)

    def to_outside(t):
        return remote(part.at[t], outside.at[t], part_send.at[t], outer_recv.at[t], inner)

    def across(t):
        return remote(part.at[t], inside.at[t], part_send.at[t], inner_recv.at[t], inner)

    def outward(t):
        return remote(take.at[t], inside.at[t], total_send.at[t], inner_recv.at[t], outer)

    def final_copy(t, target):
        return remote(take.at[t], target, final_send.at[t], final_recv.at[t], twin)

    def own_copy(t, target):
        return pltpu.make_async_copy(take.at[t], target, own_sem.at[t])

    def block_of(j, panels):
        rows = (j // panels) * CHUNK
        return rows, pl.ds(pl.multiple_of((j % panels) * PANEL, PANEL), PANEL)

    def deliver(t, target):
        final_copy(t, target).start()
        own_copy(t, target).start()

    some_target = outs[-1].at[mine]

    barrier = pltpu.get_barrier_semaphore()
    for peer in ({"ctx": inner}, {"ctx": twin}, {"tp": 1 - tp}):
        pl.semaphore_signal(barrier, inc=1, device_id=peer, device_id_type=pl.DeviceIdType.MESH)

    @pl.when(has_outer)
    def _():
        pl.semaphore_signal(
            barrier, inc=1, device_id={"ctx": outer}, device_id_type=pl.DeviceIdType.MESH
        )

    pl.semaphore_wait(barrier, 3 + has_outer.astype(jnp.int32))
    for copy in later_loads:
        copy.start()
    small_ref[...] = jnp.zeros_like(small_ref)
    small_ref[8:16, :] = small_in_ref[...]
    norm_sum[...] = jnp.zeros_like(norm_sum)
    lag = jnp.where(middle, 3, LAG)

    def one(t, carry):
        slot = t % RING
        begin = 0

        @pl.when(t == terms[0][0] * terms[0][1] - 1)
        def _():
            for copy in later_loads:
                copy.wait()

        for n, (blocks, panels) in enumerate(terms):
            left, right = factors[2 * n], factors[2 * n + 1]

            @pl.when((t >= begin) & (t < begin + blocks * panels))
            def _(left=left, right=right, panels=panels, begin=begin):
                start, cols = block_of(t - begin, panels)
                rows = pl.ds(pl.multiple_of(start, CHUNK), CHUNK)
                work[slot] = dot(left[:, rows], right[:, cols], 0, 0)

            begin += blocks * panels

        @pl.when(t == begin)
        def _():
            work[slot] = small_ref[...]

        @pl.when(t < count)
        def _():
            give[t] = work[slot, theirs, :].astype(BF)
            give_copy(t).start()

        tb = t - 2

        @pl.when((tb >= 0) & (tb < count))
        def _():
            give_copy(tb).wait()
            total = work[(t + RING - 2) % RING, mine, :] + take[tb].astype(F32)

            @pl.when(has_outer)
            def _():
                to_outside(tb).wait_recv()
                part[tb] = (total + outside[tb].astype(F32)).astype(BF)

            @pl.when(jnp.logical_not(has_outer))
            def _():
                part[tb] = total.astype(BF)

            @pl.when(middle)
            def _():
                across(tb).start()

            @pl.when(jnp.logical_not(middle))
            def _():
                to_outside(tb).start()

        tc = t - lag

        @pl.when((tc >= 0) & (tc < count))
        def _():
            across(tc).wait_recv()

            @pl.when(middle)
            def _():
                take[tc] = (part[tc].astype(F32) + inside[tc].astype(F32)).astype(BF)

            @pl.when(jnp.logical_not(middle))
            def _():
                take[tc] = inside[tc]

            @pl.when(has_outer)
            def _():
                outward(tc).start()

            begin = 0
            for n, (blocks, panels) in enumerate(terms):

                @pl.when((tc >= begin) & (tc < begin + blocks * panels))
                def _(n=n, panels=panels, begin=begin):
                    start, cols = block_of(tc - begin, panels)
                    rows = pl.ds(pl.multiple_of(start + core * half, half), half)
                    deliver(tc, outs[n].at[rows, cols])

                begin += blocks * panels

            @pl.when(tc == begin)
            def _():
                deliver(tc, some_target)

        other_work(t)
        return carry

    lax.fori_loop(0, count + LAG, one, 0)

    def drain(t, carry):
        across(t).wait_send()
        final_copy(t, some_target).wait_send()
        final_copy(t, some_target).wait_recv()
        own_copy(t, some_target).wait()

        @pl.when(has_outer)
        def _():
            outward(t).wait_send()

        return carry

    lax.fori_loop(0, count, drain, 0)


def last_call(starts, factors, attention, norms, small):
    shapes = [(a.shape[1], b.shape[1]) for a, b in factors[:3]]
    first, qkv = factors[3][0], norms[0]
    shapes.append((first.shape[1], qkv.shape[1]))
    terms = tuple((x // CHUNK, y // PANEL) for x, y in shapes)
    count = sum(x * y for x, y in terms) + 1
    total, width = first.shape[0], D // 2
    rows, tokens = MB * ROWS, total // (MB * ROWS)
    slots = pltpu.VMEM((count, CHUNK // 2, PANEL), BF)
    flat = [factors[0][0], factors[0][1], factors[1][0], factors[1][1], factors[2][0], first]
    flat = flat + list(attention) + list(norms) + [small]
    dma = pltpu.SemaphoreType.DMA
    *sums, du = pl.pallas_call(
        partial(last_kernel, (count, terms)),
        in_specs=[SMEM] + [ANYWHERE if n in LATER else IN_VMEM for n in range(len(flat))],
        out_specs=[ANYWHERE] * 5 + [IN_VMEM],
        out_shape=[shaped(x, BF) for x in shapes]
        + [shaped((CHUNK, PANEL), BF), shaped((total, width), F32)],
        scratch_shapes=[
            pltpu.VMEM((total, qkv.shape[1]), BF),
            pltpu.VMEM((CHUNK, PANEL), F32),
            pltpu.VMEM((rows, tokens, width), BF),
            pltpu.VMEM((rows, tokens, width), BF),
            pltpu.VMEM((8, D), F32),
            pltpu.VMEM((8, width), F32),
            pltpu.VMEM((8, width), F32),
            dma((rows,)), dma((rows,)), dma((2,)),
            pltpu.VMEM((RING, CHUNK, PANEL), F32),
        ]
        + [slots] * 4
        + [dma((count,))] * 9
        + [pltpu.VMEM(flat[n].shape, flat[n].dtype) for n in LATER] + [dma((len(LATER),))],
        compiler_params=pltpu.CompilerParams(
            collective_id=0, has_side_effects=True, vmem_limit_bytes=REDUCE_LIMIT
        ),
        cost_estimate=pl.CostEstimate(
            flops=count * 2 * CHUNK * PANEL * 512, bytes_accessed=40 << 20, transcendentals=0
        ),
    )(starts, *flat)
    return [g.astype(F32) for g in sums[:-1]], sums[-1].astype(F32), du


def fits_last(factors, qkv, pairs):
    sizes = [(a.shape[1], b.shape[1]) for a, b in factors] + [qkv.shape]
    even = all(x % CHUNK == 0 and y % PANEL == 0 for x, y in sizes)
    ahead = sum(x // CHUNK * (y // PANEL) for x, y in sizes[:-1])
    units = MB * ROWS * (pairs + 2) + 8
    line = lax.axis_size("ctx") % 4 == 0 and lax.axis_size("tp") == 2
    return even and line and units <= ahead and pairs <= 8


def exchange(forward, starts_ref, own_ref, got_ref, bufs, tokens):
    (twin_buf, in_buf, out_buf, back_buf, twin_sem, send_sem, recv_sem, back_send, back_recv) = bufs
    rows, pairs = own_ref.shape[:2]
    part = rows // 2
    chunks, width = in_buf.shape[:2]
    split = pairs // width
    place, chips = lax.axis_index("ctx"), lax.axis_size("ctx") // 2
    core, z = place % 2, place // 2
    away = z if forward else chips - 1 - z
    first, last = away == 0, away == chips - 1
    step = 2 if forward else -2
    twin = place + 1 - 2 * core
    leads = core == (0 if forward else 1)
    lead = 2 * z + (0 if forward else 1)
    other = 2 * z + (1 if forward else 0)

    def remote(src, dst, send, recv, to):
        return pltpu.make_async_remote_copy(
            src_ref=src, dst_ref=dst, send_sem=send, recv_sem=recv,
            device_id={"ctx": to}, device_id_type=pl.DeviceIdType.MESH,
        )

    def twin_copy():
        theirs = own_ref.at[pl.ds((1 - core) * part, part)]
        return remote(theirs, twin_buf, twin_sem.at[0], twin_sem.at[1], twin)

    def onward(j):
        return remote(out_buf.at[j], in_buf.at[j], send_sem.at[j], recv_sem.at[j], place + step)

    def where_of(j):
        return core * part + j // split, pl.ds((j % split) * width, width)

    def back(j):
        row, cols = where_of(j)
        return remote(back_buf.at[j], got_ref.at[row, cols], back_send.at[j], back_recv.at[j], twin)

    def passing(row, at):
        end = count_starts(starts_ref, row, at * tokens + tokens - 1)
        return (end == count_starts(starts_ref, row, at * tokens - 1)).astype(F32)

    def begin():
        barrier = pltpu.get_barrier_semaphore()

        def greet(peer):
            pl.semaphore_signal(
                barrier, inc=1, device_id={"ctx": peer}, device_id_type=pl.DeviceIdType.MESH
            )

        greet(twin)

        @pl.when(jnp.logical_not(first))
        def _():
            greet(place - step)

        pl.semaphore_wait(barrier, 2 - last.astype(jnp.int32))
        twin_copy().start()

    def advance(i):
        @pl.when(i == 0)
        def _():
            twin_copy().wait_recv()

        j = i - HOP * away

        @pl.when((j >= 0) & (j < chunks))
        def _():
            row, cols = where_of(j)

            @pl.when(first)
            def _():
                in_buf[j] = jnp.zeros(in_buf.shape[1:], F32)

            @pl.when(jnp.logical_not(first))
            def _():
                onward(j).wait_recv()

            mine, theirs = own_ref[row, cols], twin_buf[j // split, cols]
            entering_lead = in_buf[j]
            entering_other = jnp.where(leads, mine, theirs) + passing(row, lead) * entering_lead

            @pl.when(jnp.logical_not(last))
            def _():
                out_buf[j] = (
                    jnp.where(leads, theirs, mine) + passing(row, other) * entering_other
                )
                onward(j).start()

            got_ref[row, cols] = jnp.where(leads, entering_lead, entering_other)
            back_buf[j] = jnp.where(leads, entering_other, entering_lead)
            back(j).start()

    def finish():
        twin_copy().wait_send()

        def one(j, carry):
            back(j).wait_send()
            back(j).wait_recv()

            @pl.when(jnp.logical_not(last))
            def _():
                onward(j).wait_send()

            return carry

        lax.fori_loop(0, chunks, one, 0)

    return begin, advance, finish, (chips - 1) * HOP + chunks


def exchange_scratch(rows, pairs):
    width = pairs // 2 if pairs % 2 == 0 else pairs
    chunks = rows // 2 * (pairs // width)
    one = pltpu.VMEM((chunks, width, HELD, PAIR), F32)
    return [
        pltpu.VMEM((rows // 2, pairs, HELD, PAIR), F32), one, one, one,
        pltpu.SemaphoreType.DMA((2,)),
    ] + [pltpu.SemaphoreType.DMA((chunks,))] * 4


def tile(n):
    return pl.ds(pl.multiple_of(n * TILE, TILE), TILE)


def run_tiles(first_count, first_body, second_count, second_body, loads, link):
    begin, advance, finish, steps = link
    for _, copy in loads[:-1]:
        copy(0).start()
    begin()
    for n, (count, copy) in enumerate(loads):
        start_all(0 if n == len(loads) - 1 else 1, count, copy)
    both = first_count + second_count

    def one(i, carry):
        @pl.when(i < first_count)
        def _():
            first_body(i)

        @pl.when((i >= first_count) & (i < both))
        def _():
            second_body(i - first_count)

        advance(i)
        return carry

    lax.fori_loop(0, max(both, steps), one, 0)
    finish()


def start_all(begin, count, copy):
    def one(n, carry):
        copy(n).start()
        return carry

    lax.fori_loop(begin, count, one, 0)


def feed_forward_kernel(
    tokens, starts_ref, own_ref, norm_ref, up_ref, bias_ref, down_ref,
    pre_ref, hidden_ref, mlp_ref, got_ref,
    up_buf, down_buf, up_sem, down_sem, *bufs,
):
    ups, downs = up_ref.shape[1] // TILE, down_ref.shape[1] // TILE

    def up_copy(n):
        return pltpu.make_async_copy(up_ref.at[:, tile(n)], up_buf.at[:, tile(n)], up_sem.at[n])

    def down_copy(n):
        return pltpu.make_async_copy(
            down_ref.at[:, tile(n)], down_buf.at[:, tile(n)], down_sem.at[n]
        )

    loads = ((ups, up_copy), (downs, down_copy))

    def up(n):
        up_copy(n).wait()
        pre = dot(norm_ref[...], up_buf[:, tile(n)]) + bias_ref[:, tile(n)]
        pre_ref[:, tile(n)] = pre
        hidden = 0.5 * pre * (1.0 + lax.erf(pre * math.sqrt(0.5)))
        hidden_ref[:, tile(n)] = hidden.astype(BF)

    def down(n):
        down_copy(n).wait()
        mlp_ref[:, tile(n)] = dot(hidden_ref[...], down_buf[:, tile(n)])

    link = exchange(True, starts_ref, own_ref, got_ref, bufs, tokens)
    run_tiles(ups, up, downs, down, loads, link)


def feed_backward_kernel(
    tokens, starts_ref, own_ref, grad_ref, pre_ref, down_ref, up_ref,
    grad_pre_ref, grad_norm_ref, got_ref,
    pre_buf, down_buf, up_buf, pre_sem, down_sem, up_sem, *bufs,
):
    downs, ups = down_ref.shape[0] // TILE, up_ref.shape[0] // TILE

    def pre_copy(n):
        return pltpu.make_async_copy(pre_ref.at[:, tile(n)], pre_buf.at[:, tile(n)], pre_sem.at[n])

    def down_copy(n):
        return pltpu.make_async_copy(down_ref.at[tile(n)], down_buf.at[tile(n)], down_sem.at[n])

    def up_copy(n):
        return pltpu.make_async_copy(up_ref.at[tile(n)], up_buf.at[tile(n)], up_sem.at[n])

    loads = ((downs, down_copy), (downs, pre_copy), (ups, up_copy))

    def down(n):
        down_copy(n).wait()
        pre_copy(n).wait()
        grad = dot(grad_ref[...], down_buf[tile(n), :], 1, 1)
        pre = pre_buf[:, tile(n)]
        cdf = 0.5 * (1.0 + lax.erf(pre * math.sqrt(0.5)))
        slope = cdf + pre * jnp.exp(-0.5 * pre * pre) * (1.0 / math.sqrt(2.0 * math.pi))
        grad_pre_ref[:, tile(n)] = (grad * slope).astype(BF)

    def up(n):
        up_copy(n).wait()
        grad_norm_ref[:, tile(n)] = dot(grad_pre_ref[...], up_buf[tile(n), :], 1, 1)

    link = exchange(False, starts_ref, own_ref, got_ref, bufs, tokens)
    run_tiles(downs, down, ups, up, loads, link)


IN_VMEM = pl.BlockSpec(memory_space=pltpu.VMEM)
ANYWHERE = pl.BlockSpec(memory_space=pl.ANY)


def link_call(kernel, number, in_specs, out_shape, scratch, flops):
    return pl.pallas_call(
        kernel,
        in_specs=in_specs,
        out_specs=[IN_VMEM] * len(out_shape),
        out_shape=out_shape,
        scratch_shapes=scratch,
        compiler_params=pltpu.CompilerParams(
            collective_id=number, has_side_effects=True, vmem_limit_bytes=VMEM_LIMIT
        ),
        cost_estimate=pl.CostEstimate(flops=flops, bytes_accessed=16 << 20, transcendentals=0),
    )


def feed_forward(starts, state, norm, w_up, b_up, w_down):
    total, units = norm.shape[0], w_up.shape[1]
    rows, pairs = state.shape[:2]
    return link_call(
        partial(feed_forward_kernel, total // rows),
        1,
        [SMEM, IN_VMEM, IN_VMEM, ANYWHERE, IN_VMEM, ANYWHERE],
        [
            shaped((total, units), F32), shaped((total, units), BF), shaped((total, D), F32),
            shaped(state.shape, F32),
        ],
        [
            pltpu.VMEM(w_up.shape, BF), pltpu.VMEM(w_down.shape, BF),
            pltpu.SemaphoreType.DMA((units // TILE,)), pltpu.SemaphoreType.DMA((D // TILE,)),
        ]
        + exchange_scratch(rows, pairs),
        4 * total * units * D,
    )(starts, state, norm, w_up, b_up.reshape(1, units), w_down)


def feed_backward(starts, state, grad, pre, w_down, w_up):
    total, units = pre.shape
    rows, pairs = state.shape[:2]
    return link_call(
        partial(feed_backward_kernel, total // rows),
        2,
        [SMEM, IN_VMEM, IN_VMEM, ANYWHERE, ANYWHERE, ANYWHERE],
        [shaped((total, units), BF), shaped((total, D), F32), shaped(state.shape, F32)],
        [
            pltpu.VMEM(pre.shape, F32), pltpu.VMEM(w_down.shape, BF), pltpu.VMEM(w_up.shape, BF),
            pltpu.SemaphoreType.DMA((units // TILE,)), pltpu.SemaphoreType.DMA((units // TILE,)),
            pltpu.SemaphoreType.DMA((D // TILE,)),
        ]
        + exchange_scratch(rows, pairs),
        4 * total * units * D,
    )(starts, state, grad, pre, w_down, w_up)


STEPS = 8


def hand_over_kernel(sender, part_ref, base_ref, full_ref, out_ref, *bufs):
    (
        away_buf, sum_buf, pass_buf,
        sum_send, sum_recv, pass_send, pass_recv, spread_send, spread_recv,
    ) = bufs
    width = base_ref.shape[1]
    height = base_ref.shape[0] // STEPS
    pipe, tp = lax.axis_index("pipe"), lax.axis_index("tp")
    sends = pipe == sender
    own = pl.ds(pl.multiple_of(tp * width, width), width)
    away = pl.ds(pl.multiple_of((1 - tp) * width, width), width)

    def rows(c):
        return slice(c * height, (c + 1) * height)

    def remote(src, dst, send, recv, to):
        return pltpu.make_async_remote_copy(
            src_ref=src, dst_ref=dst, send_sem=send, recv_sem=recv,
            device_id=to, device_id_type=pl.DeviceIdType.MESH,
        )

    def sum_copy(c):
        return remote(away_buf.at[c], sum_buf.at[c], sum_send.at[c], sum_recv.at[c], {"tp": 1 - tp})

    def pass_copy(c):
        target = out_ref.at[rows(c), own]
        return remote(pass_buf.at[c], target, pass_send.at[c], pass_recv.at[c], {"pipe": 1 - pipe})

    def spread_copy(c):
        piece = out_ref.at[rows(c), own]
        return remote(piece, piece, spread_send.at[c], spread_recv.at[c], {"tp": 1 - tp})

    barrier = pltpu.get_barrier_semaphore()

    def greet(to):
        pl.semaphore_signal(barrier, inc=1, device_id=to, device_id_type=pl.DeviceIdType.MESH)

    greet({"tp": 1 - tp})

    @pl.when(jnp.logical_not(sends))
    def _():
        greet({"pipe": 1 - pipe})

    pl.semaphore_wait(barrier, 1 + sends.astype(jnp.int32))

    @pl.when(sends)
    def _():
        for c in range(STEPS):
            away_buf[c] = part_ref[rows(c), away].astype(BF)
            sum_copy(c).start()
        for c in range(STEPS):
            out_ref[rows(c), :] = full_ref[rows(c), :]
            sum_copy(c).wait_recv()
            total = part_ref[rows(c), own] + sum_buf[c].astype(F32) + base_ref[rows(c), :]
            pass_buf[c] = total.astype(BF)
            pass_copy(c).start()
        for c in range(STEPS):
            sum_copy(c).wait_send()
            pass_copy(c).wait_send()

    @pl.when(jnp.logical_not(sends))
    def _():
        for c in range(STEPS):
            pass_copy(c).wait_recv()
            spread_copy(c).start()
        for c in range(STEPS):
            spread_copy(c).wait_send()
            spread_copy(c).wait_recv()


def hand_over(sender, part, base, full):
    total, width = base.shape
    piece = pltpu.VMEM((STEPS, total // STEPS, width), BF)
    return pl.pallas_call(
        partial(hand_over_kernel, sender),
        in_specs=[IN_VMEM] * 3,
        out_specs=IN_VMEM,
        out_shape=shaped(full.shape, BF),
        scratch_shapes=[piece] * 3 + [pltpu.SemaphoreType.DMA((STEPS,))] * 6,
        compiler_params=pltpu.CompilerParams(
            collective_id=3 + sender, has_side_effects=True, vmem_limit_bytes=VMEM_LIMIT
        ),
        cost_estimate=pl.CostEstimate(flops=1 << 20, bytes_accessed=8 << 20, transcendentals=0),
    )(part, base, full)


def gather_tp(value):
    if lax.axis_size("tp") != 2:
        return lax.all_gather(value, "tp", axis=1, tiled=True)
    other = lax.ppermute(value, "tp", [(0, 1), (1, 0)])
    return jnp.where(
        lax.axis_index("tp") == 0,
        jnp.concatenate([value, other], 1),
        jnp.concatenate([other, value], 1),
    )


def scatter_tp(value):
    peers = lax.axis_size("tp")
    if peers != 2:
        return lax.psum_scatter(value, "tp", scatter_dimension=1, tiled=True)
    me = lax.axis_index("tp")
    width = value.shape[1] // 2
    left, right = value[:, :width], value[:, width:]
    other = lax.ppermute(jnp.where(me == 0, right, left).astype(BF), "tp", [(0, 1), (1, 0)])
    return jnp.where(me == 0, left, right) + other.astype(F32)


def local(
    section_inputs,
    doc_starts,
    ln_gains,
    ln_shifts,
    qkv_weight,
    qkv_bias,
    feature_weight,
    dense_weight,
    out_bias,
    up_weight,
    up_bias,
    down_weight,
):
    section = lax.axis_index("pipe")
    place = lax.axis_index("ctx")
    width = section_inputs.shape[-1]
    tokens = section_inputs.shape[3]
    rows = MB * ROWS
    total = rows * tokens
    heads = feature_weight.shape[1]
    pairs = heads // 2
    gain, shift = ln_gains[0], ln_shifts[0]
    w_qkv, w_dense, w_up, w_down = qkv_weight[0], dense_weight[0], up_weight[0], down_weight[0]
    b_qkv = qkv_bias[0].reshape(pairs, 1, 3 * PAIR)
    b_up, b_out = up_bias[0], out_bias[0]
    feat = feature_weight[0].reshape(pairs, 1, PAIR)
    starts = doc_starts.reshape(rows, NDOC)
    place_in = place.astype(jnp.int32).reshape(1, 1)
    high, low = table_pair()
    same, down, up = rotary_tables(place, tokens)
    tables = (same, down, up, high, low)
    table_specs = [whole((tokens, PAIR))] * 3 + [whole((PAIR, PAIR))] * 2
    state_shape = shaped((rows, pairs, HELD, PAIR), F32)
    state_spec = pl.BlockSpec((rows, 1, HELD, PAIR), lambda p: (0, p, 0, 0))
    low_shape, full_shape = shaped((total, pairs * PAIR), BF), shaped((total, pairs * PAIR), F32)
    unit = 2 * rows * tokens * PAIR * PAIR * pairs

    def forward(u_low):
        u = u_low.astype(F32)
        centered = u - jnp.mean(u, -1, keepdims=True)
        inv = lax.rsqrt(jnp.mean(centered * centered, -1, keepdims=True) + norm_eps)
        xhat = centered * inv
        first = (xhat * gain[0] + shift[0]).astype(BF)
        second = (xhat * gain[1] + shift[1]).astype(BF)
        q, k, v, state = call(
            features_kernel,
            pairs,
            [SMEM, SMEM, whole((total, D)), column(D, 3 * PAIR), stacked(1, 3 * PAIR),
             stacked(1, PAIR)] + table_specs,
            [column(total, PAIR)] * 3 + [state_spec],
            [low_shape] * 3 + [state_shape],
            30 * unit,
        )(starts, place_in, first, w_qkv, b_qkv, feat, *tables)
        pre, hidden, mlp, state_in = feed_forward(starts, state, second, w_up, b_up, w_down)
        att_low, att, den = call(
            attend_kernel,
            pairs,
            [SMEM, SMEM] + [column(total, PAIR)] * 3 + [state_spec],
            [column(total, PAIR)] * 3,
            [low_shape, full_shape, full_shape],
            8 * unit,
        )(starts, place_in, q, k, v, state_in)
        part = jnp.dot(att_low, w_dense, preferred_element_type=F32) + mlp
        kept = (xhat, inv, first, second, q, k, v, pre, hidden, att_low, att, den, state_in)
        return part, kept

    def backward(dy, own, kept, want):
        xhat, inv, first, second, q, k, v, pre, hidden, att_low, att, den, state_in = kept
        ga = lax.dot_general(
            dy, w_dense, (((1,), (1,)), ((), ())), preferred_element_type=F32
        ).astype(BF)
        (state,) = call(
            back_state_kernel,
            pairs,
            [SMEM, SMEM] + [column(total, PAIR)] * 4,
            [state_spec],
            [state_shape],
            3 * unit,
        )(starts, place_in, q, ga, att, den)
        grad_pre, grad_second, later = feed_backward(starts, state, dy, pre, w_down, w_up)
        large = ((hidden, dy), (second, grad_pre), (att_low, dy))
        up_sum = jnp.sum(grad_pre.astype(F32), 0) if want else None
        out_sum = jnp.sum(own.astype(F32), 0)
        if want and fits_last(large, w_qkv, pairs):
            extra = jnp.concatenate([up_sum, out_sum])
            extra = jnp.pad(extra, (0, 8 * PANEL - extra.size)).reshape(8, PANEL)
            weights, flat, du = last_call(
                starts,
                large + ((first, None),),
                (q, k, v, ga, att, den, state_in, later, feat) + tables,
                (w_qkv, grad_second, xhat, inv, gain),
                extra,
            )
            ends = up_sum.size // PANEL
            little = (
                flat[:pairs, : 3 * PAIR].reshape(-1),
                flat[:pairs, 3 * PAIR :].reshape(heads, FEAT),
                flat[8 + ends : 8 + ends + out_sum.size // PANEL].reshape(-1),
                flat[8 : 8 + ends].reshape(-1),
                flat[16:20],
            )
            return du, (weights, little)
        grad_proj, sums = call(
            back_kernel,
            pairs,
            [SMEM, SMEM] + [column(total, PAIR)] * 6
            + [state_spec, state_spec, stacked(1, PAIR)] + table_specs,
            [column(total, 3 * PAIR), stacked(8, PAIR)],
            [shaped((total, pairs * 3 * PAIR), BF), shaped((pairs, 8, PAIR), F32)],
            20 * unit,
        )(starts, place_in, q, k, v, ga, att, den, state_in, later, feat, *tables)
        grad_first = lax.dot_general(
            grad_proj, w_qkv, (((1,), (1,)), ((), ())), preferred_element_type=F32
        )
        both = grad_first * gain[0] + grad_second * gain[1]
        part = inv * (
            both
            - jnp.mean(both, -1, keepdims=True)
            - xhat * jnp.mean(both * xhat, -1, keepdims=True)
        )
        if not want:
            return part, None
        norm_sums = jnp.stack(
            [
                jnp.sum(grad_first * xhat, 0),
                jnp.sum(grad_second * xhat, 0),
                jnp.sum(grad_first, 0),
                jnp.sum(grad_second, 0),
            ]
        )
        norm_sums = lax.psum_scatter(norm_sums, "tp", scatter_dimension=1, tiled=True)
        little = (
            sums[:, 1:4, :].reshape(pairs * 3 * PAIR),
            sums[:, 0, :].reshape(heads, FEAT),
            out_sum,
            up_sum,
            norm_sums,
        )
        products = tuple(dot(a, b, 0, 0).astype(BF) for a, b in large + ((first, grad_proj),))
        weights = [g.astype(F32) for g in lax.psum(products, "ctx")]
        return scatter_tp(part) + own.astype(F32), (weights, lax.psum(little, "ctx"))

    mine = section_inputs[0].reshape(total, width)
    mine_full = gather_tp(mine)
    tp_place = lax.axis_index("tp")

    def own_part(full):
        return lax.dynamic_slice_in_dim(full, tp_place * width, width, 1)

    def next_section(sender, part, base):
        if lax.axis_size("tp") == 2 and total % (16 * STEPS) == 0:
            return hand_over(sender, part, base, mine_full)
        sent = (scatter_tp(part) + base).astype(BF)
        sent = lax.ppermute(sent, "pipe", [(sender, 1 - sender)])
        return jnp.where(section == sender, mine_full, gather_tp(sent))

    wide = mine.astype(F32)
    part, _ = forward(mine_full)
    full_in = next_section(0, part, wide + b_out)
    part, kept = forward(full_in)
    y1 = scatter_tp(part) + own_part(full_in).astype(F32) + b_out
    part, _ = backward(mine_full, mine, kept, False)
    full_grad = next_section(1, part, wide)
    y1, full_grad = lax.optimization_barrier((y1, full_grad))
    own_grad = own_part(full_grad)
    du0, (weights, little) = backward(full_grad, own_grad, kept, True)
    g_down, g_up, g_dense, g_qkv = weights
    g_qkv_bias, g_feat, g_out_bias, g_up_bias, norm_sums = little
    section_ends = jnp.where(section == 0, du0, y1).reshape(1, MB, ROWS, tokens, width)
    grads = (
        norm_sums[:2], norm_sums[2:], g_qkv, g_qkv_bias, g_feat, g_dense, g_out_bias,
        g_up, g_up_bias, g_down,
    )
    return (section_ends,) + tuple(g[None] for g in grads)


def solution(mesh):
    in_specs = (
        P("pipe", None, None, "ctx", "tp"),
        P(),
        P("pipe", None, None),
        P("pipe", None, None),
        P("pipe", None, "tp"),
        P("pipe", "tp"),
        P("pipe", "tp", None),
        P("pipe", "tp", None),
        P("pipe", "tp"),
        P("pipe", None, "tp"),
        P("pipe", "tp"),
        P("pipe", "tp", None),
    )
    out_specs = (
        P("pipe", None, None, "ctx", "tp"),
        P("pipe", None, "tp"),
        P("pipe", None, "tp"),
        P("pipe", None, "tp"),
        P("pipe", "tp"),
        P("pipe", "tp", None),
        P("pipe", "tp", None),
        P("pipe", "tp"),
        P("pipe", None, "tp"),
        P("pipe", "tp"),
        P("pipe", "tp", None),
    )
    return jax.shard_map(local, mesh=mesh, in_specs=in_specs, out_specs=out_specs, check_vma=False)
```

```python
from functools import partial
import math

import jax
import jax.numpy as jnp
from jax import lax
from jax.experimental import pallas as pl
from jax.experimental.pallas import tpu as pltpu
from jax.sharding import PartitionSpec as P

D = 1024
HD = 64
ROT = 16
FEAT = 64
MB = 4
ROWS = 1
NDOC = 4
PAIR = 2 * HD
HELD = HD + 8
TILE = 256
HOP = 3

BF = jnp.bfloat16
F32 = jnp.float32
HIGHEST = lax.Precision.HIGHEST
norm_eps = 1e-05
VMEM_LIMIT = 56 * 1024 * 1024
REDUCE_LIMIT = 60 * 1024 * 1024


def feature_table():
    index_rows = jnp.arange(HD, dtype=jnp.int32)[:, None]
    index_cols = jnp.arange(HD, dtype=jnp.int32)[None, :]
    cosine = jnp.cos(
        math.pi * (index_rows.astype(F32) + 0.5) * index_cols.astype(F32) / HD
    )
    scaling = jnp.where(index_cols == 0, math.sqrt(1.0 / HD), math.sqrt(2.0 / HD))
    lattice_index = (
        (jnp.arange(HD, dtype=jnp.int32)[:, None] + 1)
        * (17 * jnp.arange(FEAT, dtype=jnp.int32)[None, :] + 5)
        % 257
    )
    lattice = math.sqrt(2.0) * jnp.cos(2.0 * math.pi * lattice_index.astype(F32) / 257.0)
    return jnp.dot(cosine * scaling, lattice, precision=HIGHEST) / math.sqrt(HD)


def table_pair():
    table = feature_table()
    zero = jnp.zeros_like(table)
    both = jnp.concatenate(
        [jnp.concatenate([table, zero], 1), jnp.concatenate([zero, table], 1)], 0
    )
    high = lax.reduce_precision(both, 8, 7).astype(BF)
    return high, (both - high.astype(F32)).astype(BF)


def rotary_tables(place, tokens):
    half = ROT // 2
    positions = place * tokens + jnp.arange(tokens, dtype=jnp.int32)
    inv_freq = 10000.0 ** (-(2.0 * jnp.arange(half).astype(F32)) / ROT)
    angles = positions.astype(F32)[:, None] * inv_freq[None, :]
    cos, sin = jnp.cos(angles), jnp.sin(angles)
    rest = jnp.ones((tokens, HD - ROT), F32)
    none = jnp.zeros((tokens, half), F32)
    same = jnp.concatenate([cos, cos, rest], 1)
    down = jnp.concatenate([-sin, none, 0.0 * rest], 1)
    up = jnp.concatenate([none, sin, 0.0 * rest], 1)
    return tuple(jnp.concatenate([t, t], 1) for t in (same, down, up))


def dot(a, b, ca=1, cb=0):
    return lax.dot_general(a, b, (((ca,), (cb,)), ((), ())), preferred_element_type=F32)


def split_dot(a, b, cb=0):
    high = a.astype(BF)
    low = (a - high.astype(F32)).astype(BF)
    return dot(high, b, 1, cb) + dot(low, b, 1, cb)


def lane_masks(rows):
    low = lax.broadcasted_iota(jnp.int32, (rows, PAIR), 1) < HD
    first = low.astype(F32)
    return low, first.astype(BF), (1.0 - first).astype(BF)


def count_starts(starts_ref, row, position):
    total = jnp.int32(0)
    for n in range(NDOC):
        total = total + (starts_ref[row, n] <= position).astype(jnp.int32)
    return total


def seg_grid(starts_ref, row, base, shape, dim):
    position = base + lax.broadcasted_iota(jnp.int32, shape, dim)
    total = jnp.zeros(shape, jnp.int32)
    for n in range(NDOC):
        total = total + (starts_ref[row, n] <= position).astype(jnp.int32)
    return total


def causal_mask(starts_ref, row, base, tokens):
    shape = (tokens, tokens)
    same = seg_grid(starts_ref, row, base, shape, 0) == seg_grid(starts_ref, row, base, shape, 1)
    earlier = lax.broadcasted_iota(jnp.int32, shape, 1) <= lax.broadcasted_iota(
        jnp.int32, shape, 0
    )
    rows = lax.broadcasted_iota(jnp.int32, shape, 0) < tokens // 2
    cols = lax.broadcasted_iota(jnp.int32, shape, 1) < tokens // 2
    mask = same & earlier
    return mask.astype(F32), (mask & (rows == cols)).astype(F32)


def middle_state(starts_ref, row, base, tokens, k, v, state_in, total_in, low):
    half = tokens // 2
    end = count_starts(starts_ref, row, base + half - 1)
    passing = (end == count_starts(starts_ref, row, base - 1)).astype(F32)
    seg = seg_grid(starts_ref, row, base, (half, PAIR), 0)
    key = k[:half] * (seg == end).astype(F32).astype(BF)
    state = passing * state_in + compact(dot(key, v[:half], 0, 0), low)
    total = passing * total_in + jnp.sum(key.astype(F32), 0, keepdims=True)
    later = seg_grid(starts_ref, row, base + half, (half, PAIR), 0)
    return state.astype(BF), total, (later == end).astype(F32)


def entering_mask(starts_ref, row, base, tokens):
    seg = seg_grid(starts_ref, row, base, (tokens, PAIR), 0)
    return (seg == count_starts(starts_ref, row, base - 1)).astype(F32)


def leaving_mask(starts_ref, row, base, tokens):
    seg = seg_grid(starts_ref, row, base, (tokens, PAIR), 0)
    return (seg == count_starts(starts_ref, row, base + tokens - 1)).astype(F32)


def rotate(x, same, down, up):
    half = ROT // 2
    return x * same + pltpu.roll(x, PAIR - half, 1) * down + pltpu.roll(x, half, 1) * up


def rotate_back(x, same, down, up):
    half = ROT // 2
    return x * same + pltpu.roll(x * down, half, 1) + pltpu.roll(x * up, PAIR - half, 1)


def compact(state, low):
    return jnp.where(low[:HD], state[:HD], state[HD:])


def spread(state, first, second):
    return jnp.concatenate([state * first[:HD], state * second[:HD]], 0)


def keep_state(state_ref, row, product, summands, low):
    state_ref[row, 0, :HD] = compact(product, low)
    total = jnp.sum(summands, 0, keepdims=True)
    state_ref[row, 0, HD:] = jnp.broadcast_to(total, (HELD - HD, PAIR))


def features_kernel(
    starts_ref, place_ref, norm_ref, weight_ref, bias_ref, feat_ref,
    same_ref, down_ref, up_ref, high_ref, low_ref,
    q_ref, k_ref, v_ref, state_ref,
):
    tokens = same_ref.shape[0]
    base = place_ref[0, 0] * tokens
    low, first, second = lane_masks(tokens)
    feat = feat_ref[0]
    proj = dot(norm_ref[...], weight_ref[...]) + bias_ref[0]
    c0, c1, c2 = proj[:, :PAIR], proj[:, PAIR : 2 * PAIR], proj[:, 2 * PAIR :]
    left = lane_masks(proj.shape[0])[0]
    v_ref[...] = jnp.where(left, c1, c2).astype(BF)
    same, down, up = (
        jnp.concatenate([t[...]] * (MB * ROWS), 0) for t in (same_ref, down_ref, up_ref)
    )
    query, key = jnp.where(left, c0, c1), pltpu.roll(jnp.where(left, c2, c0), HD, 1)
    for x, out_ref in ((query, q_ref), (key, k_ref)):
        x = rotate(x, same, down, up)
        arg = split_dot(x, high_ref[...]) + dot(x.astype(BF), low_ref[...])
        out_ref[...] = (feat * jnp.exp(arg)).astype(BF)
    for row in range(MB * ROWS):
        here = slice(row * tokens, (row + 1) * tokens)
        leaving = leaving_mask(starts_ref, row, base, tokens)
        key_out = k_ref[here, :] * leaving.astype(BF)
        keep_state(state_ref, row, dot(key_out, v_ref[here, :], 0, 0), key_out.astype(F32), low)


def attend_kernel(
    starts_ref, place_ref, q_ref, k_ref, v_ref, state_ref, low_ref, out_ref, den_ref
):
    tokens = q_ref.shape[0] // (MB * ROWS)
    base = place_ref[0, 0] * tokens
    low, first, second = lane_masks(tokens)
    ones = head_ones()
    for row in range(MB * ROWS):
        here = slice(row * tokens, (row + 1) * tokens)
        q, k, v = q_ref[here, :], k_ref[here, :], v_ref[here, :]
        mask, mask_in = causal_mask(starts_ref, row, base, tokens)
        enter = entering_mask(starts_ref, row, base, tokens)
        carry, total = state_ref[row, 0, :HD], state_ref[row, 0, HD : HD + 1]
        state = carry.astype(BF)
        middle, _, reach = middle_state(starts_ref, row, base, tokens, k, v, carry, total, low)
        half = tokens // 2
        num = jnp.concatenate(
            [
                dot(q[:half] * enter[:half].astype(BF), spread(state, first, second)),
                dot(q[half:] * reach.astype(BF), spread(middle, first, second)),
            ],
            0,
        )
        for head in (first, second):
            scores = dot(q * head, k, 1, 1) * mask_in
            num = num + dot(scores.astype(BF), v * head)
        totals = dot(mask.astype(BF), k) + enter * total
        den = split_dot(q.astype(F32) * totals, ones)
        att = num / den
        low_ref[here, :] = att.astype(BF)
        out_ref[here, :] = att
        den_ref[here, :] = den


def head_ones():
    rows = lax.broadcasted_iota(jnp.int32, (PAIR, PAIR), 0) < HD
    cols = lax.broadcasted_iota(jnp.int32, (PAIR, PAIR), 1) < HD
    return (rows == cols).astype(F32).astype(BF)


def head_spread():
    rows = lax.broadcasted_iota(jnp.int32, (PAIR, 2 * PAIR), 0) < HD
    cols = lax.broadcasted_iota(jnp.int32, (PAIR, 2 * PAIR), 1) < PAIR
    return (rows == cols).astype(F32).astype(BF)


def back_state_kernel(
    starts_ref, place_ref, q_ref, ga_ref, att_ref, den_ref, state_ref
):
    tokens = q_ref.shape[0] // (MB * ROWS)
    base = place_ref[0, 0] * tokens
    low, first, second = lane_masks(tokens)
    ones = head_ones()
    for row in range(MB * ROWS):
        here = slice(row * tokens, (row + 1) * tokens)
        grad_num = (ga_ref[here, :].astype(F32) / den_ref[here, :]).astype(BF)
        grad_den = -split_dot(grad_num.astype(F32) * att_ref[here, :], ones)
        enter = entering_mask(starts_ref, row, base, tokens)
        query = q_ref[here, :] * enter.astype(BF)
        keep_state(state_ref, row, dot(query, grad_num, 0, 0), grad_den * query.astype(F32), low)


def back_unit(starts_ref, row, base, q, k, v, ga, att, den, held, later_held, tables):
    same, down, up, high, low_table = tables
    tokens = q.shape[0]
    half = tokens // 2
    low, first, second = lane_masks(tokens)
    grad_num = (ga.astype(F32) / den).astype(BF)
    both = -split_dot(grad_num.astype(F32) * att, head_spread())
    dens = (both[:, :PAIR], both[:, PAIR:])
    grad_den = jnp.where(low, dens[0], dens[1])
    mask, mask_in = causal_mask(starts_ref, row, base, tokens)
    enter = entering_mask(starts_ref, row, base, tokens)
    leave = leaving_mask(starts_ref, row, base, tokens)
    carry, total = held[:HD], held[HD : HD + 1]
    middle, middle_total, reach = middle_state(
        starts_ref, row, base, tokens, k, v, carry, total, low
    )
    state, middle = spread(carry.astype(BF), first, second), spread(middle, first, second)
    gq = jnp.concatenate(
        [
            enter[:half] * (dot(grad_num[:half], state, 1, 1) + grad_den[:half] * total),
            reach * (dot(grad_num[half:], middle, 1, 1) + grad_den[half:] * middle_total),
        ],
        0,
    )
    later = later_held[:HD]
    later_high = later.astype(BF)
    later_low = spread((later - later_high.astype(F32)).astype(BF), first, second)
    later_high = spread(later_high, first, second)
    gk = leave * (
        dot(v, later_high, 1, 1) + dot(v, later_low, 1, 1) + later_held[HD : HD + 1]
    )
    gv = leave * (dot(k, later_high) + dot(k, later_low))
    for head, grad_head_den in zip((first, second), dens):
        q_head, grad_head = q * head, grad_num * head
        scores = (dot(q_head, k, 1, 1) * mask).astype(BF)
        grad_scores = dot(grad_head, v, 1, 1) + grad_head_den
        gq = gq + dot((grad_scores * mask_in).astype(BF), k * head)
        gk = gk + dot((grad_scores * mask).astype(BF), q_head, 0, 0)
        gv = gv + dot(scores, grad_head, 0, 0)
    arg_grads = (gq * q.astype(F32), gk * k.astype(F32))
    feat_sum = jnp.sum(arg_grads[0] + arg_grads[1], 0, keepdims=True)
    turned = []
    for x in arg_grads:
        x = split_dot(x, high, 1) + dot(x.astype(BF), low_table, 1, 1)
        turned.append(rotate_back(x, same, down, up))
    dq, dk = turned[0], pltpu.roll(turned[1], HD, 1)
    parts = (jnp.where(low, dq, dk), jnp.where(low, gv, dq), jnp.where(low, dk, gv))
    return tuple(part.astype(BF) for part in parts), feat_sum


def back_kernel(
    starts_ref, place_ref, q_ref, k_ref, v_ref, ga_ref, att_ref, den_ref,
    state_ref, later_ref, feat_ref,
    same_ref, down_ref, up_ref, high_ref, low_ref,
    grad_ref, sums_ref,
):
    tokens = q_ref.shape[0] // (MB * ROWS)
    base = place_ref[0, 0] * tokens
    tables = tuple(t[...] for t in (same_ref, down_ref, up_ref, high_ref, low_ref))
    sums_ref[...] = jnp.zeros_like(sums_ref)
    for row in range(MB * ROWS):
        here = slice(row * tokens, (row + 1) * tokens)
        values = [r[here, :] for r in (q_ref, k_ref, v_ref, ga_ref, att_ref, den_ref)]
        parts, feat_sum = back_unit(
            starts_ref, row, base, *values, state_ref[row, 0], later_ref[row, 0], tables
        )
        sums_ref[0, 0:1, :] += feat_sum / feat_ref[0]
        for n, part in enumerate(parts):
            grad_ref[here, n * PAIR : (n + 1) * PAIR] = part
            sums_ref[0, n + 1 : n + 2, :] += jnp.sum(part.astype(F32), 0, keepdims=True)


SMEM = pl.BlockSpec(memory_space=pltpu.SMEM)


def whole(shape):
    return pl.BlockSpec(shape, lambda p: (0,) * len(shape))


def column(rows, width):
    return pl.BlockSpec((rows, width), lambda p: (0, p))


def stacked(*shape):
    return pl.BlockSpec((1,) + shape, lambda p: (p,) + (0,) * len(shape))


def call(kernel, pairs, in_specs, out_specs, out_shape, flops):
    return pl.pallas_call(
        kernel,
        grid=(pairs,),
        in_specs=in_specs,
        out_specs=out_specs,
        out_shape=out_shape,
        compiler_params=pltpu.CompilerParams(vmem_limit_bytes=VMEM_LIMIT),
        cost_estimate=pl.CostEstimate(flops=flops, bytes_accessed=8 << 20, transcendentals=0),
    )


def shaped(shape, dtype):
    return jax.ShapeDtypeStruct(shape, dtype)


CHUNK = 256
PANEL = 512
RING = 4
LAG = 7


def last_kernel(plan, *refs):
    count, terms = plan
    (
        starts_ref, hidden_ref, dy_ref, low_ref, second_any, first_any,
        q_ref, k_ref, v_ref, ga_ref, att_ref, den_ref, state_ref, own_ref, feat_ref,
        same_ref, down_ref, up_ref, high_table_ref, low_table_ref,
        qkv_any, xhat_any, inv_ref, gain_ref, pre_any, w_down_any, w_up_any, small_in_ref,
    ) = refs[:28]
    outs, du_ref = refs[28:33], refs[33]
    (
        proj, small_ref, away_buf, come_buf, norm_sum, norm_away, norm_come,
        sum_send, sum_recv, norm_sem,
        work, give, take, outside, inside,
        give_send, give_recv, part_send, outer_recv, inner_recv, total_send,
        final_send, final_recv, own_sem,
        second_ref, first_ref, qkv_ref, xhat_ref, load_sem,
        grad_pre_ref, grad_second_ref, later_ref, pre_ring, down_ring, up_ring,
        pre_sem, down_sem, up_sem, *link_bufs,
    ) = refs[34:]
    part = give
    later_loads = [
        pltpu.make_async_copy(source, buffer, load_sem.at[n])
        for n, (source, buffer) in enumerate(
            (
                (second_any, second_ref), (first_any, first_ref), (qkv_any, qkv_ref),
                (xhat_any, xhat_ref),
            )
        )
    ]
    factors = (
        hidden_ref, dy_ref, low_ref, dy_ref, second_ref, grad_pre_ref, first_ref, proj
    )
    rows, pairs = state_ref.shape[:2]
    tokens, width = q_ref.shape[0] // rows, du_ref.shape[1]
    units = rows * pairs
    tp = lax.axis_index("tp")
    my_cols = pl.ds(pl.multiple_of(tp * width, width), width)
    half = CHUNK // 2
    place, peers = lax.axis_index("ctx"), lax.axis_size("ctx")
    core, z, chips = place % 2, place // 2, peers // 2
    below = z < chips // 2
    middle = (z == chips // 2 - 1) | (z == chips // 2)
    has_outer = (z != 0) & (z != chips - 1)
    step = jnp.where(below, 2, -2)
    inner, outer, twin = place + step, place - step, place + 1 - 2 * core
    mine = pl.ds(pl.multiple_of(core * half, half), half)
    theirs = pl.ds(pl.multiple_of((1 - core) * half, half), half)

    def remote(src, dst, send, recv, to):
        return pltpu.make_async_remote_copy(
            src_ref=src, dst_ref=dst, send_sem=send, recv_sem=recv,
            device_id={"ctx": to}, device_id_type=pl.DeviceIdType.MESH,
        )

    def to_tp(src, dst, send, recv):
        return pltpu.make_async_remote_copy(
            src_ref=src, dst_ref=dst, send_sem=send, recv_sem=recv,
            device_id={"tp": 1 - tp}, device_id_type=pl.DeviceIdType.MESH,
        )

    def sum_copy(m):
        return to_tp(away_buf.at[m], come_buf.at[m], sum_send.at[m], sum_recv.at[m])

    def norm_copy():
        return to_tp(norm_away, norm_come, norm_sem.at[0], norm_sem.at[1])

    def split_cols(x):
        left, right = x[:, :width], x[:, width:]
        return jnp.where(tp == 0, left, right), jnp.where(tp == 0, right, left)

    def row_block(m):
        return pl.ds(pl.multiple_of(m * tokens, tokens), tokens)

    downs, ups = w_down_any.shape[0] // TILE, w_up_any.shape[0] // TILE
    begin_link, advance, finish_link, _ = exchange(
        False, starts_ref, own_ref, later_ref, link_bufs, tokens, 1, False
    )

    def down_copies(n):
        return (
            pltpu.make_async_copy(w_down_any.at[tile(n)], down_ring.at[n % 2], down_sem.at[n % 2]),
            pltpu.make_async_copy(pre_any.at[:, tile(n)], pre_ring.at[n % 2], pre_sem.at[n % 2]),
        )

    def up_copy(n):
        return pltpu.make_async_copy(w_up_any.at[tile(n)], up_ring.at[n % 2], up_sem.at[n % 2])

    def down_step(n):
        for copy in down_copies(n):
            copy.wait()
        pre = pre_ring[n % 2]
        grad = dot(dy_ref[...], down_ring[n % 2], 1, 1)
        cdf = 0.5 * (1.0 + lax.erf(pre * math.sqrt(0.5)))
        slope = cdf + pre * jnp.exp(-0.5 * pre * pre) * (1.0 / math.sqrt(2.0 * math.pi))
        grad = (grad * slope).astype(BF)
        grad_pre_ref[:, tile(n)] = grad
        per_row = PANEL // TILE
        line = (lax.broadcasted_iota(jnp.int32, (8, TILE), 0) == n // per_row).astype(F32)
        cols = pl.ds(pl.multiple_of(n % per_row * TILE, TILE), TILE)
        small_ref[8:16, cols] += line * jnp.sum(grad.astype(F32), 0, keepdims=True)

        @pl.when(n + 2 < downs)
        def _():
            for copy in down_copies(n + 2):
                copy.start()

    def up_step(n):
        up_copy(n).wait()
        grad_second_ref[:, tile(n)] = dot(grad_pre_ref[...], up_ring[n % 2], 1, 1)

        @pl.when(n + 2 < ups)
        def _():
            up_copy(n + 2).start()

    def attention_step(i):
        p, row = i // rows, i % rows
        here, cols = row_block(row), pl.ds(pl.multiple_of(p * PAIR, PAIR), PAIR)
        tables = tuple(
            t[...] for t in (same_ref, down_ref, up_ref, high_table_ref, low_table_ref)
        )
        values = [r[here, cols] for r in (q_ref, k_ref, v_ref, ga_ref, att_ref, den_ref)]
        parts, feat_sum = back_unit(
            starts_ref, row, place * tokens, *values, state_ref[row, p], later_ref[row, p], tables
        )
        line = (lax.broadcasted_iota(jnp.int32, (8, PAIR), 0) == p).astype(F32)
        small_ref[:8, 3 * PAIR : 4 * PAIR] += line * (feat_sum / feat_ref[p])
        for n, piece in enumerate(parts):
            proj[here, pl.ds(pl.multiple_of((3 * p + n) * PAIR, PAIR), PAIR)] = piece
            small_ref[:8, n * PAIR : (n + 1) * PAIR] += line * jnp.sum(
                piece.astype(F32), 0, keepdims=True
            )

    def norm_step(m):
        here = row_block(m)
        one, two, xhat = dot(proj[here, :], qkv_ref[...], 1, 1), grad_second_ref[here, :], xhat_ref[here, :]
        for n, x in enumerate((one * xhat, two * xhat, one, two)):
            norm_sum[n : n + 1, :] += jnp.sum(x, 0, keepdims=True)
        both = one * gain_ref[0:1, :] + two * gain_ref[1:2, :]
        leaving = inv_ref[here, :] * (
            both
            - jnp.mean(both, -1, keepdims=True)
            - xhat * jnp.mean(both * xhat, -1, keepdims=True)
        )
        kept, sent = split_cols(leaving)
        away_buf[m] = sent.astype(BF)
        sum_copy(m).start()
        du_ref[here, :] = kept + dy_ref[here, my_cols].astype(F32)

    def other_work(step):
        @pl.when(step < downs)
        def _():
            down_step(step)

        @pl.when((step >= downs) & (step < downs + ups))
        def _():
            up_step(step - downs)

        advance(step)
        i = step - downs - ups

        @pl.when(i == 0)
        def _():
            finish_link()

        @pl.when((i >= 0) & (i < units))
        def _():
            attention_step(i)

        @pl.when((i >= units) & (i < units + rows))
        def _():
            norm_step(i - units)

        @pl.when(i == units + rows)
        def _():
            kept, sent = split_cols(norm_sum[...])
            norm_away[...] = sent
            norm_copy().start()
            small_ref[16:24, :] = kept

        late = i - (units + rows + 3)

        @pl.when((late >= 0) & (late < rows))
        def _():
            sum_copy(late).wait()
            du_ref[row_block(late), :] += come_buf[late].astype(F32)

        @pl.when(late == rows)
        def _():
            norm_copy().wait()
            small_ref[16:24, :] += norm_come[...]

    def give_copy(t):
        return remote(give.at[t], take.at[t], give_send.at[t], give_recv.at[t], twin)

    def to_outside(t):
        return remote(part.at[t], outside.at[t], part_send.at[t], outer_recv.at[t], inner)

    def across(t):
        return remote(part.at[t], inside.at[t], part_send.at[t], inner_recv.at[t], inner)

    def outward(t):
        return remote(take.at[t], inside.at[t], total_send.at[t], inner_recv.at[t], outer)

    def final_copy(t, target):
        return remote(take.at[t], target, final_send.at[t], final_recv.at[t], twin)

    def own_copy(t, target):
        return pltpu.make_async_copy(take.at[t], target, own_sem.at[t])

    def block_of(j, panels):
        rows = (j // panels) * CHUNK
        return rows, pl.ds(pl.multiple_of((j % panels) * PANEL, PANEL), PANEL)

    def deliver(t, target):
        final_copy(t, target).start()
        own_copy(t, target).start()

    some_target = outs[-1].at[mine]

    barrier = pltpu.get_barrier_semaphore()
    for peer in ({"ctx": inner}, {"ctx": twin}, {"tp": 1 - tp}):
        pl.semaphore_signal(barrier, inc=1, device_id=peer, device_id_type=pl.DeviceIdType.MESH)

    @pl.when(has_outer)
    def _():
        pl.semaphore_signal(
            barrier, inc=1, device_id={"ctx": outer}, device_id_type=pl.DeviceIdType.MESH
        )

    pl.semaphore_wait(barrier, 3 + has_outer.astype(jnp.int32))
    begin_link()
    for n in range(2):
        for copy in down_copies(n):
            copy.start()
        up_copy(n).start()
    for copy in later_loads:
        copy.start()
    small_ref[...] = jnp.zeros_like(small_ref)
    small_ref[8:16, :] = small_in_ref[...]
    norm_sum[...] = jnp.zeros_like(norm_sum)
    lag = jnp.where(middle, 3, LAG)

    def one(t, carry):
        slot = t % RING
        begin = 0

        @pl.when(t == downs)
        def _():
            for copy in later_loads:
                copy.wait()

        for n, (blocks, panels) in enumerate(terms):
            left, right = factors[2 * n], factors[2 * n + 1]

            @pl.when((t >= begin) & (t < begin + blocks * panels))
            def _(left=left, right=right, panels=panels, begin=begin):
                start, cols = block_of(t - begin, panels)
                rows = pl.ds(pl.multiple_of(start, CHUNK), CHUNK)
                work[slot] = dot(left[:, rows], right[:, cols], 0, 0)

            begin += blocks * panels

        @pl.when(t == begin)
        def _():
            work[slot] = small_ref[...]

        @pl.when(t < count)
        def _():
            give[t] = work[slot, theirs, :].astype(BF)
            give_copy(t).start()

        tb = t - 2

        @pl.when((tb >= 0) & (tb < count))
        def _():
            give_copy(tb).wait()
            total = work[(t + RING - 2) % RING, mine, :] + take[tb].astype(F32)

            @pl.when(has_outer)
            def _():
                to_outside(tb).wait_recv()
                part[tb] = (total + outside[tb].astype(F32)).astype(BF)

            @pl.when(jnp.logical_not(has_outer))
            def _():
                part[tb] = total.astype(BF)

            @pl.when(middle)
            def _():
                across(tb).start()

            @pl.when(jnp.logical_not(middle))
            def _():
                to_outside(tb).start()

        tc = t - lag

        @pl.when((tc >= 0) & (tc < count))
        def _():
            across(tc).wait_recv()

            @pl.when(middle)
            def _():
                take[tc] = (part[tc].astype(F32) + inside[tc].astype(F32)).astype(BF)

            @pl.when(jnp.logical_not(middle))
            def _():
                take[tc] = inside[tc]

            @pl.when(has_outer)
            def _():
                outward(tc).start()

            begin = 0
            for n, (blocks, panels) in enumerate(terms):

                @pl.when((tc >= begin) & (tc < begin + blocks * panels))
                def _(n=n, panels=panels, begin=begin):
                    start, cols = block_of(tc - begin, panels)
                    rows = pl.ds(pl.multiple_of(start + core * half, half), half)
                    deliver(tc, outs[n].at[rows, cols])

                begin += blocks * panels

            @pl.when(tc == begin)
            def _():
                deliver(tc, some_target)

        other_work(t)
        return carry

    lax.fori_loop(0, count + LAG, one, 0)

    def drain(t, carry):
        across(t).wait_send()
        final_copy(t, some_target).wait_send()
        final_copy(t, some_target).wait_recv()
        own_copy(t, some_target).wait()

        @pl.when(has_outer)
        def _():
            outward(t).wait_send()

        return carry

    lax.fori_loop(0, count, drain, 0)


def last_call(starts, factors, attention, norms, feed, small):
    second, first = factors[4:]
    own, qkv = attention[7], norms[0]
    pre, w_down, w_up = feed
    total, width = first.shape[0], D // 2
    rows, tokens = MB * ROWS, total // (MB * ROWS)
    shapes = [
        (factors[0].shape[1], D), (factors[3].shape[1], D), (D, pre.shape[1]), (D, qkv.shape[1])
    ]
    terms = tuple((x // CHUNK, y // PANEL) for x, y in shapes)
    count = sum(x * y for x, y in terms) + 1
    slots = pltpu.VMEM((count, CHUNK // 2, PANEL), BF)
    flat = [factors[0], factors[1], factors[3], second, first]
    flat = flat + list(attention) + list(norms) + list(feed) + [small]
    later = [n for n, x in enumerate(flat) if any(x is y for y in (second, first, qkv, norms[1]))]
    outside = later + [n for n, x in enumerate(flat) if any(x is y for y in feed)]
    dma = pltpu.SemaphoreType.DMA
    *sums, du = pl.pallas_call(
        partial(last_kernel, (count, terms)),
        in_specs=[SMEM] + [ANYWHERE if n in outside else IN_VMEM for n in range(len(flat))],
        out_specs=[ANYWHERE] * 5 + [IN_VMEM],
        out_shape=[shaped(x, BF) for x in shapes]
        + [shaped((CHUNK, PANEL), BF), shaped((total, width), F32)],
        scratch_shapes=[
            pltpu.VMEM((total, qkv.shape[1]), BF),
            pltpu.VMEM((CHUNK, PANEL), F32),
            pltpu.VMEM((rows, tokens, width), BF),
            pltpu.VMEM((rows, tokens, width), BF),
            pltpu.VMEM((8, D), F32),
            pltpu.VMEM((8, width), F32),
            pltpu.VMEM((8, width), F32),
            dma((rows,)), dma((rows,)), dma((2,)),
            pltpu.VMEM((RING, CHUNK, PANEL), F32),
        ]
        + [slots] * 4
        + [dma((count,))] * 9
        + [pltpu.VMEM(flat[n].shape, flat[n].dtype) for n in later]
        + [dma((len(later),))]
        + [
            pltpu.VMEM(pre.shape, BF), pltpu.VMEM((total, D), F32), pltpu.VMEM(own.shape, F32),
            pltpu.VMEM((2, total, TILE), F32), pltpu.VMEM((2, TILE, D), BF),
            pltpu.VMEM((2, TILE, w_up.shape[1]), BF),
            dma((2,)), dma((2,)), dma((2,)),
        ]
        + exchange_scratch(rows, own.shape[1]),
        compiler_params=pltpu.CompilerParams(
            collective_id=0, has_side_effects=True, vmem_limit_bytes=REDUCE_LIMIT
        ),
        cost_estimate=pl.CostEstimate(
            flops=count * 2 * CHUNK * PANEL * 512, bytes_accessed=40 << 20, transcendentals=0
        ),
    )(starts, *flat)
    return [g.astype(F32) for g in sums[:-1]], sums[-1].astype(F32), du


def fits_last(units, qkv, pairs):
    sizes = [(units, D), (pairs * PAIR, D), (D, units), qkv.shape]
    even = all(x % CHUNK == 0 and y % PANEL == 0 for x, y in sizes)
    chunks = [x // CHUNK * (y // PANEL) for x, y in sizes]
    ahead = sum(chunks[:-1])
    rows, chips = MB * ROWS, lax.axis_size("ctx") // 2
    feed = units // TILE + D // TILE
    line = chips % 2 == 0 and lax.axis_size("tp") == 2 and pairs % 2 == 0 and pairs <= 8
    fits = feed + rows * pairs <= ahead and feed + rows * (pairs + 2) + 3 < sum(chunks)
    return even and line and fits and chips + 4 <= feed and units < 8 * PANEL


def exchange(forward, starts_ref, own_ref, got_ref, bufs, tokens, hop=HOP, greeting=True):
    (twin_buf, in_buf, out_buf, back_buf, twin_sem, send_sem, recv_sem, back_send, back_recv) = bufs
    rows, pairs = own_ref.shape[:2]
    part = rows // 2
    chunks, width = in_buf.shape[:2]
    split = pairs // width
    place, chips = lax.axis_index("ctx"), lax.axis_size("ctx") // 2
    core, z = place % 2, place // 2
    away = z if forward else chips - 1 - z
    first, last = away == 0, away == chips - 1
    step = 2 if forward else -2
    twin = place + 1 - 2 * core
    leads = core == (0 if forward else 1)
    lead = 2 * z + (0 if forward else 1)
    other = 2 * z + (1 if forward else 0)

    def remote(src, dst, send, recv, to):
        return pltpu.make_async_remote_copy(
            src_ref=src, dst_ref=dst, send_sem=send, recv_sem=recv,
            device_id={"ctx": to}, device_id_type=pl.DeviceIdType.MESH,
        )

    def twin_copy():
        theirs = own_ref.at[pl.ds((1 - core) * part, part)]
        return remote(theirs, twin_buf, twin_sem.at[0], twin_sem.at[1], twin)

    def onward(j):
        return remote(out_buf.at[j], in_buf.at[j], send_sem.at[j], recv_sem.at[j], place + step)

    def where_of(j):
        return core * part + j // split, pl.ds((j % split) * width, width)

    def back(j):
        row, cols = where_of(j)
        return remote(back_buf.at[j], got_ref.at[row, cols], back_send.at[j], back_recv.at[j], twin)

    def passing(row, at):
        end = count_starts(starts_ref, row, at * tokens + tokens - 1)
        return (end == count_starts(starts_ref, row, at * tokens - 1)).astype(F32)

    def begin():
        if not greeting:
            twin_copy().start()
            return
        barrier = pltpu.get_barrier_semaphore()

        def greet(peer):
            pl.semaphore_signal(
                barrier, inc=1, device_id={"ctx": peer}, device_id_type=pl.DeviceIdType.MESH
            )

        greet(twin)

        @pl.when(jnp.logical_not(first))
        def _():
            greet(place - step)

        pl.semaphore_wait(barrier, 2 - last.astype(jnp.int32))
        twin_copy().start()

    def advance(i):
        @pl.when(i == 0)
        def _():
            twin_copy().wait_recv()

        j = i - hop * away

        @pl.when((j >= 0) & (j < chunks))
        def _():
            row, cols = where_of(j)

            @pl.when(first)
            def _():
                in_buf[j] = jnp.zeros(in_buf.shape[1:], F32)

            @pl.when(jnp.logical_not(first))
            def _():
                onward(j).wait_recv()

            mine, theirs = own_ref[row, cols], twin_buf[j // split, cols]
            entering_lead = in_buf[j]
            entering_other = jnp.where(leads, mine, theirs) + passing(row, lead) * entering_lead

            @pl.when(jnp.logical_not(last))
            def _():
                out_buf[j] = (
                    jnp.where(leads, theirs, mine) + passing(row, other) * entering_other
                )
                onward(j).start()

            got_ref[row, cols] = jnp.where(leads, entering_lead, entering_other)
            back_buf[j] = jnp.where(leads, entering_other, entering_lead)
            back(j).start()

    def finish():
        twin_copy().wait_send()

        def one(j, carry):
            back(j).wait_send()
            back(j).wait_recv()

            @pl.when(jnp.logical_not(last))
            def _():
                onward(j).wait_send()

            return carry

        lax.fori_loop(0, chunks, one, 0)

    return begin, advance, finish, (chips - 1) * hop + chunks


def exchange_scratch(rows, pairs):
    width = pairs // 2 if pairs % 2 == 0 else pairs
    chunks = rows // 2 * (pairs // width)
    one = pltpu.VMEM((chunks, width, HELD, PAIR), F32)
    return [
        pltpu.VMEM((rows // 2, pairs, HELD, PAIR), F32), one, one, one,
        pltpu.SemaphoreType.DMA((2,)),
    ] + [pltpu.SemaphoreType.DMA((chunks,))] * 4


def tile(n):
    return pl.ds(pl.multiple_of(n * TILE, TILE), TILE)


def run_tiles(first_count, first_body, second_count, second_body, loads, link):
    begin, advance, finish, steps = link
    for _, copy in loads[:-1]:
        copy(0).start()
    begin()
    for n, (count, copy) in enumerate(loads):
        start_all(0 if n == len(loads) - 1 else 1, count, copy)
    both = first_count + second_count

    def one(i, carry):
        @pl.when(i < first_count)
        def _():
            first_body(i)

        @pl.when((i >= first_count) & (i < both))
        def _():
            second_body(i - first_count)

        advance(i)
        return carry

    lax.fori_loop(0, max(both, steps), one, 0)
    finish()


def start_all(begin, count, copy):
    def one(n, carry):
        copy(n).start()
        return carry

    lax.fori_loop(begin, count, one, 0)


def feed_forward_kernel(
    tokens, starts_ref, own_ref, norm_ref, up_ref, bias_ref, down_ref,
    pre_ref, hidden_ref, mlp_ref, got_ref,
    up_buf, down_buf, up_sem, down_sem, *bufs,
):
    ups, downs = up_ref.shape[1] // TILE, down_ref.shape[1] // TILE

    def up_copy(n):
        return pltpu.make_async_copy(up_ref.at[:, tile(n)], up_buf.at[:, tile(n)], up_sem.at[n])

    def down_copy(n):
        return pltpu.make_async_copy(
            down_ref.at[:, tile(n)], down_buf.at[:, tile(n)], down_sem.at[n]
        )

    loads = ((ups, up_copy), (downs, down_copy))

    def up(n):
        up_copy(n).wait()
        pre = dot(norm_ref[...], up_buf[:, tile(n)]) + bias_ref[:, tile(n)]
        pre_ref[:, tile(n)] = pre
        hidden = 0.5 * pre * (1.0 + lax.erf(pre * math.sqrt(0.5)))
        hidden_ref[:, tile(n)] = hidden.astype(BF)

    def down(n):
        down_copy(n).wait()
        mlp_ref[:, tile(n)] = dot(hidden_ref[...], down_buf[:, tile(n)])

    link = exchange(True, starts_ref, own_ref, got_ref, bufs, tokens)
    run_tiles(ups, up, downs, down, loads, link)


def feed_backward_kernel(
    tokens, starts_ref, own_ref, grad_ref, pre_ref, down_ref, up_ref,
    grad_pre_ref, grad_norm_ref, got_ref,
    pre_buf, down_buf, up_buf, pre_sem, down_sem, up_sem, *bufs,
):
    downs, ups = down_ref.shape[0] // TILE, up_ref.shape[0] // TILE

    def pre_copy(n):
        return pltpu.make_async_copy(pre_ref.at[:, tile(n)], pre_buf.at[:, tile(n)], pre_sem.at[n])

    def down_copy(n):
        return pltpu.make_async_copy(down_ref.at[tile(n)], down_buf.at[tile(n)], down_sem.at[n])

    def up_copy(n):
        return pltpu.make_async_copy(up_ref.at[tile(n)], up_buf.at[tile(n)], up_sem.at[n])

    loads = ((downs, down_copy), (downs, pre_copy), (ups, up_copy))

    def down(n):
        down_copy(n).wait()
        pre_copy(n).wait()
        grad = dot(grad_ref[...], down_buf[tile(n), :], 1, 1)
        pre = pre_buf[:, tile(n)]
        cdf = 0.5 * (1.0 + lax.erf(pre * math.sqrt(0.5)))
        slope = cdf + pre * jnp.exp(-0.5 * pre * pre) * (1.0 / math.sqrt(2.0 * math.pi))
        grad_pre_ref[:, tile(n)] = (grad * slope).astype(BF)

    def up(n):
        up_copy(n).wait()
        grad_norm_ref[:, tile(n)] = dot(grad_pre_ref[...], up_buf[tile(n), :], 1, 1)

    link = exchange(False, starts_ref, own_ref, got_ref, bufs, tokens)
    run_tiles(downs, down, ups, up, loads, link)


IN_VMEM = pl.BlockSpec(memory_space=pltpu.VMEM)
ANYWHERE = pl.BlockSpec(memory_space=pl.ANY)


def link_call(kernel, number, in_specs, out_shape, scratch, flops):
    return pl.pallas_call(
        kernel,
        in_specs=in_specs,
        out_specs=[IN_VMEM] * len(out_shape),
        out_shape=out_shape,
        scratch_shapes=scratch,
        compiler_params=pltpu.CompilerParams(
            collective_id=number, has_side_effects=True, vmem_limit_bytes=VMEM_LIMIT
        ),
        cost_estimate=pl.CostEstimate(flops=flops, bytes_accessed=16 << 20, transcendentals=0),
    )


def feed_forward(starts, state, norm, w_up, b_up, w_down):
    total, units = norm.shape[0], w_up.shape[1]
    rows, pairs = state.shape[:2]
    return link_call(
        partial(feed_forward_kernel, total // rows),
        1,
        [SMEM, IN_VMEM, IN_VMEM, ANYWHERE, IN_VMEM, ANYWHERE],
        [
            shaped((total, units), F32), shaped((total, units), BF), shaped((total, D), F32),
            shaped(state.shape, F32),
        ],
        [
            pltpu.VMEM(w_up.shape, BF), pltpu.VMEM(w_down.shape, BF),
            pltpu.SemaphoreType.DMA((units // TILE,)), pltpu.SemaphoreType.DMA((D // TILE,)),
        ]
        + exchange_scratch(rows, pairs),
        4 * total * units * D,
    )(starts, state, norm, w_up, b_up.reshape(1, units), w_down)


def feed_backward(starts, state, grad, pre, w_down, w_up):
    total, units = pre.shape
    rows, pairs = state.shape[:2]
    return link_call(
        partial(feed_backward_kernel, total // rows),
        2,
        [SMEM, IN_VMEM, IN_VMEM, ANYWHERE, ANYWHERE, ANYWHERE],
        [shaped((total, units), BF), shaped((total, D), F32), shaped(state.shape, F32)],
        [
            pltpu.VMEM(pre.shape, F32), pltpu.VMEM(w_down.shape, BF), pltpu.VMEM(w_up.shape, BF),
            pltpu.SemaphoreType.DMA((units // TILE,)), pltpu.SemaphoreType.DMA((units // TILE,)),
            pltpu.SemaphoreType.DMA((D // TILE,)),
        ]
        + exchange_scratch(rows, pairs),
        4 * total * units * D,
    )(starts, state, grad, pre, w_down, w_up)


STEPS = 8


def hand_over_kernel(sender, part_ref, base_ref, full_ref, out_ref, *bufs):
    (
        away_buf, sum_buf, pass_buf,
        sum_send, sum_recv, pass_send, pass_recv, spread_send, spread_recv,
    ) = bufs
    width = base_ref.shape[1]
    height = base_ref.shape[0] // STEPS
    pipe, tp = lax.axis_index("pipe"), lax.axis_index("tp")
    sends = pipe == sender
    own = pl.ds(pl.multiple_of(tp * width, width), width)
    away = pl.ds(pl.multiple_of((1 - tp) * width, width), width)

    def rows(c):
        return slice(c * height, (c + 1) * height)

    def remote(src, dst, send, recv, to):
        return pltpu.make_async_remote_copy(
            src_ref=src, dst_ref=dst, send_sem=send, recv_sem=recv,
            device_id=to, device_id_type=pl.DeviceIdType.MESH,
        )

    def sum_copy(c):
        return remote(away_buf.at[c], sum_buf.at[c], sum_send.at[c], sum_recv.at[c], {"tp": 1 - tp})

    def pass_copy(c):
        target = out_ref.at[rows(c), own]
        return remote(pass_buf.at[c], target, pass_send.at[c], pass_recv.at[c], {"pipe": 1 - pipe})

    def spread_copy(c):
        piece = out_ref.at[rows(c), own]
        return remote(piece, piece, spread_send.at[c], spread_recv.at[c], {"tp": 1 - tp})

    barrier = pltpu.get_barrier_semaphore()

    def greet(to):
        pl.semaphore_signal(barrier, inc=1, device_id=to, device_id_type=pl.DeviceIdType.MESH)

    greet({"tp": 1 - tp})

    @pl.when(jnp.logical_not(sends))
    def _():
        greet({"pipe": 1 - pipe})

    pl.semaphore_wait(barrier, 1 + sends.astype(jnp.int32))

    @pl.when(sends)
    def _():
        for c in range(STEPS):
            away_buf[c] = part_ref[rows(c), away].astype(BF)
            sum_copy(c).start()
        for c in range(STEPS):
            out_ref[rows(c), :] = full_ref[rows(c), :]
            sum_copy(c).wait_recv()
            total = part_ref[rows(c), own] + sum_buf[c].astype(F32) + base_ref[rows(c), :]
            pass_buf[c] = total.astype(BF)
            pass_copy(c).start()
        for c in range(STEPS):
            sum_copy(c).wait_send()
            pass_copy(c).wait_send()

    @pl.when(jnp.logical_not(sends))
    def _():
        for c in range(STEPS):
            pass_copy(c).wait_recv()
            spread_copy(c).start()
        for c in range(STEPS):
            spread_copy(c).wait_send()
            spread_copy(c).wait_recv()


def hand_over(sender, part, base, full):
    total, width = base.shape
    piece = pltpu.VMEM((STEPS, total // STEPS, width), BF)
    return pl.pallas_call(
        partial(hand_over_kernel, sender),
        in_specs=[IN_VMEM] * 3,
        out_specs=IN_VMEM,
        out_shape=shaped(full.shape, BF),
        scratch_shapes=[piece] * 3 + [pltpu.SemaphoreType.DMA((STEPS,))] * 6,
        compiler_params=pltpu.CompilerParams(
            collective_id=3 + sender, has_side_effects=True, vmem_limit_bytes=VMEM_LIMIT
        ),
        cost_estimate=pl.CostEstimate(flops=1 << 20, bytes_accessed=8 << 20, transcendentals=0),
    )(part, base, full)


def gather_tp(value):
    if lax.axis_size("tp") != 2:
        return lax.all_gather(value, "tp", axis=1, tiled=True)
    other = lax.ppermute(value, "tp", [(0, 1), (1, 0)])
    return jnp.where(
        lax.axis_index("tp") == 0,
        jnp.concatenate([value, other], 1),
        jnp.concatenate([other, value], 1),
    )


def scatter_tp(value):
    peers = lax.axis_size("tp")
    if peers != 2:
        return lax.psum_scatter(value, "tp", scatter_dimension=1, tiled=True)
    me = lax.axis_index("tp")
    width = value.shape[1] // 2
    left, right = value[:, :width], value[:, width:]
    other = lax.ppermute(jnp.where(me == 0, right, left).astype(BF), "tp", [(0, 1), (1, 0)])
    return jnp.where(me == 0, left, right) + other.astype(F32)


def local(
    section_inputs,
    doc_starts,
    ln_gains,
    ln_shifts,
    qkv_weight,
    qkv_bias,
    feature_weight,
    dense_weight,
    out_bias,
    up_weight,
    up_bias,
    down_weight,
):
    section = lax.axis_index("pipe")
    place = lax.axis_index("ctx")
    width = section_inputs.shape[-1]
    tokens = section_inputs.shape[3]
    rows = MB * ROWS
    total = rows * tokens
    heads = feature_weight.shape[1]
    pairs = heads // 2
    gain, shift = ln_gains[0], ln_shifts[0]
    w_qkv, w_dense, w_up, w_down = qkv_weight[0], dense_weight[0], up_weight[0], down_weight[0]
    b_qkv = qkv_bias[0].reshape(pairs, 1, 3 * PAIR)
    b_up, b_out = up_bias[0], out_bias[0]
    feat = feature_weight[0].reshape(pairs, 1, PAIR)
    starts = doc_starts.reshape(rows, NDOC)
    place_in = place.astype(jnp.int32).reshape(1, 1)
    high, low = table_pair()
    same, down, up = rotary_tables(place, tokens)
    tables = (same, down, up, high, low)
    table_specs = [whole((tokens, PAIR))] * 3 + [whole((PAIR, PAIR))] * 2
    state_shape = shaped((rows, pairs, HELD, PAIR), F32)
    state_spec = pl.BlockSpec((rows, 1, HELD, PAIR), lambda p: (0, p, 0, 0))
    low_shape, full_shape = shaped((total, pairs * PAIR), BF), shaped((total, pairs * PAIR), F32)
    unit = 2 * rows * tokens * PAIR * PAIR * pairs

    def forward(u_low):
        u = u_low.astype(F32)
        centered = u - jnp.mean(u, -1, keepdims=True)
        inv = lax.rsqrt(jnp.mean(centered * centered, -1, keepdims=True) + norm_eps)
        xhat = centered * inv
        first = (xhat * gain[0] + shift[0]).astype(BF)
        second = (xhat * gain[1] + shift[1]).astype(BF)
        q, k, v, state = call(
            features_kernel,
            pairs,
            [SMEM, SMEM, whole((total, D)), column(D, 3 * PAIR), stacked(1, 3 * PAIR),
             stacked(1, PAIR)] + table_specs,
            [column(total, PAIR)] * 3 + [state_spec],
            [low_shape] * 3 + [state_shape],
            30 * unit,
        )(starts, place_in, first, w_qkv, b_qkv, feat, *tables)
        pre, hidden, mlp, state_in = feed_forward(starts, state, second, w_up, b_up, w_down)
        att_low, att, den = call(
            attend_kernel,
            pairs,
            [SMEM, SMEM] + [column(total, PAIR)] * 3 + [state_spec],
            [column(total, PAIR)] * 3,
            [low_shape, full_shape, full_shape],
            8 * unit,
        )(starts, place_in, q, k, v, state_in)
        part = jnp.dot(att_low, w_dense, preferred_element_type=F32) + mlp
        kept = (xhat, inv, first, second, q, k, v, pre, hidden, att_low, att, den, state_in)
        return part, kept

    def backward(dy, own, kept, want):
        xhat, inv, first, second, q, k, v, pre, hidden, att_low, att, den, state_in = kept
        ga = lax.dot_general(
            dy, w_dense, (((1,), (1,)), ((), ())), preferred_element_type=F32
        ).astype(BF)
        (state,) = call(
            back_state_kernel,
            pairs,
            [SMEM, SMEM] + [column(total, PAIR)] * 4,
            [state_spec],
            [state_shape],
            3 * unit,
        )(starts, place_in, q, ga, att, den)
        out_sum = jnp.sum(own.astype(F32), 0)
        up_size = w_up.shape[1]
        if want and fits_last(up_size, w_qkv, pairs):
            extra = jnp.concatenate([jnp.zeros((up_size,), F32), out_sum])
            extra = jnp.pad(extra, (0, 8 * PANEL - extra.size)).reshape(8, PANEL)
            weights, flat, du = last_call(
                starts,
                (hidden, dy, None, att_low, second, first),
                (q, k, v, ga, att, den, state_in, state, feat) + tables,
                (w_qkv, xhat, inv, gain),
                (pre, w_down, w_up),
                extra,
            )
            g_down, g_dense, g_up, g_qkv = weights
            weights = (g_down, g_up, g_dense, g_qkv)
            ends = up_size // PANEL
            little = (
                flat[:pairs, : 3 * PAIR].reshape(-1),
                flat[:pairs, 3 * PAIR :].reshape(heads, FEAT),
                flat[8 + ends : 8 + ends + out_sum.size // PANEL].reshape(-1),
                flat[8 : 8 + ends].reshape(-1),
                flat[16:20],
            )
            return du, (weights, little)
        grad_pre, grad_second, later = feed_backward(starts, state, dy, pre, w_down, w_up)
        large = ((hidden, dy), (second, grad_pre), (att_low, dy))
        up_sum = jnp.sum(grad_pre.astype(F32), 0) if want else None
        grad_proj, sums = call(
            back_kernel,
            pairs,
            [SMEM, SMEM] + [column(total, PAIR)] * 6
            + [state_spec, state_spec, stacked(1, PAIR)] + table_specs,
            [column(total, 3 * PAIR), stacked(8, PAIR)],
            [shaped((total, pairs * 3 * PAIR), BF), shaped((pairs, 8, PAIR), F32)],
            20 * unit,
        )(starts, place_in, q, k, v, ga, att, den, state_in, later, feat, *tables)
        grad_first = lax.dot_general(
            grad_proj, w_qkv, (((1,), (1,)), ((), ())), preferred_element_type=F32
        )
        both = grad_first * gain[0] + grad_second * gain[1]
        part = inv * (
            both
            - jnp.mean(both, -1, keepdims=True)
            - xhat * jnp.mean(both * xhat, -1, keepdims=True)
        )
        if not want:
            return part, None
        norm_sums = jnp.stack(
            [
                jnp.sum(grad_first * xhat, 0),
                jnp.sum(grad_second * xhat, 0),
                jnp.sum(grad_first, 0),
                jnp.sum(grad_second, 0),
            ]
        )
        norm_sums = lax.psum_scatter(norm_sums, "tp", scatter_dimension=1, tiled=True)
        little = (
            sums[:, 1:4, :].reshape(pairs * 3 * PAIR),
            sums[:, 0, :].reshape(heads, FEAT),
            out_sum,
            up_sum,
            norm_sums,
        )
        products = tuple(dot(a, b, 0, 0).astype(BF) for a, b in large + ((first, grad_proj),))
        weights = [g.astype(F32) for g in lax.psum(products, "ctx")]
        return scatter_tp(part) + own.astype(F32), (weights, lax.psum(little, "ctx"))

    mine = section_inputs[0].reshape(total, width)
    mine_full = gather_tp(mine)
    tp_place = lax.axis_index("tp")

    def own_part(full):
        return lax.dynamic_slice_in_dim(full, tp_place * width, width, 1)

    def next_section(sender, part, base):
        if lax.axis_size("tp") == 2 and total % (16 * STEPS) == 0:
            return hand_over(sender, part, base, mine_full)
        sent = (scatter_tp(part) + base).astype(BF)
        sent = lax.ppermute(sent, "pipe", [(sender, 1 - sender)])
        return jnp.where(section == sender, mine_full, gather_tp(sent))

    wide = mine.astype(F32)
    part, _ = forward(mine_full)
    full_in = next_section(0, part, wide + b_out)
    part, kept = forward(full_in)
    y1 = scatter_tp(part) + own_part(full_in).astype(F32) + b_out
    part, _ = backward(mine_full, mine, kept, False)
    full_grad = next_section(1, part, wide)
    y1, full_grad = lax.optimization_barrier((y1, full_grad))
    own_grad = own_part(full_grad)
    du0, (weights, little) = backward(full_grad, own_grad, kept, True)
    g_down, g_up, g_dense, g_qkv = weights
    g_qkv_bias, g_feat, g_out_bias, g_up_bias, norm_sums = little
    section_ends = jnp.where(section == 0, du0, y1).reshape(1, MB, ROWS, tokens, width)
    grads = (
        norm_sums[:2], norm_sums[2:], g_qkv, g_qkv_bias, g_feat, g_dense, g_out_bias,
        g_up, g_up_bias, g_down,
    )
    return (section_ends,) + tuple(g[None] for g in grads)


def solution(mesh):
    in_specs = (
        P("pipe", None, None, "ctx", "tp"),
        P(),
        P("pipe", None, None),
        P("pipe", None, None),
        P("pipe", None, "tp"),
        P("pipe", "tp"),
        P("pipe", "tp", None),
        P("pipe", "tp", None),
        P("pipe", "tp"),
        P("pipe", None, "tp"),
        P("pipe", "tp"),
        P("pipe", "tp", None),
    )
    out_specs = (
        P("pipe", None, None, "ctx", "tp"),
        P("pipe", None, "tp"),
        P("pipe", None, "tp"),
        P("pipe", None, "tp"),
        P("pipe", "tp"),
        P("pipe", "tp", None),
        P("pipe", "tp", None),
        P("pipe", "tp"),
        P("pipe", None, "tp"),
        P("pipe", "tp"),
        P("pipe", "tp", None),
    )
    return jax.shard_map(local, mesh=mesh, in_specs=in_specs, out_specs=out_specs, check_vma=False)
```

```python
from functools import partial
import math

import jax
import jax.numpy as jnp
from jax import lax
from jax.experimental import pallas as pl
from jax.experimental.pallas import tpu as pltpu
from jax.sharding import PartitionSpec as P

D = 1024
HD = 64
ROT = 16
FEAT = 64
MB = 4
ROWS = 1
NDOC = 4
PAIR = 2 * HD
HELD = HD + 8
TILE = 256
HOP = 3

BF = jnp.bfloat16
F32 = jnp.float32
HIGHEST = lax.Precision.HIGHEST
norm_eps = 1e-05
VMEM_LIMIT = 56 * 1024 * 1024
REDUCE_LIMIT = 60 * 1024 * 1024


def feature_table():
    index_rows = jnp.arange(HD, dtype=jnp.int32)[:, None]
    index_cols = jnp.arange(HD, dtype=jnp.int32)[None, :]
    cosine = jnp.cos(
        math.pi * (index_rows.astype(F32) + 0.5) * index_cols.astype(F32) / HD
    )
    scaling = jnp.where(index_cols == 0, math.sqrt(1.0 / HD), math.sqrt(2.0 / HD))
    lattice_index = (
        (jnp.arange(HD, dtype=jnp.int32)[:, None] + 1)
        * (17 * jnp.arange(FEAT, dtype=jnp.int32)[None, :] + 5)
        % 257
    )
    lattice = math.sqrt(2.0) * jnp.cos(2.0 * math.pi * lattice_index.astype(F32) / 257.0)
    return jnp.dot(cosine * scaling, lattice, precision=HIGHEST) / math.sqrt(HD)


def table_pair():
    table = feature_table()
    zero = jnp.zeros_like(table)
    both = jnp.concatenate(
        [jnp.concatenate([table, zero], 1), jnp.concatenate([zero, table], 1)], 0
    )
    high = lax.reduce_precision(both, 8, 7).astype(BF)
    return high, (both - high.astype(F32)).astype(BF)


def rotary_tables(place, tokens):
    half = ROT // 2
    positions = place * tokens + jnp.arange(tokens, dtype=jnp.int32)
    inv_freq = 10000.0 ** (-(2.0 * jnp.arange(half).astype(F32)) / ROT)
    angles = positions.astype(F32)[:, None] * inv_freq[None, :]
    cos, sin = jnp.cos(angles), jnp.sin(angles)
    rest = jnp.ones((tokens, HD - ROT), F32)
    none = jnp.zeros((tokens, half), F32)
    same = jnp.concatenate([cos, cos, rest], 1)
    down = jnp.concatenate([-sin, none, 0.0 * rest], 1)
    up = jnp.concatenate([none, sin, 0.0 * rest], 1)
    return tuple(jnp.concatenate([t, t], 1) for t in (same, down, up))


def dot(a, b, ca=1, cb=0):
    return lax.dot_general(a, b, (((ca,), (cb,)), ((), ())), preferred_element_type=F32)


def split_dot(a, b, cb=0):
    high = a.astype(BF)
    low = (a - high.astype(F32)).astype(BF)
    return dot(high, b, 1, cb) + dot(low, b, 1, cb)


def lane_masks(rows):
    low = lax.broadcasted_iota(jnp.int32, (rows, PAIR), 1) < HD
    first = low.astype(F32)
    return low, first.astype(BF), (1.0 - first).astype(BF)


def count_starts(starts_ref, row, position):
    total = jnp.int32(0)
    for n in range(NDOC):
        total = total + (starts_ref[row, n] <= position).astype(jnp.int32)
    return total


def seg_grid(starts_ref, row, base, shape, dim):
    position = base + lax.broadcasted_iota(jnp.int32, shape, dim)
    total = jnp.zeros(shape, jnp.int32)
    for n in range(NDOC):
        total = total + (starts_ref[row, n] <= position).astype(jnp.int32)
    return total


def causal_mask(starts_ref, row, base, tokens):
    shape = (tokens, tokens)
    same = seg_grid(starts_ref, row, base, shape, 0) == seg_grid(starts_ref, row, base, shape, 1)
    earlier = lax.broadcasted_iota(jnp.int32, shape, 1) <= lax.broadcasted_iota(
        jnp.int32, shape, 0
    )
    rows = lax.broadcasted_iota(jnp.int32, shape, 0) < tokens // 2
    cols = lax.broadcasted_iota(jnp.int32, shape, 1) < tokens // 2
    mask = same & earlier
    return mask.astype(F32), (mask & (rows == cols)).astype(F32)


def middle_state(starts_ref, row, base, tokens, k, v, state_in, total_in, low):
    half = tokens // 2
    end = count_starts(starts_ref, row, base + half - 1)
    passing = (end == count_starts(starts_ref, row, base - 1)).astype(F32)
    seg = seg_grid(starts_ref, row, base, (half, PAIR), 0)
    key = k[:half] * (seg == end).astype(F32).astype(BF)
    state = passing * state_in + compact(dot(key, v[:half], 0, 0), low)
    total = passing * total_in + jnp.sum(key.astype(F32), 0, keepdims=True)
    later = seg_grid(starts_ref, row, base + half, (half, PAIR), 0)
    return state.astype(BF), total, (later == end).astype(F32)


def entering_mask(starts_ref, row, base, tokens):
    seg = seg_grid(starts_ref, row, base, (tokens, PAIR), 0)
    return (seg == count_starts(starts_ref, row, base - 1)).astype(F32)


def leaving_mask(starts_ref, row, base, tokens):
    seg = seg_grid(starts_ref, row, base, (tokens, PAIR), 0)
    return (seg == count_starts(starts_ref, row, base + tokens - 1)).astype(F32)


def rotate(x, same, down, up):
    half = ROT // 2
    return x * same + pltpu.roll(x, PAIR - half, 1) * down + pltpu.roll(x, half, 1) * up


def rotate_back(x, same, down, up):
    half = ROT // 2
    return x * same + pltpu.roll(x * down, half, 1) + pltpu.roll(x * up, PAIR - half, 1)


def compact(state, low):
    return jnp.where(low[:HD], state[:HD], state[HD:])


def spread(state, first, second):
    return jnp.concatenate([state * first[:HD], state * second[:HD]], 0)


def keep_state(state_ref, row, product, summands, low):
    state_ref[row, 0, :HD] = compact(product, low)
    total = jnp.sum(summands, 0, keepdims=True)
    state_ref[row, 0, HD:] = jnp.broadcast_to(total, (HELD - HD, PAIR))


def features_kernel(
    starts_ref, place_ref, norm_ref, weight_ref, bias_ref, feat_ref,
    same_ref, down_ref, up_ref, high_ref, low_ref,
    q_ref, k_ref, v_ref, state_ref,
):
    tokens = same_ref.shape[0]
    base = place_ref[0, 0] * tokens
    low, first, second = lane_masks(tokens)
    feat = feat_ref[0]
    proj = dot(norm_ref[...], weight_ref[...]) + bias_ref[0]
    c0, c1, c2 = proj[:, :PAIR], proj[:, PAIR : 2 * PAIR], proj[:, 2 * PAIR :]
    left = lane_masks(proj.shape[0])[0]
    v_ref[...] = jnp.where(left, c1, c2).astype(BF)
    same, down, up = (
        jnp.concatenate([t[...]] * (MB * ROWS), 0) for t in (same_ref, down_ref, up_ref)
    )
    query, key = jnp.where(left, c0, c1), pltpu.roll(jnp.where(left, c2, c0), HD, 1)
    for x, out_ref in ((query, q_ref), (key, k_ref)):
        x = rotate(x, same, down, up)
        arg = split_dot(x, high_ref[...]) + dot(x.astype(BF), low_ref[...])
        out_ref[...] = (feat * jnp.exp(arg)).astype(BF)
    for row in range(MB * ROWS):
        here = slice(row * tokens, (row + 1) * tokens)
        leaving = leaving_mask(starts_ref, row, base, tokens)
        key_out = k_ref[here, :] * leaving.astype(BF)
        keep_state(state_ref, row, dot(key_out, v_ref[here, :], 0, 0), key_out.astype(F32), low)


def attend_kernel(
    starts_ref, place_ref, q_ref, k_ref, v_ref, state_ref, low_ref, out_ref, den_ref
):
    tokens = q_ref.shape[0] // (MB * ROWS)
    base = place_ref[0, 0] * tokens
    low, first, second = lane_masks(tokens)
    ones = head_ones()
    for row in range(MB * ROWS):
        here = slice(row * tokens, (row + 1) * tokens)
        q, k, v = q_ref[here, :], k_ref[here, :], v_ref[here, :]
        mask, mask_in = causal_mask(starts_ref, row, base, tokens)
        enter = entering_mask(starts_ref, row, base, tokens)
        carry, total = state_ref[row, 0, :HD], state_ref[row, 0, HD : HD + 1]
        state = carry.astype(BF)
        middle, _, reach = middle_state(starts_ref, row, base, tokens, k, v, carry, total, low)
        half = tokens // 2
        num = jnp.concatenate(
            [
                dot(q[:half] * enter[:half].astype(BF), spread(state, first, second)),
                dot(q[half:] * reach.astype(BF), spread(middle, first, second)),
            ],
            0,
        )
        for head in (first, second):
            scores = dot(q * head, k, 1, 1) * mask_in
            num = num + dot(scores.astype(BF), v * head)
        totals = dot(mask.astype(BF), k) + enter * total
        den = split_dot(q.astype(F32) * totals, ones)
        att = num / den
        low_ref[here, :] = att.astype(BF)
        out_ref[here, :] = att
        den_ref[here, :] = den


def head_ones():
    rows = lax.broadcasted_iota(jnp.int32, (PAIR, PAIR), 0) < HD
    cols = lax.broadcasted_iota(jnp.int32, (PAIR, PAIR), 1) < HD
    return (rows == cols).astype(F32).astype(BF)


def head_spread():
    rows = lax.broadcasted_iota(jnp.int32, (PAIR, 2 * PAIR), 0) < HD
    cols = lax.broadcasted_iota(jnp.int32, (PAIR, 2 * PAIR), 1) < PAIR
    return (rows == cols).astype(F32).astype(BF)


def back_state_kernel(
    starts_ref, place_ref, q_ref, ga_ref, att_ref, den_ref, state_ref
):
    tokens = q_ref.shape[0] // (MB * ROWS)
    base = place_ref[0, 0] * tokens
    low, first, second = lane_masks(tokens)
    ones = head_ones()
    for row in range(MB * ROWS):
        here = slice(row * tokens, (row + 1) * tokens)
        grad_num = (ga_ref[here, :].astype(F32) / den_ref[here, :]).astype(BF)
        grad_den = -split_dot(grad_num.astype(F32) * att_ref[here, :], ones)
        enter = entering_mask(starts_ref, row, base, tokens)
        query = q_ref[here, :] * enter.astype(BF)
        keep_state(state_ref, row, dot(query, grad_num, 0, 0), grad_den * query.astype(F32), low)


def back_unit(starts_ref, row, base, q, k, v, ga, att, den, held, later_held, tables):
    same, down, up, high, low_table = tables
    tokens = q.shape[0]
    half = tokens // 2
    low, first, second = lane_masks(tokens)
    grad_num = (ga.astype(F32) / den).astype(BF)
    both = -split_dot(grad_num.astype(F32) * att, head_spread())
    dens = (both[:, :PAIR], both[:, PAIR:])
    grad_den = jnp.where(low, dens[0], dens[1])
    mask, mask_in = causal_mask(starts_ref, row, base, tokens)
    enter = entering_mask(starts_ref, row, base, tokens)
    leave = leaving_mask(starts_ref, row, base, tokens)
    carry, total = held[:HD], held[HD : HD + 1]
    middle, middle_total, reach = middle_state(
        starts_ref, row, base, tokens, k, v, carry, total, low
    )
    state, middle = spread(carry.astype(BF), first, second), spread(middle, first, second)
    gq = jnp.concatenate(
        [
            enter[:half] * (dot(grad_num[:half], state, 1, 1) + grad_den[:half] * total),
            reach * (dot(grad_num[half:], middle, 1, 1) + grad_den[half:] * middle_total),
        ],
        0,
    )
    later = later_held[:HD]
    later_high = later.astype(BF)
    later_low = spread((later - later_high.astype(F32)).astype(BF), first, second)
    later_high = spread(later_high, first, second)
    gk = leave * (
        dot(v, later_high, 1, 1) + dot(v, later_low, 1, 1) + later_held[HD : HD + 1]
    )
    gv = leave * (dot(k, later_high) + dot(k, later_low))
    for head, grad_head_den in zip((first, second), dens):
        q_head, grad_head = q * head, grad_num * head
        scores = (dot(q_head, k, 1, 1) * mask).astype(BF)
        grad_scores = dot(grad_head, v, 1, 1) + grad_head_den
        gq = gq + dot((grad_scores * mask_in).astype(BF), k * head)
        gk = gk + dot((grad_scores * mask).astype(BF), q_head, 0, 0)
        gv = gv + dot(scores, grad_head, 0, 0)
    arg_grads = (gq * q.astype(F32), gk * k.astype(F32))
    feat_sum = jnp.sum(arg_grads[0] + arg_grads[1], 0, keepdims=True)
    turned = []
    for x in arg_grads:
        x = split_dot(x, high, 1) + dot(x.astype(BF), low_table, 1, 1)
        turned.append(rotate_back(x, same, down, up))
    dq, dk = turned[0], pltpu.roll(turned[1], HD, 1)
    parts = (jnp.where(low, dq, dk), jnp.where(low, gv, dq), jnp.where(low, dk, gv))
    return tuple(part.astype(BF) for part in parts), feat_sum


def back_kernel(
    starts_ref, place_ref, q_ref, k_ref, v_ref, ga_ref, att_ref, den_ref,
    state_ref, later_ref, feat_ref,
    same_ref, down_ref, up_ref, high_ref, low_ref,
    grad_ref, sums_ref,
):
    tokens = q_ref.shape[0] // (MB * ROWS)
    base = place_ref[0, 0] * tokens
    tables = tuple(t[...] for t in (same_ref, down_ref, up_ref, high_ref, low_ref))
    sums_ref[...] = jnp.zeros_like(sums_ref)
    for row in range(MB * ROWS):
        here = slice(row * tokens, (row + 1) * tokens)
        values = [r[here, :] for r in (q_ref, k_ref, v_ref, ga_ref, att_ref, den_ref)]
        parts, feat_sum = back_unit(
            starts_ref, row, base, *values, state_ref[row, 0], later_ref[row, 0], tables
        )
        sums_ref[0, 0:1, :] += feat_sum / feat_ref[0]
        for n, part in enumerate(parts):
            grad_ref[here, n * PAIR : (n + 1) * PAIR] = part
            sums_ref[0, n + 1 : n + 2, :] += jnp.sum(part.astype(F32), 0, keepdims=True)


SMEM = pl.BlockSpec(memory_space=pltpu.SMEM)


def whole(shape):
    return pl.BlockSpec(shape, lambda p: (0,) * len(shape))


def column(rows, width):
    return pl.BlockSpec((rows, width), lambda p: (0, p))


def stacked(*shape):
    return pl.BlockSpec((1,) + shape, lambda p: (p,) + (0,) * len(shape))


def call(kernel, pairs, in_specs, out_specs, out_shape, flops):
    return pl.pallas_call(
        kernel,
        grid=(pairs,),
        in_specs=in_specs,
        out_specs=out_specs,
        out_shape=out_shape,
        compiler_params=pltpu.CompilerParams(vmem_limit_bytes=VMEM_LIMIT),
        cost_estimate=pl.CostEstimate(flops=flops, bytes_accessed=8 << 20, transcendentals=0),
    )


def shaped(shape, dtype):
    return jax.ShapeDtypeStruct(shape, dtype)


CHUNK = 256
PANEL = 512
RING = 4
LAG = 12


def last_kernel(plan, *refs):
    count, terms = plan
    (
        starts_ref, hidden_ref, dy_ref, low_ref, second_any, first_any,
        q_ref, k_ref, v_ref, ga_ref, att_ref, den_ref, state_ref, own_ref, feat_ref,
        same_ref, down_ref, up_ref, high_table_ref, low_table_ref,
        qkv_any, xhat_any, inv_ref, gain_ref, pre_any, w_down_any, w_up_any, small_in_ref,
    ) = refs[:28]
    outs, du_ref = refs[28:33], refs[33]
    (
        proj, small_ref, away_buf, come_buf, norm_sum, norm_away, norm_come,
        sum_send, sum_recv, norm_sem,
        work, give, take, outside, inside,
        give_send, give_recv, part_send, outer_recv, inner_recv, total_send,
        final_send, final_recv, own_sem,
        second_ref, first_ref, qkv_ref, xhat_ref, load_sem,
        grad_pre_ref, grad_second_ref, later_ref, pre_ring, down_ring, up_ring,
        pre_sem, down_sem, up_sem, *link_bufs,
    ) = refs[34:]
    part = give
    later_loads = [
        pltpu.make_async_copy(source, buffer, load_sem.at[n])
        for n, (source, buffer) in enumerate(
            (
                (second_any, second_ref), (first_any, first_ref), (qkv_any, qkv_ref),
                (xhat_any, xhat_ref),
            )
        )
    ]
    factors = (
        hidden_ref, dy_ref, low_ref, dy_ref, second_ref, grad_pre_ref, first_ref, proj
    )
    rows, pairs = state_ref.shape[:2]
    tokens, width = q_ref.shape[0] // rows, du_ref.shape[1]
    units = rows * pairs
    tp = lax.axis_index("tp")
    my_cols = pl.ds(pl.multiple_of(tp * width, width), width)
    half = CHUNK // 2
    place, peers = lax.axis_index("ctx"), lax.axis_size("ctx")
    core, z, chips = place % 2, place // 2, peers // 2
    below = z < chips // 2
    middle = (z == chips // 2 - 1) | (z == chips // 2)
    has_outer = (z != 0) & (z != chips - 1)
    step = jnp.where(below, 2, -2)
    inner, outer, twin = place + step, place - step, place + 1 - 2 * core
    mine = pl.ds(pl.multiple_of(core * half, half), half)
    theirs = pl.ds(pl.multiple_of((1 - core) * half, half), half)

    def remote(src, dst, send, recv, to):
        return pltpu.make_async_remote_copy(
            src_ref=src, dst_ref=dst, send_sem=send, recv_sem=recv,
            device_id={"ctx": to}, device_id_type=pl.DeviceIdType.MESH,
        )

    def to_tp(src, dst, send, recv):
        return pltpu.make_async_remote_copy(
            src_ref=src, dst_ref=dst, send_sem=send, recv_sem=recv,
            device_id={"tp": 1 - tp}, device_id_type=pl.DeviceIdType.MESH,
        )

    def sum_copy(m):
        return to_tp(away_buf.at[m], come_buf.at[m], sum_send.at[m], sum_recv.at[m])

    def norm_copy():
        return to_tp(norm_away, norm_come, norm_sem.at[0], norm_sem.at[1])

    def split_cols(x):
        left, right = x[:, :width], x[:, width:]
        return jnp.where(tp == 0, left, right), jnp.where(tp == 0, right, left)

    def row_block(m):
        return pl.ds(pl.multiple_of(m * tokens, tokens), tokens)

    downs, ups = w_down_any.shape[0] // TILE, w_up_any.shape[0] // TILE
    begin_link, advance, finish_link, _ = exchange(
        False, starts_ref, own_ref, later_ref, link_bufs, tokens, 1, False
    )

    def down_copies(n):
        return (
            pltpu.make_async_copy(w_down_any.at[tile(n)], down_ring.at[n % 2], down_sem.at[n % 2]),
            pltpu.make_async_copy(pre_any.at[:, tile(n)], pre_ring.at[n % 2], pre_sem.at[n % 2]),
        )

    def up_copy(n):
        return pltpu.make_async_copy(w_up_any.at[tile(n)], up_ring.at[n % 2], up_sem.at[n % 2])

    def down_step(n):
        for copy in down_copies(n):
            copy.wait()
        pre = pre_ring[n % 2]
        grad = dot(dy_ref[...], down_ring[n % 2], 1, 1)
        cdf = 0.5 * (1.0 + lax.erf(pre * math.sqrt(0.5)))
        slope = cdf + pre * jnp.exp(-0.5 * pre * pre) * (1.0 / math.sqrt(2.0 * math.pi))
        grad = (grad * slope).astype(BF)
        grad_pre_ref[:, tile(n)] = grad
        per_row = PANEL // TILE
        line = (lax.broadcasted_iota(jnp.int32, (8, TILE), 0) == n // per_row).astype(F32)
        cols = pl.ds(pl.multiple_of(n % per_row * TILE, TILE), TILE)
        small_ref[8:16, cols] += line * jnp.sum(grad.astype(F32), 0, keepdims=True)

        @pl.when(n + 2 < downs)
        def _():
            for copy in down_copies(n + 2):
                copy.start()

    def up_step(n):
        up_copy(n).wait()
        grad_second_ref[:, tile(n)] = dot(grad_pre_ref[...], up_ring[n % 2], 1, 1)

        @pl.when(n + 2 < ups)
        def _():
            up_copy(n + 2).start()

    def attention_step(i):
        p, row = i // rows, i % rows
        here, cols = row_block(row), pl.ds(pl.multiple_of(p * PAIR, PAIR), PAIR)
        tables = tuple(
            t[...] for t in (same_ref, down_ref, up_ref, high_table_ref, low_table_ref)
        )
        values = [r[here, cols] for r in (q_ref, k_ref, v_ref, ga_ref, att_ref, den_ref)]
        parts, feat_sum = back_unit(
            starts_ref, row, place * tokens, *values, state_ref[row, p], later_ref[row, p], tables
        )
        line = (lax.broadcasted_iota(jnp.int32, (8, PAIR), 0) == p).astype(F32)
        small_ref[:8, 3 * PAIR : 4 * PAIR] += line * (feat_sum / feat_ref[p])
        for n, piece in enumerate(parts):
            proj[here, pl.ds(pl.multiple_of((3 * p + n) * PAIR, PAIR), PAIR)] = piece
            small_ref[:8, n * PAIR : (n + 1) * PAIR] += line * jnp.sum(
                piece.astype(F32), 0, keepdims=True
            )

    def norm_step(m):
        here = row_block(m)
        one, two, xhat = dot(proj[here, :], qkv_ref[...], 1, 1), grad_second_ref[here, :], xhat_ref[here, :]
        for n, x in enumerate((one * xhat, two * xhat, one, two)):
            norm_sum[n : n + 1, :] += jnp.sum(x, 0, keepdims=True)
        both = one * gain_ref[0:1, :] + two * gain_ref[1:2, :]
        leaving = inv_ref[here, :] * (
            both
            - jnp.mean(both, -1, keepdims=True)
            - xhat * jnp.mean(both * xhat, -1, keepdims=True)
        )
        kept, sent = split_cols(leaving)
        away_buf[m] = sent.astype(BF)
        sum_copy(m).start()
        du_ref[here, :] = kept + dy_ref[here, my_cols].astype(F32)

    def other_work(step):
        @pl.when(step < downs)
        def _():
            down_step(step)

        @pl.when((step >= downs) & (step < downs + ups))
        def _():
            up_step(step - downs)

        advance(step)
        i = step - downs - ups

        @pl.when(i == 0)
        def _():
            finish_link()

        @pl.when((i >= 0) & (i < units))
        def _():
            attention_step(i)

        @pl.when((i >= units) & (i < units + rows))
        def _():
            norm_step(i - units)

        @pl.when(i == units + rows)
        def _():
            kept, sent = split_cols(norm_sum[...])
            norm_away[...] = sent
            norm_copy().start()
            small_ref[16:24, :] = kept

        late = i - (units + rows + 3)

        @pl.when((late >= 0) & (late < rows))
        def _():
            sum_copy(late).wait()
            du_ref[row_block(late), :] += come_buf[late].astype(F32)

        @pl.when(late == rows)
        def _():
            norm_copy().wait()
            small_ref[16:24, :] += norm_come[...]

    def give_copy(t):
        return remote(give.at[t], take.at[t], give_send.at[t], give_recv.at[t], twin)

    def to_outside(t):
        return remote(part.at[t], outside.at[t], part_send.at[t], outer_recv.at[t], inner)

    def across(t):
        return remote(part.at[t], inside.at[t], part_send.at[t], inner_recv.at[t], inner)

    def outward(t):
        return remote(take.at[t], inside.at[t], total_send.at[t], inner_recv.at[t], outer)

    def final_copy(t, target):
        return remote(take.at[t], target, final_send.at[t], final_recv.at[t], twin)

    def own_copy(t, target):
        return pltpu.make_async_copy(take.at[t], target, own_sem.at[t])

    def block_of(j, panels):
        rows = (j // panels) * CHUNK
        return rows, pl.ds(pl.multiple_of((j % panels) * PANEL, PANEL), PANEL)

    def deliver(t, target):
        final_copy(t, target).start()
        own_copy(t, target).start()

    some_target = outs[-1].at[mine]

    barrier = pltpu.get_barrier_semaphore()
    for peer in ({"ctx": inner}, {"ctx": twin}, {"tp": 1 - tp}):
        pl.semaphore_signal(barrier, inc=1, device_id=peer, device_id_type=pl.DeviceIdType.MESH)

    @pl.when(has_outer)
    def _():
        pl.semaphore_signal(
            barrier, inc=1, device_id={"ctx": outer}, device_id_type=pl.DeviceIdType.MESH
        )

    pl.semaphore_wait(barrier, 3 + has_outer.astype(jnp.int32))
    begin_link()
    for n in range(2):
        for copy in down_copies(n):
            copy.start()
        up_copy(n).start()
    for copy in later_loads:
        copy.start()
    small_ref[...] = jnp.zeros_like(small_ref)
    small_ref[8:16, :] = small_in_ref[...]
    norm_sum[...] = jnp.zeros_like(norm_sum)
    lag = jnp.where(middle, 5, LAG)

    def one(t, carry):
        slot = t % RING
        begin = 0

        @pl.when(t == downs)
        def _():
            for copy in later_loads:
                copy.wait()

        for n, (blocks, panels) in enumerate(terms):
            left, right = factors[2 * n], factors[2 * n + 1]

            @pl.when((t >= begin) & (t < begin + blocks * panels))
            def _(left=left, right=right, panels=panels, begin=begin):
                start, cols = block_of(t - begin, panels)
                rows = pl.ds(pl.multiple_of(start, CHUNK), CHUNK)
                work[slot] = dot(left[:, rows], right[:, cols], 0, 0)

            begin += blocks * panels

        @pl.when(t == begin)
        def _():
            work[slot] = small_ref[...]

        @pl.when(t < count)
        def _():
            give[t] = work[slot, theirs, :].astype(BF)
            give_copy(t).start()

        tb = t - 2

        @pl.when((tb >= 0) & (tb < count))
        def _():
            give_copy(tb).wait()
            total = work[(t + RING - 2) % RING, mine, :] + take[tb].astype(F32)

            @pl.when(has_outer)
            def _():
                to_outside(tb).wait_recv()
                part[tb] = (total + outside[tb].astype(F32)).astype(BF)

            @pl.when(jnp.logical_not(has_outer))
            def _():
                part[tb] = total.astype(BF)

            @pl.when(middle)
            def _():
                across(tb).start()

            @pl.when(jnp.logical_not(middle))
            def _():
                to_outside(tb).start()

        tc = t - lag

        @pl.when((tc >= 0) & (tc < count))
        def _():
            across(tc).wait_recv()

            @pl.when(middle)
            def _():
                take[tc] = (part[tc].astype(F32) + inside[tc].astype(F32)).astype(BF)

            @pl.when(jnp.logical_not(middle))
            def _():
                take[tc] = inside[tc]

            @pl.when(has_outer)
            def _():
                outward(tc).start()

            begin = 0
            for n, (blocks, panels) in enumerate(terms):

                @pl.when((tc >= begin) & (tc < begin + blocks * panels))
                def _(n=n, panels=panels, begin=begin):
                    start, cols = block_of(tc - begin, panels)
                    rows = pl.ds(pl.multiple_of(start + core * half, half), half)
                    deliver(tc, outs[n].at[rows, cols])

                begin += blocks * panels

            @pl.when(tc == begin)
            def _():
                deliver(tc, some_target)

        other_work(t)
        return carry

    lax.fori_loop(0, count + LAG, one, 0)

    def drain(t, carry):
        across(t).wait_send()
        final_copy(t, some_target).wait_send()
        final_copy(t, some_target).wait_recv()
        own_copy(t, some_target).wait()

        @pl.when(has_outer)
        def _():
            outward(t).wait_send()

        return carry

    lax.fori_loop(0, count, drain, 0)


def last_call(starts, factors, attention, norms, feed, small):
    second, first = factors[4:]
    own, qkv = attention[7], norms[0]
    pre, w_down, w_up = feed
    total, width = first.shape[0], D // 2
    rows, tokens = MB * ROWS, total // (MB * ROWS)
    shapes = [
        (factors[0].shape[1], D), (factors[3].shape[1], D), (D, pre.shape[1]), (D, qkv.shape[1])
    ]
    terms = tuple((x // CHUNK, y // PANEL) for x, y in shapes)
    count = sum(x * y for x, y in terms) + 1
    slots = pltpu.VMEM((count, CHUNK // 2, PANEL), BF)
    flat = [factors[0], factors[1], factors[3], second, first]
    flat = flat + list(attention) + list(norms) + list(feed) + [small]
    later = [n for n, x in enumerate(flat) if any(x is y for y in (second, first, qkv, norms[1]))]
    outside = later + [n for n, x in enumerate(flat) if any(x is y for y in feed)]
    dma = pltpu.SemaphoreType.DMA
    *sums, du = pl.pallas_call(
        partial(last_kernel, (count, terms)),
        in_specs=[SMEM] + [ANYWHERE if n in outside else IN_VMEM for n in range(len(flat))],
        out_specs=[ANYWHERE] * 5 + [IN_VMEM],
        out_shape=[shaped(x, BF) for x in shapes]
        + [shaped((CHUNK, PANEL), BF), shaped((total, width), F32)],
        scratch_shapes=[
            pltpu.VMEM((total, qkv.shape[1]), BF),
            pltpu.VMEM((CHUNK, PANEL), F32),
            pltpu.VMEM((rows, tokens, width), BF),
            pltpu.VMEM((rows, tokens, width), BF),
            pltpu.VMEM((8, D), F32),
            pltpu.VMEM((8, width), F32),
            pltpu.VMEM((8, width), F32),
            dma((rows,)), dma((rows,)), dma((2,)),
            pltpu.VMEM((RING, CHUNK, PANEL), F32),
        ]
        + [slots] * 4
        + [dma((count,))] * 9
        + [pltpu.VMEM(flat[n].shape, flat[n].dtype) for n in later]
        + [dma((len(later),))]
        + [
            pltpu.VMEM(pre.shape, BF), pltpu.VMEM((total, D), F32), pltpu.VMEM(own.shape, F32),
            pltpu.VMEM((2, total, TILE), F32), pltpu.VMEM((2, TILE, D), BF),
            pltpu.VMEM((2, TILE, w_up.shape[1]), BF),
            dma((2,)), dma((2,)), dma((2,)),
        ]
        + exchange_scratch(rows, own.shape[1]),
        compiler_params=pltpu.CompilerParams(
            collective_id=0, has_side_effects=True, vmem_limit_bytes=REDUCE_LIMIT
        ),
        cost_estimate=pl.CostEstimate(
            flops=count * 2 * CHUNK * PANEL * 512, bytes_accessed=40 << 20, transcendentals=0
        ),
    )(starts, *flat)
    return [g.astype(F32) for g in sums[:-1]], sums[-1].astype(F32), du


def fits_last(units, qkv, pairs):
    sizes = [(units, D), (pairs * PAIR, D), (D, units), qkv.shape]
    even = all(x % CHUNK == 0 and y % PANEL == 0 for x, y in sizes)
    chunks = [x // CHUNK * (y // PANEL) for x, y in sizes]
    ahead = sum(chunks[:-1])
    rows, chips = MB * ROWS, lax.axis_size("ctx") // 2
    feed = units // TILE + D // TILE
    line = chips % 2 == 0 and lax.axis_size("tp") == 2 and pairs % 2 == 0 and pairs <= 8
    fits = feed + rows * pairs <= ahead and feed + rows * (pairs + 2) + 3 < sum(chunks)
    return even and line and fits and chips + 4 <= feed and units < 8 * PANEL


def exchange(forward, starts_ref, own_ref, got_ref, bufs, tokens, hop=HOP, greeting=True):
    (twin_buf, in_buf, out_buf, back_buf, twin_sem, send_sem, recv_sem, back_send, back_recv) = bufs
    rows, pairs = own_ref.shape[:2]
    part = rows // 2
    chunks, width = in_buf.shape[:2]
    split = pairs // width
    place, chips = lax.axis_index("ctx"), lax.axis_size("ctx") // 2
    core, z = place % 2, place // 2
    away = z if forward else chips - 1 - z
    first, last = away == 0, away == chips - 1
    step = 2 if forward else -2
    twin = place + 1 - 2 * core
    leads = core == (0 if forward else 1)
    lead = 2 * z + (0 if forward else 1)
    other = 2 * z + (1 if forward else 0)

    def remote(src, dst, send, recv, to):
        return pltpu.make_async_remote_copy(
            src_ref=src, dst_ref=dst, send_sem=send, recv_sem=recv,
            device_id={"ctx": to}, device_id_type=pl.DeviceIdType.MESH,
        )

    def twin_copy():
        theirs = own_ref.at[pl.ds((1 - core) * part, part)]
        return remote(theirs, twin_buf, twin_sem.at[0], twin_sem.at[1], twin)

    def onward(j):
        return remote(out_buf.at[j], in_buf.at[j], send_sem.at[j], recv_sem.at[j], place + step)

    def where_of(j):
        return core * part + j // split, pl.ds((j % split) * width, width)

    def back(j):
        row, cols = where_of(j)
        return remote(back_buf.at[j], got_ref.at[row, cols], back_send.at[j], back_recv.at[j], twin)

    def passing(row, at):
        end = count_starts(starts_ref, row, at * tokens + tokens - 1)
        return (end == count_starts(starts_ref, row, at * tokens - 1)).astype(F32)

    def begin():
        if not greeting:
            twin_copy().start()
            return
        barrier = pltpu.get_barrier_semaphore()

        def greet(peer):
            pl.semaphore_signal(
                barrier, inc=1, device_id={"ctx": peer}, device_id_type=pl.DeviceIdType.MESH
            )

        greet(twin)

        @pl.when(jnp.logical_not(first))
        def _():
            greet(place - step)

        pl.semaphore_wait(barrier, 2 - last.astype(jnp.int32))
        twin_copy().start()

    def advance(i):
        @pl.when(i == 0)
        def _():
            twin_copy().wait_recv()

        j = i - hop * away

        @pl.when((j >= 0) & (j < chunks))
        def _():
            row, cols = where_of(j)

            @pl.when(first)
            def _():
                in_buf[j] = jnp.zeros(in_buf.shape[1:], F32)

            @pl.when(jnp.logical_not(first))
            def _():
                onward(j).wait_recv()

            mine, theirs = own_ref[row, cols], twin_buf[j // split, cols]
            entering_lead = in_buf[j]
            entering_other = jnp.where(leads, mine, theirs) + passing(row, lead) * entering_lead

            @pl.when(jnp.logical_not(last))
            def _():
                out_buf[j] = (
                    jnp.where(leads, theirs, mine) + passing(row, other) * entering_other
                )
                onward(j).start()

            got_ref[row, cols] = jnp.where(leads, entering_lead, entering_other)
            back_buf[j] = jnp.where(leads, entering_other, entering_lead)
            back(j).start()

    def finish():
        twin_copy().wait_send()

        def one(j, carry):
            back(j).wait_send()
            back(j).wait_recv()

            @pl.when(jnp.logical_not(last))
            def _():
                onward(j).wait_send()

            return carry

        lax.fori_loop(0, chunks, one, 0)

    return begin, advance, finish, (chips - 1) * hop + chunks


def exchange_scratch(rows, pairs):
    width = pairs // 2 if pairs % 2 == 0 else pairs
    chunks = rows // 2 * (pairs // width)
    one = pltpu.VMEM((chunks, width, HELD, PAIR), F32)
    return [
        pltpu.VMEM((rows // 2, pairs, HELD, PAIR), F32), one, one, one,
        pltpu.SemaphoreType.DMA((2,)),
    ] + [pltpu.SemaphoreType.DMA((chunks,))] * 4


def tile(n):
    return pl.ds(pl.multiple_of(n * TILE, TILE), TILE)


def run_tiles(first_count, first_body, second_count, second_body, loads, link):
    begin, advance, finish, steps = link
    for _, copy in loads[:-1]:
        copy(0).start()
    begin()
    for n, (count, copy) in enumerate(loads):
        start_all(0 if n == len(loads) - 1 else 1, count, copy)
    both = first_count + second_count

    def one(i, carry):
        @pl.when(i < first_count)
        def _():
            first_body(i)

        @pl.when((i >= first_count) & (i < both))
        def _():
            second_body(i - first_count)

        advance(i)
        return carry

    lax.fori_loop(0, max(both, steps), one, 0)
    finish()


def start_all(begin, count, copy):
    def one(n, carry):
        copy(n).start()
        return carry

    lax.fori_loop(begin, count, one, 0)


def feed_forward_kernel(
    tokens, starts_ref, own_ref, norm_ref, up_ref, bias_ref, down_ref,
    pre_ref, hidden_ref, mlp_ref, got_ref,
    up_buf, down_buf, up_sem, down_sem, *bufs,
):
    ups, downs = up_ref.shape[1] // TILE, down_ref.shape[1] // TILE

    def up_copy(n):
        return pltpu.make_async_copy(up_ref.at[:, tile(n)], up_buf.at[:, tile(n)], up_sem.at[n])

    def down_copy(n):
        return pltpu.make_async_copy(
            down_ref.at[:, tile(n)], down_buf.at[:, tile(n)], down_sem.at[n]
        )

    loads = ((ups, up_copy), (downs, down_copy))

    def up(n):
        up_copy(n).wait()
        pre = dot(norm_ref[...], up_buf[:, tile(n)]) + bias_ref[:, tile(n)]
        pre_ref[:, tile(n)] = pre
        hidden = 0.5 * pre * (1.0 + lax.erf(pre * math.sqrt(0.5)))
        hidden_ref[:, tile(n)] = hidden.astype(BF)

    def down(n):
        down_copy(n).wait()
        mlp_ref[:, tile(n)] = dot(hidden_ref[...], down_buf[:, tile(n)])

    link = exchange(True, starts_ref, own_ref, got_ref, bufs, tokens)
    run_tiles(ups, up, downs, down, loads, link)


def feed_backward_kernel(
    tokens, starts_ref, own_ref, grad_ref, pre_ref, down_ref, up_ref,
    grad_pre_ref, grad_norm_ref, got_ref,
    pre_buf, down_buf, up_buf, pre_sem, down_sem, up_sem, *bufs,
):
    downs, ups = down_ref.shape[0] // TILE, up_ref.shape[0] // TILE

    def pre_copy(n):
        return pltpu.make_async_copy(pre_ref.at[:, tile(n)], pre_buf.at[:, tile(n)], pre_sem.at[n])

    def down_copy(n):
        return pltpu.make_async_copy(down_ref.at[tile(n)], down_buf.at[tile(n)], down_sem.at[n])

    def up_copy(n):
        return pltpu.make_async_copy(up_ref.at[tile(n)], up_buf.at[tile(n)], up_sem.at[n])

    loads = ((downs, down_copy), (downs, pre_copy), (ups, up_copy))

    def down(n):
        down_copy(n).wait()
        pre_copy(n).wait()
        grad = dot(grad_ref[...], down_buf[tile(n), :], 1, 1)
        pre = pre_buf[:, tile(n)]
        cdf = 0.5 * (1.0 + lax.erf(pre * math.sqrt(0.5)))
        slope = cdf + pre * jnp.exp(-0.5 * pre * pre) * (1.0 / math.sqrt(2.0 * math.pi))
        grad_pre_ref[:, tile(n)] = (grad * slope).astype(BF)

    def up(n):
        up_copy(n).wait()
        grad_norm_ref[:, tile(n)] = dot(grad_pre_ref[...], up_buf[tile(n), :], 1, 1)

    link = exchange(False, starts_ref, own_ref, got_ref, bufs, tokens)
    run_tiles(downs, down, ups, up, loads, link)


IN_VMEM = pl.BlockSpec(memory_space=pltpu.VMEM)
ANYWHERE = pl.BlockSpec(memory_space=pl.ANY)


def link_call(kernel, number, in_specs, out_shape, scratch, flops):
    return pl.pallas_call(
        kernel,
        in_specs=in_specs,
        out_specs=[IN_VMEM] * len(out_shape),
        out_shape=out_shape,
        scratch_shapes=scratch,
        compiler_params=pltpu.CompilerParams(
            collective_id=number, has_side_effects=True, vmem_limit_bytes=VMEM_LIMIT
        ),
        cost_estimate=pl.CostEstimate(flops=flops, bytes_accessed=16 << 20, transcendentals=0),
    )


def feed_forward(starts, state, norm, w_up, b_up, w_down):
    total, units = norm.shape[0], w_up.shape[1]
    rows, pairs = state.shape[:2]
    return link_call(
        partial(feed_forward_kernel, total // rows),
        1,
        [SMEM, IN_VMEM, IN_VMEM, ANYWHERE, IN_VMEM, ANYWHERE],
        [
            shaped((total, units), F32), shaped((total, units), BF), shaped((total, D), F32),
            shaped(state.shape, F32),
        ],
        [
            pltpu.VMEM(w_up.shape, BF), pltpu.VMEM(w_down.shape, BF),
            pltpu.SemaphoreType.DMA((units // TILE,)), pltpu.SemaphoreType.DMA((D // TILE,)),
        ]
        + exchange_scratch(rows, pairs),
        4 * total * units * D,
    )(starts, state, norm, w_up, b_up.reshape(1, units), w_down)


def feed_backward(starts, state, grad, pre, w_down, w_up):
    total, units = pre.shape
    rows, pairs = state.shape[:2]
    return link_call(
        partial(feed_backward_kernel, total // rows),
        2,
        [SMEM, IN_VMEM, IN_VMEM, ANYWHERE, ANYWHERE, ANYWHERE],
        [shaped((total, units), BF), shaped((total, D), F32), shaped(state.shape, F32)],
        [
            pltpu.VMEM(pre.shape, F32), pltpu.VMEM(w_down.shape, BF), pltpu.VMEM(w_up.shape, BF),
            pltpu.SemaphoreType.DMA((units // TILE,)), pltpu.SemaphoreType.DMA((units // TILE,)),
            pltpu.SemaphoreType.DMA((D // TILE,)),
        ]
        + exchange_scratch(rows, pairs),
        4 * total * units * D,
    )(starts, state, grad, pre, w_down, w_up)


STEPS = 8


def hand_over_kernel(sender, part_ref, base_ref, full_ref, out_ref, *bufs):
    (
        away_buf, sum_buf, pass_buf,
        sum_send, sum_recv, pass_send, pass_recv, spread_send, spread_recv,
    ) = bufs
    width = base_ref.shape[1]
    height = base_ref.shape[0] // STEPS
    pipe, tp = lax.axis_index("pipe"), lax.axis_index("tp")
    sends = pipe == sender
    own = pl.ds(pl.multiple_of(tp * width, width), width)
    away = pl.ds(pl.multiple_of((1 - tp) * width, width), width)

    def rows(c):
        return slice(c * height, (c + 1) * height)

    def remote(src, dst, send, recv, to):
        return pltpu.make_async_remote_copy(
            src_ref=src, dst_ref=dst, send_sem=send, recv_sem=recv,
            device_id=to, device_id_type=pl.DeviceIdType.MESH,
        )

    def sum_copy(c):
        return remote(away_buf.at[c], sum_buf.at[c], sum_send.at[c], sum_recv.at[c], {"tp": 1 - tp})

    def pass_copy(c):
        target = out_ref.at[rows(c), own]
        return remote(pass_buf.at[c], target, pass_send.at[c], pass_recv.at[c], {"pipe": 1 - pipe})

    def spread_copy(c):
        piece = out_ref.at[rows(c), own]
        return remote(piece, piece, spread_send.at[c], spread_recv.at[c], {"tp": 1 - tp})

    barrier = pltpu.get_barrier_semaphore()

    def greet(to):
        pl.semaphore_signal(barrier, inc=1, device_id=to, device_id_type=pl.DeviceIdType.MESH)

    greet({"tp": 1 - tp})

    @pl.when(jnp.logical_not(sends))
    def _():
        greet({"pipe": 1 - pipe})

    pl.semaphore_wait(barrier, 1 + sends.astype(jnp.int32))

    @pl.when(sends)
    def _():
        for c in range(STEPS):
            away_buf[c] = part_ref[rows(c), away].astype(BF)
            sum_copy(c).start()
        for c in range(STEPS):
            out_ref[rows(c), :] = full_ref[rows(c), :]
            sum_copy(c).wait_recv()
            total = part_ref[rows(c), own] + sum_buf[c].astype(F32) + base_ref[rows(c), :]
            pass_buf[c] = total.astype(BF)
            pass_copy(c).start()
        for c in range(STEPS):
            sum_copy(c).wait_send()
            pass_copy(c).wait_send()

    @pl.when(jnp.logical_not(sends))
    def _():
        for c in range(STEPS):
            pass_copy(c).wait_recv()
            spread_copy(c).start()
        for c in range(STEPS):
            spread_copy(c).wait_send()
            spread_copy(c).wait_recv()


def hand_over(sender, part, base, full):
    total, width = base.shape
    piece = pltpu.VMEM((STEPS, total // STEPS, width), BF)
    return pl.pallas_call(
        partial(hand_over_kernel, sender),
        in_specs=[IN_VMEM] * 3,
        out_specs=IN_VMEM,
        out_shape=shaped(full.shape, BF),
        scratch_shapes=[piece] * 3 + [pltpu.SemaphoreType.DMA((STEPS,))] * 6,
        compiler_params=pltpu.CompilerParams(
            collective_id=3 + sender, has_side_effects=True, vmem_limit_bytes=VMEM_LIMIT
        ),
        cost_estimate=pl.CostEstimate(flops=1 << 20, bytes_accessed=8 << 20, transcendentals=0),
    )(part, base, full)


def gather_tp(value):
    if lax.axis_size("tp") != 2:
        return lax.all_gather(value, "tp", axis=1, tiled=True)
    other = lax.ppermute(value, "tp", [(0, 1), (1, 0)])
    return jnp.where(
        lax.axis_index("tp") == 0,
        jnp.concatenate([value, other], 1),
        jnp.concatenate([other, value], 1),
    )


def scatter_tp(value):
    peers = lax.axis_size("tp")
    if peers != 2:
        return lax.psum_scatter(value, "tp", scatter_dimension=1, tiled=True)
    me = lax.axis_index("tp")
    width = value.shape[1] // 2
    left, right = value[:, :width], value[:, width:]
    other = lax.ppermute(jnp.where(me == 0, right, left).astype(BF), "tp", [(0, 1), (1, 0)])
    return jnp.where(me == 0, left, right) + other.astype(F32)


def local(
    section_inputs,
    doc_starts,
    ln_gains,
    ln_shifts,
    qkv_weight,
    qkv_bias,
    feature_weight,
    dense_weight,
    out_bias,
    up_weight,
    up_bias,
    down_weight,
):
    section = lax.axis_index("pipe")
    place = lax.axis_index("ctx")
    width = section_inputs.shape[-1]
    tokens = section_inputs.shape[3]
    rows = MB * ROWS
    total = rows * tokens
    heads = feature_weight.shape[1]
    pairs = heads // 2
    gain, shift = ln_gains[0], ln_shifts[0]
    w_qkv, w_dense, w_up, w_down = qkv_weight[0], dense_weight[0], up_weight[0], down_weight[0]
    b_qkv = qkv_bias[0].reshape(pairs, 1, 3 * PAIR)
    b_up, b_out = up_bias[0], out_bias[0]
    feat = feature_weight[0].reshape(pairs, 1, PAIR)
    starts = doc_starts.reshape(rows, NDOC)
    place_in = place.astype(jnp.int32).reshape(1, 1)
    high, low = table_pair()
    same, down, up = rotary_tables(place, tokens)
    tables = (same, down, up, high, low)
    table_specs = [whole((tokens, PAIR))] * 3 + [whole((PAIR, PAIR))] * 2
    state_shape = shaped((rows, pairs, HELD, PAIR), F32)
    state_spec = pl.BlockSpec((rows, 1, HELD, PAIR), lambda p: (0, p, 0, 0))
    low_shape, full_shape = shaped((total, pairs * PAIR), BF), shaped((total, pairs * PAIR), F32)
    unit = 2 * rows * tokens * PAIR * PAIR * pairs

    def forward(u_low):
        u = u_low.astype(F32)
        centered = u - jnp.mean(u, -1, keepdims=True)
        inv = lax.rsqrt(jnp.mean(centered * centered, -1, keepdims=True) + norm_eps)
        xhat = centered * inv
        first = (xhat * gain[0] + shift[0]).astype(BF)
        second = (xhat * gain[1] + shift[1]).astype(BF)
        q, k, v, state = call(
            features_kernel,
            pairs,
            [SMEM, SMEM, whole((total, D)), column(D, 3 * PAIR), stacked(1, 3 * PAIR),
             stacked(1, PAIR)] + table_specs,
            [column(total, PAIR)] * 3 + [state_spec],
            [low_shape] * 3 + [state_shape],
            30 * unit,
        )(starts, place_in, first, w_qkv, b_qkv, feat, *tables)
        pre, hidden, mlp, state_in = feed_forward(starts, state, second, w_up, b_up, w_down)
        att_low, att, den = call(
            attend_kernel,
            pairs,
            [SMEM, SMEM] + [column(total, PAIR)] * 3 + [state_spec],
            [column(total, PAIR)] * 3,
            [low_shape, full_shape, full_shape],
            8 * unit,
        )(starts, place_in, q, k, v, state_in)
        part = jnp.dot(att_low, w_dense, preferred_element_type=F32) + mlp
        kept = (xhat, inv, first, second, q, k, v, pre, hidden, att_low, att, den, state_in)
        return part, kept

    def backward(dy, own, kept, want):
        xhat, inv, first, second, q, k, v, pre, hidden, att_low, att, den, state_in = kept
        ga = lax.dot_general(
            dy, w_dense, (((1,), (1,)), ((), ())), preferred_element_type=F32
        ).astype(BF)
        (state,) = call(
            back_state_kernel,
            pairs,
            [SMEM, SMEM] + [column(total, PAIR)] * 4,
            [state_spec],
            [state_shape],
            3 * unit,
        )(starts, place_in, q, ga, att, den)
        out_sum = jnp.sum(own.astype(F32), 0)
        up_size = w_up.shape[1]
        if want and fits_last(up_size, w_qkv, pairs):
            extra = jnp.concatenate([jnp.zeros((up_size,), F32), out_sum])
            extra = jnp.pad(extra, (0, 8 * PANEL - extra.size)).reshape(8, PANEL)
            weights, flat, du = last_call(
                starts,
                (hidden, dy, None, att_low, second, first),
                (q, k, v, ga, att, den, state_in, state, feat) + tables,
                (w_qkv, xhat, inv, gain),
                (pre, w_down, w_up),
                extra,
            )
            g_down, g_dense, g_up, g_qkv = weights
            weights = (g_down, g_up, g_dense, g_qkv)
            ends = up_size // PANEL
            little = (
                flat[:pairs, : 3 * PAIR].reshape(-1),
                flat[:pairs, 3 * PAIR :].reshape(heads, FEAT),
                flat[8 + ends : 8 + ends + out_sum.size // PANEL].reshape(-1),
                flat[8 : 8 + ends].reshape(-1),
                flat[16:20],
            )
            return du, (weights, little)
        grad_pre, grad_second, later = feed_backward(starts, state, dy, pre, w_down, w_up)
        large = ((hidden, dy), (second, grad_pre), (att_low, dy))
        up_sum = jnp.sum(grad_pre.astype(F32), 0) if want else None
        grad_proj, sums = call(
            back_kernel,
            pairs,
            [SMEM, SMEM] + [column(total, PAIR)] * 6
            + [state_spec, state_spec, stacked(1, PAIR)] + table_specs,
            [column(total, 3 * PAIR), stacked(8, PAIR)],
            [shaped((total, pairs * 3 * PAIR), BF), shaped((pairs, 8, PAIR), F32)],
            20 * unit,
        )(starts, place_in, q, k, v, ga, att, den, state_in, later, feat, *tables)
        grad_first = lax.dot_general(
            grad_proj, w_qkv, (((1,), (1,)), ((), ())), preferred_element_type=F32
        )
        both = grad_first * gain[0] + grad_second * gain[1]
        part = inv * (
            both
            - jnp.mean(both, -1, keepdims=True)
            - xhat * jnp.mean(both * xhat, -1, keepdims=True)
        )
        if not want:
            return part, None
        norm_sums = jnp.stack(
            [
                jnp.sum(grad_first * xhat, 0),
                jnp.sum(grad_second * xhat, 0),
                jnp.sum(grad_first, 0),
                jnp.sum(grad_second, 0),
            ]
        )
        norm_sums = lax.psum_scatter(norm_sums, "tp", scatter_dimension=1, tiled=True)
        little = (
            sums[:, 1:4, :].reshape(pairs * 3 * PAIR),
            sums[:, 0, :].reshape(heads, FEAT),
            out_sum,
            up_sum,
            norm_sums,
        )
        products = tuple(dot(a, b, 0, 0).astype(BF) for a, b in large + ((first, grad_proj),))
        weights = [g.astype(F32) for g in lax.psum(products, "ctx")]
        return scatter_tp(part) + own.astype(F32), (weights, lax.psum(little, "ctx"))

    mine = section_inputs[0].reshape(total, width)
    mine_full = gather_tp(mine)
    tp_place = lax.axis_index("tp")

    def own_part(full):
        return lax.dynamic_slice_in_dim(full, tp_place * width, width, 1)

    def next_section(sender, part, base):
        if lax.axis_size("tp") == 2 and total % (16 * STEPS) == 0:
            return hand_over(sender, part, base, mine_full)
        sent = (scatter_tp(part) + base).astype(BF)
        sent = lax.ppermute(sent, "pipe", [(sender, 1 - sender)])
        return jnp.where(section == sender, mine_full, gather_tp(sent))

    wide = mine.astype(F32)
    part, _ = forward(mine_full)
    full_in = next_section(0, part, wide + b_out)
    part, kept = forward(full_in)
    y1 = scatter_tp(part) + own_part(full_in).astype(F32) + b_out
    part, _ = backward(mine_full, mine, kept, False)
    full_grad = next_section(1, part, wide)
    y1, full_grad = lax.optimization_barrier((y1, full_grad))
    own_grad = own_part(full_grad)
    du0, (weights, little) = backward(full_grad, own_grad, kept, True)
    g_down, g_up, g_dense, g_qkv = weights
    g_qkv_bias, g_feat, g_out_bias, g_up_bias, norm_sums = little
    section_ends = jnp.where(section == 0, du0, y1).reshape(1, MB, ROWS, tokens, width)
    grads = (
        norm_sums[:2], norm_sums[2:], g_qkv, g_qkv_bias, g_feat, g_dense, g_out_bias,
        g_up, g_up_bias, g_down,
    )
    return (section_ends,) + tuple(g[None] for g in grads)


def solution(mesh):
    in_specs = (
        P("pipe", None, None, "ctx", "tp"),
        P(),
        P("pipe", None, None),
        P("pipe", None, None),
        P("pipe", None, "tp"),
        P("pipe", "tp"),
        P("pipe", "tp", None),
        P("pipe", "tp", None),
        P("pipe", "tp"),
        P("pipe", None, "tp"),
        P("pipe", "tp"),
        P("pipe", "tp", None),
    )
    out_specs = (
        P("pipe", None, None, "ctx", "tp"),
        P("pipe", None, "tp"),
        P("pipe", None, "tp"),
        P("pipe", None, "tp"),
        P("pipe", "tp"),
        P("pipe", "tp", None),
        P("pipe", "tp", None),
        P("pipe", "tp"),
        P("pipe", None, "tp"),
        P("pipe", "tp"),
        P("pipe", "tp", None),
    )
    return jax.shard_map(local, mesh=mesh, in_specs=in_specs, out_specs=out_specs, check_vma=False)
```

```python
from functools import partial
import math

import jax
import jax.numpy as jnp
from jax import lax
from jax.experimental import pallas as pl
from jax.experimental.pallas import tpu as pltpu
from jax.sharding import PartitionSpec as P

D = 1024
HD = 64
ROT = 16
FEAT = 64
MB = 4
ROWS = 1
NDOC = 4
PAIR = 2 * HD
HELD = HD + 8
TILE = 256
HOP = 3

BF = jnp.bfloat16
F32 = jnp.float32
HIGHEST = lax.Precision.HIGHEST
norm_eps = 1e-05
VMEM_LIMIT = 56 * 1024 * 1024
REDUCE_LIMIT = 60 * 1024 * 1024


def feature_table():
    index_rows = jnp.arange(HD, dtype=jnp.int32)[:, None]
    index_cols = jnp.arange(HD, dtype=jnp.int32)[None, :]
    cosine = jnp.cos(
        math.pi * (index_rows.astype(F32) + 0.5) * index_cols.astype(F32) / HD
    )
    scaling = jnp.where(index_cols == 0, math.sqrt(1.0 / HD), math.sqrt(2.0 / HD))
    lattice_index = (
        (jnp.arange(HD, dtype=jnp.int32)[:, None] + 1)
        * (17 * jnp.arange(FEAT, dtype=jnp.int32)[None, :] + 5)
        % 257
    )
    lattice = math.sqrt(2.0) * jnp.cos(2.0 * math.pi * lattice_index.astype(F32) / 257.0)
    return jnp.dot(cosine * scaling, lattice, precision=HIGHEST) / math.sqrt(HD)


def table_pair():
    table = feature_table()
    zero = jnp.zeros_like(table)
    both = jnp.concatenate(
        [jnp.concatenate([table, zero], 1), jnp.concatenate([zero, table], 1)], 0
    )
    high = lax.reduce_precision(both, 8, 7).astype(BF)
    return high, (both - high.astype(F32)).astype(BF)


def rotary_tables(place, tokens):
    half = ROT // 2
    positions = place * tokens + jnp.arange(tokens, dtype=jnp.int32)
    inv_freq = 10000.0 ** (-(2.0 * jnp.arange(half).astype(F32)) / ROT)
    angles = positions.astype(F32)[:, None] * inv_freq[None, :]
    cos, sin = jnp.cos(angles), jnp.sin(angles)
    rest = jnp.ones((tokens, HD - ROT), F32)
    none = jnp.zeros((tokens, half), F32)
    same = jnp.concatenate([cos, cos, rest], 1)
    down = jnp.concatenate([-sin, none, 0.0 * rest], 1)
    up = jnp.concatenate([none, sin, 0.0 * rest], 1)
    return tuple(jnp.concatenate([t, t], 1) for t in (same, down, up))


def dot(a, b, ca=1, cb=0):
    return lax.dot_general(a, b, (((ca,), (cb,)), ((), ())), preferred_element_type=F32)


def split_dot(a, b, cb=0):
    high = a.astype(BF)
    low = (a - high.astype(F32)).astype(BF)
    return dot(high, b, 1, cb) + dot(low, b, 1, cb)


def lane_masks(rows):
    low = lax.broadcasted_iota(jnp.int32, (rows, PAIR), 1) < HD
    first = low.astype(F32)
    return low, first.astype(BF), (1.0 - first).astype(BF)


def count_starts(starts_ref, row, position):
    total = jnp.int32(0)
    for n in range(NDOC):
        total = total + (starts_ref[row, n] <= position).astype(jnp.int32)
    return total


def seg_grid(starts_ref, row, base, shape, dim):
    position = base + lax.broadcasted_iota(jnp.int32, shape, dim)
    total = jnp.zeros(shape, jnp.int32)
    for n in range(NDOC):
        total = total + (starts_ref[row, n] <= position).astype(jnp.int32)
    return total


def causal_mask(starts_ref, row, base, tokens):
    shape = (tokens, tokens)
    same = seg_grid(starts_ref, row, base, shape, 0) == seg_grid(starts_ref, row, base, shape, 1)
    earlier = lax.broadcasted_iota(jnp.int32, shape, 1) <= lax.broadcasted_iota(
        jnp.int32, shape, 0
    )
    rows = lax.broadcasted_iota(jnp.int32, shape, 0) < tokens // 2
    cols = lax.broadcasted_iota(jnp.int32, shape, 1) < tokens // 2
    mask = same & earlier
    return mask.astype(F32), (mask & (rows == cols)).astype(F32)


def middle_state(starts_ref, row, base, tokens, k, v, state_in, total_in, low):
    half = tokens // 2
    end = count_starts(starts_ref, row, base + half - 1)
    passing = (end == count_starts(starts_ref, row, base - 1)).astype(F32)
    seg = seg_grid(starts_ref, row, base, (half, PAIR), 0)
    key = k[:half] * (seg == end).astype(F32).astype(BF)
    state = passing * state_in + compact(dot(key, v[:half], 0, 0), low)
    total = passing * total_in + jnp.sum(key.astype(F32), 0, keepdims=True)
    later = seg_grid(starts_ref, row, base + half, (half, PAIR), 0)
    return state.astype(BF), total, (later == end).astype(F32)


def entering_mask(starts_ref, row, base, tokens):
    seg = seg_grid(starts_ref, row, base, (tokens, PAIR), 0)
    return (seg == count_starts(starts_ref, row, base - 1)).astype(F32)


def leaving_mask(starts_ref, row, base, tokens):
    seg = seg_grid(starts_ref, row, base, (tokens, PAIR), 0)
    return (seg == count_starts(starts_ref, row, base + tokens - 1)).astype(F32)


def rotate(x, same, down, up):
    half = ROT // 2
    return x * same + pltpu.roll(x, PAIR - half, 1) * down + pltpu.roll(x, half, 1) * up


def rotate_back(x, same, down, up):
    half = ROT // 2
    return x * same + pltpu.roll(x * down, half, 1) + pltpu.roll(x * up, PAIR - half, 1)


def compact(state, low):
    return jnp.where(low[:HD], state[:HD], state[HD:])


def spread(state, first, second):
    return jnp.concatenate([state * first[:HD], state * second[:HD]], 0)


def keep_state(state_ref, row, product, summands, low):
    state_ref[row, 0, :HD] = compact(product, low)
    total = jnp.sum(summands, 0, keepdims=True)
    state_ref[row, 0, HD:] = jnp.broadcast_to(total, (HELD - HD, PAIR))


def features_kernel(
    starts_ref, place_ref, norm_ref, weight_ref, bias_ref, feat_ref,
    same_ref, down_ref, up_ref, high_ref, low_ref,
    q_ref, k_ref, v_ref, state_ref,
):
    tokens = same_ref.shape[0]
    base = place_ref[0, 0] * tokens
    low, first, second = lane_masks(tokens)
    feat = feat_ref[0]
    proj = dot(norm_ref[...], weight_ref[...]) + bias_ref[0]
    c0, c1, c2 = proj[:, :PAIR], proj[:, PAIR : 2 * PAIR], proj[:, 2 * PAIR :]
    left = lane_masks(proj.shape[0])[0]
    v_ref[...] = jnp.where(left, c1, c2).astype(BF)
    same, down, up = (
        jnp.concatenate([t[...]] * (MB * ROWS), 0) for t in (same_ref, down_ref, up_ref)
    )
    query, key = jnp.where(left, c0, c1), pltpu.roll(jnp.where(left, c2, c0), HD, 1)
    for x, out_ref in ((query, q_ref), (key, k_ref)):
        x = rotate(x, same, down, up)
        arg = split_dot(x, high_ref[...]) + dot(x.astype(BF), low_ref[...])
        out_ref[...] = (feat * jnp.exp(arg)).astype(BF)
    for row in range(MB * ROWS):
        here = slice(row * tokens, (row + 1) * tokens)
        leaving = leaving_mask(starts_ref, row, base, tokens)
        key_out = k_ref[here, :] * leaving.astype(BF)
        keep_state(state_ref, row, dot(key_out, v_ref[here, :], 0, 0), key_out.astype(F32), low)


def attend_kernel(
    starts_ref, place_ref, q_ref, k_ref, v_ref, state_ref, low_ref, out_ref, den_ref
):
    tokens = q_ref.shape[0] // (MB * ROWS)
    base = place_ref[0, 0] * tokens
    low, first, second = lane_masks(tokens)
    ones = head_ones()
    for row in range(MB * ROWS):
        here = slice(row * tokens, (row + 1) * tokens)
        q, k, v = q_ref[here, :], k_ref[here, :], v_ref[here, :]
        mask, mask_in = causal_mask(starts_ref, row, base, tokens)
        enter = entering_mask(starts_ref, row, base, tokens)
        carry, total = state_ref[row, 0, :HD], state_ref[row, 0, HD : HD + 1]
        state = carry.astype(BF)
        middle, _, reach = middle_state(starts_ref, row, base, tokens, k, v, carry, total, low)
        half = tokens // 2
        num = jnp.concatenate(
            [
                dot(q[:half] * enter[:half].astype(BF), spread(state, first, second)),
                dot(q[half:] * reach.astype(BF), spread(middle, first, second)),
            ],
            0,
        )
        for head in (first, second):
            scores = dot(q * head, k, 1, 1) * mask_in
            num = num + dot(scores.astype(BF), v * head)
        totals = dot(mask.astype(BF), k) + enter * total
        den = split_dot(q.astype(F32) * totals, ones)
        att = num / den
        low_ref[here, :] = att.astype(BF)
        out_ref[here, :] = att
        den_ref[here, :] = den


def head_ones():
    rows = lax.broadcasted_iota(jnp.int32, (PAIR, PAIR), 0) < HD
    cols = lax.broadcasted_iota(jnp.int32, (PAIR, PAIR), 1) < HD
    return (rows == cols).astype(F32).astype(BF)


def head_spread():
    rows = lax.broadcasted_iota(jnp.int32, (PAIR, 2 * PAIR), 0) < HD
    cols = lax.broadcasted_iota(jnp.int32, (PAIR, 2 * PAIR), 1) < PAIR
    return (rows == cols).astype(F32).astype(BF)


def back_state_kernel(
    starts_ref, place_ref, q_ref, ga_ref, att_ref, den_ref, state_ref
):
    tokens = q_ref.shape[0] // (MB * ROWS)
    base = place_ref[0, 0] * tokens
    low, first, second = lane_masks(tokens)
    ones = head_ones()
    for row in range(MB * ROWS):
        here = slice(row * tokens, (row + 1) * tokens)
        grad_num = (ga_ref[here, :].astype(F32) / den_ref[here, :]).astype(BF)
        grad_den = -split_dot(grad_num.astype(F32) * att_ref[here, :], ones)
        enter = entering_mask(starts_ref, row, base, tokens)
        query = q_ref[here, :] * enter.astype(BF)
        keep_state(state_ref, row, dot(query, grad_num, 0, 0), grad_den * query.astype(F32), low)


def back_unit(starts_ref, row, base, q, k, v, ga, att, den, held, later_held, tables):
    same, down, up, high, low_table = tables
    tokens = q.shape[0]
    half = tokens // 2
    low, first, second = lane_masks(tokens)
    grad_num = (ga.astype(F32) / den).astype(BF)
    both = -split_dot(grad_num.astype(F32) * att, head_spread())
    dens = (both[:, :PAIR], both[:, PAIR:])
    grad_den = jnp.where(low, dens[0], dens[1])
    mask, mask_in = causal_mask(starts_ref, row, base, tokens)
    enter = entering_mask(starts_ref, row, base, tokens)
    leave = leaving_mask(starts_ref, row, base, tokens)
    carry, total = held[:HD], held[HD : HD + 1]
    middle, middle_total, reach = middle_state(
        starts_ref, row, base, tokens, k, v, carry, total, low
    )
    state, middle = spread(carry.astype(BF), first, second), spread(middle, first, second)
    gq = jnp.concatenate(
        [
            enter[:half] * (dot(grad_num[:half], state, 1, 1) + grad_den[:half] * total),
            reach * (dot(grad_num[half:], middle, 1, 1) + grad_den[half:] * middle_total),
        ],
        0,
    )
    later = later_held[:HD]
    later_high = later.astype(BF)
    later_low = spread((later - later_high.astype(F32)).astype(BF), first, second)
    later_high = spread(later_high, first, second)
    gk = leave * (
        dot(v, later_high, 1, 1) + dot(v, later_low, 1, 1) + later_held[HD : HD + 1]
    )
    gv = leave * (dot(k, later_high) + dot(k, later_low))
    for head, grad_head_den in zip((first, second), dens):
        q_head, grad_head = q * head, grad_num * head
        scores = (dot(q_head, k, 1, 1) * mask).astype(BF)
        grad_scores = dot(grad_head, v, 1, 1) + grad_head_den
        gq = gq + dot((grad_scores * mask_in).astype(BF), k * head)
        gk = gk + dot((grad_scores * mask).astype(BF), q_head, 0, 0)
        gv = gv + dot(scores, grad_head, 0, 0)
    arg_grads = (gq * q.astype(F32), gk * k.astype(F32))
    feat_sum = jnp.sum(arg_grads[0] + arg_grads[1], 0, keepdims=True)
    turned = []
    for x in arg_grads:
        x = split_dot(x, high, 1) + dot(x.astype(BF), low_table, 1, 1)
        turned.append(rotate_back(x, same, down, up))
    dq, dk = turned[0], pltpu.roll(turned[1], HD, 1)
    parts = (jnp.where(low, dq, dk), jnp.where(low, gv, dq), jnp.where(low, dk, gv))
    return tuple(part.astype(BF) for part in parts), feat_sum


def back_kernel(
    starts_ref, place_ref, q_ref, k_ref, v_ref, ga_ref, att_ref, den_ref,
    state_ref, later_ref, feat_ref,
    same_ref, down_ref, up_ref, high_ref, low_ref,
    grad_ref, sums_ref,
):
    tokens = q_ref.shape[0] // (MB * ROWS)
    base = place_ref[0, 0] * tokens
    tables = tuple(t[...] for t in (same_ref, down_ref, up_ref, high_ref, low_ref))
    sums_ref[...] = jnp.zeros_like(sums_ref)
    for row in range(MB * ROWS):
        here = slice(row * tokens, (row + 1) * tokens)
        values = [r[here, :] for r in (q_ref, k_ref, v_ref, ga_ref, att_ref, den_ref)]
        parts, feat_sum = back_unit(
            starts_ref, row, base, *values, state_ref[row, 0], later_ref[row, 0], tables
        )
        sums_ref[0, 0:1, :] += feat_sum / feat_ref[0]
        for n, part in enumerate(parts):
            grad_ref[here, n * PAIR : (n + 1) * PAIR] = part
            sums_ref[0, n + 1 : n + 2, :] += jnp.sum(part.astype(F32), 0, keepdims=True)


SMEM = pl.BlockSpec(memory_space=pltpu.SMEM)


def whole(shape):
    return pl.BlockSpec(shape, lambda p: (0,) * len(shape))


def column(rows, width):
    return pl.BlockSpec((rows, width), lambda p: (0, p))


def stacked(*shape):
    return pl.BlockSpec((1,) + shape, lambda p: (p,) + (0,) * len(shape))


def call(kernel, pairs, in_specs, out_specs, out_shape, flops):
    return pl.pallas_call(
        kernel,
        grid=(pairs,),
        in_specs=in_specs,
        out_specs=out_specs,
        out_shape=out_shape,
        compiler_params=pltpu.CompilerParams(vmem_limit_bytes=VMEM_LIMIT),
        cost_estimate=pl.CostEstimate(flops=flops, bytes_accessed=8 << 20, transcendentals=0),
    )


def shaped(shape, dtype):
    return jax.ShapeDtypeStruct(shape, dtype)


CHUNK = 256
PANEL = 512
RING = 4
LAG = 10


def last_kernel(plan, *refs):
    count, terms = plan
    (
        starts_ref, hidden_ref, dy_ref, low_ref, second_any, first_any,
        q_ref, k_ref, v_ref, ga_ref, att_ref, den_ref, state_ref, own_ref, feat_ref,
        same_ref, down_ref, up_ref, high_table_ref, low_table_ref,
        qkv_any, xhat_any, inv_ref, gain_ref, pre_any, w_down_any, w_up_any, small_in_ref,
    ) = refs[:28]
    outs, du_ref = refs[28:33], refs[33]
    (
        proj, small_ref, away_buf, come_buf, norm_sum, norm_away, norm_come,
        sum_send, sum_recv, norm_sem,
        work, give, take, outside, inside,
        give_send, give_recv, part_send, outer_recv, inner_recv, total_send,
        final_send, final_recv, own_sem,
        second_ref, first_ref, qkv_ref, xhat_ref, load_sem,
        grad_pre_ref, grad_second_ref, later_ref, pre_ring, down_ring, up_ring,
        pre_sem, down_sem, up_sem, *link_bufs,
    ) = refs[34:]
    part = give
    later_loads = [
        pltpu.make_async_copy(source, buffer, load_sem.at[n])
        for n, (source, buffer) in enumerate(
            (
                (second_any, second_ref), (first_any, first_ref), (qkv_any, qkv_ref),
                (xhat_any, xhat_ref),
            )
        )
    ]
    factors = (
        hidden_ref, dy_ref, low_ref, dy_ref, second_ref, grad_pre_ref, first_ref, proj
    )
    rows, pairs = state_ref.shape[:2]
    tokens, width = q_ref.shape[0] // rows, du_ref.shape[1]
    units = rows * pairs
    tp = lax.axis_index("tp")
    my_cols = pl.ds(pl.multiple_of(tp * width, width), width)
    half = CHUNK // 2
    place, peers = lax.axis_index("ctx"), lax.axis_size("ctx")
    core, z, chips = place % 2, place // 2, peers // 2
    below = z < chips // 2
    middle = (z == chips // 2 - 1) | (z == chips // 2)
    has_outer = (z != 0) & (z != chips - 1)
    step = jnp.where(below, 2, -2)
    inner, outer, twin = place + step, place - step, place + 1 - 2 * core
    mine = pl.ds(pl.multiple_of(core * half, half), half)
    theirs = pl.ds(pl.multiple_of((1 - core) * half, half), half)

    def remote(src, dst, send, recv, to):
        return pltpu.make_async_remote_copy(
            src_ref=src, dst_ref=dst, send_sem=send, recv_sem=recv,
            device_id={"ctx": to}, device_id_type=pl.DeviceIdType.MESH,
        )

    def to_tp(src, dst, send, recv):
        return pltpu.make_async_remote_copy(
            src_ref=src, dst_ref=dst, send_sem=send, recv_sem=recv,
            device_id={"tp": 1 - tp}, device_id_type=pl.DeviceIdType.MESH,
        )

    def sum_copy(m):
        return to_tp(away_buf.at[m], come_buf.at[m], sum_send.at[m], sum_recv.at[m])

    def norm_copy():
        return to_tp(norm_away, norm_come, norm_sem.at[0], norm_sem.at[1])

    def split_cols(x):
        left, right = x[:, :width], x[:, width:]
        return jnp.where(tp == 0, left, right), jnp.where(tp == 0, right, left)

    def row_block(m):
        return pl.ds(pl.multiple_of(m * tokens, tokens), tokens)

    downs, ups = w_down_any.shape[0] // TILE, w_up_any.shape[0] // TILE
    begin_link, advance, finish_link, _ = exchange(
        False, starts_ref, own_ref, later_ref, link_bufs, tokens, 1, False
    )

    def down_copies(n):
        return (
            pltpu.make_async_copy(w_down_any.at[tile(n)], down_ring.at[n % 2], down_sem.at[n % 2]),
            pltpu.make_async_copy(pre_any.at[:, tile(n)], pre_ring.at[n % 2], pre_sem.at[n % 2]),
        )

    def up_copy(n):
        return pltpu.make_async_copy(w_up_any.at[tile(n)], up_ring.at[n % 2], up_sem.at[n % 2])

    def down_step(n):
        for copy in down_copies(n):
            copy.wait()
        pre = pre_ring[n % 2]
        grad = dot(dy_ref[...], down_ring[n % 2], 1, 1)
        cdf = 0.5 * (1.0 + lax.erf(pre * math.sqrt(0.5)))
        slope = cdf + pre * jnp.exp(-0.5 * pre * pre) * (1.0 / math.sqrt(2.0 * math.pi))
        grad = (grad * slope).astype(BF)
        grad_pre_ref[:, tile(n)] = grad
        per_row = PANEL // TILE
        line = (lax.broadcasted_iota(jnp.int32, (8, TILE), 0) == n // per_row).astype(F32)
        cols = pl.ds(pl.multiple_of(n % per_row * TILE, TILE), TILE)
        small_ref[8:16, cols] += line * jnp.sum(grad.astype(F32), 0, keepdims=True)

        @pl.when(n + 2 < downs)
        def _():
            for copy in down_copies(n + 2):
                copy.start()

    def up_step(n):
        up_copy(n).wait()
        grad_second_ref[:, tile(n)] = dot(grad_pre_ref[...], up_ring[n % 2], 1, 1)

        @pl.when(n + 2 < ups)
        def _():
            up_copy(n + 2).start()

    def attention_step(i):
        p, row = i // rows, i % rows
        here, cols = row_block(row), pl.ds(pl.multiple_of(p * PAIR, PAIR), PAIR)
        tables = tuple(
            t[...] for t in (same_ref, down_ref, up_ref, high_table_ref, low_table_ref)
        )
        values = [r[here, cols] for r in (q_ref, k_ref, v_ref, ga_ref, att_ref, den_ref)]
        parts, feat_sum = back_unit(
            starts_ref, row, place * tokens, *values, state_ref[row, p], later_ref[row, p], tables
        )
        line = (lax.broadcasted_iota(jnp.int32, (8, PAIR), 0) == p).astype(F32)
        small_ref[:8, 3 * PAIR : 4 * PAIR] += line * (feat_sum / feat_ref[p])
        for n, piece in enumerate(parts):
            proj[here, pl.ds(pl.multiple_of((3 * p + n) * PAIR, PAIR), PAIR)] = piece
            small_ref[:8, n * PAIR : (n + 1) * PAIR] += line * jnp.sum(
                piece.astype(F32), 0, keepdims=True
            )

    def norm_step(m):
        here = row_block(m)
        one, two, xhat = dot(proj[here, :], qkv_ref[...], 1, 1), grad_second_ref[here, :], xhat_ref[here, :]
        for n, x in enumerate((one * xhat, two * xhat, one, two)):
            norm_sum[n : n + 1, :] += jnp.sum(x, 0, keepdims=True)
        both = one * gain_ref[0:1, :] + two * gain_ref[1:2, :]
        leaving = inv_ref[here, :] * (
            both
            - jnp.mean(both, -1, keepdims=True)
            - xhat * jnp.mean(both * xhat, -1, keepdims=True)
        )
        kept, sent = split_cols(leaving)
        away_buf[m] = sent.astype(BF)
        sum_copy(m).start()
        du_ref[here, :] = kept + dy_ref[here, my_cols].astype(F32)

    def other_work(step):
        @pl.when(step < downs)
        def _():
            down_step(step)

        @pl.when((step >= downs) & (step < downs + ups))
        def _():
            up_step(step - downs)

        advance(step)
        i = step - downs - ups

        @pl.when(i == 0)
        def _():
            finish_link()

        @pl.when((i >= 0) & (i < units))
        def _():
            attention_step(i)

        @pl.when((i >= units) & (i < units + rows))
        def _():
            norm_step(i - units)

        @pl.when(i == units + rows)
        def _():
            kept, sent = split_cols(norm_sum[...])
            norm_away[...] = sent
            norm_copy().start()
            small_ref[16:24, :] = kept

        late = i - (units + rows + 3)

        @pl.when((late >= 0) & (late < rows))
        def _():
            sum_copy(late).wait()
            du_ref[row_block(late), :] += come_buf[late].astype(F32)

        @pl.when(late == rows)
        def _():
            norm_copy().wait()
            small_ref[16:24, :] += norm_come[...]

    def give_copy(t):
        return remote(give.at[t], take.at[t], give_send.at[t], give_recv.at[t], twin)

    def to_outside(t):
        return remote(part.at[t], outside.at[t], part_send.at[t], outer_recv.at[t], inner)

    def across(t):
        return remote(part.at[t], inside.at[t], part_send.at[t], inner_recv.at[t], inner)

    def outward(t):
        return remote(take.at[t], inside.at[t], total_send.at[t], inner_recv.at[t], outer)

    def final_copy(t, target):
        return remote(take.at[t], target, final_send.at[t], final_recv.at[t], twin)

    def own_copy(t, target):
        return pltpu.make_async_copy(take.at[t], target, own_sem.at[t])

    def block_of(j, panels):
        rows = (j // panels) * CHUNK
        return rows, pl.ds(pl.multiple_of((j % panels) * PANEL, PANEL), PANEL)

    def deliver(t, target):
        final_copy(t, target).start()
        own_copy(t, target).start()

    some_target = outs[-1].at[mine]

    barrier = pltpu.get_barrier_semaphore()
    for peer in ({"ctx": inner}, {"ctx": twin}, {"tp": 1 - tp}):
        pl.semaphore_signal(barrier, inc=1, device_id=peer, device_id_type=pl.DeviceIdType.MESH)

    @pl.when(has_outer)
    def _():
        pl.semaphore_signal(
            barrier, inc=1, device_id={"ctx": outer}, device_id_type=pl.DeviceIdType.MESH
        )

    pl.semaphore_wait(barrier, 3 + has_outer.astype(jnp.int32))
    begin_link()
    for n in range(2):
        for copy in down_copies(n):
            copy.start()
        up_copy(n).start()
    for copy in later_loads:
        copy.start()
    small_ref[...] = jnp.zeros_like(small_ref)
    small_ref[8:16, :] = small_in_ref[...]
    norm_sum[...] = jnp.zeros_like(norm_sum)
    lag = jnp.where(middle, 4, LAG)

    def one(t, carry):
        slot = t % RING
        begin = 0

        @pl.when(t == downs)
        def _():
            for copy in later_loads:
                copy.wait()

        for n, (blocks, panels) in enumerate(terms):
            left, right = factors[2 * n], factors[2 * n + 1]

            @pl.when((t >= begin) & (t < begin + blocks * panels))
            def _(left=left, right=right, panels=panels, begin=begin):
                start, cols = block_of(t - begin, panels)
                rows = pl.ds(pl.multiple_of(start, CHUNK), CHUNK)
                work[slot] = dot(left[:, rows], right[:, cols], 0, 0)

            begin += blocks * panels

        @pl.when(t == begin)
        def _():
            work[slot] = small_ref[...]

        @pl.when(t < count)
        def _():
            give[t] = work[slot, theirs, :].astype(BF)
            give_copy(t).start()

        tb = t - 2

        @pl.when((tb >= 0) & (tb < count))
        def _():
            give_copy(tb).wait()
            total = work[(t + RING - 2) % RING, mine, :] + take[tb].astype(F32)

            @pl.when(has_outer)
            def _():
                to_outside(tb).wait_recv()
                part[tb] = (total + outside[tb].astype(F32)).astype(BF)

            @pl.when(jnp.logical_not(has_outer))
            def _():
                part[tb] = total.astype(BF)

            @pl.when(middle)
            def _():
                across(tb).start()

            @pl.when(jnp.logical_not(middle))
            def _():
                to_outside(tb).start()

        tc = t - lag

        @pl.when((tc >= 0) & (tc < count))
        def _():
            across(tc).wait_recv()

            @pl.when(middle)
            def _():
                take[tc] = (part[tc].astype(F32) + inside[tc].astype(F32)).astype(BF)

            @pl.when(jnp.logical_not(middle))
            def _():
                take[tc] = inside[tc]

            @pl.when(has_outer)
            def _():
                outward(tc).start()

            begin = 0
            for n, (blocks, panels) in enumerate(terms):

                @pl.when((tc >= begin) & (tc < begin + blocks * panels))
                def _(n=n, panels=panels, begin=begin):
                    start, cols = block_of(tc - begin, panels)
                    rows = pl.ds(pl.multiple_of(start + core * half, half), half)
                    deliver(tc, outs[n].at[rows, cols])

                begin += blocks * panels

            @pl.when(tc == begin)
            def _():
                deliver(tc, some_target)

        other_work(t)
        return carry

    lax.fori_loop(0, count + LAG, one, 0)

    def drain(t, carry):
        across(t).wait_send()
        final_copy(t, some_target).wait_send()
        final_copy(t, some_target).wait_recv()
        own_copy(t, some_target).wait()

        @pl.when(has_outer)
        def _():
            outward(t).wait_send()

        return carry

    lax.fori_loop(0, count, drain, 0)


def last_call(starts, factors, attention, norms, feed, small):
    second, first = factors[4:]
    own, qkv = attention[7], norms[0]
    pre, w_down, w_up = feed
    total, width = first.shape[0], D // 2
    rows, tokens = MB * ROWS, total // (MB * ROWS)
    shapes = [
        (factors[0].shape[1], D), (factors[3].shape[1], D), (D, pre.shape[1]), (D, qkv.shape[1])
    ]
    terms = tuple((x // CHUNK, y // PANEL) for x, y in shapes)
    count = sum(x * y for x, y in terms) + 1
    slots = pltpu.VMEM((count, CHUNK // 2, PANEL), BF)
    flat = [factors[0], factors[1], factors[3], second, first]
    flat = flat + list(attention) + list(norms) + list(feed) + [small]
    later = [n for n, x in enumerate(flat) if any(x is y for y in (second, first, qkv, norms[1]))]
    outside = later + [n for n, x in enumerate(flat) if any(x is y for y in feed)]
    dma = pltpu.SemaphoreType.DMA
    *sums, du = pl.pallas_call(
        partial(last_kernel, (count, terms)),
        in_specs=[SMEM] + [ANYWHERE if n in outside else IN_VMEM for n in range(len(flat))],
        out_specs=[ANYWHERE] * 5 + [IN_VMEM],
        out_shape=[shaped(x, BF) for x in shapes]
        + [shaped((CHUNK, PANEL), BF), shaped((total, width), F32)],
        scratch_shapes=[
            pltpu.VMEM((total, qkv.shape[1]), BF),
            pltpu.VMEM((CHUNK, PANEL), F32),
            pltpu.VMEM((rows, tokens, width), BF),
            pltpu.VMEM((rows, tokens, width), BF),
            pltpu.VMEM((8, D), F32),
            pltpu.VMEM((8, width), F32),
            pltpu.VMEM((8, width), F32),
            dma((rows,)), dma((rows,)), dma((2,)),
            pltpu.VMEM((RING, CHUNK, PANEL), F32),
        ]
        + [slots] * 4
        + [dma((count,))] * 9
        + [pltpu.VMEM(flat[n].shape, flat[n].dtype) for n in later]
        + [dma((len(later),))]
        + [
            pltpu.VMEM(pre.shape, BF), pltpu.VMEM((total, D), F32), pltpu.VMEM(own.shape, F32),
            pltpu.VMEM((2, total, TILE), F32), pltpu.VMEM((2, TILE, D), BF),
            pltpu.VMEM((2, TILE, w_up.shape[1]), BF),
            dma((2,)), dma((2,)), dma((2,)),
        ]
        + exchange_scratch(rows, own.shape[1]),
        compiler_params=pltpu.CompilerParams(
            collective_id=0, has_side_effects=True, vmem_limit_bytes=REDUCE_LIMIT
        ),
        cost_estimate=pl.CostEstimate(
            flops=count * 2 * CHUNK * PANEL * 512, bytes_accessed=40 << 20, transcendentals=0
        ),
    )(starts, *flat)
    return [g.astype(F32) for g in sums[:-1]], sums[-1].astype(F32), du


def fits_last(units, qkv, pairs):
    sizes = [(units, D), (pairs * PAIR, D), (D, units), qkv.shape]
    even = all(x % CHUNK == 0 and y % PANEL == 0 for x, y in sizes)
    chunks = [x // CHUNK * (y // PANEL) for x, y in sizes]
    ahead = sum(chunks[:-1])
    rows, chips = MB * ROWS, lax.axis_size("ctx") // 2
    feed = units // TILE + D // TILE
    line = chips % 2 == 0 and lax.axis_size("tp") == 2 and pairs % 2 == 0 and pairs <= 8
    fits = feed + rows * pairs <= ahead and feed + rows * (pairs + 2) + 3 < sum(chunks)
    return even and line and fits and chips + 4 <= feed and units < 8 * PANEL


def exchange(forward, starts_ref, own_ref, got_ref, bufs, tokens, hop=HOP, greeting=True):
    (twin_buf, in_buf, out_buf, back_buf, twin_sem, send_sem, recv_sem, back_send, back_recv) = bufs
    rows, pairs = own_ref.shape[:2]
    part = rows // 2
    chunks, width = in_buf.shape[:2]
    split = pairs // width
    place, chips = lax.axis_index("ctx"), lax.axis_size("ctx") // 2
    core, z = place % 2, place // 2
    away = z if forward else chips - 1 - z
    first, last = away == 0, away == chips - 1
    step = 2 if forward else -2
    twin = place + 1 - 2 * core
    leads = core == (0 if forward else 1)
    lead = 2 * z + (0 if forward else 1)
    other = 2 * z + (1 if forward else 0)

    def remote(src, dst, send, recv, to):
        return pltpu.make_async_remote_copy(
            src_ref=src, dst_ref=dst, send_sem=send, recv_sem=recv,
            device_id={"ctx": to}, device_id_type=pl.DeviceIdType.MESH,
        )

    def twin_copy():
        theirs = own_ref.at[pl.ds((1 - core) * part, part)]
        return remote(theirs, twin_buf, twin_sem.at[0], twin_sem.at[1], twin)

    def onward(j):
        return remote(out_buf.at[j], in_buf.at[j], send_sem.at[j], recv_sem.at[j], place + step)

    def where_of(j):
        return core * part + j // split, pl.ds((j % split) * width, width)

    def back(j):
        row, cols = where_of(j)
        return remote(back_buf.at[j], got_ref.at[row, cols], back_send.at[j], back_recv.at[j], twin)

    def passing(row, at):
        end = count_starts(starts_ref, row, at * tokens + tokens - 1)
        return (end == count_starts(starts_ref, row, at * tokens - 1)).astype(F32)

    def begin():
        if not greeting:
            twin_copy().start()
            return
        barrier = pltpu.get_barrier_semaphore()

        def greet(peer):
            pl.semaphore_signal(
                barrier, inc=1, device_id={"ctx": peer}, device_id_type=pl.DeviceIdType.MESH
            )

        greet(twin)

        @pl.when(jnp.logical_not(first))
        def _():
            greet(place - step)

        pl.semaphore_wait(barrier, 2 - last.astype(jnp.int32))
        twin_copy().start()

    def advance(i):
        @pl.when(i == 0)
        def _():
            twin_copy().wait_recv()

        j = i - hop * away

        @pl.when((j >= 0) & (j < chunks))
        def _():
            row, cols = where_of(j)

            @pl.when(first)
            def _():
                in_buf[j] = jnp.zeros(in_buf.shape[1:], F32)

            @pl.when(jnp.logical_not(first))
            def _():
                onward(j).wait_recv()

            mine, theirs = own_ref[row, cols], twin_buf[j // split, cols]
            entering_lead = in_buf[j]
            entering_other = jnp.where(leads, mine, theirs) + passing(row, lead) * entering_lead

            @pl.when(jnp.logical_not(last))
            def _():
                out_buf[j] = (
                    jnp.where(leads, theirs, mine) + passing(row, other) * entering_other
                )
                onward(j).start()

            got_ref[row, cols] = jnp.where(leads, entering_lead, entering_other)
            back_buf[j] = jnp.where(leads, entering_other, entering_lead)
            back(j).start()

    def finish():
        twin_copy().wait_send()

        def one(j, carry):
            back(j).wait_send()
            back(j).wait_recv()

            @pl.when(jnp.logical_not(last))
            def _():
                onward(j).wait_send()

            return carry

        lax.fori_loop(0, chunks, one, 0)

    return begin, advance, finish, (chips - 1) * hop + chunks


def exchange_scratch(rows, pairs):
    width = pairs // 2 if pairs % 2 == 0 else pairs
    chunks = rows // 2 * (pairs // width)
    one = pltpu.VMEM((chunks, width, HELD, PAIR), F32)
    return [
        pltpu.VMEM((rows // 2, pairs, HELD, PAIR), F32), one, one, one,
        pltpu.SemaphoreType.DMA((2,)),
    ] + [pltpu.SemaphoreType.DMA((chunks,))] * 4


def tile(n):
    return pl.ds(pl.multiple_of(n * TILE, TILE), TILE)


def run_tiles(first_count, first_body, second_count, second_body, loads, link):
    begin, advance, finish, steps = link
    for _, copy in loads[:-1]:
        copy(0).start()
    begin()
    for n, (count, copy) in enumerate(loads):
        start_all(0 if n == len(loads) - 1 else 1, count, copy)
    both = first_count + second_count

    def one(i, carry):
        @pl.when(i < first_count)
        def _():
            first_body(i)

        @pl.when((i >= first_count) & (i < both))
        def _():
            second_body(i - first_count)

        advance(i)
        return carry

    lax.fori_loop(0, max(both, steps), one, 0)
    finish()


def start_all(begin, count, copy):
    def one(n, carry):
        copy(n).start()
        return carry

    lax.fori_loop(begin, count, one, 0)


def feed_forward_kernel(
    tokens, starts_ref, own_ref, norm_ref, up_ref, bias_ref, down_ref,
    pre_ref, hidden_ref, mlp_ref, got_ref,
    up_buf, down_buf, up_sem, down_sem, *bufs,
):
    ups, downs = up_ref.shape[1] // TILE, down_ref.shape[1] // TILE

    def up_copy(n):
        return pltpu.make_async_copy(up_ref.at[:, tile(n)], up_buf.at[:, tile(n)], up_sem.at[n])

    def down_copy(n):
        return pltpu.make_async_copy(
            down_ref.at[:, tile(n)], down_buf.at[:, tile(n)], down_sem.at[n]
        )

    loads = ((ups, up_copy), (downs, down_copy))

    def up(n):
        up_copy(n).wait()
        pre = dot(norm_ref[...], up_buf[:, tile(n)]) + bias_ref[:, tile(n)]
        pre_ref[:, tile(n)] = pre
        hidden = 0.5 * pre * (1.0 + lax.erf(pre * math.sqrt(0.5)))
        hidden_ref[:, tile(n)] = hidden.astype(BF)

    def down(n):
        down_copy(n).wait()
        mlp_ref[:, tile(n)] = dot(hidden_ref[...], down_buf[:, tile(n)])

    link = exchange(True, starts_ref, own_ref, got_ref, bufs, tokens)
    run_tiles(ups, up, downs, down, loads, link)


def feed_backward_kernel(
    tokens, starts_ref, own_ref, grad_ref, pre_ref, down_ref, up_ref,
    grad_pre_ref, grad_norm_ref, got_ref,
    pre_buf, down_buf, up_buf, pre_sem, down_sem, up_sem, *bufs,
):
    downs, ups = down_ref.shape[0] // TILE, up_ref.shape[0] // TILE

    def pre_copy(n):
        return pltpu.make_async_copy(pre_ref.at[:, tile(n)], pre_buf.at[:, tile(n)], pre_sem.at[n])

    def down_copy(n):
        return pltpu.make_async_copy(down_ref.at[tile(n)], down_buf.at[tile(n)], down_sem.at[n])

    def up_copy(n):
        return pltpu.make_async_copy(up_ref.at[tile(n)], up_buf.at[tile(n)], up_sem.at[n])

    loads = ((downs, down_copy), (downs, pre_copy), (ups, up_copy))

    def down(n):
        down_copy(n).wait()
        pre_copy(n).wait()
        grad = dot(grad_ref[...], down_buf[tile(n), :], 1, 1)
        pre = pre_buf[:, tile(n)]
        cdf = 0.5 * (1.0 + lax.erf(pre * math.sqrt(0.5)))
        slope = cdf + pre * jnp.exp(-0.5 * pre * pre) * (1.0 / math.sqrt(2.0 * math.pi))
        grad_pre_ref[:, tile(n)] = (grad * slope).astype(BF)

    def up(n):
        up_copy(n).wait()
        grad_norm_ref[:, tile(n)] = dot(grad_pre_ref[...], up_buf[tile(n), :], 1, 1)

    link = exchange(False, starts_ref, own_ref, got_ref, bufs, tokens)
    run_tiles(downs, down, ups, up, loads, link)


IN_VMEM = pl.BlockSpec(memory_space=pltpu.VMEM)
ANYWHERE = pl.BlockSpec(memory_space=pl.ANY)


def link_call(kernel, number, in_specs, out_shape, scratch, flops):
    return pl.pallas_call(
        kernel,
        in_specs=in_specs,
        out_specs=[IN_VMEM] * len(out_shape),
        out_shape=out_shape,
        scratch_shapes=scratch,
        compiler_params=pltpu.CompilerParams(
            collective_id=number, has_side_effects=True, vmem_limit_bytes=VMEM_LIMIT
        ),
        cost_estimate=pl.CostEstimate(flops=flops, bytes_accessed=16 << 20, transcendentals=0),
    )


def feed_forward(starts, state, norm, w_up, b_up, w_down):
    total, units = norm.shape[0], w_up.shape[1]
    rows, pairs = state.shape[:2]
    return link_call(
        partial(feed_forward_kernel, total // rows),
        1,
        [SMEM, IN_VMEM, IN_VMEM, ANYWHERE, IN_VMEM, ANYWHERE],
        [
            shaped((total, units), F32), shaped((total, units), BF), shaped((total, D), F32),
            shaped(state.shape, F32),
        ],
        [
            pltpu.VMEM(w_up.shape, BF), pltpu.VMEM(w_down.shape, BF),
            pltpu.SemaphoreType.DMA((units // TILE,)), pltpu.SemaphoreType.DMA((D // TILE,)),
        ]
        + exchange_scratch(rows, pairs),
        4 * total * units * D,
    )(starts, state, norm, w_up, b_up.reshape(1, units), w_down)


def feed_backward(starts, state, grad, pre, w_down, w_up):
    total, units = pre.shape
    rows, pairs = state.shape[:2]
    return link_call(
        partial(feed_backward_kernel, total // rows),
        2,
        [SMEM, IN_VMEM, IN_VMEM, ANYWHERE, ANYWHERE, ANYWHERE],
        [shaped((total, units), BF), shaped((total, D), F32), shaped(state.shape, F32)],
        [
            pltpu.VMEM(pre.shape, F32), pltpu.VMEM(w_down.shape, BF), pltpu.VMEM(w_up.shape, BF),
            pltpu.SemaphoreType.DMA((units // TILE,)), pltpu.SemaphoreType.DMA((units // TILE,)),
            pltpu.SemaphoreType.DMA((D // TILE,)),
        ]
        + exchange_scratch(rows, pairs),
        4 * total * units * D,
    )(starts, state, grad, pre, w_down, w_up)


STEPS = 8


def hand_over_kernel(sender, part_ref, base_ref, full_ref, out_ref, *bufs):
    (
        away_buf, sum_buf, pass_buf,
        sum_send, sum_recv, pass_send, pass_recv, spread_send, spread_recv,
    ) = bufs
    width = base_ref.shape[1]
    height = base_ref.shape[0] // STEPS
    pipe, tp = lax.axis_index("pipe"), lax.axis_index("tp")
    sends = pipe == sender
    own = pl.ds(pl.multiple_of(tp * width, width), width)
    away = pl.ds(pl.multiple_of((1 - tp) * width, width), width)

    def rows(c):
        return slice(c * height, (c + 1) * height)

    def remote(src, dst, send, recv, to):
        return pltpu.make_async_remote_copy(
            src_ref=src, dst_ref=dst, send_sem=send, recv_sem=recv,
            device_id=to, device_id_type=pl.DeviceIdType.MESH,
        )

    def sum_copy(c):
        return remote(away_buf.at[c], sum_buf.at[c], sum_send.at[c], sum_recv.at[c], {"tp": 1 - tp})

    def pass_copy(c):
        target = out_ref.at[rows(c), own]
        return remote(pass_buf.at[c], target, pass_send.at[c], pass_recv.at[c], {"pipe": 1 - pipe})

    def spread_copy(c):
        piece = out_ref.at[rows(c), own]
        return remote(piece, piece, spread_send.at[c], spread_recv.at[c], {"tp": 1 - tp})

    barrier = pltpu.get_barrier_semaphore()

    def greet(to):
        pl.semaphore_signal(barrier, inc=1, device_id=to, device_id_type=pl.DeviceIdType.MESH)

    greet({"tp": 1 - tp})

    @pl.when(jnp.logical_not(sends))
    def _():
        greet({"pipe": 1 - pipe})

    pl.semaphore_wait(barrier, 1 + sends.astype(jnp.int32))

    @pl.when(sends)
    def _():
        for c in range(STEPS):
            away_buf[c] = part_ref[rows(c), away].astype(BF)
            sum_copy(c).start()
        for c in range(STEPS):
            out_ref[rows(c), :] = full_ref[rows(c), :]
            sum_copy(c).wait_recv()
            total = part_ref[rows(c), own] + sum_buf[c].astype(F32) + base_ref[rows(c), :]
            pass_buf[c] = total.astype(BF)
            pass_copy(c).start()
        for c in range(STEPS):
            sum_copy(c).wait_send()
            pass_copy(c).wait_send()

    @pl.when(jnp.logical_not(sends))
    def _():
        for c in range(STEPS):
            pass_copy(c).wait_recv()
            spread_copy(c).start()
        for c in range(STEPS):
            spread_copy(c).wait_send()
            spread_copy(c).wait_recv()


def hand_over(sender, part, base, full):
    total, width = base.shape
    piece = pltpu.VMEM((STEPS, total // STEPS, width), BF)
    return pl.pallas_call(
        partial(hand_over_kernel, sender),
        in_specs=[IN_VMEM] * 3,
        out_specs=IN_VMEM,
        out_shape=shaped(full.shape, BF),
        scratch_shapes=[piece] * 3 + [pltpu.SemaphoreType.DMA((STEPS,))] * 6,
        compiler_params=pltpu.CompilerParams(
            collective_id=3 + sender, has_side_effects=True, vmem_limit_bytes=VMEM_LIMIT
        ),
        cost_estimate=pl.CostEstimate(flops=1 << 20, bytes_accessed=8 << 20, transcendentals=0),
    )(part, base, full)


def gather_tp(value):
    if lax.axis_size("tp") != 2:
        return lax.all_gather(value, "tp", axis=1, tiled=True)
    other = lax.ppermute(value, "tp", [(0, 1), (1, 0)])
    return jnp.where(
        lax.axis_index("tp") == 0,
        jnp.concatenate([value, other], 1),
        jnp.concatenate([other, value], 1),
    )


def scatter_tp(value):
    peers = lax.axis_size("tp")
    if peers != 2:
        return lax.psum_scatter(value, "tp", scatter_dimension=1, tiled=True)
    me = lax.axis_index("tp")
    width = value.shape[1] // 2
    left, right = value[:, :width], value[:, width:]
    other = lax.ppermute(jnp.where(me == 0, right, left).astype(BF), "tp", [(0, 1), (1, 0)])
    return jnp.where(me == 0, left, right) + other.astype(F32)


def local(
    section_inputs,
    doc_starts,
    ln_gains,
    ln_shifts,
    qkv_weight,
    qkv_bias,
    feature_weight,
    dense_weight,
    out_bias,
    up_weight,
    up_bias,
    down_weight,
):
    section = lax.axis_index("pipe")
    place = lax.axis_index("ctx")
    width = section_inputs.shape[-1]
    tokens = section_inputs.shape[3]
    rows = MB * ROWS
    total = rows * tokens
    heads = feature_weight.shape[1]
    pairs = heads // 2
    gain, shift = ln_gains[0], ln_shifts[0]
    w_qkv, w_dense, w_up, w_down = qkv_weight[0], dense_weight[0], up_weight[0], down_weight[0]
    b_qkv = qkv_bias[0].reshape(pairs, 1, 3 * PAIR)
    b_up, b_out = up_bias[0], out_bias[0]
    feat = feature_weight[0].reshape(pairs, 1, PAIR)
    starts = doc_starts.reshape(rows, NDOC)
    place_in = place.astype(jnp.int32).reshape(1, 1)
    high, low = table_pair()
    same, down, up = rotary_tables(place, tokens)
    tables = (same, down, up, high, low)
    table_specs = [whole((tokens, PAIR))] * 3 + [whole((PAIR, PAIR))] * 2
    state_shape = shaped((rows, pairs, HELD, PAIR), F32)
    state_spec = pl.BlockSpec((rows, 1, HELD, PAIR), lambda p: (0, p, 0, 0))
    low_shape, full_shape = shaped((total, pairs * PAIR), BF), shaped((total, pairs * PAIR), F32)
    unit = 2 * rows * tokens * PAIR * PAIR * pairs

    def forward(u_low):
        u = u_low.astype(F32)
        centered = u - jnp.mean(u, -1, keepdims=True)
        inv = lax.rsqrt(jnp.mean(centered * centered, -1, keepdims=True) + norm_eps)
        xhat = centered * inv
        first = (xhat * gain[0] + shift[0]).astype(BF)
        second = (xhat * gain[1] + shift[1]).astype(BF)
        q, k, v, state = call(
            features_kernel,
            pairs,
            [SMEM, SMEM, whole((total, D)), column(D, 3 * PAIR), stacked(1, 3 * PAIR),
             stacked(1, PAIR)] + table_specs,
            [column(total, PAIR)] * 3 + [state_spec],
            [low_shape] * 3 + [state_shape],
            30 * unit,
        )(starts, place_in, first, w_qkv, b_qkv, feat, *tables)
        pre, hidden, mlp, state_in = feed_forward(starts, state, second, w_up, b_up, w_down)
        att_low, att, den = call(
            attend_kernel,
            pairs,
            [SMEM, SMEM] + [column(total, PAIR)] * 3 + [state_spec],
            [column(total, PAIR)] * 3,
            [low_shape, full_shape, full_shape],
            8 * unit,
        )(starts, place_in, q, k, v, state_in)
        part = jnp.dot(att_low, w_dense, preferred_element_type=F32) + mlp
        kept = (xhat, inv, first, second, q, k, v, pre, hidden, att_low, att, den, state_in)
        return part, kept

    def backward(dy, own, kept, want):
        xhat, inv, first, second, q, k, v, pre, hidden, att_low, att, den, state_in = kept
        ga = lax.dot_general(
            dy, w_dense, (((1,), (1,)), ((), ())), preferred_element_type=F32
        ).astype(BF)
        (state,) = call(
            back_state_kernel,
            pairs,
            [SMEM, SMEM] + [column(total, PAIR)] * 4,
            [state_spec],
            [state_shape],
            3 * unit,
        )(starts, place_in, q, ga, att, den)
        out_sum = jnp.sum(own.astype(F32), 0)
        up_size = w_up.shape[1]
        if want and fits_last(up_size, w_qkv, pairs):
            extra = jnp.concatenate([jnp.zeros((up_size,), F32), out_sum])
            extra = jnp.pad(extra, (0, 8 * PANEL - extra.size)).reshape(8, PANEL)
            weights, flat, du = last_call(
                starts,
                (hidden, dy, None, att_low, second, first),
                (q, k, v, ga, att, den, state_in, state, feat) + tables,
                (w_qkv, xhat, inv, gain),
                (pre, w_down, w_up),
                extra,
            )
            g_down, g_dense, g_up, g_qkv = weights
            weights = (g_down, g_up, g_dense, g_qkv)
            ends = up_size // PANEL
            little = (
                flat[:pairs, : 3 * PAIR].reshape(-1),
                flat[:pairs, 3 * PAIR :].reshape(heads, FEAT),
                flat[8 + ends : 8 + ends + out_sum.size // PANEL].reshape(-1),
                flat[8 : 8 + ends].reshape(-1),
                flat[16:20],
            )
            return du, (weights, little)
        grad_pre, grad_second, later = feed_backward(starts, state, dy, pre, w_down, w_up)
        large = ((hidden, dy), (second, grad_pre), (att_low, dy))
        up_sum = jnp.sum(grad_pre.astype(F32), 0) if want else None
        grad_proj, sums = call(
            back_kernel,
            pairs,
            [SMEM, SMEM] + [column(total, PAIR)] * 6
            + [state_spec, state_spec, stacked(1, PAIR)] + table_specs,
            [column(total, 3 * PAIR), stacked(8, PAIR)],
            [shaped((total, pairs * 3 * PAIR), BF), shaped((pairs, 8, PAIR), F32)],
            20 * unit,
        )(starts, place_in, q, k, v, ga, att, den, state_in, later, feat, *tables)
        grad_first = lax.dot_general(
            grad_proj, w_qkv, (((1,), (1,)), ((), ())), preferred_element_type=F32
        )
        both = grad_first * gain[0] + grad_second * gain[1]
        part = inv * (
            both
            - jnp.mean(both, -1, keepdims=True)
            - xhat * jnp.mean(both * xhat, -1, keepdims=True)
        )
        if not want:
            return part, None
        norm_sums = jnp.stack(
            [
                jnp.sum(grad_first * xhat, 0),
                jnp.sum(grad_second * xhat, 0),
                jnp.sum(grad_first, 0),
                jnp.sum(grad_second, 0),
            ]
        )
        norm_sums = lax.psum_scatter(norm_sums, "tp", scatter_dimension=1, tiled=True)
        little = (
            sums[:, 1:4, :].reshape(pairs * 3 * PAIR),
            sums[:, 0, :].reshape(heads, FEAT),
            out_sum,
            up_sum,
            norm_sums,
        )
        products = tuple(dot(a, b, 0, 0).astype(BF) for a, b in large + ((first, grad_proj),))
        weights = [g.astype(F32) for g in lax.psum(products, "ctx")]
        return scatter_tp(part) + own.astype(F32), (weights, lax.psum(little, "ctx"))

    mine = section_inputs[0].reshape(total, width)
    mine_full = gather_tp(mine)
    tp_place = lax.axis_index("tp")

    def own_part(full):
        return lax.dynamic_slice_in_dim(full, tp_place * width, width, 1)

    def next_section(sender, part, base):
        if lax.axis_size("tp") == 2 and total % (16 * STEPS) == 0:
            return hand_over(sender, part, base, mine_full)
        sent = (scatter_tp(part) + base).astype(BF)
        sent = lax.ppermute(sent, "pipe", [(sender, 1 - sender)])
        return jnp.where(section == sender, mine_full, gather_tp(sent))

    wide = mine.astype(F32)
    part, _ = forward(mine_full)
    full_in = next_section(0, part, wide + b_out)
    part, kept = forward(full_in)
    y1 = scatter_tp(part) + own_part(full_in).astype(F32) + b_out
    part, _ = backward(mine_full, mine, kept, False)
    full_grad = next_section(1, part, wide)
    y1, full_grad = lax.optimization_barrier((y1, full_grad))
    own_grad = own_part(full_grad)
    du0, (weights, little) = backward(full_grad, own_grad, kept, True)
    g_down, g_up, g_dense, g_qkv = weights
    g_qkv_bias, g_feat, g_out_bias, g_up_bias, norm_sums = little
    section_ends = jnp.where(section == 0, du0, y1).reshape(1, MB, ROWS, tokens, width)
    grads = (
        norm_sums[:2], norm_sums[2:], g_qkv, g_qkv_bias, g_feat, g_dense, g_out_bias,
        g_up, g_up_bias, g_down,
    )
    return (section_ends,) + tuple(g[None] for g in grads)


def solution(mesh):
    in_specs = (
        P("pipe", None, None, "ctx", "tp"),
        P(),
        P("pipe", None, None),
        P("pipe", None, None),
        P("pipe", None, "tp"),
        P("pipe", "tp"),
        P("pipe", "tp", None),
        P("pipe", "tp", None),
        P("pipe", "tp"),
        P("pipe", None, "tp"),
        P("pipe", "tp"),
        P("pipe", "tp", None),
    )
    out_specs = (
        P("pipe", None, None, "ctx", "tp"),
        P("pipe", None, "tp"),
        P("pipe", None, "tp"),
        P("pipe", None, "tp"),
        P("pipe", "tp"),
        P("pipe", "tp", None),
        P("pipe", "tp", None),
        P("pipe", "tp"),
        P("pipe", None, "tp"),
        P("pipe", "tp"),
        P("pipe", "tp", None),
    )
    return jax.shard_map(local, mesh=mesh, in_specs=in_specs, out_specs=out_specs, check_vma=False)
```
